32 devices in a mesh: seq: 8 (over z, x), ch: 4 (over y, core).
Axes of the slice: x: 2, y: 2, z: 4, core: 2. Of those that a mesh axis runs over, the one named last changes fastest.
Arguments:
- inputs: bfloat16 [8192, 768], P('seq')
- cotangent: bfloat16 [8192, 768], P('seq')
- starts: int32 [8], replicated, may hold values from 1 to 8191, as said below
- master_conv: float32 [3, 768, 384], P(None, 'seq', 'ch'), may hold values from -0.125 to 0.125
- first_conv: float32 [3, 768, 384], P(None, 'seq', 'ch')
- second_conv: float32 [3, 768, 384], P(None, 'seq', 'ch')
- master_point: float32 [384, 768], P('ch', 'seq'), may hold values from -0.3125 to 0.3125
- first_point: float32 [384, 768], P('ch', 'seq')
- second_point: float32 [384, 768], P('ch', 'seq')
- norm_in: float32 [2, 768], replicated
- first_in: float32 [2, 768], replicated
- second_in: float32 [2, 768], replicated
- norm_mid: float32 [2, 384], P(None, 'ch')
- first_mid: float32 [2, 384], P(None, 'ch')
- second_mid: float32 [2, 384], P(None, 'ch')
Outputs:
- block_out: bfloat16 [8192, 768], P('seq')
- input_grad: float32 [8192, 768], P('seq')
- first_conv_new: float32 [3, 768, 384], P(None, 'seq', 'ch')
- second_conv_new: float32 [3, 768, 384], P(None, 'seq', 'ch')
- conv_new: float32 [3, 768, 384], P(None, 'seq', 'ch')
- first_point_new: float32 [384, 768], P('ch', 'seq')
- second_point_new: float32 [384, 768], P('ch', 'seq')
- point_new: float32 [384, 768], P('ch', 'seq')
- first_in_new: float32 [2, 768], replicated
- second_in_new: float32 [2, 768], replicated
- norm_in_new: float32 [2, 768], replicated
- first_mid_new: float32 [2, 384], P(None, 'ch')
- second_mid_new: float32 [2, 384], P(None, 'ch')
- norm_mid_new: float32 [2, 384], P(None, 'ch')
The draws below stay inside these ranges and needn't reach their ends.
Inputs may be any that keep to these rules, and one draw needn't show every extreme that they name: starts[k] = starts[0] + k * 1024, with starts[0] between 1 and min(1024, 1024) - 1.
All inputs are finite; a program needn't handle non-finite values.
Results may differ from the reference program's by a relative error of at most 0.0068.
Values may be sent and summed in bfloat16 or wider, within the bound.
No kernel may reach another device: no remote copies, remote signals or barrier semaphores. Data moves between devices by JAX's collectives and lax.ppermute only.
A program may use at most 64 MiB of HBM per device.

```python
import math
import jax
import jax.numpy as jnp
from jax import lax

C = 768
B = 384
KERNEL_WIDTH = 3
DILATION_BINS = 9
WIN = 1024
STEP = 10
BINS_DEV = 1024
BINS = 8192
NWIN = 8


def rising_rows(fraction, lower):
    return lower + fraction


def first_moment(key, shape, size_grad):
    return jax.random.normal(key, shape, jnp.float32) * (0.1 / 0.9) * size_grad


def second_moment(key, shape, size_grad):
    factor = jnp.exp(jax.random.uniform(key, shape, jnp.float32, math.log(0.5), math.log(8.0)))
    return factor * (0.001 / 0.999) * size_grad * size_grad


def norm_params(key, width):
    key_gain, key_bias = jax.random.split(key, 2)
    gains = jnp.clip(1.0 + 0.15 * jax.random.normal(key_gain, (width,), jnp.float32), 0.4, 1.6)
    biases = 0.3 * jax.random.normal(key_bias, (width,), jnp.float32)
    return jnp.stack([gains, biases])


def draw_inputs(key, part):
    key = jax.random.fold_in(key, 11)
    key_jitter, key_rows, key_cols, key_means = jax.random.split(key, 4)
    fraction = jnp.arange(BINS, dtype=jnp.float32) / BINS
    jitter = jax.random.normal(key_jitter, (BINS, C), jnp.float32)
    rising = rising_rows(fraction, 0.5)
    mean_size = 0.5
    row_scale = jnp.exp(jax.random.uniform(key_rows, (BINS,), jnp.float32, math.log(0.3), math.log(3.0))) * rising
    col_scale = jnp.exp(jax.random.uniform(key_cols, (C,), jnp.float32, math.log(0.5), math.log(2.0)))
    offsets = jax.random.normal(key_means, (C,), jnp.float32) * mean_size
    return (jitter * row_scale[:, None] * col_scale[None, :] + offsets[None, :]).astype(jnp.bfloat16)


def draw_cotangent(key, part):
    key = jax.random.fold_in(key, 12)
    fraction = jnp.arange(BINS, dtype=jnp.float32) / BINS
    jitter = jax.random.normal(key, (BINS, C), jnp.float32)
    rising = rising_rows(fraction, 0.5)
    return (jitter * rising[:, None]).astype(jnp.bfloat16)


def draw_starts(key, part):
    key = jax.random.fold_in(key, 13)
    phase = jax.random.randint(key, (), 1, min(BINS_DEV, WIN), jnp.int32)
    return phase + WIN * jnp.arange(NWIN, dtype=jnp.int32)


def draw_first_conv(key, part):
    key = jax.random.fold_in(key, 14)
    return first_moment(key, (KERNEL_WIDTH, C, B), 0.8 * BINS ** 0.5)


def draw_second_conv(key, part):
    key = jax.random.fold_in(key, 15)
    return second_moment(key, (KERNEL_WIDTH, C, B), 0.8 * BINS ** 0.5)


def draw_first_point(key, part):
    key = jax.random.fold_in(key, 16)
    return first_moment(key, (B, C), 0.7 * BINS ** 0.5)


def draw_second_point(key, part):
    key = jax.random.fold_in(key, 17)
    return second_moment(key, (B, C), 0.7 * BINS ** 0.5)


def draw_norm_in(key, part):
    key = jax.random.fold_in(key, 18)
    return norm_params(key, C)


def draw_first_in(key, part):
    key = jax.random.fold_in(key, 19)
    return first_moment(key, (2, C), 0.6 * BINS ** 0.5)


def draw_second_in(key, part):
    key = jax.random.fold_in(key, 20)
    return second_moment(key, (2, C), 0.6 * BINS ** 0.5)


def draw_norm_mid(key, part):
    key = jax.random.fold_in(key, 21)
    return norm_params(key, B)


def draw_first_mid(key, part):
    key = jax.random.fold_in(key, 22)
    return first_moment(key, (2, B), 0.6 * BINS ** 0.5)


def draw_second_mid(key, part):
    key = jax.random.fold_in(key, 23)
    return second_moment(key, (2, B), 0.6 * BINS ** 0.5)


def block_levels(key, shape, cuts, smallest, high):
    factor_of = 1.0
    for axis_at, blocks in cuts:
        heights = jax.random.uniform(jax.random.fold_in(jax.random.fold_in(key, 6), axis_at), (blocks,), jnp.float32, smallest / len(cuts), high / len(cuts))
        factor_of = factor_of * jnp.repeat(jnp.exp(heights), shape[axis_at] // blocks).reshape((-1,) + (1,) * (len(shape) - 1 - axis_at))
    return factor_of


def centred(own_key, shape, scale, most, pieces=(), kind=jnp.bfloat16):
    gain = block_levels(own_key, shape, pieces, -0.22, 0.18) if pieces else 1.0
    array = jax.random.normal(own_key, shape, jnp.float32) * scale * gain
    return jnp.minimum(jnp.maximum(array, -most), most).astype(kind)


def setup_inputs(seed: int = 0) -> dict:
    key_of = jax.random.split(jax.random.key(seed), 16)
    return {
        "inputs": draw_inputs(jax.random.fold_in(key_of[15], 71), 0),
        "cotangent": draw_cotangent(jax.random.fold_in(key_of[15], 71), 0),
        "starts": draw_starts(jax.random.fold_in(key_of[15], 71), 0),
        "master_conv": centred(key_of[3], (KERNEL_WIDTH, C, B), (KERNEL_WIDTH * C) ** -0.5, 0.125, ((1, 8), (2, 4)), jnp.float32),
        "first_conv": draw_first_conv(jax.random.fold_in(key_of[15], 71), 0),
        "second_conv": draw_second_conv(jax.random.fold_in(key_of[15], 71), 0),
        "master_point": centred(key_of[6], (B, C), B ** -0.5, 0.3125, ((0, 4), (1, 8)), jnp.float32),
        "first_point": draw_first_point(jax.random.fold_in(key_of[15], 71), 0),
        "second_point": draw_second_point(jax.random.fold_in(key_of[15], 71), 0),
        "norm_in": draw_norm_in(jax.random.fold_in(key_of[15], 71), 0),
        "first_in": draw_first_in(jax.random.fold_in(key_of[15], 71), 0),
        "second_in": draw_second_in(jax.random.fold_in(key_of[15], 71), 0),
        "norm_mid": draw_norm_mid(jax.random.fold_in(key_of[15], 71), 0),
        "first_mid": draw_first_mid(jax.random.fold_in(key_of[15], 71), 0),
        "second_mid": draw_second_mid(jax.random.fold_in(key_of[15], 71), 0),
    }


NORM_EPS = 1e-05
ADAM_EPS = 1e-08
BETA_ONE = 0.9
BETA_TWO = 0.999
RATE_WEIGHT = 0.05
RATE_NORM = 0.5
DECAY_WEIGHT = 0.01

@jax.custom_vjp
def low(v):
    return lax.optimization_barrier(v.astype(jnp.bfloat16)).astype(jnp.float32)

@jax.custom_vjp
def low_back(v):
    return v

def low_keep(v):
    return (low(v), None)

def low_pass(kept, grad):
    return (grad,)

def back_keep(v):
    return (v, None)

def back_low(kept, grad):
    return (low(grad),)
low.defvjp(low_keep, low_pass)
low_back.defvjp(back_keep, back_low)

def window_masks(starts, bin_count):
    positions = jnp.arange(bin_count, dtype=jnp.int32)

    def window_of(neighbors):
        return lax.optimization_barrier(jnp.sum((neighbors[:, None] >= starts[None, :]).astype(jnp.int32), axis=1))
    own_window = window_of(positions)
    mask_list = []
    for kernel_index in range(KERNEL_WIDTH):
        bin_shift = (kernel_index - KERNEL_WIDTH // 2) * DILATION_BINS
        neighbors = positions + bin_shift
        inside = (neighbors >= 0) & (neighbors < bin_count) & (window_of(neighbors) == own_window)
        mask_list.append(inside.astype(jnp.float32))
    return mask_list

def shifted(values, bin_shift):
    receptive_span = DILATION_BINS * (KERNEL_WIDTH // 2)
    padded = jnp.pad(values, ((receptive_span, receptive_span), (0, 0)))
    return padded[receptive_span + bin_shift:receptive_span + bin_shift + values.shape[0]]

def batch_norm(values, params):
    average = lax.optimization_barrier(jnp.mean(values, axis=0))
    variance = lax.optimization_barrier(jnp.mean(values * values, axis=0)) - average * average
    centered = (values - average) * lax.rsqrt(variance + NORM_EPS)
    return centered * params[0] + params[1]

def forward(values, norm_in, master_conv, norm_mid, master_point, mask_list):
    hidden_in = low(jax.nn.gelu(batch_norm(values, norm_in)))
    conv_w = low(master_conv)
    conv_out = jnp.zeros((values.shape[0], master_conv.shape[2]), jnp.float32)
    for kernel_index in range(KERNEL_WIDTH):
        bin_shift = (kernel_index - KERNEL_WIDTH // 2) * DILATION_BINS
        product = jnp.dot(shifted(hidden_in, bin_shift), conv_w[kernel_index], preferred_element_type=jnp.float32, precision=lax.Precision.HIGHEST)
        conv_out = conv_out + mask_list[kernel_index][:, None] * product
    conv_out = low_back(conv_out)
    hidden_mid = low(jax.nn.gelu(batch_norm(conv_out, norm_mid)))
    point_w = low(master_point)
    return values + jnp.dot(hidden_mid, point_w, preferred_element_type=jnp.float32, precision=lax.Precision.HIGHEST)

def adamw(weights_old, first_moment_state, second_mom, gradient, step_rate, decay_rate):
    first_next = BETA_ONE * first_moment_state + (1.0 - BETA_ONE) * gradient
    second_next = BETA_TWO * second_mom + (1.0 - BETA_TWO) * gradient * gradient
    corrected = first_next / (1.0 - BETA_ONE ** STEP) / (jnp.sqrt(second_next / (1.0 - BETA_TWO ** STEP)) + ADAM_EPS)
    weights_new = weights_old - step_rate * (corrected + decay_rate * weights_old)
    return (first_next, second_next, weights_new)

def reference(inputs, cotangent, starts, master_conv, first_conv, second_conv, master_point, first_point, second_point, norm_in, first_in, second_in, norm_mid, first_mid, second_mid):
    values = inputs.astype(jnp.float32)
    mask_list = window_masks(starts, values.shape[0])

    def closed(a_values, a_norm_in, a_conv, a_norm_mid, a_point):
        return forward(a_values, a_norm_in, a_conv, a_norm_mid, a_point, mask_list)
    result, pullback = jax.vjp(closed, values, norm_in, master_conv, norm_mid, master_point)
    grad_x, grad_in, grad_conv, grad_mid, grad_point = pullback(cotangent.astype(jnp.float32))
    conv_first, conv_second, conv_next = adamw(master_conv, first_conv, second_conv, grad_conv, RATE_WEIGHT, DECAY_WEIGHT)
    point_first, point_second, point_next = adamw(master_point, first_point, second_point, grad_point, RATE_WEIGHT, DECAY_WEIGHT)
    in_first, in_second, in_next = adamw(norm_in, first_in, second_in, grad_in, RATE_NORM, 0.0)
    mid_first, mid_second, mid_next = adamw(norm_mid, first_mid, second_mid, grad_mid, RATE_NORM, 0.0)
    return (result.astype(jnp.bfloat16), grad_x, conv_first, conv_second, conv_next, point_first, point_second, point_next, in_first, in_second, in_next, mid_first, mid_second, mid_next)
```

```python
import jax
import jax.numpy as jnp
from jax import lax
from jax.sharding import PartitionSpec as P

KERNEL_WIDTH = 3
DILATION_BINS = 9
STEP = 10


NORM_EPS = 1e-05
ADAM_EPS = 1e-08
BETA_ONE = 0.9
BETA_TWO = 0.999
RATE_WEIGHT = 0.05
RATE_NORM = 0.5
DECAY_WEIGHT = 0.01


def gather_blocks(x, axis):
    size, own = lax.axis_size(axis), lax.axis_index(axis)
    blocks = x[None]
    reach = size // 2
    while reach:
        other = lax.ppermute(blocks, axis, [(i, i ^ reach) for i in range(size)])
        high = (own // reach) % 2 == 1
        pair = [jnp.where(high, other, blocks), jnp.where(high, blocks, other)]
        blocks = jnp.stack(pair, axis=1).reshape((-1,) + x.shape)
        reach //= 2
    return blocks


def scatter_sum(blocks, axis):
    size, own = lax.axis_size(axis), lax.axis_index(axis)
    reach = 1
    while reach < size:
        pairs = blocks.reshape((-1, 2) + blocks.shape[1:])
        high = (own // reach) % 2 == 1
        kept = jnp.where(high, pairs[:, 1], pairs[:, 0])
        sent = jnp.where(high, pairs[:, 0], pairs[:, 1]).astype(jnp.bfloat16)
        got = lax.ppermute(sent, axis, [(i, i ^ reach) for i in range(size)])
        blocks = kept + got.astype(jnp.float32)
        reach *= 2
    return blocks[0]


def each(x, axes):
    size = lax.axis_size(axes)
    copies = jnp.broadcast_to(x[None], (size,) + x.shape)
    return lax.all_to_all(copies, axes, 0, 0, tiled=True)


def moments(total, bin_count):
    average = total[0] / bin_count
    variance = total[1] / bin_count - average * average
    return average, lax.rsqrt(variance + NORM_EPS)


def window_masks(starts, positions, bin_count):

    def window_of(neighbors):
        return jnp.sum((neighbors[:, None] >= starts[None, :]).astype(jnp.int32), axis=1)

    own_window = window_of(positions)
    mask_list = []
    for kernel_index in range(KERNEL_WIDTH):
        bin_shift = (kernel_index - KERNEL_WIDTH // 2) * DILATION_BINS
        neighbors = positions + bin_shift
        inside = (neighbors >= 0) & (neighbors < bin_count) & (window_of(neighbors) == own_window)
        mask_list.append(inside.astype(jnp.float32))
    return mask_list


def adamw(weights_old, first_moment_state, second_mom, gradient, step_rate, decay_rate):
    first_next = BETA_ONE * first_moment_state + (1.0 - BETA_ONE) * gradient
    second_next = BETA_TWO * second_mom + (1.0 - BETA_TWO) * gradient * gradient
    corrected = (
        first_next
        / (1.0 - BETA_ONE**STEP)
        / (jnp.sqrt(second_next / (1.0 - BETA_TWO**STEP)) + ADAM_EPS)
    )
    weights_new = weights_old - step_rate * (corrected + decay_rate * weights_old)
    return (first_next, second_next, weights_new)


def shards(
    inputs, cotangent, starts,
    master_conv, first_conv, second_conv,
    master_point, first_point, second_point,
    norm_in, first_in, second_in,
    norm_mid, first_mid, second_mid,
):
    rows, width = inputs.shape
    seq_size, ch_size = lax.axis_size("seq"), lax.axis_size("ch")
    own_ch = lax.axis_index("ch")
    bin_count = rows * seq_size
    span = DILATION_BINS * (KERNEL_WIDTH // 2)
    slim = master_conv.shape[2]
    mid = slim * ch_size
    shifts = [(j - KERNEL_WIDTH // 2) * DILATION_BINS for j in range(KERNEL_WIDTH)]

    up = [(i, i + 1) for i in range(seq_size - 1)]
    down = [(j, i) for i, j in up]
    last = jnp.concatenate([inputs[rows - 2 * span :], cotangent[rows - span :]])
    first = jnp.concatenate([inputs[: 2 * span], cotangent[:span]])
    before = lax.ppermute(last, "seq", up)
    after = lax.ppermute(first, "seq", down)
    x_ext = jnp.concatenate([before[: 2 * span], inputs, after[: 2 * span]]).astype(jnp.float32)
    cot_ext = jnp.concatenate([before[2 * span :], cotangent, after[2 * span :]])

    positions = lax.axis_index("seq") * rows - span + jnp.arange(rows + 2 * span, dtype=jnp.int32)
    masks = window_masks(starts, positions, bin_count)
    masks = [mask * ((positions >= 0) & (positions < bin_count)) for mask in masks]

    conv_low = jnp.concatenate(list(master_conv.astype(jnp.bfloat16)), axis=1)
    conv_own = gather_blocks(conv_low, "seq").reshape(width, KERNEL_WIDTH * slim)
    point_own = gather_blocks(master_point.astype(jnp.bfloat16).T, "seq").reshape(width, slim)

    values = inputs.astype(jnp.float32)
    total_in = each(jnp.stack([jnp.sum(values, 0), jnp.sum(values * values, 0)]), "seq").sum(0)
    mean_in, root_in = moments(total_in, bin_count)
    pre_in = (x_ext - mean_in) * root_in * norm_in[0] + norm_in[1]
    hidden_in = jax.nn.gelu(pre_in).astype(jnp.bfloat16)

    products = jnp.dot(hidden_in, conv_own, preferred_element_type=jnp.float32)
    conv_out = 0.0
    for j, shift in enumerate(shifts):
        part = products[span + shift : span + shift + rows + 2 * span, j * slim : (j + 1) * slim]
        conv_out = conv_out + part * masks[j][:, None]
    mine = conv_out[span : span + rows]
    sums = jnp.stack([jnp.sum(mine, 0), jnp.sum(mine * mine, 0)])
    local_mean = sums[0] / rows
    conv_rest = (conv_out - local_mean).astype(jnp.bfloat16)

    all_rest = gather_blocks(conv_rest, "ch")
    all_rest = jnp.concatenate([all_rest[q] for q in range(ch_size)], axis=1)
    all_sums = each(sums, ("seq", "ch")).reshape(seq_size, ch_size, 2, slim)
    all_sums = jnp.transpose(all_sums, (0, 2, 1, 3)).reshape(seq_size, 2, mid)
    mean_mid, root_mid = moments(jnp.sum(all_sums, 0), bin_count)
    local_mean_all = lax.dynamic_index_in_dim(all_sums, lax.axis_index("seq"), 0, False)[0] / rows

    point_all = gather_blocks(point_own, "ch")
    point_all = jnp.concatenate([point_all[q] for q in range(ch_size)], axis=1)
    conv_all = gather_blocks(conv_own, "ch")

    params_mid = gather_blocks(norm_mid, "ch")
    params_mid = jnp.concatenate([params_mid[q] for q in range(ch_size)], axis=1)
    centered_mid = (all_rest.astype(jnp.float32) - (mean_mid - local_mean_all)) * root_mid
    pre_mid = centered_mid * params_mid[0] + params_mid[1]
    upstream_mid = jnp.dot(cot_ext, point_all, preferred_element_type=jnp.float32)
    gelu_mid, pull_mid = jax.vjp(jax.nn.gelu, pre_mid)
    d_mid = pull_mid(upstream_mid)[0]
    hidden_mid = gelu_mid[span : span + rows].astype(jnp.bfloat16)
    d_own, c_own = d_mid[span : span + rows], centered_mid[span : span + rows]
    total_mid = each(jnp.stack([jnp.sum(d_own * c_own, 0), jnp.sum(d_own, 0)]), "seq").sum(0)

    branch = lax.dot_general(
        hidden_mid, point_all, (((1,), (1,)), ((), ())), preferred_element_type=jnp.float32
    )
    block_out = (values + branch).astype(jnp.bfloat16)
    hidden_slim = lax.dynamic_slice_in_dim(hidden_mid, own_ch * slim, slim, axis=1)
    grad_point = lax.dot_general(
        cotangent, hidden_slim, (((0,), (0,)), ((), ())), preferred_element_type=jnp.float32
    )

    grad_out = root_mid * params_mid[0] * (
        d_mid - total_mid[1] / bin_count - centered_mid * total_mid[0] / bin_count
    )
    terms = []
    for j, shift in enumerate(shifts):
        masked = grad_out * masks[j][:, None]
        terms.append(masked[span - shift : span - shift + rows].astype(jnp.bfloat16))
    hidden_own = hidden_in[2 * span : 2 * span + rows]
    slim_terms = [lax.dynamic_slice_in_dim(t, own_ch * slim, slim, axis=1) for t in terms]
    grad_conv = lax.dot_general(
        hidden_own,
        jnp.concatenate(slim_terms, axis=1),
        (((0,), (0,)), ((), ())),
        preferred_element_type=jnp.float32,
    )
    upstream_in = 0.0
    for j in range(KERNEL_WIDTH):
        taps = [conv_all[q][:, j * slim : (j + 1) * slim] for q in range(ch_size)]
        upstream_in = upstream_in + lax.dot_general(
            terms[j],
            jnp.concatenate(taps, axis=1),
            (((1,), (1,)), ((), ())),
            preferred_element_type=jnp.float32,
        )
    d_in = jax.vjp(jax.nn.gelu, pre_in[2 * span : 2 * span + rows])[1](upstream_in)[0]
    centered_in = (values - mean_in) * root_in
    grad_in = each(jnp.stack([jnp.sum(d_in * centered_in, 0), jnp.sum(d_in, 0)]), "seq").sum(0)
    input_grad = cotangent.astype(jnp.float32) + root_in * norm_in[0] * (
        d_in - grad_in[1] / bin_count - centered_in * grad_in[0] / bin_count
    )

    both = jnp.concatenate([grad_conv, grad_point], axis=1)
    both = scatter_sum(both.reshape(seq_size, width // seq_size, -1), "seq")
    conv_sum = jnp.stack([both[:, j * slim : (j + 1) * slim] for j in range(KERNEL_WIDTH)])
    point_sum = both[:, KERNEL_WIDTH * slim :].T

    grad_mid = lax.dynamic_slice_in_dim(total_mid, own_ch * slim, slim, axis=1)
    conv_new = adamw(master_conv, first_conv, second_conv, conv_sum, RATE_WEIGHT, DECAY_WEIGHT)
    point_new = adamw(
        master_point, first_point, second_point, point_sum, RATE_WEIGHT, DECAY_WEIGHT
    )
    in_new = adamw(norm_in, first_in, second_in, grad_in, RATE_NORM, 0.0)
    mid_new = adamw(norm_mid, first_mid, second_mid, grad_mid, RATE_NORM, 0.0)
    return (block_out, input_grad) + conv_new + point_new + in_new + mid_new


def solution(mesh):
    in_specs = (
        P("seq", None),
        P("seq", None),
        P(),
        P(None, "seq", "ch"),
        P(None, "seq", "ch"),
        P(None, "seq", "ch"),
        P("ch", "seq"),
        P("ch", "seq"),
        P("ch", "seq"),
        P(),
        P(),
        P(),
        P(None, "ch"),
        P(None, "ch"),
        P(None, "ch"),
    )
    out_specs = (
        P("seq", None),
        P("seq", None),
        P(None, "seq", "ch"),
        P(None, "seq", "ch"),
        P(None, "seq", "ch"),
        P("ch", "seq"),
        P("ch", "seq"),
        P("ch", "seq"),
        P(),
        P(),
        P(),
        P(None, "ch"),
        P(None, "ch"),
        P(None, "ch"),
    )
    return jax.shard_map(shards, mesh=mesh, in_specs=in_specs, out_specs=out_specs, check_vma=False)
```

```python
import functools

import jax
import jax.numpy as jnp
from jax import lax
from jax.experimental import pallas as pl
from jax.experimental.pallas import tpu as pltpu
from jax.sharding import PartitionSpec as P

KERNEL_WIDTH = 3
DILATION_BINS = 9
WIN = 1024
STEP = 10

NORM_EPS = 1e-05
ADAM_EPS = 1e-08
BETA_ONE = 0.9
BETA_TWO = 0.999
RATE_WEIGHT = 0.05
RATE_NORM = 0.5
DECAY_WEIGHT = 0.01

LANES = 128
EDGE = 16
RIM = 2 * EDGE
GELU_A = 0.7978845608028654
GELU_B = 0.044715
SHIFTS = [(j - KERNEL_WIDTH // 2) * DILATION_BINS for j in range(KERNEL_WIDTH)]
ROW_DIMS = (((0,), (0,)), ((), ()))
LANE_DIMS = (((1,), (1,)), ((), ()))
F32, BF16 = jnp.float32, jnp.bfloat16


def call(body, outs, args, scratch=(), smem=(), flops=0, limit=24):
    spaces = [pltpu.SMEM if k in smem else pltpu.VMEM for k in range(len(args))]
    size = lambda a: a.size * a.dtype.itemsize
    return pl.pallas_call(
        body,
        out_shape=[jax.ShapeDtypeStruct(s, t) for s, t in outs],
        in_specs=[pl.BlockSpec(memory_space=s) for s in spaces],
        out_specs=[pl.BlockSpec(memory_space=pltpu.VMEM) for _ in outs],
        scratch_shapes=[pltpu.VMEM(s, t) for s, t in scratch],
        compiler_params=pltpu.CompilerParams(vmem_limit_bytes=limit * 2**20),
        cost_estimate=pl.CostEstimate(
            flops=flops, bytes_accessed=sum(size(a) for a in args), transcendentals=0
        ),
    )(*args)


def up_to(size, step):
    return -(-size // step) * step


def split_three(v):
    high = v.astype(BF16).astype(F32)
    rest = v - high
    middle = rest.astype(BF16).astype(F32)
    return high, middle, rest - middle


def gelu_and_slope(v):
    square = v * v
    t = jnp.tanh(v * (GELU_A + (GELU_A * GELU_B) * square))
    half = 0.5 * (1.0 + t)
    slope = half + (0.5 * v) * (1.0 - t * t) * (GELU_A + (3.0 * GELU_A * GELU_B) * square)
    return v * half, slope


def reach_of(first, count, shift, start, bin_count):
    here = first + lax.broadcasted_iota(jnp.int32, (count, LANES), 0)
    there = here + shift
    inside = (here >= 0) & (here < bin_count) & (there >= 0) & (there < bin_count)
    return inside & (((here - start) >> 10) == ((there - start) >> 10))


def pack_kernel(conv_ref, out_ref):
    depth, slim = conv_ref.shape[1:]
    out_ref[...] = jnp.zeros_like(out_ref)
    for j in range(KERNEL_WIDTH):
        out_ref[:depth, j * LANES : j * LANES + slim] = conv_ref[j].astype(BF16)


def stats_kernel(x_ref, head_ref, tail_ref, point_ref, sent_ref, last_ref, first_ref, sum_ref):
    rows, width = x_ref.shape
    tiles = width // LANES
    slim, depth = point_ref.shape

    def step(k, carry):
        v = x_ref[pl.ds(pl.multiple_of(k * 32, 32), 32), :].astype(F32)
        v = v.reshape(4, 8, width)
        return carry[0] + v.sum(0), carry[1] + (v * v).sum(0)

    zero = jnp.zeros((8, width), F32)
    one, two = lax.fori_loop(0, rows // 32, step, (zero, zero), unroll=4)
    sum_ref[...] = jnp.zeros_like(sum_ref)
    for stat, total in enumerate((one, two)):
        parts = split_three(jnp.sum(total, 0, keepdims=True))
        for k in range(tiles):
            for p, part in enumerate(parts):
                row = p * 2 * tiles + stat * tiles + k
                sum_ref[row : row + 1, :] = part[:, k * LANES : (k + 1) * LANES]
    base = sent_ref.shape[1] - sum_ref.shape[0]
    sent_ref[...] = jnp.zeros_like(sent_ref)
    turned = point_ref[...].T.astype(BF16)
    sums = sum_ref[...].astype(BF16)
    for d in range(sent_ref.shape[0]):
        sent_ref[d, :depth, :slim] = turned
        sent_ref[d, base:, :] = sums
    last_ref[:RIM, :] = x_ref[rows - RIM :, :]
    last_ref[RIM:, :] = tail_ref[...]
    first_ref[:RIM, :] = x_ref[:RIM, :]
    first_ref[RIM:, :] = head_ref[...]


def act_kernel(x_ref, before_ref, after_ref, got_ref, norm_ref, hid_ref, slope_ref, vec_ref, point_ref, *, bin_count, depth):
    rows, width = x_ref.shape
    tiles = width // LANES
    count, height = got_ref.shape[:2]
    area = up_to(6 * tiles, 16)
    total = got_ref[0, height - area :, :].astype(F32)
    for d in range(1, count):
        total = total + got_ref[d, height - area :, :].astype(F32)
    total = total[: 2 * tiles] + total[2 * tiles : 4 * tiles] + total[4 * tiles : 6 * tiles]
    for d in range(count):
        point_ref[d] = got_ref[d, :depth, :]
    for k in range(tiles):
        lanes = slice(k * LANES, (k + 1) * LANES)
        mean = total[k : k + 1] / bin_count
        square = total[tiles + k : tiles + k + 1] / bin_count
        root = lax.rsqrt(square - mean * mean + NORM_EPS)
        gain = root * norm_ref[0:1, lanes]
        vec_ref[0:1, lanes] = root
        vec_ref[1:2, lanes] = -mean * root
        vec_ref[2:3, lanes] = gain
        vec_ref[3:4, lanes] = norm_ref[1:2, lanes] - mean * gain

    gain, bias = vec_ref[2:3, :], vec_ref[3:4, :]
    for src, at in ((before_ref, 0), (after_ref, RIM + rows)):
        for k in range(0, RIM, 16):
            hidden, _ = gelu_and_slope(src[k : k + 16, :].astype(F32) * gain + bias)
            hid_ref[at + k : at + k + 16, :] = hidden.astype(BF16)

    def step(k, carry):
        at = pl.multiple_of(k * 16, 16)
        v = x_ref[pl.ds(at, 16), :].astype(F32) * vec_ref[2:3, :] + vec_ref[3:4, :]
        hidden, slope = gelu_and_slope(v)
        hid_ref[pl.ds(pl.multiple_of(at + RIM, 16), 16), :] = hidden.astype(BF16)
        slope_ref[pl.ds(at, 16), :] = slope
        return carry

    lax.fori_loop(0, rows // 16, step, 0, unroll=2)


def conv_kernel(start_ref, hid_ref, *refs, relatives, bin_count):
    pieces, (norm_ref, weight_ref, rest_ref, sent_ref, stack, prod, out) = refs[:-7], refs[-7:]
    width = hid_ref.shape[1]
    rows = hid_ref.shape[0] - 2 * RIM
    slim = norm_ref.shape[1]
    own = lax.axis_index("seq")
    at = 0
    for piece in pieces:
        for k in range(piece.shape[0]):
            stack[own ^ relatives[at]] = piece[k].astype(stack.dtype)
            at += 1
    weight_ref[...] = stack[...].reshape(width, -1).astype(BF16)
    chunk = (rows + 2 * RIM) // 4
    for k in range(4):
        prod[k * chunk : (k + 1) * chunk, :] = jnp.dot(
            hid_ref[k * chunk : (k + 1) * chunk, :], weight_ref[...], preferred_element_type=F32
        )
    first = own * rows
    start = start_ref[0]

    def rows_of(begin, count):
        value = 0.0
        for j, shift in enumerate(SHIFTS):
            part = prod[begin + EDGE + shift : begin + EDGE + shift + count, j * LANES : (j + 1) * LANES]
            mask = reach_of(first + begin - EDGE, count, shift, start, bin_count)
            value = value + jnp.where(mask, part, 0.0)
        out[begin : begin + count, :] = value
        return value

    rows_of(0, EDGE)
    rows_of(EDGE + rows, EDGE)
    one = two = jnp.zeros((8, LANES), F32)
    step = 128
    for k in range(rows // step):
        value = rows_of(EDGE + k * step, step).reshape(step // 8, 8, LANES)
        one = one + value.sum(0)
        two = two + (value * value).sum(0)
    one, two = jnp.sum(one, 0, keepdims=True), jnp.sum(two, 0, keepdims=True)
    sent_ref[...] = jnp.zeros_like(sent_ref)
    for d in range(sent_ref.shape[0]):
        sent_ref[d, 0:1, :] = one
        sent_ref[d, 1:2, :] = two
        sent_ref[d, 2:4, :slim] = norm_ref[...]
    mean = one / rows
    rest_ref[...] = (out[...] - mean).astype(BF16)


def upstream_kernel(cot_ref, before_ref, after_ref, *refs):
    pieces, (up_ref, point_ref) = refs[:-2], refs[-2:]
    rows, width = cot_ref.shape
    at = 0
    for piece in pieces:
        for k in range(piece.shape[0]):
            point_ref[:, at * LANES : (at + 1) * LANES] = piece[k]
            at += 1
    point = point_ref[...]
    up_ref[:EDGE, :] = jnp.dot(before_ref[RIM:, :], point, preferred_element_type=F32)
    up_ref[EDGE + rows :, :] = jnp.dot(after_ref[RIM:, :], point, preferred_element_type=F32)
    chunk = rows // 4
    for k in range(4):
        up_ref[EDGE + k * chunk : EDGE + (k + 1) * chunk, :] = jnp.dot(
            cot_ref[k * chunk : (k + 1) * chunk, :], point, preferred_element_type=F32
        )


def mid_kernel(got_ref, up_ref, *refs, relatives, bin_count, seq_size):
    pieces, (hid_ref, d_ref, sent_ref, vec_ref) = refs[:-4], refs[-4:]
    rows = hid_ref.shape[0]
    ch_size = len(relatives)
    own_seq, own_ch = lax.axis_index("seq"), lax.axis_index("ch")
    blocks = [(piece, k) for piece in pieces for k in range(piece.shape[0])]
    for r, (piece, k) in enumerate(blocks):
        lanes = slice(r * LANES, (r + 1) * LANES)
        q = own_ch ^ relatives[r]
        total = got_ref[q]
        for s in range(1, seq_size):
            total = total + got_ref[s * ch_size + q]
        mine = got_ref[own_seq * ch_size + q]
        mean = total[0:1] / bin_count
        root = lax.rsqrt(total[1:2] / bin_count - mean * mean + NORM_EPS)
        offset = (mine[0:1] / rows - mean) * root
        gain, bias = mine[2:3], mine[3:4]
        vec_ref[0:1, lanes] = root
        vec_ref[1:2, lanes] = offset
        vec_ref[2:3, lanes] = gain
        vec_ref[3:4, lanes] = bias

        def rows_of(begin, count):
            centered = piece[k, pl.ds(begin, count), :].astype(F32) * root + offset
            hidden, slope = gelu_and_slope(centered * gain + bias)
            d = up_ref[pl.ds(begin, count), lanes] * slope
            d_ref[pl.ds(begin, count), lanes] = d
            return centered, hidden, d

        rows_of(0, EDGE)
        rows_of(EDGE + rows, EDGE)
        step = 64

        def body(i, carry):
            begin = pl.multiple_of(EDGE + i * step, 16)
            centered, hidden, d = rows_of(begin, step)
            hid_ref[pl.ds(pl.multiple_of(i * step, 16), step), lanes] = hidden.astype(BF16)
            d = d.reshape(step // 8, 8, LANES)
            return carry[0] + (d * centered.reshape(d.shape)).sum(0), carry[1] + d.sum(0)

        zero = jnp.zeros((8, LANES), F32)
        gain_sum, bias_sum = lax.fori_loop(0, rows // step, body, (zero, zero))
        gain_sum = jnp.sum(gain_sum, 0, keepdims=True)
        bias_sum = jnp.sum(bias_sum, 0, keepdims=True)
        for d in range(seq_size):
            sent_ref[d, 0:1, lanes] = gain_sum
            sent_ref[d, 1:2, lanes] = bias_sum


def out_kernel(x_ref, cot_ref, hid_ref, point_ref, out_ref, grad_ref):
    rows = x_ref.shape[0]
    chunk = rows // 4
    point = point_ref[...]
    for k in range(4):
        part = slice(k * chunk, (k + 1) * chunk)
        branch = lax.dot_general(hid_ref[part, :], point, LANE_DIMS, preferred_element_type=F32)
        out_ref[part, :] = (x_ref[part, :].astype(F32) + branch).astype(BF16)
    grad_ref[...] = lax.dot_general(
        cot_ref[...], hid_ref[:, :LANES], ROW_DIMS, preferred_element_type=F32
    )


def weight_grad_kernel(start_ref, got_ref, vec_ref, d_ref, hid_ref, point_ref, *refs, bin_count, depth):
    pieces, (term_ref, kept_ref, sent_ref, total_ref, grad, full) = refs[:-6], refs[-6:]
    rows = term_ref.shape[0]
    blocks = [(piece, k) for piece in pieces for k in range(piece.shape[0])]
    own = lax.axis_index("seq")
    first = own * rows
    start = start_ref[0]
    total = got_ref[0]
    for s in range(1, got_ref.shape[0]):
        total = total + got_ref[s]
    total_ref[...] = total
    step = 64
    for r, (piece, k) in enumerate(blocks):
        lanes = slice(r * LANES, (r + 1) * LANES)
        root, offset, gain = vec_ref[0:1, lanes], vec_ref[1:2, lanes], vec_ref[2:3, lanes]
        scale = root * gain
        pull = scale * total[0:1, lanes] / bin_count
        slant = pull * root
        level = scale * total[1:2, lanes] / bin_count + pull * offset
        for begin in range(0, rows + RIM, 96):
            part = slice(begin, min(begin + 96, rows + RIM))
            rest = piece[k, part, :].astype(F32)
            grad[part, :] = d_ref[part, lanes] * scale - (rest * slant + level)
        for j, shift in enumerate(SHIFTS):
            at = (r * KERNEL_WIDTH + j) * LANES
            for begin in range(0, rows, step):
                mask = reach_of(first + begin - shift, step, shift, start, bin_count)
                value = grad[EDGE + begin - shift : EDGE + begin - shift + step, :]
                term_ref[begin : begin + step, at : at + LANES] = jnp.where(mask, value, 0.0).astype(BF16)
    wide = KERNEL_WIDTH * LANES
    full[:, :wide] = lax.dot_general(
        hid_ref[RIM : RIM + rows, :], term_ref[:, :wide], ROW_DIMS, preferred_element_type=F32
    )
    full[:, wide:] = point_ref[...]
    low = own % 2
    for k in range(kept_ref.shape[0]):
        kept_ref[k] = full[pl.ds(pl.multiple_of((2 * k + low) * depth, 8), depth), :]
        sent_ref[k] = full[pl.ds(pl.multiple_of((2 * k + 1 - low) * depth, 8), depth), :].astype(BF16)


def input_grad_kernel(x_ref, slope_ref, vec_ref, term_ref, weight_ref, d_ref, sent_ref):
    rows, width = x_ref.shape
    root, offset = vec_ref[0:1, :], vec_ref[1:2, :]
    one = two = jnp.zeros((8, width), F32)
    step = 128
    for k in range(rows // step):
        part = slice(k * step, (k + 1) * step)
        up = lax.dot_general(term_ref[part, :], weight_ref[...], LANE_DIMS, preferred_element_type=F32)
        d = up * slope_ref[part, :]
        d_ref[part, :] = d
        centered = x_ref[part, :].astype(F32) * root + offset
        one = one + (d * centered).reshape(step // 8, 8, width).sum(0)
        two = two + d.reshape(step // 8, 8, width).sum(0)
    one, two = jnp.sum(one, 0, keepdims=True), jnp.sum(two, 0, keepdims=True)
    for d in range(sent_ref.shape[0]):
        sent_ref[d, 0:1, :] = one
        sent_ref[d, 1:2, :] = two


def final_kernel(x_ref, cot_ref, d_ref, vec_ref, got_ref, out_ref, total_ref, *, bin_count):
    rows, width = x_ref.shape
    total = got_ref[0]
    for s in range(1, got_ref.shape[0]):
        total = total + got_ref[s]
    total_ref[...] = total
    root, offset, scale = vec_ref[0:1, :], vec_ref[1:2, :], vec_ref[2:3, :]
    pull = scale * total[0:1] / bin_count
    slant = pull * root
    level = scale * total[1:2] / bin_count + pull * offset
    step = 16

    def body(i, carry):
        at = pl.ds(pl.multiple_of(i * step, 16), step)
        value = x_ref[at, :].astype(F32) * slant + level
        out_ref[at, :] = cot_ref[at, :].astype(F32) + (d_ref[at, :] * scale - value)
        return carry

    lax.fori_loop(0, rows // step, body, 0, unroll=4)


def flip(axis, reach):
    return [(i, i ^ reach) for i in range(lax.axis_size(axis))]


def relatives_of(size):
    found, reach = [0], size // 2
    while reach:
        found, reach = found + [r ^ reach for r in found], reach // 2
    return found


def gather_pieces(x, axis):
    pieces, reach = [x[None]], lax.axis_size(axis) // 2
    while reach:
        held = pieces[0] if len(pieces) == 1 else jnp.concatenate(pieces)
        pieces.append(lax.ppermute(held, axis, flip(axis, reach)))
        reach //= 2
    return pieces


def spread(copies, axes):
    return lax.all_to_all(copies, axes, 0, 0, tiled=True)


def adamw(weights_old, first_moment_state, second_mom, gradient, step_rate, decay_rate):
    first_next = BETA_ONE * first_moment_state + (1.0 - BETA_ONE) * gradient
    second_next = BETA_TWO * second_mom + (1.0 - BETA_TWO) * gradient * gradient
    corrected = (
        first_next
        / (1.0 - BETA_ONE**STEP)
        / (jnp.sqrt(second_next / (1.0 - BETA_TWO**STEP)) + ADAM_EPS)
    )
    weights_new = weights_old - step_rate * (corrected + decay_rate * weights_old)
    return (first_next, second_next, weights_new)


def shards(
    inputs,
    cotangent,
    starts,
    master_conv,
    first_conv,
    second_conv,
    master_point,
    first_point,
    second_point,
    norm_in,
    first_in,
    second_in,
    norm_mid,
    first_mid,
    second_mid,
):
    rows, width = inputs.shape
    seq_size, ch_size = lax.axis_size("seq"), lax.axis_size("ch")
    bin_count = rows * seq_size
    depth, slim = master_conv.shape[1:]
    tiles = width // LANES
    wide = KERNEL_WIDTH * LANES
    seq_relatives, ch_relatives = relatives_of(seq_size), relatives_of(ch_size)
    mid = ch_size * LANES
    ext = rows + 2 * EDGE

    (conv_low,) = call(pack_kernel, [((depth, wide), BF16)], [master_conv])
    area = up_to(6 * tiles, 16)
    height = up_to(depth, 16) + area
    sent_in, last, first = call(
        stats_kernel,
        [((seq_size, height, LANES), BF16)] + [((RIM + EDGE, width), BF16)] * 2,
        [inputs, cotangent[:EDGE], cotangent[rows - EDGE :], master_point],
        scratch=[((area, LANES), F32)],
    )
    conv_pieces = gather_pieces(conv_low, "seq")
    got_in = spread(sent_in, "seq")
    up = [(i, i + 1) for i in range(seq_size - 1)]
    down = [(j, i) for i, j in up]
    before = lax.ppermute(last, "seq", up)
    after = lax.ppermute(first, "seq", down)
    hidden_in, slope_in, vec_in, point_own = call(
        functools.partial(act_kernel, bin_count=bin_count, depth=depth),
        [
            ((rows + 2 * RIM, width), BF16),
            ((rows, width), F32),
            ((8, width), F32),
            ((seq_size, depth, LANES), BF16),
        ],
        [inputs, before, after, got_in, norm_in],
        flops=40 * rows * width,
    )
    point_pieces = gather_pieces(point_own.reshape(width, LANES), "ch")

    stack_type = BF16 if depth % 16 == 0 else F32
    conv_own, rest, sent_mid = call(
        functools.partial(conv_kernel, relatives=seq_relatives, bin_count=bin_count),
        [
            ((width, wide), BF16),
            ((ext, LANES), BF16),
            ((seq_size * ch_size, 4, LANES), F32),
        ],
        [starts, hidden_in] + conv_pieces + [norm_mid],
        scratch=[
            ((seq_size, depth, wide), stack_type),
            ((rows + 2 * RIM, wide), F32),
            ((ext, LANES), F32),
        ],
        smem=(0,),
        flops=2 * rows * width * wide,
    )
    rest_pieces = gather_pieces(rest, "ch")
    got_mid = spread(sent_mid, ("seq", "ch"))
    upstream, point_all = call(
        upstream_kernel,
        [((ext, mid), F32), ((width, mid), BF16)],
        [cotangent, before, after] + point_pieces,
        flops=2 * rows * width * mid,
    )
    conv_all = jnp.concatenate(
        [piece[k] for piece in gather_pieces(conv_own, "ch") for k in range(piece.shape[0])], axis=1
    )
    hidden_mid, d_mid, sent_back, vec_mid = call(
        functools.partial(
            mid_kernel, relatives=ch_relatives, bin_count=bin_count, seq_size=seq_size
        ),
        [((rows, mid), BF16), ((ext, mid), F32), ((seq_size, 2, mid), F32), ((8, mid), F32)],
        [got_mid, upstream] + rest_pieces,
        flops=40 * rows * mid,
    )
    got_back = spread(sent_back, "seq")
    block_out, grad_point = call(
        out_kernel,
        [((rows, width), BF16), ((width, LANES), F32)],
        [inputs, cotangent, hidden_mid, point_all],
        flops=2 * rows * width * (mid + LANES),
    )
    terms, kept, sent, total_mid = call(
        functools.partial(weight_grad_kernel, bin_count=bin_count, depth=depth),
        [
            ((rows, ch_size * wide), BF16),
            ((seq_size // 2, depth, wide + LANES), F32),
            ((seq_size // 2, depth, wide + LANES), BF16),
            ((2, mid), F32),
        ],
        [starts, got_back, vec_mid, d_mid, hidden_in, grad_point] + rest_pieces,
        scratch=[((ext, LANES), F32), ((width, wide + LANES), F32)],
        smem=(0,),
        flops=2 * rows * width * wide,
    )
    d_in, sent_first = call(
        input_grad_kernel,
        [((rows, width), F32), ((seq_size, 2, width), F32)],
        [inputs, slope_in, vec_in, terms, conv_all],
        flops=2 * rows * width * ch_size * wide,
    )
    got_first = spread(sent_first, "seq")
    input_grad, total_in = call(
        functools.partial(final_kernel, bin_count=bin_count),
        [((rows, width), F32), ((2, width), F32)],
        [inputs, cotangent, d_in, vec_in, got_first],
        flops=10 * rows * width,
    )

    own = lax.axis_index("seq")
    reach = 1
    while True:
        got = lax.ppermute(sent, "seq", flip("seq", reach))
        blocks = kept + got.astype(F32)
        reach *= 2
        if reach == seq_size:
            break
        pairs = blocks.reshape((-1, 2) + blocks.shape[1:])
        high = (own // reach) % 2 == 1
        kept = jnp.where(high, pairs[:, 1], pairs[:, 0])
        sent = jnp.where(high, pairs[:, 0], pairs[:, 1]).astype(BF16)
    both = blocks[0]
    conv_sum = jnp.stack(
        [both[:, j * LANES : j * LANES + slim] for j in range(KERNEL_WIDTH)]
    )
    point_sum = both[:, wide : wide + slim].T

    conv_new = adamw(master_conv, first_conv, second_conv, conv_sum, RATE_WEIGHT, DECAY_WEIGHT)
    point_new = adamw(
        master_point, first_point, second_point, point_sum, RATE_WEIGHT, DECAY_WEIGHT
    )
    in_new = adamw(norm_in, first_in, second_in, total_in, RATE_NORM, 0.0)
    mid_new = adamw(norm_mid, first_mid, second_mid, total_mid[:, :slim], RATE_NORM, 0.0)
    return (block_out, input_grad) + conv_new + point_new + in_new + mid_new


def solution(mesh):
    in_specs = (
        P("seq", None),
        P("seq", None),
        P(),
        P(None, "seq", "ch"),
        P(None, "seq", "ch"),
        P(None, "seq", "ch"),
        P("ch", "seq"),
        P("ch", "seq"),
        P("ch", "seq"),
        P(),
        P(),
        P(),
        P(None, "ch"),
        P(None, "ch"),
        P(None, "ch"),
    )
    out_specs = (
        P("seq", None),
        P("seq", None),
        P(None, "seq", "ch"),
        P(None, "seq", "ch"),
        P(None, "seq", "ch"),
        P("ch", "seq"),
        P("ch", "seq"),
        P("ch", "seq"),
        P(),
        P(),
        P(),
        P(None, "ch"),
        P(None, "ch"),
        P(None, "ch"),
    )
    return jax.shard_map(shards, mesh=mesh, in_specs=in_specs, out_specs=out_specs, check_vma=False)
```

```python
import functools

import jax
import jax.numpy as jnp
from jax import lax
from jax.experimental import pallas as pl
from jax.experimental.pallas import tpu as pltpu
from jax.sharding import PartitionSpec as P

KERNEL_WIDTH = 3
DILATION_BINS = 9
WIN = 1024
STEP = 10

NORM_EPS = 1e-05
ADAM_EPS = 1e-08
BETA_ONE = 0.9
BETA_TWO = 0.999
RATE_WEIGHT = 0.05
RATE_NORM = 0.5
DECAY_WEIGHT = 0.01

LANES = 128
EDGE = 16
RIM = 2 * EDGE
GELU_A = 0.7978845608028654
GELU_B = 0.044715
SHIFTS = [(j - KERNEL_WIDTH // 2) * DILATION_BINS for j in range(KERNEL_WIDTH)]
ROW_DIMS = (((0,), (0,)), ((), ()))
LANE_DIMS = (((1,), (1,)), ((), ()))
F32, BF16 = jnp.float32, jnp.bfloat16


def call(body, outs, args, scratch=(), smem=(), after=(), flops=0, limit=16):
    spaces = [pltpu.SMEM if k in smem else pltpu.VMEM for k in range(len(args))]
    spaces += [pl.ANY] * len(after)
    size = lambda a: a.size * a.dtype.itemsize

    def kernel(*refs):
        body(*refs[: len(args)], *refs[len(spaces) :])

    return pl.pallas_call(
        kernel,
        out_shape=[jax.ShapeDtypeStruct(s, t) for s, t in outs],
        in_specs=[pl.BlockSpec(memory_space=s) for s in spaces],
        out_specs=[pl.BlockSpec(memory_space=pltpu.VMEM) for _ in outs],
        scratch_shapes=[pltpu.VMEM(s, t) for s, t in scratch],
        compiler_params=pltpu.CompilerParams(vmem_limit_bytes=limit * 2**20),
        cost_estimate=pl.CostEstimate(
            flops=flops, bytes_accessed=sum(size(a) for a in args), transcendentals=0
        ),
        name=getattr(body, "func", body).__name__,
    )(*args, *after)


def up_to(size, step):
    return -(-size // step) * step


def split_three(v):
    high = v.astype(BF16).astype(F32)
    rest = v - high
    middle = rest.astype(BF16).astype(F32)
    return high, middle, rest - middle


def gelu_and_slope(v):
    square = v * v
    t = jnp.tanh(v * (GELU_A + (GELU_A * GELU_B) * square))
    half = 0.5 * (1.0 + t)
    slope = half + (0.5 * v) * (1.0 - t * t) * (GELU_A + (3.0 * GELU_A * GELU_B) * square)
    return v * half, slope


def reach_of(first, count, shift, start, bin_count):
    here = first + lax.broadcasted_iota(jnp.int32, (count, LANES), 0)
    there = here + shift
    inside = (here >= 0) & (here < bin_count) & (there >= 0) & (there < bin_count)
    return inside & (((here - start) >> 10) == ((there - start) >> 10))


def pack_kernel(conv_ref, out_ref):
    depth, slim = conv_ref.shape[1:]
    out_ref[...] = jnp.zeros_like(out_ref)
    for j in range(KERNEL_WIDTH):
        out_ref[:depth, j * LANES : j * LANES + slim] = conv_ref[j].astype(BF16)


def stats_kernel(x_ref, head_ref, tail_ref, point_ref, sum_ref, turned_ref, last_ref, first_ref):
    rows, width = x_ref.shape
    tiles = width // LANES
    slim, depth = point_ref.shape

    def step(k, carry):
        v = x_ref[pl.ds(pl.multiple_of(k * 32, 32), 32), :].astype(F32)
        v = v.reshape(4, 8, width)
        return carry[0] + v.sum(0), carry[1] + (v * v).sum(0)

    zero = jnp.zeros((8, width), F32)
    one, two = lax.fori_loop(0, rows // 32, step, (zero, zero), unroll=4)
    sum_ref[...] = jnp.zeros_like(sum_ref)
    for stat, total in enumerate((one, two)):
        total = jnp.sum(total, 0, keepdims=True)
        for k in range(tiles):
            row = stat * tiles + k
            sum_ref[row : row + 1, :] = total[:, k * LANES : (k + 1) * LANES]
    turned_ref[...] = jnp.zeros_like(turned_ref)
    turned_ref[:, :slim] = point_ref[...].T.astype(BF16)
    last_ref[:RIM, :] = x_ref[rows - RIM :, :]
    last_ref[RIM:, :] = tail_ref[...]
    first_ref[:RIM, :] = x_ref[:RIM, :]
    first_ref[RIM:, :] = head_ref[...]


def act_kernel(
    x_ref, before_ref, after_ref, one_ref, two_ref, norm_ref, hid_ref, slope_ref, vec_ref, *, bin_count
):
    rows, width = x_ref.shape
    tiles = width // LANES
    total = one_ref[...] + two_ref[...]
    for k in range(tiles):
        lanes = slice(k * LANES, (k + 1) * LANES)
        mean = total[k : k + 1, :] / bin_count
        square = total[tiles + k : tiles + k + 1, :] / bin_count
        root = lax.rsqrt(square - mean * mean + NORM_EPS)
        gain = root * norm_ref[0:1, lanes]
        vec_ref[0:1, lanes] = root
        vec_ref[1:2, lanes] = -mean * root
        vec_ref[2:3, lanes] = gain
        vec_ref[3:4, lanes] = norm_ref[1:2, lanes] - mean * gain

    gain, bias = vec_ref[2:3, :], vec_ref[3:4, :]
    for src, at in ((before_ref, 0), (after_ref, RIM + rows)):
        for k in range(0, RIM, 16):
            hidden, _ = gelu_and_slope(src[k : k + 16, :].astype(F32) * gain + bias)
            hid_ref[at + k : at + k + 16, :] = hidden.astype(BF16)

    def step(k, carry):
        at = pl.multiple_of(k * 16, 16)
        v = x_ref[pl.ds(at, 16), :].astype(F32) * vec_ref[2:3, :] + vec_ref[3:4, :]
        hidden, slope = gelu_and_slope(v)
        hid_ref[pl.ds(pl.multiple_of(at + RIM, 16), 16), :] = hidden.astype(BF16)
        slope_ref[pl.ds(at, 16), :] = slope
        return carry

    lax.fori_loop(0, rows // 16, step, 0, unroll=2)


def place(pieces, relatives, stack, own):
    at = 0
    for piece in pieces:
        for k in range(piece.shape[0]):
            stack[own ^ relatives[at]] = piece[k].astype(stack.dtype)
            at += 1
    return stack[...].reshape(-1, stack.shape[2]).astype(BF16)


def place_kernel(*refs, relatives):
    pieces, (out_ref, stack) = refs[:-2], refs[-2:]
    out_ref[...] = place(pieces, relatives, stack, lax.axis_index("seq"))


def conv_kernel(start_ref, hid_ref, *refs, relatives, bin_count):
    pieces, (weight_ref, out_ref, sum_ref, stack, prod) = refs[:-5], refs[-5:]
    rows = hid_ref.shape[0] - 2 * RIM
    own = lax.axis_index("seq")
    weight_ref[...] = place(pieces, relatives, stack, own)
    for at in range(0, weight_ref.shape[1], 256):
        part = slice(at, min(at + 256, weight_ref.shape[1]))
        prod[:, part] = jnp.dot(hid_ref[...], weight_ref[:, part], preferred_element_type=F32)
    first = own * rows
    start = start_ref[0]

    def rows_of(begin, count):
        value = 0.0
        for j, shift in enumerate(SHIFTS):
            part = prod[begin + EDGE + shift : begin + EDGE + shift + count, j * LANES : (j + 1) * LANES]
            mask = reach_of(first + begin - EDGE, count, shift, start, bin_count)
            value = value + jnp.where(mask, part, 0.0)
        out_ref[begin : begin + count, :] = value
        return value

    rows_of(0, EDGE)
    rows_of(EDGE + rows, EDGE)
    one = two = jnp.zeros((8, LANES), F32)
    step = 128
    for k in range(rows // step):
        value = rows_of(EDGE + k * step, step).reshape(step // 8, 8, LANES)
        one = one + value.sum(0)
        two = two + (value * value).sum(0)
    sum_ref[...] = jnp.zeros_like(sum_ref)
    sum_ref[0:1, :] = jnp.sum(one, 0, keepdims=True)
    sum_ref[1:2, :] = jnp.sum(two, 0, keepdims=True)


def upstream_kernel(cot_ref, before_ref, after_ref, *refs, relatives):
    pieces, (up_ref, point_ref, stack) = refs[:-3], refs[-3:]
    rows = cot_ref.shape[0]
    point_ref[...] = place(pieces, relatives, stack, lax.axis_index("seq"))
    for ref, part, at in (
        (before_ref, slice(RIM, RIM + EDGE), 0),
        (cot_ref, slice(0, rows), EDGE),
        (after_ref, slice(RIM, RIM + EDGE), EDGE + rows),
    ):
        value = jnp.dot(ref[part, :], point_ref[...], preferred_element_type=F32)
        up_ref[at : at + value.shape[0], :] = value


def mid_kernel(
    one_ref, two_ref, conv_ref, up_ref, norm_ref, hid_ref, d_ref, cen_ref, sent_ref, vec_ref, *, bin_count
):
    rows = hid_ref.shape[0]
    slim = norm_ref.shape[1]
    total = one_ref[...] + two_ref[...]
    mean = total[0:1] / bin_count
    root = lax.rsqrt(total[1:2] / bin_count - mean * mean + NORM_EPS)
    vec_ref[...] = jnp.zeros_like(vec_ref)
    vec_ref[0:1, :] = root
    vec_ref[1:3, :slim] = norm_ref[...]
    gain, bias = vec_ref[1:2, :], vec_ref[2:3, :]

    def rows_of(begin, count):
        centered = (conv_ref[pl.ds(begin, count), :] - mean) * root
        hidden, slope = gelu_and_slope(centered * gain + bias)
        d = up_ref[pl.ds(begin, count), :] * slope
        cen_ref[pl.ds(begin, count), :] = centered
        d_ref[pl.ds(begin, count), :] = d
        return centered, hidden, d

    rows_of(0, EDGE)
    rows_of(EDGE + rows, EDGE)
    step = 64

    def body(i, carry):
        begin = pl.multiple_of(EDGE + i * step, 16)
        centered, hidden, d = rows_of(begin, step)
        hid_ref[pl.ds(pl.multiple_of(i * step, 16), step), :] = hidden.astype(BF16)
        d = d.reshape(step // 8, 8, LANES)
        return carry[0] + (d * centered.reshape(d.shape)).sum(0), carry[1] + d.sum(0)

    zero = jnp.zeros((8, LANES), F32)
    gain_sum, bias_sum = lax.fori_loop(0, rows // step, body, (zero, zero), unroll=2)
    gain_sum = jnp.sum(gain_sum, 0, keepdims=True)
    bias_sum = jnp.sum(bias_sum, 0, keepdims=True)
    for d in range(sent_ref.shape[0]):
        sent_ref[d, 0:1, :] = gain_sum
        sent_ref[d, 1:2, :] = bias_sum


def conv_back_kernel(got_ref, vec_ref, d_ref, cen_ref, hid_ref, point_ref, grad_ref, total_ref, both_ref, *, bin_count):
    rows = hid_ref.shape[0]
    total = got_ref[0]
    for s in range(1, got_ref.shape[0]):
        total = total + got_ref[s]
    total_ref[...] = total
    scale = vec_ref[0:1, :] * vec_ref[1:2, :]
    pull, level = total[0:1] / bin_count, total[1:2] / bin_count
    for begin in range(0, rows + RIM, 96):
        part = slice(begin, min(begin + 96, rows + RIM))
        grad_ref[part, :] = (scale * (d_ref[part, :] - level - cen_ref[part, :] * pull)).astype(BF16)
    both_ref[:rows, :] = hid_ref[...]
    both_ref[rows:, :] = point_ref[...]


def out_kernel(x_ref, *refs):
    parts, (out_ref, hidden, point) = refs[:-3], refs[-3:]
    rows = x_ref.shape[0]
    for r, part in enumerate(parts):
        hidden[:, r * LANES : (r + 1) * LANES] = part[:rows, :]
        point[:, r * LANES : (r + 1) * LANES] = part[rows:, :]
    for at in range(0, x_ref.shape[1], 256):
        part = slice(at, at + 256)
        branch = lax.dot_general(
            hidden[...], point[part, :], LANE_DIMS, preferred_element_type=F32
        )
        out_ref[:, part] = (x_ref[:, part].astype(F32) + branch).astype(BF16)


def halve(blocks, kept_ref, sent_ref, high):
    for k in range(kept_ref.shape[0]):
        kept_ref[k] = blocks(2 * k + high)
        sent_ref[k] = blocks(2 * k + 1 - high).astype(BF16)


def terms_of(part, grad, term_ref, at, first, start, bin_count):
    rows = term_ref.shape[0]
    step = 64
    grad[...] = part[...].astype(F32)
    for j, shift in enumerate(SHIFTS):
        lanes = slice(at + j * LANES, at + (j + 1) * LANES)
        for begin in range(0, rows, step):
            mask = reach_of(first + begin - shift, step, shift, start, bin_count)
            value = grad[EDGE + begin - shift : EDGE + begin - shift + step, :]
            term_ref[begin : begin + step, lanes] = jnp.where(mask, value, 0.0).astype(BF16)


def weight_grad_kernel(
    start_ref, part_ref, hid_ref, cot_ref, mid_ref, term_ref, kept_ref, sent_ref, grad, full, *, bin_count, depth, slim
):
    rows = term_ref.shape[0]
    own = lax.axis_index("seq")
    terms_of(part_ref, grad, term_ref, 0, own * rows, start_ref[0], bin_count)
    taps = lax.dot_general(
        hid_ref[RIM : RIM + rows, :], term_ref[...], ROW_DIMS, preferred_element_type=F32
    )
    point = lax.dot_general(cot_ref[...], mid_ref[...], ROW_DIMS, preferred_element_type=F32)
    parts = [taps[:, j * LANES : j * LANES + slim] for j in range(KERNEL_WIDTH)] + [point[:, :slim]]
    full[...] = jnp.concatenate(parts, axis=1)
    high = own % 2
    halve(lambda k: full[pl.ds(pl.multiple_of(k * depth, 8), depth), :], kept_ref, sent_ref, high)


def fold_kernel(old_ref, got_ref, kept_ref, sent_ref, *, reach):
    high = (lax.axis_index("seq") // reach) % 2
    halve(lambda k: old_ref[k] + got_ref[k].astype(F32), kept_ref, sent_ref, high)


def adamw(weights_old, first_moment_state, second_mom, gradient, step_rate, decay_rate):
    first_next = BETA_ONE * first_moment_state + (1.0 - BETA_ONE) * gradient
    second_next = BETA_TWO * second_mom + (1.0 - BETA_TWO) * gradient * gradient
    corrected = (
        first_next
        / (1.0 - BETA_ONE**STEP)
        / (jnp.sqrt(second_next / (1.0 - BETA_TWO**STEP)) + ADAM_EPS)
    )
    weights_new = weights_old - step_rate * (corrected + decay_rate * weights_old)
    return (first_next, second_next, weights_new)


def weight_step_kernel(old_ref, got_ref, total_ref, *refs):
    conv, point, mid, outs = refs[:3], refs[3:6], refs[6:9], refs[9:]
    slim = conv[0].shape[2]
    both = old_ref[0] + got_ref[0].astype(F32)
    for j in range(KERNEL_WIDTH):
        grad = both[:, j * slim : (j + 1) * slim]
        new = adamw(*(ref[j] for ref in conv), grad, RATE_WEIGHT, DECAY_WEIGHT)
        for ref, value in zip(outs[:3], new):
            ref[j] = value
    grad = both[:, KERNEL_WIDTH * slim :].T
    new = adamw(*(ref[...] for ref in point), grad, RATE_WEIGHT, DECAY_WEIGHT)
    for ref, value in zip(outs[3:6], new):
        ref[...] = value
    new = adamw(*(ref[...] for ref in mid), total_ref[:, :slim], RATE_NORM, 0.0)
    for ref, value in zip(outs[6:], new):
        ref[...] = value


def first_half_kernel(start_ref, own_ref, *refs, bin_count):
    up_ref, term, weight, grad = refs[-4:]
    count = (len(refs) - 4 + 1) // 2
    grads, weights = refs[: count - 1], refs[count - 1 : -4]
    rows = up_ref.shape[0]
    wide = KERNEL_WIDTH * LANES
    first = lax.axis_index("seq") * rows
    term[:, :wide] = own_ref[...]
    for r, part in enumerate(grads):
        terms_of(part, grad, term, (r + 1) * wide, first, start_ref[0], bin_count)
    for r, piece in enumerate(weights):
        weight[:, r * wide : (r + 1) * wide] = piece[...]
    for at in range(0, up_ref.shape[1], 256):
        part = slice(at, at + 256)
        up_ref[:, part] = lax.dot_general(
            term[...], weight[part, :], LANE_DIMS, preferred_element_type=F32
        )


def second_half_kernel(start_ref, x_ref, slope_ref, vec_ref, part_ref, *refs, bin_count):
    d_ref, sum_ref, term, weight, grad = refs[-5:]
    count = (len(refs) - 5) // 2
    grads, weights = refs[:count], refs[count:-5]
    rows, width = x_ref.shape
    wide = KERNEL_WIDTH * LANES
    first = lax.axis_index("seq") * rows
    for r, part in enumerate(grads):
        terms_of(part, grad, term, r * wide, first, start_ref[0], bin_count)
    for r, piece in enumerate(weights):
        weight[:, r * wide : (r + 1) * wide] = piece[...]
    for at in range(0, width, 256):
        part = slice(at, at + 256)
        up = lax.dot_general(term[...], weight[part, :], LANE_DIMS, preferred_element_type=F32)
        d = (up + part_ref[:, part]) * slope_ref[:, part]
        d_ref[:, part] = d
        centered = x_ref[:, part].astype(F32) * vec_ref[0:1, part] + vec_ref[1:2, part]
        sum_ref[0:1, part] = jnp.sum(d * centered, 0, keepdims=True)
        sum_ref[1:2, part] = jnp.sum(d, 0, keepdims=True)


def final_kernel(x_ref, cot_ref, d_ref, vec_ref, one_ref, two_ref, *refs, bin_count):
    norms, out_ref, news = refs[:3], refs[3], refs[4:]
    rows, width = x_ref.shape
    total = one_ref[...] + two_ref[...]
    new = adamw(*(ref[...] for ref in norms), total, RATE_NORM, 0.0)
    for ref, value in zip(news, new):
        ref[...] = value
    root, offset, scale = vec_ref[0:1, :], vec_ref[1:2, :], vec_ref[2:3, :]
    pull = scale * total[0:1] / bin_count
    slant = pull * root
    level = scale * total[1:2] / bin_count + pull * offset
    step = 16

    def body(i, carry):
        at = pl.ds(pl.multiple_of(i * step, 16), step)
        value = x_ref[at, :].astype(F32) * slant + level
        out_ref[at, :] = cot_ref[at, :].astype(F32) + (d_ref[at, :] * scale - value)
        return carry

    lax.fori_loop(0, rows // step, body, 0, unroll=4)


def flip(axis, reach):
    return [(i, i ^ reach) for i in range(lax.axis_size(axis))]


def relatives_of(order):
    found = [0]
    for reach in order:
        found = found + [r ^ reach for r in found]
    return found


def descending(size):
    return [size >> k for k in range(1, size.bit_length())]


def round_kernel(*refs):
    ins, outs = refs[: 6 + (len(refs) - 9) // 2], refs[6 + (len(refs) - 9) // 2 :]
    for k in range(2):
        one, two, out = ins[2 * k], ins[2 * k + 1], outs[k]
        size = one.shape[0]
        out[:size] = one[...]
        out[size:] = two[...]
    outs[2][...] = ins[4][...] + ins[5][...]
    for src, out in zip(ins[6:], outs[3:]):
        out[...] = src[...]


def add_kernel(one_ref, two_ref, out_ref):
    out_ref[...] = one_ref[...] + two_ref[...]


def add(one, two, after=()):
    return call(add_kernel, [(one.shape, one.dtype)], [one, two], after=after)[0]


def swap(x, axis, reach):
    return lax.ppermute(x, axis, flip(axis, reach))


def gather_parts(x, reaches):
    parts = [x]
    for reach in reaches:
        parts += [swap(part, "ch", reach) for part in parts]
    return parts


def spread(copies, axes):
    return lax.all_to_all(copies, axes, 0, 0, tiled=True)


def shards(
    inputs,
    cotangent,
    starts,
    master_conv,
    first_conv,
    second_conv,
    master_point,
    first_point,
    second_point,
    norm_in,
    first_in,
    second_in,
    norm_mid,
    first_mid,
    second_mid,
):
    rows, width = inputs.shape
    seq_size, ch_size = lax.axis_size("seq"), lax.axis_size("ch")
    bin_count = rows * seq_size
    depth, slim = master_conv.shape[1:]
    tiles = width // LANES
    wide = KERNEL_WIDTH * LANES
    weight_order = descending(seq_size)
    sum_order = weight_order[::-1]
    point_order = [1] + weight_order[:-1]
    ch_order = descending(ch_size)
    ext = rows + 2 * EDGE

    (conv_low,) = call(pack_kernel, [((depth, wide), BF16)], [master_conv])
    sums_in, point_low, last, first = call(
        stats_kernel,
        [((up_to(2 * tiles, 8), LANES), F32), ((depth, LANES), BF16)]
        + [((RIM + EDGE, width), BF16)] * 2,
        [inputs, cotangent[:EDGE], cotangent[rows - EDGE :], master_point],
    )
    up = [(i, i + 1) for i in range(seq_size - 1)]
    down = [(j, i) for i, j in up]
    before = lax.ppermute(last, "seq", up)
    after = lax.ppermute(first, "seq", down)
    held = [conv_low[None], point_low[None], sums_in]
    rounds = len(weight_order)
    top, lower = ch_order[0], ch_order[1:]
    for k in range(rounds):
        got = [
            swap(x, "seq", order[k]) for x, order in zip(held, (weight_order, point_order, sum_order))
        ]
        if k < rounds - 1:
            extra = [before, after] if k == rounds - 2 else []
            shapes = [((2 * x.shape[0],) + x.shape[1:], BF16) for x in held[:2]]
            held = call(
                round_kernel,
                shapes + [(x.shape, x.dtype) for x in [sums_in, *extra]],
                [held[0], got[0], held[1], got[1], held[2], got[2], *extra],
            )
            if extra:
                before, after = held[3:]
                held = held[:3]
    far_one = swap(held[0], "ch", top)
    hidden_in, slope_in, vec_in = call(
        functools.partial(act_kernel, bin_count=bin_count),
        [((rows + 2 * RIM, width), BF16), ((rows, width), F32), ((8, width), F32)],
        [inputs, before, after, held[2], got[2], norm_in],
        flops=40 * rows * width,
    )

    stack_type = BF16 if depth % 16 == 0 else F32
    conv_own, conv_out, sums_mid = call(
        functools.partial(
            conv_kernel, relatives=relatives_of(weight_order), bin_count=bin_count
        ),
        [((width, wide), BF16), ((ext, LANES), F32), ((8, LANES), F32)],
        [starts, hidden_in, held[0], got[0]],
        scratch=[((seq_size, depth, wide), stack_type), ((rows + 2 * RIM, wide), F32)],
        smem=(0,),
        flops=2 * rows * width * wide,
    )
    far_two = swap(got[0], "ch", top)
    upstream, point_own = call(
        functools.partial(upstream_kernel, relatives=relatives_of(point_order)),
        [((ext, LANES), F32), ((width, LANES), BF16)],
        [cotangent, before, after, held[1], got[1]],
        scratch=[((seq_size, depth, LANES), stack_type)],
        after=[sums_mid],
        flops=2 * rows * width * LANES,
    )
    (conv_far,) = call(
        functools.partial(place_kernel, relatives=relatives_of(weight_order)),
        [((width, wide), BF16)],
        [far_one, far_two],
        scratch=[((seq_size, depth, wide), stack_type)],
        after=[upstream],
    )
    total = sums_mid
    for k, reach in enumerate(sum_order):
        total_got = swap(total, "seq", reach)
        if k < rounds - 1:
            total = add(total, total_got, [conv_far] if k == rounds - 2 else [upstream])
    conv_near, conv_far = gather_parts(conv_own, lower), gather_parts(conv_far, lower)
    hidden_mid, d_mid, centered, sent_back, vec_mid = call(
        functools.partial(mid_kernel, bin_count=bin_count),
        [
            ((rows, LANES), BF16),
            ((ext, LANES), F32),
            ((ext, LANES), F32),
            ((seq_size, 2, LANES), F32),
            ((8, LANES), F32),
        ],
        [total, total_got, conv_out, upstream, norm_mid],
        after=[*conv_near[1:], *conv_far[1:]],
        flops=40 * rows * LANES,
    )
    got_back = spread(sent_back, "seq")
    grad_own, total_mid, both = call(
        functools.partial(conv_back_kernel, bin_count=bin_count),
        [((ext, LANES), BF16), ((2, LANES), F32), ((rows + width, LANES), BF16)],
        [got_back, vec_mid, d_mid, centered, hidden_mid, point_own],
    )
    grad_near = gather_parts(grad_own, lower)
    grad_far = gather_parts(swap(grad_own, "ch", top), lower)
    half = seq_size // 2
    terms, kept, sent = call(
        functools.partial(weight_grad_kernel, bin_count=bin_count, depth=depth, slim=slim),
        [
            ((rows, wide), BF16),
            ((half, depth, 4 * slim), F32),
            ((half, depth, 4 * slim), BF16),
        ],
        [starts, grad_own, hidden_in, cotangent, hidden_mid],
        scratch=[((ext, LANES), F32), ((width, 4 * slim), F32)],
        smem=(0,),
        flops=2 * rows * width * (wide + LANES),
    )
    side = ch_size // 2 * wide
    (up_part,) = call(
        functools.partial(first_half_kernel, bin_count=bin_count),
        [((rows, width), F32)],
        [starts, terms, *grad_near[1:], *conv_near],
        scratch=[((rows, side), BF16), ((width, side), BF16), ((ext, LANES), F32)],
        smem=(0,),
        flops=2 * rows * width * side,
    )
    both_far = swap(both, "ch", top)
    d_in, sums_back = call(
        functools.partial(second_half_kernel, bin_count=bin_count),
        [((rows, width), F32), ((2, width), F32)],
        [starts, inputs, slope_in, vec_in, up_part, *grad_far, *conv_far],
        scratch=[((rows, side), BF16), ((width, side), BF16), ((ext, LANES), F32)],
        smem=(0,),
        flops=2 * rows * width * side,
    )
    parts = gather_parts(both, lower) + gather_parts(both_far, lower)
    (block_out,) = call(
        out_kernel,
        [((rows, width), BF16)],
        [inputs, *parts],
        scratch=[((rows, ch_size * LANES), BF16), ((width, ch_size * LANES), BF16)],
        after=[sums_back],
        flops=2 * rows * width * ch_size * LANES,
    )
    total_back = sums_back
    for k, reach in enumerate(sum_order):
        total_got = swap(total_back, "seq", reach)
        got = swap(sent, "seq", reach)
        if k < rounds - 1:
            half //= 2
            kept, sent = call(
                functools.partial(fold_kernel, reach=2 * reach),
                [((half, depth, 4 * slim), F32), ((half, depth, 4 * slim), BF16)],
                [kept, got],
                after=[total_back],
            )
            total_back = add(total_back, total_got, [sent] + [block_out] * (k == rounds - 2))
    input_grad, *in_new = call(
        functools.partial(final_kernel, bin_count=bin_count),
        [((rows, width), F32)] + [((2, width), F32)] * 3,
        [inputs, cotangent, d_in, vec_in, total_back, total_got, norm_in, first_in, second_in],
        flops=10 * rows * width,
    )
    news = call(
        weight_step_kernel,
        [(master_conv.shape, F32)] * 3 + [(master_point.shape, F32)] * 3 + [(norm_mid.shape, F32)] * 3,
        [kept, got, total_mid, master_conv, first_conv, second_conv]
        + [master_point, first_point, second_point, norm_mid, first_mid, second_mid],
    )
    return (block_out, input_grad, *news[:6], *in_new, *news[6:])


def solution(mesh):
    in_specs = (
        P("seq", None),
        P("seq", None),
        P(),
        P(None, "seq", "ch"),
        P(None, "seq", "ch"),
        P(None, "seq", "ch"),
        P("ch", "seq"),
        P("ch", "seq"),
        P("ch", "seq"),
        P(),
        P(),
        P(),
        P(None, "ch"),
        P(None, "ch"),
        P(None, "ch"),
    )
    out_specs = (
        P("seq", None),
        P("seq", None),
        P(None, "seq", "ch"),
        P(None, "seq", "ch"),
        P(None, "seq", "ch"),
        P("ch", "seq"),
        P("ch", "seq"),
        P("ch", "seq"),
        P(),
        P(),
        P(),
        P(None, "ch"),
        P(None, "ch"),
        P(None, "ch"),
    )
    return jax.shard_map(shards, mesh=mesh, in_specs=in_specs, out_specs=out_specs, check_vma=False)
```

```python
import functools

import jax
import jax.numpy as jnp
from jax import lax
from jax.experimental import pallas as pl
from jax.experimental.pallas import tpu as pltpu
from jax.sharding import PartitionSpec as P

KERNEL_WIDTH = 3
DILATION_BINS = 9
WIN = 1024
STEP = 10

NORM_EPS = 1e-05
ADAM_EPS = 1e-08
BETA_ONE = 0.9
BETA_TWO = 0.999
RATE_WEIGHT = 0.05
RATE_NORM = 0.5
DECAY_WEIGHT = 0.01

LANES = 128
EDGE = 16
RIM = 2 * EDGE
SUMS = 48
GELU_A = 0.7978845608028654
GELU_B = 0.044715
SHIFTS = [(j - KERNEL_WIDTH // 2) * DILATION_BINS for j in range(KERNEL_WIDTH)]
ROW_DIMS = (((0,), (0,)), ((), ()))
LANE_DIMS = (((1,), (1,)), ((), ()))
F32, BF16 = jnp.float32, jnp.bfloat16


def call(body, outs, args, scratch=(), smem=(), away=(), after=(), sems=0, away_outs=(), limit=16):
    spaces = [pltpu.SMEM if k in smem else pltpu.VMEM for k in range(len(args))]
    spaces = [pltpu.HBM if k in away else space for k, space in enumerate(spaces)]
    spaces += [pl.ANY] * len(after)

    args = [
        pltpu.with_memory_space_constraint(x, pltpu.HBM) if k in away else x
        for k, x in enumerate(args)
    ]

    def kernel(*refs):
        body(*refs[: len(args)], *refs[len(spaces) :])

    return pl.pallas_call(
        kernel,
        out_shape=[jax.ShapeDtypeStruct(s, t) for s, t in outs],
        in_specs=[pl.BlockSpec(memory_space=s) for s in spaces],
        out_specs=[
            pl.BlockSpec(memory_space=pltpu.HBM if k in away_outs else pltpu.VMEM)
            for k in range(len(outs))
        ],
        scratch_shapes=[pltpu.VMEM(s, t) for s, t in scratch]
        + [pltpu.SemaphoreType.DMA((sems,))] * (sems > 0),
        compiler_params=pltpu.CompilerParams(vmem_limit_bytes=limit * 2**20),
        cost_estimate=pl.CostEstimate(flops=1, bytes_accessed=1, transcendentals=0),
        name=getattr(body, "func", body).__name__,
    )(*args, *after)


def up_to(size, step):
    return -(-size // step) * step


def split_three(v):
    high = v.astype(BF16).astype(F32)
    rest = v - high
    middle = rest.astype(BF16).astype(F32)
    return high, middle, rest - middle


def gelu_and_slope(v):
    square = v * v
    t = jnp.tanh(v * (GELU_A + (GELU_A * GELU_B) * square))
    half = 0.5 * (1.0 + t)
    slope = half + (0.5 * v) * (1.0 - t * t) * (GELU_A + (3.0 * GELU_A * GELU_B) * square)
    return v * half, slope


def reach_of(first, count, shift, start, bin_count):
    here = first + lax.broadcasted_iota(jnp.int32, (count, LANES), 0)
    there = here + shift
    inside = (here >= 0) & (here < bin_count) & (there >= 0) & (there < bin_count)
    return inside & (((here - start) >> 10) == ((there - start) >> 10))


def folds(depth, slim):
    return 3 * (LANES - slim) == slim and depth % 32 == 0


def fold_rows(block):
    rows, slim = block.shape
    quarter, width = rows // 4, LANES - slim
    side = [block[3 * quarter :, p * width : (p + 1) * width] for p in range(3)]
    return jnp.concatenate([block[: 3 * quarter], jnp.concatenate(side, axis=0)], axis=1)


def unfold_rows(block, slim):
    quarter, width = block.shape[0] // 3, LANES - slim
    side = [block[p * quarter : (p + 1) * quarter, slim:] for p in range(3)]
    side.append(jnp.zeros((quarter, width), block.dtype))
    lane = lax.broadcasted_iota(jnp.int32, block.shape, 1)
    return jnp.concatenate([jnp.where(lane < slim, block, 0.0), jnp.concatenate(side, axis=1)], axis=0)


def first_kernel(
    x_hbm, cot_hbm, conv_hbm, point_hbm, x_ref, weight_ref, near_ref, rim_ref, edge_ref, conv_ref, point_ref, sum_ref, sems
):
    rows, width = x_ref.shape
    tiles = width // LANES
    depth, slim = conv_ref.shape[1:]
    chunks = sems.shape[0] - 4
    chunk = rows // chunks
    copies = [
        pltpu.make_async_copy(conv_hbm, conv_ref, sems.at[0]),
        pltpu.make_async_copy(point_hbm, point_ref, sems.at[1]),
        pltpu.make_async_copy(cot_hbm.at[pl.ds(0, EDGE)], edge_ref.at[0], sems.at[2]),
        pltpu.make_async_copy(cot_hbm.at[pl.ds(rows - EDGE, EDGE)], edge_ref.at[1], sems.at[3]),
    ]
    for k in range(chunks):
        part = pl.ds(k * chunk, chunk)
        copies.append(pltpu.make_async_copy(x_hbm.at[part], x_ref.at[part], sems.at[4 + k]))
    for copy in copies:
        copy.start()
    weight_ref[...] = jnp.zeros_like(weight_ref)
    near_ref[...] = jnp.zeros_like(near_ref)
    sum_ref[...] = jnp.zeros_like(sum_ref)
    copies[0].wait()
    for j in range(KERNEL_WIDTH):
        if folds(depth, slim):
            weight_ref[0, :, j * LANES : (j + 1) * LANES] = fold_rows(conv_ref[j]).astype(BF16)
        else:
            weight_ref[0, :, j * LANES : j * LANES + slim] = conv_ref[j].astype(BF16)
    copies[1].wait()
    near_ref[SUMS : SUMS + depth, :slim] = point_ref[...].T.astype(BF16)

    def step(k, carry):
        v = x_ref[pl.ds(pl.multiple_of(k * 32, 32), 32), :].astype(F32)
        v = v.reshape(4, 8, width)
        return carry[0] + v.sum(0), carry[1] + (v * v).sum(0)

    totals = (jnp.zeros((8, width), F32),) * 2
    for k in range(chunks):
        copies[4 + k].wait()
        totals = lax.fori_loop(
            k * chunk // 32, (k + 1) * chunk // 32, step, totals, unroll=chunk // 32
        )
    for stat, total in enumerate(totals):
        total = jnp.sum(total, 0, keepdims=True)
        for k in range(tiles):
            row = stat * tiles + k
            sum_ref[row : row + 1, :] = total[:, k * LANES : (k + 1) * LANES]
    put_sums(near_ref, sum_ref[...])
    copies[2].wait()
    copies[3].wait()
    for side in range(2):
        begin = (rows - RIM) * side
        rim_ref[side, :RIM, :] = x_ref[begin : begin + RIM, :]
        rim_ref[side, RIM:, :] = edge_ref[side]


def put_sums(ref, value):
    for p, part in enumerate(split_three(value)):
        ref[p * 16 : (p + 1) * 16, :] = part.astype(BF16)


def get_sums(ref):
    return sum(ref[p * 16 : (p + 1) * 16, :].astype(F32) for p in range(3))


def act_kernel(
    x_ref, cot_hbm, rim_ref, one_ref, two_ref, norm_ref, hid_ref, vec_ref, cot_ref, sems, *, bin_count
):
    copy = pltpu.make_async_copy(cot_hbm, cot_ref, sems.at[0])
    copy.start()
    rows, width = x_ref.shape
    tiles = width // LANES
    total = get_sums(one_ref) + get_sums(two_ref)
    for k in range(tiles):
        lanes = slice(k * LANES, (k + 1) * LANES)
        mean = total[k : k + 1, :] / bin_count
        square = total[tiles + k : tiles + k + 1, :] / bin_count
        root = lax.rsqrt(square - mean * mean + NORM_EPS)
        gain = root * norm_ref[0:1, lanes]
        vec_ref[0:1, lanes] = root
        vec_ref[1:2, lanes] = -mean * root
        vec_ref[2:3, lanes] = gain
        vec_ref[3:4, lanes] = norm_ref[1:2, lanes] - mean * gain

    gain, bias = vec_ref[2:3, :], vec_ref[3:4, :]
    for side, at in enumerate((0, RIM + rows)):
        for k in range(0, RIM, 16):
            hidden, _ = gelu_and_slope(rim_ref[side, k : k + 16, :].astype(F32) * gain + bias)
            hid_ref[at + k : at + k + 16, :] = hidden.astype(BF16)

    def step(k, carry):
        at = pl.multiple_of(k * 16, 16)
        v = x_ref[pl.ds(at, 16), :].astype(F32) * vec_ref[2:3, :] + vec_ref[3:4, :]
        hid_ref[pl.ds(pl.multiple_of(at + RIM, 16), 16), :] = gelu_and_slope(v)[0].astype(BF16)
        return carry

    lax.fori_loop(0, rows // 16, step, 0, unroll=2)
    copy.wait()


def place(pieces, relatives, stack, own, slim):
    depth = stack.shape[1]
    at = 0
    for piece in pieces:
        for k in range(piece.shape[0]):
            block = piece[k].astype(F32)
            for j in range(KERNEL_WIDTH):
                part = block[:, j * LANES : (j + 1) * LANES]
                if folds(depth, slim):
                    part = unfold_rows(part, slim)
                stack[own ^ relatives[at], :, j * LANES : (j + 1) * LANES] = part.astype(stack.dtype)
            at += 1
    return stack[...].reshape(-1, stack.shape[2]).astype(BF16)


def place_kernel(*refs, relatives, slim):
    pieces, (out_ref, stack) = refs[:-2], refs[-2:]
    out_ref[...] = place(pieces, relatives, stack, lax.axis_index("seq"), slim)


def mask_kernel(start_ref, ahead_ref, back_ref):
    rows = back_ref.shape[1]
    first = lax.axis_index("seq") * rows
    for j, shift in enumerate(SHIFTS):
        for begin in range(0, rows + RIM, 96):
            count = min(96, rows + RIM - begin)
            mask = reach_of(first + begin - EDGE, count, shift, start_ref[0], rows * lax.axis_size("seq"))
            ahead_ref[j, begin : begin + count, :] = jnp.where(mask, 1.0, 0.0)
        for begin in range(0, rows, 128):
            back_ref[j, begin : begin + 128, :] = ahead_ref[
                j, EDGE + begin - shift : EDGE + begin - shift + 128, :
            ]


def slope_kernel(x_ref, vec_ref, slope_ref):
    def step(k, carry):
        at = pl.ds(pl.multiple_of(k * 16, 16), 16)
        v = x_ref[at, :].astype(F32) * vec_ref[2:3, :] + vec_ref[3:4, :]
        slope_ref[at, :] = gelu_and_slope(v)[1]
        return carry

    lax.fori_loop(0, x_ref.shape[0] // 16, step, 0, unroll=2)


def conv_kernel(mask_ref, hid_ref, *refs, relatives, slim):
    pieces, (weight_ref, out_ref, sum_ref, all_ref, stack, prod) = refs[:-6], refs[-6:]
    size = all_ref.shape[0] // 2
    for k, piece in enumerate(pieces):
        all_ref[k * size : (k + 1) * size] = piece[...]
    rows = hid_ref.shape[0] - 2 * RIM
    weight_ref[...] = place(pieces, relatives, stack, lax.axis_index("seq"), slim)
    for at in range(0, weight_ref.shape[1], 256):
        part = slice(at, min(at + 256, weight_ref.shape[1]))
        prod[:, part] = jnp.dot(hid_ref[...], weight_ref[:, part], preferred_element_type=F32)

    def rows_of(begin, count):
        value = 0.0
        for j, shift in enumerate(SHIFTS):
            part = prod[begin + EDGE + shift : begin + EDGE + shift + count, j * LANES : (j + 1) * LANES]
            value = value + mask_ref[j, begin : begin + count, :] * part
        out_ref[begin : begin + count, :] = value
        return value

    rows_of(0, EDGE)
    rows_of(EDGE + rows, EDGE)
    one = two = jnp.zeros((8, LANES), F32)
    step = 128
    for k in range(rows // step):
        value = rows_of(EDGE + k * step, step).reshape(step // 8, 8, LANES)
        one = one + value.sum(0)
        two = two + (value * value).sum(0)
    sum_ref[...] = jnp.zeros_like(sum_ref)
    sum_ref[0:1, :] = jnp.sum(one, 0, keepdims=True)
    sum_ref[1:2, :] = jnp.sum(two, 0, keepdims=True)


def upstream_kernel(cot_ref, rim_ref, one_ref, two_ref, up_ref, point_ref, stack, *, relatives):
    rows = cot_ref.shape[0]
    depth = stack.shape[1]
    own = lax.axis_index("seq")
    count = len(relatives) // 2
    for k, relative in enumerate(relatives):
        piece = (one_ref, two_ref)[k // count]
        at = SUMS + (k % count) * up_to(depth, 16)
        stack[own ^ relative] = piece[at : at + depth, :].astype(stack.dtype)
    point_ref[...] = stack[...].reshape(point_ref.shape).astype(BF16)
    for side, at in enumerate((0, EDGE + rows)):
        up_ref[at : at + EDGE, :] = jnp.dot(
            rim_ref[side, RIM:, :], point_ref[...], preferred_element_type=F32
        )
    up_ref[EDGE : EDGE + rows, :] = jnp.dot(
        cot_ref[...], point_ref[...], preferred_element_type=F32
    )


def mid_kernel(
    total_ref, conv_ref, up_ref, norm_ref, hid_ref, d_ref, cen_ref, sent_ref, vec_ref, *, bin_count
):
    rows = hid_ref.shape[0]
    slim = norm_ref.shape[1]
    total = total_ref[...]
    mean = total[0:1] / bin_count
    root = lax.rsqrt(total[1:2] / bin_count - mean * mean + NORM_EPS)
    vec_ref[...] = jnp.zeros_like(vec_ref)
    vec_ref[0:1, :] = root
    vec_ref[1:3, :slim] = norm_ref[...]
    gain, bias = vec_ref[1:2, :], vec_ref[2:3, :]

    def rows_of(begin, count):
        centered = (conv_ref[pl.ds(begin, count), :] - mean) * root
        hidden, slope = gelu_and_slope(centered * gain + bias)
        d = up_ref[pl.ds(begin, count), :] * slope
        cen_ref[pl.ds(begin, count), :] = centered
        d_ref[pl.ds(begin, count), :] = d
        return centered, hidden, d

    rows_of(0, EDGE)
    rows_of(EDGE + rows, EDGE)
    step = 64

    def body(i, carry):
        begin = pl.multiple_of(EDGE + i * step, 16)
        centered, hidden, d = rows_of(begin, step)
        hid_ref[pl.ds(pl.multiple_of(i * step, 16), step), :] = hidden.astype(BF16)
        d = d.reshape(step // 8, 8, LANES)
        return carry[0] + (d * centered.reshape(d.shape)).sum(0), carry[1] + d.sum(0)

    zero = jnp.zeros((8, LANES), F32)
    gain_sum, bias_sum = lax.fori_loop(0, rows // step, body, (zero, zero), unroll=2)
    gain_sum = jnp.sum(gain_sum, 0, keepdims=True)
    bias_sum = jnp.sum(bias_sum, 0, keepdims=True)
    for d in range(sent_ref.shape[0]):
        sent_ref[d, 0:1, :] = gain_sum
        sent_ref[d, 1:2, :] = bias_sum


def conv_back_kernel(got_ref, vec_ref, d_ref, cen_ref, grad_ref, total_ref, grad, *, bin_count, slim):
    total = got_ref[0]
    for s in range(1, got_ref.shape[0]):
        total = total + got_ref[s]
    total_ref[...] = total
    scale = vec_ref[0:1, :] * vec_ref[1:2, :]
    pull, level = total[0:1] / bin_count, total[1:2] / bin_count
    count = d_ref.shape[0]
    for begin in range(0, count, 96):
        part = slice(begin, min(begin + 96, count))
        grad[part, :] = scale * (d_ref[part, :] - level - cen_ref[part, :] * pull)
    if folds(count, slim):
        grad_ref[...] = fold_rows(grad[:, :slim]).astype(BF16)
    else:
        grad_ref[...] = grad[...].astype(BF16)


def out_kernel(x_ref, *refs):
    parts, (out_ref, token_ref, hidden, point) = refs[:-4], refs[-4:]
    token_ref[...] = jnp.zeros_like(token_ref)
    rows = x_ref.shape[0]
    for r, part in enumerate(parts):
        hidden[:, r * LANES : (r + 1) * LANES] = part[:rows, :]
        point[:, r * LANES : (r + 1) * LANES] = part[rows:, :]
    for at in range(0, x_ref.shape[1], 256):
        part = slice(at, at + 256)
        branch = lax.dot_general(
            hidden[...], point[part, :], LANE_DIMS, preferred_element_type=F32
        )
        out_ref[:, part] = (x_ref[:, part].astype(F32) + branch).astype(BF16)


def halve(blocks, kept_ref, sent_ref, high):
    for k in range(kept_ref.shape[0]):
        kept_ref[k] = blocks(2 * k + high)
        sent_ref[k] = blocks(2 * k + 1 - high).astype(BF16)


def terms_of(part, grad, term_ref, at, mask_ref):
    rows = term_ref.shape[0]
    step = 64
    count = part.shape[0]
    grad[:count, :] = part[...].astype(F32)
    if count < grad.shape[0]:
        quarter = count // 3
        width = LANES // 4
        side = [grad[p * quarter : (p + 1) * quarter, 3 * width :] for p in range(3)]
        grad[count:, :] = jnp.concatenate(side + [jnp.zeros((quarter, width), F32)], axis=1)
    for j, shift in enumerate(SHIFTS):
        lanes = slice(at + j * LANES, at + (j + 1) * LANES)
        for begin in range(0, rows, step):
            value = grad[EDGE + begin - shift : EDGE + begin - shift + step, :]
            value = value * mask_ref[j, begin : begin + step, :]
            term_ref[begin : begin + step, lanes] = value.astype(BF16)


def weight_grad_kernel(
    mask_ref, part_ref, hid_ref, cot_ref, mid_ref, term_ref, kept_ref, sent_ref, grad, full, *, depth, slim
):
    rows = term_ref.shape[0]
    terms_of(part_ref, grad, term_ref, 0, mask_ref)
    taps = lax.dot_general(
        hid_ref[RIM : RIM + rows, :], term_ref[...], ROW_DIMS, preferred_element_type=F32
    )
    point = lax.dot_general(cot_ref[...], mid_ref[...], ROW_DIMS, preferred_element_type=F32)
    parts = [taps[:, j * LANES : j * LANES + slim] for j in range(KERNEL_WIDTH)] + [point[:, :slim]]
    full[...] = jnp.concatenate(parts, axis=1)
    high = lax.axis_index("seq") % 2
    halve(lambda k: full[pl.ds(pl.multiple_of(k * depth, 8), depth), :], kept_ref, sent_ref, high)


def fold_kernel(old_ref, got_ref, kept_ref, sent_ref, *, reach):
    high = (lax.axis_index("seq") // reach) % 2
    halve(lambda k: old_ref[k] + got_ref[k].astype(F32), kept_ref, sent_ref, high)


def adamw(weights_old, first_moment_state, second_mom, gradient, step_rate, decay_rate):
    first_next = BETA_ONE * first_moment_state + (1.0 - BETA_ONE) * gradient
    second_next = BETA_TWO * second_mom + (1.0 - BETA_TWO) * gradient * gradient
    corrected = (
        first_next
        / (1.0 - BETA_ONE**STEP)
        / (jnp.sqrt(second_next / (1.0 - BETA_TWO**STEP)) + ADAM_EPS)
    )
    weights_new = weights_old - step_rate * (corrected + decay_rate * weights_old)
    return (first_next, second_next, weights_new)


def weight_step_kernel(old_ref, got_ref, total_ref, *refs):
    conv, point, mid, outs = refs[:3], refs[3:6], refs[6:9], refs[9:]
    slim = conv[0].shape[2]
    both = old_ref[0] + got_ref[0].astype(F32)
    for j in range(KERNEL_WIDTH):
        grad = both[:, j * slim : (j + 1) * slim]
        new = adamw(*(ref[j] for ref in conv), grad, RATE_WEIGHT, DECAY_WEIGHT)
        for ref, value in zip(outs[:3], new):
            ref[j] = value
    grad = both[:, KERNEL_WIDTH * slim :].T
    new = adamw(*(ref[...] for ref in point), grad, RATE_WEIGHT, DECAY_WEIGHT)
    for ref, value in zip(outs[3:6], new):
        ref[...] = value
    new = adamw(*(ref[...] for ref in mid), total_ref[:, :slim], RATE_NORM, 0.0)
    for ref, value in zip(outs[6:], new):
        ref[...] = value


def first_half_kernel(mask_ref, own_ref, hid_ref, point_ref, *refs):
    up_ref, both_ref, term, weight, grad = refs[-5:]
    count = (len(refs) - 5 + 1) // 2
    grads, weights = refs[: count - 1], refs[count - 1 : -5]
    rows = up_ref.shape[0]
    both_ref[:rows, :] = hid_ref[...]
    both_ref[rows:, :] = point_ref[...]
    wide = KERNEL_WIDTH * LANES
    term[:, :wide] = own_ref[...]
    for r, part in enumerate(grads):
        terms_of(part, grad, term, (r + 1) * wide, mask_ref)
    for r, piece in enumerate(weights):
        weight[:, r * wide : (r + 1) * wide] = piece[...]
    for at in range(0, up_ref.shape[1], 256):
        part = slice(at, at + 256)
        up_ref[:, part] = lax.dot_general(
            term[...], weight[part, :], LANE_DIMS, preferred_element_type=F32
        )


def second_half_kernel(mask_ref, x_ref, slope_ref, vec_ref, part_ref, *refs):
    d_ref, sum_ref, term, weight, grad = refs[-5:]
    count = (len(refs) - 5) // 2
    grads, weights = refs[:count], refs[count:-5]
    rows, width = x_ref.shape
    wide = KERNEL_WIDTH * LANES
    for r, part in enumerate(grads):
        terms_of(part, grad, term, r * wide, mask_ref)
    for r, piece in enumerate(weights):
        weight[:, r * wide : (r + 1) * wide] = piece[...]
    for at in range(0, width, 256):
        part = slice(at, at + 256)
        up = lax.dot_general(term[...], weight[part, :], LANE_DIMS, preferred_element_type=F32)
        d = (up + part_ref[:, part]) * slope_ref[:, part]
        d_ref[:, part] = d
        centered = x_ref[:, part].astype(F32) * vec_ref[0:1, part] + vec_ref[1:2, part]
        sum_ref[0:1, part] = jnp.sum(d * centered, 0, keepdims=True)
        sum_ref[1:2, part] = jnp.sum(d, 0, keepdims=True)


def final_kernel(x_ref, cot_ref, d_ref, vec_ref, one_ref, two_ref, *refs, bin_count):
    norms, out_hbm, news, (out_ref, sems) = refs[:3], refs[3], refs[4:-2], refs[-2:]
    rows, width = x_ref.shape
    total = one_ref[...] + two_ref[...]
    root, offset, scale = vec_ref[0:1, :], vec_ref[1:2, :], vec_ref[2:3, :]
    pull = scale * total[0:1] / bin_count
    slant = pull * root
    level = scale * total[1:2] / bin_count + pull * offset
    step = 16
    chunk = rows // sems.shape[0]

    def body(i, carry):
        at = pl.ds(pl.multiple_of(i * step, 16), step)
        value = x_ref[at, :].astype(F32) * slant + level
        out_ref[at, :] = cot_ref[at, :].astype(F32) + (d_ref[at, :] * scale - value)
        return carry

    sends = []
    for k in range(sems.shape[0]):
        lax.fori_loop(k * chunk // step, (k + 1) * chunk // step, body, 0, unroll=4)
        part = pl.ds(k * chunk, chunk)
        sends.append(pltpu.make_async_copy(out_ref.at[part], out_hbm.at[part], sems.at[k]))
        sends[-1].start()
    new = adamw(*(ref[...] for ref in norms), total, RATE_NORM, 0.0)
    for ref, value in zip(news, new):
        ref[...] = value
    for send in sends:
        send.wait()


def flip(axis, reach):
    return [(i, i ^ reach) for i in range(lax.axis_size(axis))]


def relatives_of(order):
    found = [0]
    for reach in order:
        found = found + [r ^ reach for r in found]
    return found


def descending(size):
    return [size >> k for k in range(1, size.bit_length())]


def round_kernel(weight_one, weight_two, one_ref, two_ref, *refs, count=0):
    rims, (weight_ref, out_ref), outs = refs[:count], refs[count : count + 2], refs[count + 2 :]
    size = weight_one.shape[0]
    weight_ref[:size] = weight_one[...]
    weight_ref[size:] = weight_two[...]
    put_sums(out_ref, get_sums(one_ref) + get_sums(two_ref))
    size = (out_ref.shape[0] - SUMS) // 2
    out_ref[SUMS : SUMS + size, :] = one_ref[SUMS : SUMS + size, :]
    out_ref[SUMS + size :, :] = two_ref[SUMS : SUMS + size, :]
    odd = lax.axis_index("seq") % 2
    if len(rims) == 1:
        outs[0][...] = rims[0][1 - odd]
        outs[1][...] = rims[0][odd]
    elif rims:
        outs[0][1 - odd] = rims[0][...]
        outs[0][odd] = rims[1][...]


def copy_kernel(*refs):
    count = len(refs) // 2
    for src, out in zip(refs[:count], refs[count:]):
        out[...] = src[...]


def copies(arrays, after):
    return call(copy_kernel, [(x.shape, x.dtype) for x in arrays], arrays, after=after)


def add_kernel(one_ref, two_ref, out_ref):
    out_ref[...] = one_ref[...] + two_ref[...]


def add(one, two, after=()):
    return call(add_kernel, [(one.shape, one.dtype)], [one, two], after=after)[0]


def swap(x, axis, reach):
    return lax.ppermute(x, axis, flip(axis, reach))


def gather_parts(x, reaches):
    parts = [x]
    for reach in reaches:
        parts += [swap(part, "ch", reach) for part in parts]
    return parts


def spread(copies, axes):
    return lax.all_to_all(copies, axes, 0, 0, tiled=True)


def shards(
    inputs,
    cotangent,
    starts,
    master_conv,
    first_conv,
    second_conv,
    master_point,
    first_point,
    second_point,
    norm_in,
    first_in,
    second_in,
    norm_mid,
    first_mid,
    second_mid,
):
    rows, width = inputs.shape
    seq_size, ch_size = lax.axis_size("seq"), lax.axis_size("ch")
    bin_count = rows * seq_size
    depth, slim = master_conv.shape[1:]
    tiles = width // LANES
    wide = KERNEL_WIDTH * LANES
    weight_order = descending(seq_size)
    sum_order = weight_order[::-1]
    last_order = weight_order[:1] + sum_order[:-1]
    point_order = weight_order[:1] + [1] + weight_order[1:-1]
    ch_order = descending(ch_size)
    ext = rows + 2 * EDGE

    rounds = len(weight_order)
    top, lower = ch_order[0], ch_order[1:]
    chunks = 4
    rim = (RIM + EDGE, width)
    packed = 3 * depth // 4 if folds(depth, slim) else depth
    inputs, weight, near, rims = call(
        first_kernel,
        [
            (inputs.shape, BF16),
            ((1, packed, wide), BF16),
            ((SUMS + up_to(depth, 16), LANES), BF16),
            ((2, *rim), BF16),
        ],
        [inputs, cotangent, master_conv, master_point],
        scratch=[
            ((2, EDGE, width), BF16),
            (master_conv.shape, F32),
            (master_point.shape, F32),
            ((16, LANES), F32),
        ],
        away=(0, 1, 2, 3),
        sems=4 + chunks,
    )
    pairs = [(i, i + 1) for i in range(1, seq_size - 1, 2)]
    for k in range(rounds):
        weight_got = swap(weight, "seq", weight_order[k])
        near_got = swap(near, "seq", point_order[k])
        if k < rounds - 1:
            outs = [
                ((2 * weight.shape[0], packed, wide), BF16),
                ((SUMS + (2 << k) * up_to(depth, 16), LANES), BF16),
            ]
            args = [weight, weight_got, near, near_got]
            if k == 0:
                weight, near, *rims = call(
                    functools.partial(round_kernel, count=1), outs + [(rim, BF16)] * 2, args + [rims]
                )
                rims = [
                    swap(rims[0], "seq", 1),
                    lax.ppermute(rims[1], "seq", pairs + [(j, i) for i, j in pairs]),
                ]
                ahead, back = call(
                    mask_kernel,
                    [((KERNEL_WIDTH, ext, LANES), F32), ((KERNEL_WIDTH, rows, LANES), F32)],
                    [starts],
                    smem=(0,),
                    after=[near],
                )
            elif k == 1:
                weight, near, rims = call(
                    functools.partial(round_kernel, count=2),
                    outs + [((2, *rim), BF16)],
                    args + rims,
                    after=[back],
                )
            else:
                weight, near = call(round_kernel, outs, args)
    hidden_in, vec_in, cotangent = call(
        functools.partial(act_kernel, bin_count=bin_count),
        [((rows + 2 * RIM, width), BF16), ((8, width), F32), (cotangent.shape, BF16)],
        [inputs, cotangent, rims, near, near_got, norm_in],
        away=(1,),
        sems=1,
    )

    stack_type = BF16 if depth % 16 == 0 else F32
    conv_own, conv_out, sums_mid, weight = call(
        functools.partial(
            conv_kernel, relatives=relatives_of(weight_order), slim=slim
        ),
        [
            ((width, wide), BF16),
            ((ext, LANES), F32),
            ((8, LANES), F32),
            ((seq_size, packed, wide), BF16),
        ],
        [ahead, hidden_in, weight, weight_got],
        scratch=[((seq_size, depth, wide), stack_type), ((rows + 2 * RIM, wide), F32)],
    )
    weight = swap(weight, "ch", top)
    upstream, point_own = call(
        functools.partial(upstream_kernel, relatives=relatives_of(point_order)),
        [((ext, LANES), F32), ((width, LANES), BF16)],
        [cotangent, rims, near, near_got],
        scratch=[((seq_size, depth, LANES), stack_type)],
        after=[sums_mid],
    )
    conv_near = gather_parts(conv_own, lower)
    total = sums_mid
    for k, reach in enumerate(sum_order):
        total = add(total, swap(total, "seq", reach), [upstream])
    (conv_far,) = call(
        functools.partial(place_kernel, relatives=relatives_of(weight_order), slim=slim),
        [((width, wide), BF16)],
        [weight],
        scratch=[((seq_size, depth, wide), stack_type)],
        after=[total],
    )
    hidden_mid, d_mid, centered, sent_back, vec_mid = call(
        functools.partial(mid_kernel, bin_count=bin_count),
        [
            ((rows, LANES), BF16),
            ((ext, LANES), F32),
            ((ext, LANES), F32),
            ((seq_size, 2, LANES), F32),
            ((8, LANES), F32),
        ],
        [total, conv_out, upstream, norm_mid],
        after=[conv_far, *conv_near[1:]],
    )
    got_back = spread(sent_back, "seq")
    grad_own, total_mid = call(
        functools.partial(conv_back_kernel, bin_count=bin_count, slim=slim),
        [((3 * ext // 4 if folds(ext, slim) else ext, LANES), BF16), ((2, LANES), F32)],
        [got_back, vec_mid, d_mid, centered],
        scratch=[((ext, LANES), F32)],
    )
    grad_near = gather_parts(grad_own, lower)
    grad_far = swap(grad_own, "ch", top)
    conv_far = gather_parts(copies([conv_far], [grad_own])[0], lower)
    half = seq_size // 2
    terms, kept, sent = call(
        functools.partial(weight_grad_kernel, depth=depth, slim=slim),
        [
            ((rows, wide), BF16),
            ((half, depth, 4 * slim), F32),
            ((half, depth, 4 * slim), BF16),
        ],
        [back, grad_own, hidden_in, cotangent, hidden_mid],
        scratch=[((ext, LANES), F32), ((width, 4 * slim), F32)],
    )
    side = ch_size // 2 * wide
    up_part, both = call(
        first_half_kernel,
        [((rows, width), F32), ((rows + width, LANES), BF16)],
        [back, terms, hidden_mid, point_own, *grad_near[1:], *conv_near],
        scratch=[((rows, side), BF16), ((width, side), BF16), ((ext, LANES), F32)],
    )
    (slope_in,) = call(slope_kernel, [((rows, width), F32)], [inputs, vec_in], after=[up_part])
    grad_far = gather_parts(copies([grad_far], [slope_in])[0], lower)
    d_in, sums_back = call(
        second_half_kernel,
        [((rows, width), F32), ((2, width), F32)],
        [back, inputs, slope_in, vec_in, up_part, *grad_far, *conv_far],
        scratch=[((rows, side), BF16), ((width, side), BF16), ((ext, LANES), F32)],
    )
    both_parts = gather_parts(both, lower)
    both_far = swap(both, "ch", top)
    total_back = sums_back
    for k, reach in enumerate(sum_order):
        total_got = swap(total_back, "seq", last_order[k])
        got = swap(sent, "seq", reach)
        if k < rounds - 1:
            half //= 2
            kept, sent = call(
                functools.partial(fold_kernel, reach=2 * reach),
                [((half, depth, 4 * slim), F32), ((half, depth, 4 * slim), BF16)],
                [kept, got],
                after=[total_back],
            )
            total_back = add(total_back, total_got, [sent])
    both_parts += gather_parts(copies([both_far], [total_back])[0], lower)
    block_out, token = call(
        out_kernel,
        [((rows, width), BF16), ((8, LANES), F32)],
        [inputs, *both_parts],
        scratch=[((rows, ch_size * LANES), BF16), ((width, ch_size * LANES), BF16)],
        after=[total_back],
    )
    input_grad, *in_new = call(
        functools.partial(final_kernel, bin_count=bin_count),
        [((rows, width), F32)] + [((2, width), F32)] * 3,
        [inputs, cotangent, d_in, vec_in, total_back, total_got, norm_in, first_in, second_in],
        scratch=[((rows, width), F32)],
        after=[token],
        away_outs=(0,),
        sems=8,
    )
    news = call(
        weight_step_kernel,
        [(master_conv.shape, F32)] * 3 + [(master_point.shape, F32)] * 3 + [(norm_mid.shape, F32)] * 3,
        [kept, got, total_mid, master_conv, first_conv, second_conv]
        + [master_point, first_point, second_point, norm_mid, first_mid, second_mid],
        after=[token],
    )
    return (block_out, input_grad, *news[:6], *in_new, *news[6:])


def solution(mesh):
    in_specs = (
        P("seq", None),
        P("seq", None),
        P(),
        P(None, "seq", "ch"),
        P(None, "seq", "ch"),
        P(None, "seq", "ch"),
        P("ch", "seq"),
        P("ch", "seq"),
        P("ch", "seq"),
        P(),
        P(),
        P(),
        P(None, "ch"),
        P(None, "ch"),
        P(None, "ch"),
    )
    out_specs = (
        P("seq", None),
        P("seq", None),
        P(None, "seq", "ch"),
        P(None, "seq", "ch"),
        P(None, "seq", "ch"),
        P("ch", "seq"),
        P("ch", "seq"),
        P("ch", "seq"),
        P(),
        P(),
        P(),
        P(None, "ch"),
        P(None, "ch"),
        P(None, "ch"),
    )
    return jax.shard_map(shards, mesh=mesh, in_specs=in_specs, out_specs=out_specs, check_vma=False)
```

```python
import functools

import jax
import jax.numpy as jnp
from jax import lax
from jax.experimental import pallas as pl
from jax.experimental.pallas import tpu as pltpu
from jax.sharding import PartitionSpec as P

KERNEL_WIDTH = 3
DILATION_BINS = 9
WIN = 1024
STEP = 10

NORM_EPS = 1e-05
ADAM_EPS = 1e-08
BETA_ONE = 0.9
BETA_TWO = 0.999
RATE_WEIGHT = 0.05
RATE_NORM = 0.5
DECAY_WEIGHT = 0.01

LANES = 128
EDGE = 16
RIM = 2 * EDGE
SUMS = 48
GELU_A = 0.7978845608028654
GELU_B = 0.044715
SHIFTS = [(j - KERNEL_WIDTH // 2) * DILATION_BINS for j in range(KERNEL_WIDTH)]
ROW_DIMS = (((0,), (0,)), ((), ()))
LANE_DIMS = (((1,), (1,)), ((), ()))
F32, BF16 = jnp.float32, jnp.bfloat16


def call(body, outs, args, scratch=(), smem=(), away=(), after=(), sems=0, away_outs=(), limit=16):
    spaces = [pltpu.SMEM if k in smem else pltpu.VMEM for k in range(len(args))]
    spaces = [pltpu.HBM if k in away else space for k, space in enumerate(spaces)]
    spaces += [pl.ANY] * len(after)

    args = [
        pltpu.with_memory_space_constraint(x, pltpu.HBM) if k in away else x
        for k, x in enumerate(args)
    ]

    def kernel(*refs):
        body(*refs[: len(args)], *refs[len(spaces) :])

    return pl.pallas_call(
        kernel,
        out_shape=[jax.ShapeDtypeStruct(s, t) for s, t in outs],
        in_specs=[pl.BlockSpec(memory_space=s) for s in spaces],
        out_specs=[
            pl.BlockSpec(memory_space=pltpu.HBM if k in away_outs else pltpu.VMEM)
            for k in range(len(outs))
        ],
        scratch_shapes=[pltpu.VMEM(s, t) for s, t in scratch]
        + [pltpu.SemaphoreType.DMA((sems,))] * (sems > 0),
        compiler_params=pltpu.CompilerParams(vmem_limit_bytes=limit * 2**20),
        cost_estimate=pl.CostEstimate(flops=1, bytes_accessed=1, transcendentals=0),
        name=getattr(body, "func", body).__name__,
    )(*args, *after)


def up_to(size, step):
    return -(-size // step) * step


def split_three(v):
    high = v.astype(BF16).astype(F32)
    rest = v - high
    middle = rest.astype(BF16).astype(F32)
    return high, middle, rest - middle


def gelu_and_slope(v):
    square = v * v
    t = jnp.tanh(v * (GELU_A + (GELU_A * GELU_B) * square))
    half = 0.5 * (1.0 + t)
    slope = half + (0.5 * v) * (1.0 - t * t) * (GELU_A + (3.0 * GELU_A * GELU_B) * square)
    return v * half, slope


def reach_of(first, count, shift, start, bin_count):
    here = first + lax.broadcasted_iota(jnp.int32, (count, LANES), 0)
    there = here + shift
    inside = (here >= 0) & (here < bin_count) & (there >= 0) & (there < bin_count)
    return inside & (((here - start) >> 10) == ((there - start) >> 10))


def folds(depth, slim):
    return 3 * (LANES - slim) == slim and depth % 32 == 0


def fold_rows(block):
    rows, slim = block.shape
    quarter, width = rows // 4, LANES - slim
    side = [block[3 * quarter :, p * width : (p + 1) * width] for p in range(3)]
    return jnp.concatenate([block[: 3 * quarter], jnp.concatenate(side, axis=0)], axis=1)


def unfold_rows(block, slim):
    quarter, width = block.shape[0] // 3, LANES - slim
    side = [block[p * quarter : (p + 1) * quarter, slim:] for p in range(3)]
    side.append(jnp.zeros((quarter, width), block.dtype))
    lane = lax.broadcasted_iota(jnp.int32, block.shape, 1)
    return jnp.concatenate([jnp.where(lane < slim, block, 0.0), jnp.concatenate(side, axis=1)], axis=0)


def first_kernel(
    x_hbm, cot_hbm, conv_hbm, point_hbm, x_ref, weight_ref, near_ref, rim_ref, edge_ref, conv_ref, point_ref, sum_ref, sems
):
    rows, width = x_ref.shape
    tiles = width // LANES
    depth, slim = conv_ref.shape[1:]
    chunks = sems.shape[0] - 4
    chunk = rows // chunks
    copies = [
        pltpu.make_async_copy(conv_hbm, conv_ref, sems.at[0]),
        pltpu.make_async_copy(point_hbm, point_ref, sems.at[1]),
        pltpu.make_async_copy(cot_hbm.at[pl.ds(0, EDGE)], edge_ref.at[0], sems.at[2]),
        pltpu.make_async_copy(cot_hbm.at[pl.ds(rows - EDGE, EDGE)], edge_ref.at[1], sems.at[3]),
    ]
    for k in range(chunks):
        part = pl.ds(k * chunk, chunk)
        copies.append(pltpu.make_async_copy(x_hbm.at[part], x_ref.at[part], sems.at[4 + k]))
    for copy in copies:
        copy.start()
    weight_ref[...] = jnp.zeros_like(weight_ref)
    near_ref[...] = jnp.zeros_like(near_ref)
    sum_ref[...] = jnp.zeros_like(sum_ref)
    copies[0].wait()
    for j in range(KERNEL_WIDTH):
        if folds(depth, slim):
            weight_ref[0, :, j * LANES : (j + 1) * LANES] = fold_rows(conv_ref[j]).astype(BF16)
        else:
            weight_ref[0, :, j * LANES : j * LANES + slim] = conv_ref[j].astype(BF16)
    copies[1].wait()
    near_ref[SUMS : SUMS + depth, :slim] = point_ref[...].T.astype(BF16)

    def step(k, carry):
        v = x_ref[pl.ds(pl.multiple_of(k * 32, 32), 32), :].astype(F32)
        v = v.reshape(4, 8, width)
        return carry[0] + v.sum(0), carry[1] + (v * v).sum(0)

    totals = (jnp.zeros((8, width), F32),) * 2
    for k in range(chunks):
        copies[4 + k].wait()
        totals = lax.fori_loop(
            k * chunk // 32, (k + 1) * chunk // 32, step, totals, unroll=chunk // 32
        )
    for stat, total in enumerate(totals):
        total = jnp.sum(total, 0, keepdims=True)
        for k in range(tiles):
            row = stat * tiles + k
            sum_ref[row : row + 1, :] = total[:, k * LANES : (k + 1) * LANES]
    put_sums(near_ref, sum_ref[...])
    copies[2].wait()
    copies[3].wait()
    for side in range(2):
        begin = (rows - RIM) * side
        rim_ref[side, :RIM, :] = x_ref[begin : begin + RIM, :]
        rim_ref[side, RIM:, :] = edge_ref[side]


def put_sums(ref, value):
    for p, part in enumerate(split_three(value)):
        ref[p * 16 : (p + 1) * 16, :] = part.astype(BF16)


def get_sums(ref):
    return sum(ref[p * 16 : (p + 1) * 16, :].astype(F32) for p in range(3))


def act_kernel(
    x_ref, cot_hbm, one_ref, two_ref, norm_ref, hid_ref, vec_ref, cot_ref, sems, *, bin_count
):
    copy = pltpu.make_async_copy(cot_hbm, cot_ref, sems.at[0])
    copy.start()
    rows, width = x_ref.shape
    tiles = width // LANES
    total = get_sums(one_ref) + get_sums(two_ref)
    for k in range(tiles):
        lanes = slice(k * LANES, (k + 1) * LANES)
        mean = total[k : k + 1, :] / bin_count
        square = total[tiles + k : tiles + k + 1, :] / bin_count
        root = lax.rsqrt(square - mean * mean + NORM_EPS)
        gain = root * norm_ref[0:1, lanes]
        vec_ref[0:1, lanes] = root
        vec_ref[1:2, lanes] = -mean * root
        vec_ref[2:3, lanes] = gain
        vec_ref[3:4, lanes] = norm_ref[1:2, lanes] - mean * gain

    def step(k, carry):
        at = pl.multiple_of(k * 16, 16)
        v = x_ref[pl.ds(at, 16), :].astype(F32) * vec_ref[2:3, :] + vec_ref[3:4, :]
        hid_ref[pl.ds(at, 16), :] = gelu_and_slope(v)[0].astype(BF16)
        return carry

    lax.fori_loop(0, rows // 16, step, 0, unroll=2)
    copy.wait()


def place(pieces, relatives, stack, own, slim):
    depth = stack.shape[1]
    at = 0
    for piece in pieces:
        for k in range(piece.shape[0]):
            block = piece[k].astype(F32)
            for j in range(KERNEL_WIDTH):
                part = block[:, j * LANES : (j + 1) * LANES]
                if folds(depth, slim):
                    part = unfold_rows(part, slim)
                stack[own ^ relatives[at], :, j * LANES : (j + 1) * LANES] = part.astype(stack.dtype)
            at += 1
    return stack[...].reshape(-1, stack.shape[2]).astype(BF16)


def place_kernel(*refs, relatives, slim):
    pieces, (out_ref, stack) = refs[:-2], refs[-2:]
    out_ref[...] = place(pieces, relatives, stack, lax.axis_index("seq"), slim)


def mask_kernel(start_ref, rim_ref, ahead_ref, back_ref, near_ref, far_ref):
    odd = lax.axis_index("seq") % 2
    near_ref[...] = rim_ref[1 - odd]
    far_ref[...] = rim_ref[odd]
    rows = back_ref.shape[1]
    first = lax.axis_index("seq") * rows
    for j, shift in enumerate(SHIFTS):
        for begin in range(0, rows + RIM, 96):
            count = min(96, rows + RIM - begin)
            mask = reach_of(first + begin - EDGE, count, shift, start_ref[0], rows * lax.axis_size("seq"))
            ahead_ref[j, begin : begin + count, :] = jnp.where(mask, 1.0, 0.0)
        for begin in range(0, rows, 128):
            back_ref[j, begin : begin + 128, :] = ahead_ref[
                j, EDGE + begin - shift : EDGE + begin - shift + 128, :
            ]


def slope_kernel(x_ref, vec_ref, slope_ref, *, first):
    def step(k, carry):
        at = pl.multiple_of(k * 16, 16)
        v = x_ref[pl.ds(first + at, 16), :].astype(F32) * vec_ref[2:3, :] + vec_ref[3:4, :]
        slope_ref[pl.ds(at, 16), :] = gelu_and_slope(v)[1]
        return carry

    lax.fori_loop(0, slope_ref.shape[0] // 16, step, 0, unroll=2)


def conv_kernel(mask_ref, hid_ref, near_ref, far_ref, vec_ref, *refs, relatives, slim):
    pieces, refs = refs[:2], refs[2:]
    weight_ref, out_ref, sum_ref, rim_ref, all_ref, stack, prod, edge = refs
    size = all_ref.shape[0] // 2
    for k, piece in enumerate(pieces):
        all_ref[k * size : (k + 1) * size] = piece[...]
    odd = lax.axis_index("seq") % 2
    rim_ref[1 - odd] = near_ref[...]
    rim_ref[odd] = far_ref[...]
    for side in range(2):
        for k in range(0, RIM, 16):
            v = rim_ref[side, k : k + 16, :].astype(F32) * vec_ref[2:3, :] + vec_ref[3:4, :]
            edge[side * RIM + k : side * RIM + k + 16, :] = gelu_and_slope(v)[0].astype(BF16)
    rows = hid_ref.shape[0]
    weight_ref[...] = place(pieces, relatives, stack, lax.axis_index("seq"), slim)
    for at in range(0, weight_ref.shape[1], 256):
        part = slice(at, min(at + 256, weight_ref.shape[1]))
        prod[RIM : RIM + rows, part] = jnp.dot(
            hid_ref[...], weight_ref[:, part], preferred_element_type=F32
        )
        sides = jnp.dot(edge[...], weight_ref[:, part], preferred_element_type=F32)
        prod[:RIM, part] = sides[:RIM]
        prod[RIM + rows :, part] = sides[RIM:]

    def rows_of(begin, count):
        value = 0.0
        for j, shift in enumerate(SHIFTS):
            part = prod[begin + EDGE + shift : begin + EDGE + shift + count, j * LANES : (j + 1) * LANES]
            value = value + mask_ref[j, begin : begin + count, :] * part
        out_ref[begin : begin + count, :] = value
        return value

    rows_of(0, EDGE)
    rows_of(EDGE + rows, EDGE)
    one = two = jnp.zeros((8, LANES), F32)
    step = 128
    for k in range(rows // step):
        value = rows_of(EDGE + k * step, step).reshape(step // 8, 8, LANES)
        one = one + value.sum(0)
        two = two + (value * value).sum(0)
    sum_ref[...] = jnp.zeros_like(sum_ref)
    sum_ref[0:1, :] = jnp.sum(one, 0, keepdims=True)
    sum_ref[1:2, :] = jnp.sum(two, 0, keepdims=True)


def upstream_kernel(cot_ref, rim_ref, one_ref, two_ref, up_ref, point_ref, stack, *, relatives):
    rows = cot_ref.shape[0]
    depth = stack.shape[1]
    own = lax.axis_index("seq")
    count = len(relatives) // 2
    for k, relative in enumerate(relatives):
        piece = (one_ref, two_ref)[k // count]
        at = SUMS + (k % count) * up_to(depth, 16)
        stack[own ^ relative] = piece[at : at + depth, :].astype(stack.dtype)
    point_ref[...] = stack[...].reshape(point_ref.shape).astype(BF16)
    for side, at in enumerate((0, EDGE + rows)):
        up_ref[at : at + EDGE, :] = jnp.dot(
            rim_ref[side, RIM:, :], point_ref[...], preferred_element_type=F32
        )
    up_ref[EDGE : EDGE + rows, :] = jnp.dot(
        cot_ref[...], point_ref[...], preferred_element_type=F32
    )


def mid_kernel(
    total_ref, conv_ref, up_ref, norm_ref, hid_ref, d_ref, cen_ref, sent_ref, vec_ref, *, bin_count
):
    rows = hid_ref.shape[0]
    slim = norm_ref.shape[1]
    total = total_ref[...]
    mean = total[0:1] / bin_count
    root = lax.rsqrt(total[1:2] / bin_count - mean * mean + NORM_EPS)
    vec_ref[...] = jnp.zeros_like(vec_ref)
    vec_ref[0:1, :] = root
    vec_ref[1:3, :slim] = norm_ref[...]
    gain, bias = vec_ref[1:2, :], vec_ref[2:3, :]

    def rows_of(begin, count):
        centered = (conv_ref[pl.ds(begin, count), :] - mean) * root
        hidden, slope = gelu_and_slope(centered * gain + bias)
        d = up_ref[pl.ds(begin, count), :] * slope
        cen_ref[pl.ds(begin, count), :] = centered
        d_ref[pl.ds(begin, count), :] = d
        return centered, hidden, d

    rows_of(0, EDGE)
    rows_of(EDGE + rows, EDGE)
    step = 64

    def body(i, carry):
        begin = pl.multiple_of(EDGE + i * step, 16)
        centered, hidden, d = rows_of(begin, step)
        hid_ref[pl.ds(pl.multiple_of(i * step, 16), step), :] = hidden.astype(BF16)
        d = d.reshape(step // 8, 8, LANES)
        return carry[0] + (d * centered.reshape(d.shape)).sum(0), carry[1] + d.sum(0)

    zero = jnp.zeros((8, LANES), F32)
    gain_sum, bias_sum = lax.fori_loop(0, rows // step, body, (zero, zero), unroll=2)
    gain_sum = jnp.sum(gain_sum, 0, keepdims=True)
    bias_sum = jnp.sum(bias_sum, 0, keepdims=True)
    for d in range(sent_ref.shape[0]):
        sent_ref[d, 0:1, :] = gain_sum
        sent_ref[d, 1:2, :] = bias_sum


def conv_back_kernel(got_ref, vec_ref, d_ref, cen_ref, grad_ref, total_ref, grad, *, bin_count, slim):
    total = got_ref[0]
    for s in range(1, got_ref.shape[0]):
        total = total + got_ref[s]
    total_ref[...] = total
    scale = vec_ref[0:1, :] * vec_ref[1:2, :]
    pull, level = total[0:1] / bin_count, total[1:2] / bin_count
    count = d_ref.shape[0]
    for begin in range(0, count, 96):
        part = slice(begin, min(begin + 96, count))
        grad[part, :] = scale * (d_ref[part, :] - level - cen_ref[part, :] * pull)
    if folds(count, slim):
        grad_ref[...] = fold_rows(grad[:, :slim]).astype(BF16)
    else:
        grad_ref[...] = grad[...].astype(BF16)


def out_kernel(x_ref, *refs):
    parts, (out_ref, token_ref, hidden, point) = refs[:-4], refs[-4:]
    token_ref[...] = jnp.zeros_like(token_ref)
    rows = x_ref.shape[0]
    for r, part in enumerate(parts):
        part = part[...]
        if part.shape[0] < rows + point.shape[0]:
            part = unfold_rows(part.astype(F32), 3 * LANES // 4).astype(BF16)
        hidden[:, r * LANES : (r + 1) * LANES] = part[:rows, :]
        point[:, r * LANES : (r + 1) * LANES] = part[rows:, :]
    for at in range(0, x_ref.shape[1], 256):
        part = slice(at, at + 256)
        branch = lax.dot_general(
            hidden[...], point[part, :], LANE_DIMS, preferred_element_type=F32
        )
        out_ref[:, part] = (x_ref[:, part].astype(F32) + branch).astype(BF16)


def halve(blocks, kept_ref, sent_ref, high):
    for k in range(kept_ref.shape[0]):
        kept_ref[k] = blocks(2 * k + high)
        sent_ref[k] = blocks(2 * k + 1 - high).astype(BF16)


def bit_of(reach):
    return (lax.axis_index("seq") // reach) % 2


def terms_of(part, grad, term_ref, at, mask_ref):
    rows = term_ref.shape[0]
    step = 64
    count = part.shape[0]
    grad[:count, :] = part[...].astype(F32)
    if count < grad.shape[0]:
        quarter = count // 3
        width = LANES // 4
        side = [grad[p * quarter : (p + 1) * quarter, 3 * width :] for p in range(3)]
        grad[count:, :] = jnp.concatenate(side + [jnp.zeros((quarter, width), F32)], axis=1)
    for j, shift in enumerate(SHIFTS):
        lanes = slice(at + j * LANES, at + (j + 1) * LANES)
        for begin in range(0, rows, step):
            value = grad[EDGE + begin - shift : EDGE + begin - shift + step, :]
            value = value * mask_ref[j, begin : begin + step, :]
            term_ref[begin : begin + step, lanes] = value.astype(BF16)


def weight_grad_kernel(
    mask_ref, part_ref, hid_ref, cot_ref, mid_ref, term_ref, kept_ref, sent_ref, grad, full, *, depth, slim
):
    rows = term_ref.shape[0]
    terms_of(part_ref, grad, term_ref, 0, mask_ref)
    taps = lax.dot_general(
        hid_ref[...], term_ref[...], ROW_DIMS, preferred_element_type=F32
    )
    point = lax.dot_general(cot_ref[...], mid_ref[...], ROW_DIMS, preferred_element_type=F32)
    parts = [taps[:, j * LANES : j * LANES + slim] for j in range(KERNEL_WIDTH)] + [point[:, :slim]]
    full[...] = jnp.concatenate(parts, axis=1)
    halve(
        lambda k: full[pl.ds(pl.multiple_of(k * depth, 8), depth), :], kept_ref, sent_ref, bit_of(1)
    )


def fold_kernel(old_ref, got_ref, kept_ref, sent_ref, *, reach):
    halve(lambda k: old_ref[k] + got_ref[k].astype(F32), kept_ref, sent_ref, bit_of(reach))


def adamw(weights_old, first_moment_state, second_mom, gradient, step_rate, decay_rate):
    first_next = BETA_ONE * first_moment_state + (1.0 - BETA_ONE) * gradient
    second_next = BETA_TWO * second_mom + (1.0 - BETA_TWO) * gradient * gradient
    corrected = (
        first_next
        / (1.0 - BETA_ONE**STEP)
        / (jnp.sqrt(second_next / (1.0 - BETA_TWO**STEP)) + ADAM_EPS)
    )
    weights_new = weights_old - step_rate * (corrected + decay_rate * weights_old)
    return (first_next, second_next, weights_new)


def first_half_kernel(mask_ref, own_ref, hid_ref, point_ref, *refs):
    up_ref, both_ref, term, weight, grad = refs[-5:]
    count = (len(refs) - 5 + 1) // 2
    grads, weights = refs[: count - 1], refs[count - 1 : -5]
    rows = up_ref.shape[0]
    if both_ref.shape[0] < rows + point_ref.shape[0]:
        both = jnp.concatenate([hid_ref[...].astype(F32), point_ref[...].astype(F32)], axis=0)
        both_ref[...] = fold_rows(both[:, : 3 * LANES // 4]).astype(BF16)
    else:
        both_ref[:rows, :] = hid_ref[...]
        both_ref[rows:, :] = point_ref[...]
    wide = KERNEL_WIDTH * LANES
    term[:, :wide] = own_ref[...]
    for r, part in enumerate(grads):
        terms_of(part, grad, term, (r + 1) * wide, mask_ref)
    for r, piece in enumerate(weights):
        weight[:, r * wide : (r + 1) * wide] = piece[...]
    for at in range(0, up_ref.shape[1], 256):
        part = slice(at, at + 256)
        up_ref[:, part] = lax.dot_general(
            term[...], weight[part, :], LANE_DIMS, preferred_element_type=F32
        )


def second_half_kernel(mask_ref, x_ref, slope_one, slope_two, vec_ref, part_ref, *refs):
    d_ref, sum_ref, term, weight, grad = refs[-5:]
    count = (len(refs) - 5) // 2
    grads, weights = refs[:count], refs[count:-5]
    rows, width = x_ref.shape
    wide = KERNEL_WIDTH * LANES
    for r in range(count):
        terms_of(grads[r], grad, term, r * wide, mask_ref)
    for r, piece in enumerate(weights):
        weight[:, r * wide : (r + 1) * wide] = piece[...]
    for at in range(0, width, 256):
        part = slice(at, at + 256)
        up = lax.dot_general(term[...], weight[part, :], LANE_DIMS, preferred_element_type=F32)
        slope = jnp.concatenate([slope_one[:, part], slope_two[:, part]], axis=0)
        d = (up + part_ref[:, part]) * slope
        d_ref[:, part] = d
        centered = x_ref[:, part].astype(F32) * vec_ref[0:1, part] + vec_ref[1:2, part]
        sum_ref[0:1, part] = jnp.sum(d * centered, 0, keepdims=True)
        sum_ref[1:2, part] = jnp.sum(d, 0, keepdims=True)


def final_kernel(x_ref, cot_ref, d_ref, vec_ref, one_ref, two_ref, *refs, bin_count):
    states, late_ref, outs, (out_ref, sems) = refs[:3], refs[3], refs[4:8], refs[8:]
    late_ref[...] = jnp.zeros_like(late_ref)
    rows, width = x_ref.shape
    total = one_ref[...] + two_ref[...]
    root, offset, scale = vec_ref[0:1, :], vec_ref[1:2, :], vec_ref[2:3, :]
    pull = scale * total[0:1] / bin_count
    slant = pull * root
    level = scale * total[1:2] / bin_count + pull * offset
    step = 16
    chunk = rows // sems.shape[0]

    def body(i, carry):
        at = pl.ds(pl.multiple_of(i * step, 16), step)
        value = x_ref[at, :].astype(F32) * slant + level
        out_ref[at, :] = cot_ref[at, :].astype(F32) + (d_ref[at, :] * scale - value)
        return carry

    sends = []
    for k in range(sems.shape[0]):
        lax.fori_loop(k * chunk // step, (k + 1) * chunk // step, body, 0, unroll=4)
        part = pl.ds(k * chunk, chunk)
        sends.append(pltpu.make_async_copy(out_ref.at[part], outs[0].at[part], sems.at[k]))
        sends[-1].start()
    new = adamw(*(ref[...] for ref in states), total, RATE_NORM, 0.0)
    for ref, value in zip(outs[1:], new):
        ref[...] = value
    for send in sends:
        send.wait()


def weight_step_kernel(old_ref, got_ref, total_ref, *refs):
    conv, point, mid, outs = refs[:3], refs[3:6], refs[6:9], refs[9:]
    slim = conv[0].shape[2]
    both = old_ref[0] + got_ref[0].astype(F32)
    for j in range(KERNEL_WIDTH):
        grad = both[:, j * slim : (j + 1) * slim]
        new = adamw(*(ref[j] for ref in conv), grad, RATE_WEIGHT, DECAY_WEIGHT)
        for ref, value in zip(outs[:3], new):
            ref[j] = value
    grad = both[:, KERNEL_WIDTH * slim :].T
    new = adamw(*(ref[...] for ref in point), grad, RATE_WEIGHT, DECAY_WEIGHT)
    for ref, value in zip(outs[3:6], new):
        ref[...] = value
    new = adamw(*(ref[...] for ref in mid), total_ref[:, :slim], RATE_NORM, 0.0)
    for ref, value in zip(outs[6:], new):
        ref[...] = value


def flip(axis, reach):
    return [(i, i ^ reach) for i in range(lax.axis_size(axis))]


def relatives_of(order):
    found = [0]
    for reach in order:
        found = found + [r ^ reach for r in found]
    return found


def descending(size):
    return [size >> k for k in range(1, size.bit_length())]


def round_kernel(weight_one, weight_two, one_ref, two_ref, weight_ref, out_ref):
    size = weight_one.shape[0]
    weight_ref[:size] = weight_one[...]
    weight_ref[size:] = weight_two[...]
    put_sums(out_ref, get_sums(one_ref) + get_sums(two_ref))
    size = (out_ref.shape[0] - SUMS) // 2
    out_ref[SUMS : SUMS + size, :] = one_ref[SUMS : SUMS + size, :]
    out_ref[SUMS + size :, :] = two_ref[SUMS : SUMS + size, :]


def copy_kernel(*refs):
    count = len(refs) // 2
    for src, out in zip(refs[:count], refs[count:]):
        out[...] = src[...]


def copies(arrays, after):
    return call(copy_kernel, [(x.shape, x.dtype) for x in arrays], arrays, after=after)


def add_kernel(one_ref, two_ref, out_ref):
    out_ref[...] = one_ref[...] + two_ref[...]


def add(one, two, after=()):
    return call(add_kernel, [(one.shape, one.dtype)], [one, two], after=after)[0]


def swap(x, axis, reach):
    return lax.ppermute(x, axis, flip(axis, reach))


def gather_parts(x, reaches):
    parts = [x]
    for reach in reaches:
        parts += [swap(part, "ch", reach) for part in parts]
    return parts


def spread(copies, axes):
    return lax.all_to_all(copies, axes, 0, 0, tiled=True)


def shards(
    inputs,
    cotangent,
    starts,
    master_conv,
    first_conv,
    second_conv,
    master_point,
    first_point,
    second_point,
    norm_in,
    first_in,
    second_in,
    norm_mid,
    first_mid,
    second_mid,
):
    rows, width = inputs.shape
    seq_size, ch_size = lax.axis_size("seq"), lax.axis_size("ch")
    bin_count = rows * seq_size
    depth, slim = master_conv.shape[1:]
    tiles = width // LANES
    wide = KERNEL_WIDTH * LANES
    weight_order = descending(seq_size)
    sum_order = weight_order[::-1]
    last_order = weight_order[:1] + sum_order[:-1]
    point_order = weight_order[:1] + [1] + weight_order[1:-1]
    ch_order = descending(ch_size)
    ext = rows + 2 * EDGE

    rounds = len(weight_order)
    top, lower = ch_order[0], ch_order[1:]
    chunks = 4
    rim = (RIM + EDGE, width)
    packed = 3 * depth // 4 if folds(depth, slim) else depth
    inputs, weight, near, rims = call(
        first_kernel,
        [
            (inputs.shape, BF16),
            ((1, packed, wide), BF16),
            ((SUMS + up_to(depth, 16), LANES), BF16),
            ((2, *rim), BF16),
        ],
        [inputs, cotangent, master_conv, master_point],
        scratch=[
            ((2, EDGE, width), BF16),
            (master_conv.shape, F32),
            (master_point.shape, F32),
            ((16, LANES), F32),
        ],
        away=(0, 1, 2, 3),
        sems=4 + chunks,
    )
    pairs = [(i, i + 1) for i in range(1, seq_size - 1, 2)]
    for k in range(rounds):
        weight_got = swap(weight, "seq", weight_order[k])
        near_got = swap(near, "seq", point_order[k])
        if k < rounds - 1:
            outs = [
                ((2 * weight.shape[0], packed, wide), BF16),
                ((SUMS + (2 << k) * up_to(depth, 16), LANES), BF16),
            ]
            args = [weight, weight_got, near, near_got]
            weight, near = call(round_kernel, outs, args, after=[back] if k == 1 else [])
            if k == 0:
                ahead, back, *rims = call(
                    mask_kernel,
                    [((KERNEL_WIDTH, ext, LANES), F32), ((KERNEL_WIDTH, rows, LANES), F32)]
                    + [(rim, BF16)] * 2,
                    [starts, rims],
                    smem=(0,),
                    after=[near],
                )
                rims = [
                    swap(rims[0], "seq", 1),
                    lax.ppermute(rims[1], "seq", pairs + [(j, i) for i, j in pairs]),
                ]
    hidden_in, vec_in, cotangent = call(
        functools.partial(act_kernel, bin_count=bin_count),
        [((rows, width), BF16), ((8, width), F32), (cotangent.shape, BF16)],
        [inputs, cotangent, near, near_got, norm_in],
        away=(1,),
        sems=1,
    )

    stack_type = BF16 if depth % 16 == 0 else F32
    conv_own, conv_out, sums_mid, rims, weight = call(
        functools.partial(
            conv_kernel, relatives=relatives_of(weight_order), slim=slim
        ),
        [
            ((width, wide), BF16),
            ((ext, LANES), F32),
            ((8, LANES), F32),
            ((2, *rim), BF16),
            ((seq_size, packed, wide), BF16),
        ],
        [ahead, hidden_in, *rims, vec_in, weight, weight_got],
        scratch=[
            ((seq_size, depth, wide), stack_type),
            ((rows + 2 * RIM, wide), F32),
            ((2 * RIM, width), BF16),
        ],
    )
    weight = swap(weight, "ch", top)
    upstream, point_own = call(
        functools.partial(upstream_kernel, relatives=relatives_of(point_order)),
        [((ext, LANES), F32), ((width, LANES), BF16)],
        [cotangent, rims, near, near_got],
        scratch=[((seq_size, depth, LANES), stack_type)],
        after=[sums_mid],
    )
    conv_near = gather_parts(conv_own, lower)
    total, others, slopes = sums_mid, [upstream], []
    for k, reach in enumerate(sum_order):
        total = add(total, swap(total, "seq", reach), others)
        if k < 2:
            others = call(
                functools.partial(slope_kernel, first=k * rows // 2),
                [((rows // 2, width), F32)],
                [inputs, vec_in],
                after=[total],
            )
            slopes += others
    (conv_far,) = call(
        functools.partial(place_kernel, relatives=relatives_of(weight_order), slim=slim),
        [((width, wide), BF16)],
        [weight],
        scratch=[((seq_size, depth, wide), stack_type)],
        after=[total],
    )
    hidden_mid, d_mid, centered, sent_back, vec_mid = call(
        functools.partial(mid_kernel, bin_count=bin_count),
        [
            ((rows, LANES), BF16),
            ((ext, LANES), F32),
            ((ext, LANES), F32),
            ((seq_size, 2, LANES), F32),
            ((8, LANES), F32),
        ],
        [total, conv_out, upstream, norm_mid],
        after=[conv_far, *conv_near[1:]],
    )
    got_back = spread(sent_back, "seq")
    grad_own, total_mid = call(
        functools.partial(conv_back_kernel, bin_count=bin_count, slim=slim),
        [((3 * ext // 4 if folds(ext, slim) else ext, LANES), BF16), ((2, LANES), F32)],
        [got_back, vec_mid, d_mid, centered],
        scratch=[((ext, LANES), F32)],
    )
    grad_near = gather_parts(grad_own, lower)
    grad_far = swap(grad_own, "ch", top)
    conv_far = gather_parts(copies([conv_far], [grad_own])[0], lower)
    half = seq_size // 2
    terms, kept, sent = call(
        functools.partial(weight_grad_kernel, depth=depth, slim=slim),
        [
            ((rows, wide), BF16),
            ((half, depth, 4 * slim), F32),
            ((half, depth, 4 * slim), BF16),
        ],
        [back, grad_own, hidden_in, cotangent, hidden_mid],
        scratch=[((ext, LANES), F32), ((width, 4 * slim), F32)],
    )
    side = ch_size // 2 * wide
    up_part, both = call(
        first_half_kernel,
        [((rows, width), F32), ((3 * (rows + width) // 4 if folds(rows + width, slim) else rows + width, LANES), BF16)],
        [back, terms, hidden_mid, point_own, *grad_near[1:], *conv_near],
        scratch=[((rows, side), BF16), ((width, side), BF16), ((ext, LANES), F32)],
    )
    grad_far = gather_parts(copies([grad_far], [up_part])[0], lower)
    d_in, sums_back = call(
        second_half_kernel,
        [((rows, width), F32), ((2, width), F32)],
        [back, inputs, *slopes, vec_in, up_part, *grad_far, *conv_far],
        scratch=[((rows, side), BF16), ((width, side), BF16), ((ext, LANES), F32)],
    )
    both_parts = gather_parts(both, lower)
    both_far = swap(both, "ch", top)
    total_back = sums_back
    for k, reach in enumerate(sum_order):
        total_got = swap(total_back, "seq", last_order[k])
        got = swap(sent, "seq", reach)
        if k < rounds - 1:
            half //= 2
            kept, sent = call(
                functools.partial(fold_kernel, reach=2 * reach),
                [((half, depth, 4 * slim), F32), ((half, depth, 4 * slim), BF16)],
                [kept, got],
                after=[total_back],
            )
            total_back = add(total_back, total_got, [sent])
    both_parts += gather_parts(copies([both_far], [total_back])[0], lower)
    block_out, token = call(
        out_kernel,
        [((rows, width), BF16), ((8, LANES), F32)],
        [inputs, *both_parts],
        scratch=[((rows, ch_size * LANES), BF16), ((width, ch_size * LANES), BF16)],
        after=[total_back],
    )
    late, input_grad, *in_new = call(
        functools.partial(final_kernel, bin_count=bin_count),
        [((8, LANES), F32), ((rows, width), F32)] + [((2, width), F32)] * 3,
        [inputs, cotangent, d_in, vec_in, total_back, total_got, norm_in, first_in, second_in],
        scratch=[((rows, width), F32)],
        away_outs=(1,),
        sems=8,
        after=[token],
    )
    states = [master_conv, first_conv, second_conv, master_point, first_point, second_point]
    states += [norm_mid, first_mid, second_mid]
    news = call(
        weight_step_kernel,
        [(x.shape, F32) for x in states],
        [kept, got, total_mid] + states,
        after=[late],
    )
    return (block_out, input_grad, *news[:6], *in_new, *news[6:])


def solution(mesh):
    in_specs = (
        P("seq", None),
        P("seq", None),
        P(),
        P(None, "seq", "ch"),
        P(None, "seq", "ch"),
        P(None, "seq", "ch"),
        P("ch", "seq"),
        P("ch", "seq"),
        P("ch", "seq"),
        P(),
        P(),
        P(),
        P(None, "ch"),
        P(None, "ch"),
        P(None, "ch"),
    )
    out_specs = (
        P("seq", None),
        P("seq", None),
        P(None, "seq", "ch"),
        P(None, "seq", "ch"),
        P(None, "seq", "ch"),
        P("ch", "seq"),
        P("ch", "seq"),
        P("ch", "seq"),
        P(),
        P(),
        P(),
        P(None, "ch"),
        P(None, "ch"),
        P(None, "ch"),
    )
    return jax.shard_map(shards, mesh=mesh, in_specs=in_specs, out_specs=out_specs, check_vma=False)
```

```python
import functools

import jax
import jax.numpy as jnp
from jax import lax
from jax.experimental import pallas as pl
from jax.experimental.pallas import tpu as pltpu
from jax.sharding import PartitionSpec as P

KERNEL_WIDTH = 3
DILATION_BINS = 9
WIN = 1024
STEP = 10

NORM_EPS = 1e-05
ADAM_EPS = 1e-08
BETA_ONE = 0.9
BETA_TWO = 0.999
RATE_WEIGHT = 0.05
RATE_NORM = 0.5
DECAY_WEIGHT = 0.01

LANES = 128
EDGE = 16
RIM = 2 * EDGE
SUMS = 48
GELU_A = 0.7978845608028654
GELU_B = 0.044715
SHIFTS = [(j - KERNEL_WIDTH // 2) * DILATION_BINS for j in range(KERNEL_WIDTH)]
ROW_DIMS = (((0,), (0,)), ((), ()))
LANE_DIMS = (((1,), (1,)), ((), ()))
F32, BF16 = jnp.float32, jnp.bfloat16


def call(body, outs, args, scratch=(), smem=(), away=(), after=(), sems=0, away_outs=(), limit=16):
    spaces = [pltpu.SMEM if k in smem else pltpu.VMEM for k in range(len(args))]
    spaces = [pltpu.HBM if k in away else space for k, space in enumerate(spaces)]
    spaces += [pl.ANY] * len(after)

    args = [
        pltpu.with_memory_space_constraint(x, pltpu.HBM) if k in away else x
        for k, x in enumerate(args)
    ]

    def kernel(*refs):
        body(*refs[: len(args)], *refs[len(spaces) :])

    return pl.pallas_call(
        kernel,
        out_shape=[jax.ShapeDtypeStruct(s, t) for s, t in outs],
        in_specs=[pl.BlockSpec(memory_space=s) for s in spaces],
        out_specs=[
            pl.BlockSpec(memory_space=pltpu.HBM if k in away_outs else pltpu.VMEM)
            for k in range(len(outs))
        ],
        scratch_shapes=[pltpu.VMEM(s, t) for s, t in scratch]
        + [pltpu.SemaphoreType.DMA((sems,))] * (sems > 0),
        compiler_params=pltpu.CompilerParams(vmem_limit_bytes=limit * 2**20),
        cost_estimate=pl.CostEstimate(flops=1, bytes_accessed=1, transcendentals=0),
        name=getattr(body, "func", body).__name__,
    )(*args, *after)


def up_to(size, step):
    return -(-size // step) * step


def split_three(v):
    high = v.astype(BF16).astype(F32)
    rest = v - high
    middle = rest.astype(BF16).astype(F32)
    return high, middle, rest - middle


def gelu_and_slope(v):
    square = v * v
    t = jnp.tanh(v * (GELU_A + (GELU_A * GELU_B) * square))
    half = 0.5 * (1.0 + t)
    slope = half + (0.5 * v) * (1.0 - t * t) * (GELU_A + (3.0 * GELU_A * GELU_B) * square)
    return v * half, slope


def reach_of(first, count, shift, start, bin_count):
    here = first + lax.broadcasted_iota(jnp.int32, (count, LANES), 0)
    there = here + shift
    inside = (here >= 0) & (here < bin_count) & (there >= 0) & (there < bin_count)
    return inside & (((here - start) >> 10) == ((there - start) >> 10))


def folds(depth, slim):
    return 3 * (LANES - slim) == slim and depth % 32 == 0


def fold_rows(block):
    rows, slim = block.shape
    quarter, width = rows // 4, LANES - slim
    side = [block[3 * quarter :, p * width : (p + 1) * width] for p in range(3)]
    return jnp.concatenate([block[: 3 * quarter], jnp.concatenate(side, axis=0)], axis=1)


def unfold_rows(block, slim):
    quarter, width = block.shape[0] // 3, LANES - slim
    side = [block[p * quarter : (p + 1) * quarter, slim:] for p in range(3)]
    side.append(jnp.zeros((quarter, width), block.dtype))
    lane = lax.broadcasted_iota(jnp.int32, block.shape, 1)
    return jnp.concatenate([jnp.where(lane < slim, block, 0.0), jnp.concatenate(side, axis=1)], axis=0)


def first_kernel(
    x_hbm, cot_hbm, conv_hbm, point_hbm, x_ref, weight_ref, near_ref, near_rim, far_rim, edge_ref, conv_ref, point_ref, sum_ref, sems
):
    rows, width = x_ref.shape
    tiles = width // LANES
    depth, slim = conv_ref.shape[1:]
    chunks = sems.shape[0] - 4
    chunk = rows // chunks
    copies = [
        pltpu.make_async_copy(conv_hbm, conv_ref, sems.at[0]),
        pltpu.make_async_copy(point_hbm, point_ref, sems.at[1]),
        pltpu.make_async_copy(cot_hbm.at[pl.ds(0, EDGE)], edge_ref.at[0], sems.at[2]),
        pltpu.make_async_copy(cot_hbm.at[pl.ds(rows - EDGE, EDGE)], edge_ref.at[1], sems.at[3]),
    ]
    for k in range(chunks):
        part = pl.ds(k * chunk, chunk)
        copies.append(pltpu.make_async_copy(x_hbm.at[part], x_ref.at[part], sems.at[4 + k]))
    for copy in copies:
        copy.start()
    weight_ref[...] = jnp.zeros_like(weight_ref)
    near_ref[...] = jnp.zeros_like(near_ref)
    sum_ref[...] = jnp.zeros_like(sum_ref)
    copies[0].wait()
    for j in range(KERNEL_WIDTH):
        if folds(depth, slim):
            weight_ref[0, :, j * LANES : (j + 1) * LANES] = fold_rows(conv_ref[j]).astype(BF16)
        else:
            weight_ref[0, :, j * LANES : j * LANES + slim] = conv_ref[j].astype(BF16)
    copies[1].wait()
    near_ref[SUMS : SUMS + depth, :slim] = point_ref[...].T.astype(BF16)

    def step(k, carry):
        v = x_ref[pl.ds(pl.multiple_of(k * 32, 32), 32), :].astype(F32)
        v = v.reshape(4, 8, width)
        return carry[0] + v.sum(0), carry[1] + (v * v).sum(0)

    totals = (jnp.zeros((8, width), F32),) * 2
    for k in range(chunks):
        copies[4 + k].wait()
        totals = lax.fori_loop(
            k * chunk // 32, (k + 1) * chunk // 32, step, totals, unroll=chunk // 32
        )
    for stat, total in enumerate(totals):
        total = jnp.sum(total, 0, keepdims=True)
        for k in range(tiles):
            row = stat * tiles + k
            sum_ref[row : row + 1, :] = total[:, k * LANES : (k + 1) * LANES]
    put_sums(near_ref, sum_ref[...])
    copies[2].wait()
    copies[3].wait()
    odd = lax.axis_index("seq") % 2
    for ref, side in ((near_rim, 1 - odd), (far_rim, odd)):
        ref[:RIM, :] = x_ref[pl.ds(pl.multiple_of(side * (rows - RIM), RIM), RIM), :]
        ref[RIM:, :] = edge_ref[side]


def put_sums(ref, value):
    for p, part in enumerate(split_three(value)):
        ref[p * 16 : (p + 1) * 16, :] = part.astype(BF16)


def get_sums(ref):
    return sum(ref[p * 16 : (p + 1) * 16, :].astype(F32) for p in range(3))


def act_kernel(
    x_ref, cot_hbm, one_ref, two_ref, norm_ref, hid_ref, vec_ref, cot_ref, sems, *, bin_count
):
    copy = pltpu.make_async_copy(cot_hbm, cot_ref, sems.at[0])
    copy.start()
    rows, width = x_ref.shape
    tiles = width // LANES
    total = get_sums(one_ref) + get_sums(two_ref)
    for k in range(tiles):
        lanes = slice(k * LANES, (k + 1) * LANES)
        mean = total[k : k + 1, :] / bin_count
        square = total[tiles + k : tiles + k + 1, :] / bin_count
        root = lax.rsqrt(square - mean * mean + NORM_EPS)
        gain = root * norm_ref[0:1, lanes]
        vec_ref[0:1, lanes] = root
        vec_ref[1:2, lanes] = -mean * root
        vec_ref[2:3, lanes] = gain
        vec_ref[3:4, lanes] = norm_ref[1:2, lanes] - mean * gain

    def step(k, carry):
        at = pl.multiple_of(k * 16, 16)
        v = x_ref[pl.ds(at, 16), :].astype(F32) * vec_ref[2:3, :] + vec_ref[3:4, :]
        hid_ref[pl.ds(at, 16), :] = gelu_and_slope(v)[0].astype(BF16)
        return carry

    lax.fori_loop(0, rows // 16, step, 0, unroll=2)
    copy.wait()


def place(pieces, relatives, stack, own, slim):
    depth = stack.shape[1]
    at = 0
    for piece in pieces:
        for k in range(piece.shape[0]):
            block = piece[k].astype(F32)
            for j in range(KERNEL_WIDTH):
                part = block[:, j * LANES : (j + 1) * LANES]
                if folds(depth, slim):
                    part = unfold_rows(part, slim)
                stack[own ^ relatives[at], :, j * LANES : (j + 1) * LANES] = part.astype(stack.dtype)
            at += 1
    return stack[...].reshape(-1, stack.shape[2]).astype(BF16)


def place_kernel(*refs, relatives, slim):
    pieces, (out_ref, stack) = refs[:-2], refs[-2:]
    out_ref[...] = place(pieces, relatives, stack, lax.axis_index("seq"), slim)


def mask_kernel(start_ref, rim_ref, ahead_ref, back_ref, far_ref):
    far_ref[...] = rim_ref[...]
    rows = back_ref.shape[1]
    first = lax.axis_index("seq") * rows
    for j, shift in enumerate(SHIFTS):
        for begin in range(0, rows + RIM, 96):
            count = min(96, rows + RIM - begin)
            mask = reach_of(first + begin - EDGE, count, shift, start_ref[0], rows * lax.axis_size("seq"))
            ahead_ref[j, begin : begin + count, :] = jnp.where(mask, 1.0, 0.0)
        for begin in range(0, rows, 128):
            back_ref[j, begin : begin + 128, :] = ahead_ref[
                j, EDGE + begin - shift : EDGE + begin - shift + 128, :
            ]


def slope_kernel(x_ref, vec_ref, slope_ref, *, first):
    def step(k, carry):
        at = pl.multiple_of(k * 16, 16)
        v = x_ref[pl.ds(first + at, 16), :].astype(F32) * vec_ref[2:3, :] + vec_ref[3:4, :]
        slope_ref[pl.ds(at, 16), :] = gelu_and_slope(v)[1]
        return carry

    lax.fori_loop(0, slope_ref.shape[0] // 16, step, 0, unroll=2)


def conv_kernel(mask_ref, hid_ref, near_ref, far_ref, vec_ref, *refs, relatives, slim):
    pieces, refs = refs[:2], refs[2:]
    weight_ref, out_ref, sum_ref, rim_ref, all_ref, stack, prod, edge = refs
    size = all_ref.shape[0] // 2
    for k, piece in enumerate(pieces):
        all_ref[k * size : (k + 1) * size] = piece[...]
    odd = lax.axis_index("seq") % 2
    height, width = far_ref.shape
    rim_ref[odd] = far_ref[...]
    base = near_ref.shape[0] - width // LANES * height
    for k in range(width // LANES):
        at = base + k * height
        rim_ref[1 - odd, :, k * LANES : (k + 1) * LANES] = near_ref[at : at + height, :]
    for side in range(2):
        for k in range(0, RIM, 16):
            v = rim_ref[side, k : k + 16, :].astype(F32) * vec_ref[2:3, :] + vec_ref[3:4, :]
            edge[side * RIM + k : side * RIM + k + 16, :] = gelu_and_slope(v)[0].astype(BF16)
    rows = hid_ref.shape[0]
    weight_ref[...] = place(pieces, relatives, stack, lax.axis_index("seq"), slim)
    for at in range(0, weight_ref.shape[1], 256):
        part = slice(at, min(at + 256, weight_ref.shape[1]))
        prod[RIM : RIM + rows, part] = jnp.dot(
            hid_ref[...], weight_ref[:, part], preferred_element_type=F32
        )
        sides = jnp.dot(edge[...], weight_ref[:, part], preferred_element_type=F32)
        prod[:RIM, part] = sides[:RIM]
        prod[RIM + rows :, part] = sides[RIM:]

    def rows_of(begin, count):
        value = 0.0
        for j, shift in enumerate(SHIFTS):
            part = prod[begin + EDGE + shift : begin + EDGE + shift + count, j * LANES : (j + 1) * LANES]
            value = value + mask_ref[j, begin : begin + count, :] * part
        out_ref[begin : begin + count, :] = value
        return value

    rows_of(0, EDGE)
    rows_of(EDGE + rows, EDGE)
    one = two = jnp.zeros((8, LANES), F32)
    step = 128
    for k in range(rows // step):
        value = rows_of(EDGE + k * step, step).reshape(step // 8, 8, LANES)
        one = one + value.sum(0)
        two = two + (value * value).sum(0)
    sum_ref[...] = jnp.zeros_like(sum_ref)
    sum_ref[0:1, :] = jnp.sum(one, 0, keepdims=True)
    sum_ref[1:2, :] = jnp.sum(two, 0, keepdims=True)


def upstream_kernel(cot_ref, rim_ref, one_ref, two_ref, up_ref, point_ref, stack, *, relatives):
    rows = cot_ref.shape[0]
    depth = stack.shape[1]
    own = lax.axis_index("seq")
    count = len(relatives) // 2
    for k, relative in enumerate(relatives):
        piece = (one_ref, two_ref)[k // count]
        at = SUMS + (k % count) * up_to(depth, 16)
        stack[own ^ relative] = piece[at : at + depth, :].astype(stack.dtype)
    point_ref[...] = stack[...].reshape(point_ref.shape).astype(BF16)
    for side, at in enumerate((0, EDGE + rows)):
        up_ref[at : at + EDGE, :] = jnp.dot(
            rim_ref[side, RIM:, :], point_ref[...], preferred_element_type=F32
        )
    up_ref[EDGE : EDGE + rows, :] = jnp.dot(
        cot_ref[...], point_ref[...], preferred_element_type=F32
    )


def mid_kernel(
    total_ref, conv_ref, up_ref, norm_ref, hid_ref, d_ref, cen_ref, sent_ref, vec_ref, *, bin_count
):
    rows = hid_ref.shape[0]
    slim = norm_ref.shape[1]
    total = total_ref[...]
    mean = total[0:1] / bin_count
    root = lax.rsqrt(total[1:2] / bin_count - mean * mean + NORM_EPS)
    vec_ref[...] = jnp.zeros_like(vec_ref)
    vec_ref[0:1, :] = root
    vec_ref[1:3, :slim] = norm_ref[...]
    gain, bias = vec_ref[1:2, :], vec_ref[2:3, :]

    def rows_of(begin, count):
        centered = (conv_ref[pl.ds(begin, count), :] - mean) * root
        hidden, slope = gelu_and_slope(centered * gain + bias)
        d = up_ref[pl.ds(begin, count), :] * slope
        cen_ref[pl.ds(begin, count), :] = centered
        d_ref[pl.ds(begin, count), :] = d
        return centered, hidden, d

    rows_of(0, EDGE)
    rows_of(EDGE + rows, EDGE)
    step = 64

    def body(i, carry):
        begin = pl.multiple_of(EDGE + i * step, 16)
        centered, hidden, d = rows_of(begin, step)
        hid_ref[pl.ds(pl.multiple_of(i * step, 16), step), :] = hidden.astype(BF16)
        d = d.reshape(step // 8, 8, LANES)
        return carry[0] + (d * centered.reshape(d.shape)).sum(0), carry[1] + d.sum(0)

    zero = jnp.zeros((8, LANES), F32)
    gain_sum, bias_sum = lax.fori_loop(0, rows // step, body, (zero, zero), unroll=2)
    gain_sum = jnp.sum(gain_sum, 0, keepdims=True)
    bias_sum = jnp.sum(bias_sum, 0, keepdims=True)
    for d in range(sent_ref.shape[0]):
        sent_ref[d, 0:1, :] = gain_sum
        sent_ref[d, 1:2, :] = bias_sum


def conv_back_kernel(got_ref, vec_ref, d_ref, cen_ref, grad_ref, total_ref, grad, *, bin_count, slim):
    total = got_ref[0]
    for s in range(1, got_ref.shape[0]):
        total = total + got_ref[s]
    total_ref[...] = total
    scale = vec_ref[0:1, :] * vec_ref[1:2, :]
    pull, level = total[0:1] / bin_count, total[1:2] / bin_count
    count = d_ref.shape[0]
    for begin in range(0, count, 96):
        part = slice(begin, min(begin + 96, count))
        grad[part, :] = scale * (d_ref[part, :] - level - cen_ref[part, :] * pull)
    if folds(count, slim):
        grad_ref[...] = fold_rows(grad[:, :slim]).astype(BF16)
    else:
        grad_ref[...] = grad[...].astype(BF16)


def out_kernel(x_ref, *refs):
    parts, (out_ref, token_ref, hidden, point) = refs[:-4], refs[-4:]
    token_ref[...] = jnp.zeros_like(token_ref)
    rows = x_ref.shape[0]
    for r, part in enumerate(parts):
        part = part[...]
        if part.shape[0] < rows + point.shape[0]:
            part = unfold_rows(part.astype(F32), 3 * LANES // 4).astype(BF16)
        hidden[:, r * LANES : (r + 1) * LANES] = part[:rows, :]
        point[:, r * LANES : (r + 1) * LANES] = part[rows:, :]
    for at in range(0, x_ref.shape[1], 256):
        part = slice(at, at + 256)
        branch = lax.dot_general(
            hidden[...], point[part, :], LANE_DIMS, preferred_element_type=F32
        )
        out_ref[:, part] = (x_ref[:, part].astype(F32) + branch).astype(BF16)


def halve(blocks, kept_ref, sent_ref, high):
    for k in range(kept_ref.shape[0]):
        kept_ref[k] = blocks(2 * k + high)
        sent_ref[k] = blocks(2 * k + 1 - high).astype(BF16)


def bit_of(reach):
    return (lax.axis_index("seq") // reach) % 2


def terms_of(part, grad, term_ref, at, mask_ref):
    rows = term_ref.shape[0]
    step = 64
    count = part.shape[0]
    grad[:count, :] = part[...].astype(F32)
    if count < grad.shape[0]:
        quarter = count // 3
        width = LANES // 4
        side = [grad[p * quarter : (p + 1) * quarter, 3 * width :] for p in range(3)]
        grad[count:, :] = jnp.concatenate(side + [jnp.zeros((quarter, width), F32)], axis=1)
    for j, shift in enumerate(SHIFTS):
        lanes = slice(at + j * LANES, at + (j + 1) * LANES)
        for begin in range(0, rows, step):
            value = grad[EDGE + begin - shift : EDGE + begin - shift + step, :]
            value = value * mask_ref[j, begin : begin + step, :]
            term_ref[begin : begin + step, lanes] = value.astype(BF16)


def weight_grad_kernel(
    mask_ref, part_ref, hid_ref, cot_ref, mid_ref, term_ref, kept_ref, sent_ref, grad, full, *, depth, slim
):
    rows = term_ref.shape[0]
    terms_of(part_ref, grad, term_ref, 0, mask_ref)
    taps = lax.dot_general(
        hid_ref[...], term_ref[...], ROW_DIMS, preferred_element_type=F32
    )
    point = lax.dot_general(cot_ref[...], mid_ref[...], ROW_DIMS, preferred_element_type=F32)
    parts = [taps[:, j * LANES : j * LANES + slim] for j in range(KERNEL_WIDTH)] + [point[:, :slim]]
    full[...] = jnp.concatenate(parts, axis=1)
    halve(
        lambda k: full[pl.ds(pl.multiple_of(k * depth, 8), depth), :], kept_ref, sent_ref, bit_of(1)
    )


def fold_kernel(old_ref, got_ref, kept_ref, sent_ref, *, reach):
    halve(lambda k: old_ref[k] + got_ref[k].astype(F32), kept_ref, sent_ref, bit_of(reach))


def adamw(weights_old, first_moment_state, second_mom, gradient, step_rate, decay_rate):
    first_next = BETA_ONE * first_moment_state + (1.0 - BETA_ONE) * gradient
    second_next = BETA_TWO * second_mom + (1.0 - BETA_TWO) * gradient * gradient
    corrected = (
        first_next
        / (1.0 - BETA_ONE**STEP)
        / (jnp.sqrt(second_next / (1.0 - BETA_TWO**STEP)) + ADAM_EPS)
    )
    weights_new = weights_old - step_rate * (corrected + decay_rate * weights_old)
    return (first_next, second_next, weights_new)


def first_half_kernel(mask_ref, own_ref, hid_ref, point_ref, *refs):
    up_ref, both_ref, term, weight, grad = refs[-5:]
    count = (len(refs) - 5 + 1) // 2
    grads, weights = refs[: count - 1], refs[count - 1 : -5]
    rows = up_ref.shape[0]
    if both_ref.shape[0] < rows + point_ref.shape[0]:
        both = jnp.concatenate([hid_ref[...].astype(F32), point_ref[...].astype(F32)], axis=0)
        both_ref[...] = fold_rows(both[:, : 3 * LANES // 4]).astype(BF16)
    else:
        both_ref[:rows, :] = hid_ref[...]
        both_ref[rows:, :] = point_ref[...]
    wide = KERNEL_WIDTH * LANES
    term[:, :wide] = own_ref[...]
    for r, part in enumerate(grads):
        terms_of(part, grad, term, (r + 1) * wide, mask_ref)
    for r, piece in enumerate(weights):
        weight[:, r * wide : (r + 1) * wide] = piece[...]
    for at in range(0, up_ref.shape[1], 256):
        part = slice(at, at + 256)
        up_ref[:, part] = lax.dot_general(
            term[...], weight[part, :], LANE_DIMS, preferred_element_type=F32
        )


def second_half_kernel(mask_ref, x_ref, slope_one, slope_two, vec_ref, part_ref, *refs):
    d_ref, sum_ref, term, weight, grad = refs[-5:]
    count = (len(refs) - 5) // 2
    grads, weights = refs[:count], refs[count:-5]
    rows, width = x_ref.shape
    wide = KERNEL_WIDTH * LANES
    for r in range(count):
        terms_of(grads[r], grad, term, r * wide, mask_ref)
    for r, piece in enumerate(weights):
        weight[:, r * wide : (r + 1) * wide] = piece[...]
    for at in range(0, width, 256):
        part = slice(at, at + 256)
        up = lax.dot_general(term[...], weight[part, :], LANE_DIMS, preferred_element_type=F32)
        slope = jnp.concatenate([slope_one[:, part], slope_two[:, part]], axis=0)
        d = (up + part_ref[:, part]) * slope
        d_ref[:, part] = d
        centered = x_ref[:, part].astype(F32) * vec_ref[0:1, part] + vec_ref[1:2, part]
        sum_ref[0:1, part] = jnp.sum(d * centered, 0, keepdims=True)
        sum_ref[1:2, part] = jnp.sum(d, 0, keepdims=True)


def final_kernel(
    x_ref, cot_ref, d_ref, vec_ref, one_ref, two_ref, old_ref, got_ref, mid_ref, *refs, bin_count, chunks
):
    states, outs, refs = refs[:12], refs[12:25], refs[25:]
    held, news, out_ref, sems = refs[:12], refs[12:24], refs[24], refs[25]
    fetches = [
        pltpu.make_async_copy(src, dst, sems.at[k]) for k, (src, dst) in enumerate(zip(states, held))
    ]
    for fetch in fetches:
        fetch.start()
    rows, width = x_ref.shape
    total = one_ref[...] + two_ref[...]
    root, offset, scale = vec_ref[0:1, :], vec_ref[1:2, :], vec_ref[2:3, :]
    pull = scale * total[0:1] / bin_count
    slant = pull * root
    level = scale * total[1:2] / bin_count + pull * offset
    step = 16
    chunk = rows // chunks

    def body(i, carry):
        at = pl.ds(pl.multiple_of(i * step, 16), step)
        value = x_ref[at, :].astype(F32) * slant + level
        out_ref[at, :] = cot_ref[at, :].astype(F32) + (d_ref[at, :] * scale - value)
        return carry

    sends = []
    for k in range(chunks):
        lax.fori_loop(k * chunk // step, (k + 1) * chunk // step, body, 0, unroll=4)
        part = pl.ds(k * chunk, chunk)
        sends.append(pltpu.make_async_copy(out_ref.at[part], outs[0].at[part], sems.at[24 + k]))
        sends[-1].start()
    for fetch in fetches:
        fetch.wait()

    def step_of(first, at, grad, rate, decay):
        new = adamw(*(ref[at] for ref in held[first : first + 3]), grad, rate, decay)
        for ref, value in zip(news[first : first + 3], new):
            ref[at] = value

    slim = held[3].shape[2]
    both = old_ref[0] + got_ref[0].astype(F32)
    step_of(0, ..., total, RATE_NORM, 0.0)
    for j in range(KERNEL_WIDTH):
        step_of(3, j, both[:, j * slim : (j + 1) * slim], RATE_WEIGHT, DECAY_WEIGHT)
    step_of(6, ..., both[:, KERNEL_WIDTH * slim :].T, RATE_WEIGHT, DECAY_WEIGHT)
    step_of(9, ..., mid_ref[:, :slim], RATE_NORM, 0.0)
    for k in range(12):
        sends.append(pltpu.make_async_copy(news[k], outs[1 + k], sems.at[12 + k]))
        sends[-1].start()
    for send in sends:
        send.wait()


def flip(axis, reach):
    return [(i, i ^ reach) for i in range(lax.axis_size(axis))]


def relatives_of(order):
    found = [0]
    for reach in order:
        found = found + [r ^ reach for r in found]
    return found


def descending(size):
    return [size >> k for k in range(1, size.bit_length())]


def round_kernel(weight_one, weight_two, one_ref, two_ref, *refs):
    weight_ref, out_ref = refs[-2:]
    size = weight_one.shape[0]
    weight_ref[:size] = weight_one[...]
    weight_ref[size:] = weight_two[...]
    put_sums(out_ref, get_sums(one_ref) + get_sums(two_ref))
    rim = out_ref.shape[0] - one_ref.shape[0] * 2 + SUMS if len(refs) > 2 else 0
    size = (out_ref.shape[0] - SUMS - rim) // 2
    out_ref[SUMS : SUMS + size, :] = one_ref[SUMS : SUMS + size, :]
    out_ref[SUMS + size : SUMS + 2 * size, :] = two_ref[SUMS : SUMS + size, :]
    if rim:
        height, width = refs[0].shape
        for k in range(width // LANES):
            at = SUMS + 2 * size + k * height
            out_ref[at : at + height, :] = refs[0][:, k * LANES : (k + 1) * LANES]


def copy_kernel(*refs):
    count = len(refs) // 2
    for src, out in zip(refs[:count], refs[count:]):
        out[...] = src[...]


def copies(arrays, after):
    return call(copy_kernel, [(x.shape, x.dtype) for x in arrays], arrays, after=after)


def add_kernel(one_ref, two_ref, out_ref):
    out_ref[...] = one_ref[...] + two_ref[...]


def add(one, two, after=()):
    return call(add_kernel, [(one.shape, one.dtype)], [one, two], after=after)[0]


def swap(x, axis, reach):
    return lax.ppermute(x, axis, flip(axis, reach))


def gather_parts(x, reaches):
    parts = [x]
    for reach in reaches:
        parts += [swap(part, "ch", reach) for part in parts]
    return parts


def spread(copies, axes):
    return lax.all_to_all(copies, axes, 0, 0, tiled=True)


def shards(
    inputs,
    cotangent,
    starts,
    master_conv,
    first_conv,
    second_conv,
    master_point,
    first_point,
    second_point,
    norm_in,
    first_in,
    second_in,
    norm_mid,
    first_mid,
    second_mid,
):
    rows, width = inputs.shape
    seq_size, ch_size = lax.axis_size("seq"), lax.axis_size("ch")
    bin_count = rows * seq_size
    depth, slim = master_conv.shape[1:]
    tiles = width // LANES
    wide = KERNEL_WIDTH * LANES
    weight_order = descending(seq_size)
    sum_order = weight_order[::-1]
    last_order = weight_order[:1] + sum_order[:-1]
    point_order = weight_order[:1] + [1] + weight_order[1:-1]
    ch_order = descending(ch_size)
    ext = rows + 2 * EDGE

    rounds = len(weight_order)
    top, lower = ch_order[0], ch_order[1:]
    chunks = 4
    rim = (RIM + EDGE, width)
    packed = 3 * depth // 4 if folds(depth, slim) else depth
    inputs, weight, near, *rims = call(
        first_kernel,
        [
            (inputs.shape, BF16),
            ((1, packed, wide), BF16),
            ((SUMS + up_to(depth, 16), LANES), BF16),
            (rim, BF16),
            (rim, BF16),
        ],
        [inputs, cotangent, master_conv, master_point],
        scratch=[
            ((2, EDGE, width), BF16),
            (master_conv.shape, F32),
            (master_point.shape, F32),
            ((16, LANES), F32),
        ],
        away=(0, 1, 2, 3),
        sems=4 + chunks,
    )
    pairs = [(i, i + 1) for i in range(1, seq_size - 1, 2)]
    for k in range(rounds):
        weight_got = swap(weight, "seq", weight_order[k])
        near_got = swap(near, "seq", point_order[k])
        if k < rounds - 1:
            outs = [
                ((2 * weight.shape[0], packed, wide), BF16),
                ((SUMS + (2 << k) * up_to(depth, 16) + (tiles * rim[0] if k == 0 else 0), LANES), BF16),
            ]
            args = [weight, weight_got, near, near_got]
            if k == 0:
                weight, near = call(round_kernel, outs, args + [rims[0]])
                ahead, back, far = call(
                    mask_kernel,
                    [((KERNEL_WIDTH, ext, LANES), F32), ((KERNEL_WIDTH, rows, LANES), F32), (rim, BF16)],
                    [starts, rims[1]],
                    smem=(0,),
                    after=[near],
                )
                far = lax.ppermute(far, "seq", pairs + [(j, i) for i, j in pairs])
            else:
                if k == 1:
                    near_rim = near_got
                weight, near = call(round_kernel, outs, args, after=[back] if k == 1 else [])
    hidden_in, vec_in, cotangent = call(
        functools.partial(act_kernel, bin_count=bin_count),
        [((rows, width), BF16), ((8, width), F32), (cotangent.shape, BF16)],
        [inputs, cotangent, near, near_got, norm_in],
        away=(1,),
        sems=1,
    )

    stack_type = BF16 if depth % 16 == 0 else F32
    conv_own, conv_out, sums_mid, rims, weight = call(
        functools.partial(
            conv_kernel, relatives=relatives_of(weight_order), slim=slim
        ),
        [
            ((width, wide), BF16),
            ((ext, LANES), F32),
            ((8, LANES), F32),
            ((2, *rim), BF16),
            ((seq_size, packed, wide), BF16),
        ],
        [ahead, hidden_in, near_rim, far, vec_in, weight, weight_got],
        scratch=[
            ((seq_size, depth, wide), stack_type),
            ((rows + 2 * RIM, wide), F32),
            ((2 * RIM, width), BF16),
        ],
    )
    weight = swap(weight, "ch", top)
    upstream, point_own = call(
        functools.partial(upstream_kernel, relatives=relatives_of(point_order)),
        [((ext, LANES), F32), ((width, LANES), BF16)],
        [cotangent, rims, near, near_got],
        scratch=[((seq_size, depth, LANES), stack_type)],
        after=[sums_mid],
    )
    conv_near = gather_parts(conv_own, lower)
    total, others, slopes = sums_mid, [upstream], []
    for k, reach in enumerate(sum_order):
        total = add(total, swap(total, "seq", reach), others)
        if k < 2:
            others = call(
                functools.partial(slope_kernel, first=k * rows // 2),
                [((rows // 2, width), F32)],
                [inputs, vec_in],
                after=[total],
            )
            slopes += others
    (weight,) = copies([weight], [total])
    hidden_mid, d_mid, centered, sent_back, vec_mid = call(
        functools.partial(mid_kernel, bin_count=bin_count),
        [
            ((rows, LANES), BF16),
            ((ext, LANES), F32),
            ((ext, LANES), F32),
            ((seq_size, 2, LANES), F32),
            ((8, LANES), F32),
        ],
        [total, conv_out, upstream, norm_mid],
        after=[weight, *conv_near[1:]],
    )
    got_back = spread(sent_back, "seq")
    grad_own, total_mid = call(
        functools.partial(conv_back_kernel, bin_count=bin_count, slim=slim),
        [((3 * ext // 4 if folds(ext, slim) else ext, LANES), BF16), ((2, LANES), F32)],
        [got_back, vec_mid, d_mid, centered],
        scratch=[((ext, LANES), F32)],
    )
    grad_near = gather_parts(grad_own, lower)
    grad_far = swap(grad_own, "ch", top)
    (weight,) = copies([weight], [grad_own])
    conv_far = [
        call(
            functools.partial(place_kernel, relatives=relatives_of(weight_order), slim=slim),
            [((width, wide), BF16)],
            [part],
            scratch=[((seq_size, depth, wide), stack_type)],
        )[0]
        for part in gather_parts(weight, lower)
    ]
    half = seq_size // 2
    terms, kept, sent = call(
        functools.partial(weight_grad_kernel, depth=depth, slim=slim),
        [
            ((rows, wide), BF16),
            ((half, depth, 4 * slim), F32),
            ((half, depth, 4 * slim), BF16),
        ],
        [back, grad_own, hidden_in, cotangent, hidden_mid],
        scratch=[((ext, LANES), F32), ((width, 4 * slim), F32)],
    )
    side = ch_size // 2 * wide
    up_part, both = call(
        first_half_kernel,
        [((rows, width), F32), ((3 * (rows + width) // 4 if folds(rows + width, slim) else rows + width, LANES), BF16)],
        [back, terms, hidden_mid, point_own, *grad_near[1:], *conv_near],
        scratch=[((rows, side), BF16), ((width, side), BF16), ((ext, LANES), F32)],
    )
    grad_far = gather_parts(copies([grad_far], [up_part])[0], lower)
    d_in, sums_back = call(
        second_half_kernel,
        [((rows, width), F32), ((2, width), F32)],
        [back, inputs, *slopes, vec_in, up_part, *grad_far, *conv_far],
        scratch=[((rows, side), BF16), ((width, side), BF16), ((ext, LANES), F32)],
    )
    both_parts = gather_parts(both, lower)
    both_far = swap(both, "ch", top)
    folds_done = [(kept, sent)]
    for reach in sum_order[:-1]:
        half //= 2
        folds_done.append(
            call(
                functools.partial(fold_kernel, reach=2 * reach),
                [((half, depth, 4 * slim), F32), ((half, depth, 4 * slim), BF16)],
                [folds_done[-1][0], swap(folds_done[-1][1], "seq", reach)],
                after=[sums_back],
            )
        )
    kept, got = folds_done[-1][0], swap(folds_done[-1][1], "seq", sum_order[-1])
    total_back = sums_back
    for k in range(rounds):
        total_got = swap(total_back, "seq", last_order[k])
        if k < rounds - 1:
            follows = [folds_done[-1][1]] if k == 0 else []
            total_back = add(total_back, total_got, follows)
        if k == 0:
            both_parts += gather_parts(copies([both_far], [total_back])[0], lower)
    block_out, token = call(
        out_kernel,
        [((rows, width), BF16), ((8, LANES), F32)],
        [inputs, *both_parts],
        scratch=[((rows, ch_size * LANES), BF16), ((width, ch_size * LANES), BF16)],
        after=[total_back],
    )
    states = [norm_in, first_in, second_in, master_conv, first_conv, second_conv]
    states += [master_point, first_point, second_point, norm_mid, first_mid, second_mid]
    arrays = [inputs, cotangent, d_in, vec_in, total_back, total_got, kept, got, total_mid]
    small = [(x.shape, F32) for x in states]
    input_grad, *news = call(
        functools.partial(final_kernel, bin_count=bin_count, chunks=8),
        [((rows, width), F32)] + small,
        arrays + states,
        scratch=small + small + [((rows, width), F32)],
        away=range(len(arrays), len(arrays) + 12),
        away_outs=range(13),
        sems=24 + 8,
        after=[token],
    )
    return (block_out, input_grad, *news[3:9], *news[:3], *news[9:])


def solution(mesh):
    in_specs = (
        P("seq", None),
        P("seq", None),
        P(),
        P(None, "seq", "ch"),
        P(None, "seq", "ch"),
        P(None, "seq", "ch"),
        P("ch", "seq"),
        P("ch", "seq"),
        P("ch", "seq"),
        P(),
        P(),
        P(),
        P(None, "ch"),
        P(None, "ch"),
        P(None, "ch"),
    )
    out_specs = (
        P("seq", None),
        P("seq", None),
        P(None, "seq", "ch"),
        P(None, "seq", "ch"),
        P(None, "seq", "ch"),
        P("ch", "seq"),
        P("ch", "seq"),
        P("ch", "seq"),
        P(),
        P(),
        P(),
        P(None, "ch"),
        P(None, "ch"),
        P(None, "ch"),
    )
    return jax.shard_map(shards, mesh=mesh, in_specs=in_specs, out_specs=out_specs, check_vma=False)
```

```python
import functools

import jax
import jax.numpy as jnp
from jax import lax
from jax.experimental import pallas as pl
from jax.experimental.pallas import tpu as pltpu
from jax.sharding import PartitionSpec as P

KERNEL_WIDTH = 3
DILATION_BINS = 9
WIN = 1024
STEP = 10

NORM_EPS = 1e-05
ADAM_EPS = 1e-08
BETA_ONE = 0.9
BETA_TWO = 0.999
RATE_WEIGHT = 0.05
RATE_NORM = 0.5
DECAY_WEIGHT = 0.01

LANES = 128
EDGE = 16
RIM = 2 * EDGE
SUMS = 48
GELU_A = 0.7978845608028654
GELU_B = 0.044715
SHIFTS = [(j - KERNEL_WIDTH // 2) * DILATION_BINS for j in range(KERNEL_WIDTH)]
ROW_DIMS = (((0,), (0,)), ((), ()))
LANE_DIMS = (((1,), (1,)), ((), ()))
F32, BF16 = jnp.float32, jnp.bfloat16


def call(body, outs, args, scratch=(), smem=(), away=(), after=(), sems=0, away_outs=(), limit=16):
    spaces = [pltpu.SMEM if k in smem else pltpu.VMEM for k in range(len(args))]
    spaces = [pltpu.HBM if k in away else space for k, space in enumerate(spaces)]
    spaces += [pl.ANY] * len(after)

    args = [
        pltpu.with_memory_space_constraint(x, pltpu.HBM) if k in away else x
        for k, x in enumerate(args)
    ]

    def kernel(*refs):
        body(*refs[: len(args)], *refs[len(spaces) :])

    return pl.pallas_call(
        kernel,
        out_shape=[jax.ShapeDtypeStruct(s, t) for s, t in outs],
        in_specs=[pl.BlockSpec(memory_space=s) for s in spaces],
        out_specs=[
            pl.BlockSpec(memory_space=pltpu.HBM if k in away_outs else pltpu.VMEM)
            for k in range(len(outs))
        ],
        scratch_shapes=[pltpu.VMEM(s, t) for s, t in scratch]
        + [pltpu.SemaphoreType.DMA((sems,))] * (sems > 0),
        compiler_params=pltpu.CompilerParams(vmem_limit_bytes=limit * 2**20),
        cost_estimate=pl.CostEstimate(flops=1, bytes_accessed=1, transcendentals=0),
        name=getattr(body, "func", body).__name__,
    )(*args, *after)


def up_to(size, step):
    return -(-size // step) * step


def split_three(v):
    high = v.astype(BF16).astype(F32)
    rest = v - high
    middle = rest.astype(BF16).astype(F32)
    return high, middle, rest - middle


def gelu_and_slope(v):
    square = v * v
    t = jnp.tanh(v * (GELU_A + (GELU_A * GELU_B) * square))
    half = 0.5 * (1.0 + t)
    slope = half + (0.5 * v) * (1.0 - t * t) * (GELU_A + (3.0 * GELU_A * GELU_B) * square)
    return v * half, slope


def reach_of(first, count, shift, start, bin_count):
    here = first + lax.broadcasted_iota(jnp.int32, (count, LANES), 0)
    there = here + shift
    inside = (here >= 0) & (here < bin_count) & (there >= 0) & (there < bin_count)
    return inside & (((here - start) >> 10) == ((there - start) >> 10))


def folds(depth, slim):
    return 3 * (LANES - slim) == slim and depth % 32 == 0


def fold_rows(block):
    rows, slim = block.shape
    quarter, width = rows // 4, LANES - slim
    side = [block[3 * quarter :, p * width : (p + 1) * width] for p in range(3)]
    return jnp.concatenate([block[: 3 * quarter], jnp.concatenate(side, axis=0)], axis=1)


def unfold_rows(block, slim):
    quarter, width = block.shape[0] // 3, LANES - slim
    side = [block[p * quarter : (p + 1) * quarter, slim:] for p in range(3)]
    side.append(jnp.zeros((quarter, width), block.dtype))
    lane = lax.broadcasted_iota(jnp.int32, block.shape, 1)
    return jnp.concatenate([jnp.where(lane < slim, block, 0.0), jnp.concatenate(side, axis=1)], axis=0)


def first_kernel(
    x_hbm, cot_hbm, conv_hbm, point_hbm, x_ref, weight_ref, near_ref, near_rim, far_rim, edge_ref, conv_ref, point_ref, sum_ref, sems
):
    rows, width = x_ref.shape
    tiles = width // LANES
    depth, slim = conv_ref.shape[1:]
    chunks = sems.shape[0] - 4
    chunk = rows // chunks
    copies = [
        pltpu.make_async_copy(conv_hbm, conv_ref, sems.at[0]),
        pltpu.make_async_copy(point_hbm, point_ref, sems.at[1]),
        pltpu.make_async_copy(cot_hbm.at[pl.ds(0, EDGE)], edge_ref.at[0], sems.at[2]),
        pltpu.make_async_copy(cot_hbm.at[pl.ds(rows - EDGE, EDGE)], edge_ref.at[1], sems.at[3]),
    ]
    for k in range(chunks):
        part = pl.ds(k * chunk, chunk)
        copies.append(pltpu.make_async_copy(x_hbm.at[part], x_ref.at[part], sems.at[4 + k]))
    for copy in copies:
        copy.start()
    weight_ref[...] = jnp.zeros_like(weight_ref)
    near_ref[...] = jnp.zeros_like(near_ref)
    sum_ref[...] = jnp.zeros_like(sum_ref)
    copies[0].wait()
    for j in range(KERNEL_WIDTH):
        if folds(depth, slim):
            weight_ref[0, :, j * LANES : (j + 1) * LANES] = fold_rows(conv_ref[j]).astype(BF16)
        else:
            weight_ref[0, :, j * LANES : j * LANES + slim] = conv_ref[j].astype(BF16)
    copies[1].wait()
    near_ref[SUMS : SUMS + depth, :slim] = point_ref[...].T.astype(BF16)

    def step(k, carry):
        v = x_ref[pl.ds(pl.multiple_of(k * 32, 32), 32), :].astype(F32)
        v = v.reshape(4, 8, width)
        return carry[0] + v.sum(0), carry[1] + (v * v).sum(0)

    totals = (jnp.zeros((8, width), F32),) * 2
    for k in range(chunks):
        copies[4 + k].wait()
        totals = lax.fori_loop(
            k * chunk // 32, (k + 1) * chunk // 32, step, totals, unroll=chunk // 32
        )
    for stat, total in enumerate(totals):
        total = jnp.sum(total, 0, keepdims=True)
        for k in range(tiles):
            row = stat * tiles + k
            sum_ref[row : row + 1, :] = total[:, k * LANES : (k + 1) * LANES]
    put_sums(near_ref, sum_ref[...])
    copies[2].wait()
    copies[3].wait()
    odd = lax.axis_index("seq") % 2
    for ref, side in ((near_rim, 1 - odd), (far_rim, odd)):
        ref[:RIM, :] = x_ref[pl.ds(pl.multiple_of(side * (rows - RIM), RIM), RIM), :]
        ref[RIM:, :] = edge_ref[side]


def put_sums(ref, value):
    for p, part in enumerate(split_three(value)):
        ref[p * 16 : (p + 1) * 16, :] = part.astype(BF16)


def get_sums(ref):
    return sum(ref[p * 16 : (p + 1) * 16, :].astype(F32) for p in range(3))


def act_kernel(
    x_ref, cot_hbm, one_ref, two_ref, norm_ref, hid_ref, vec_ref, cot_ref, sems, *, bin_count
):
    copy = pltpu.make_async_copy(cot_hbm, cot_ref, sems.at[0])
    copy.start()
    rows, width = x_ref.shape
    tiles = width // LANES
    total = get_sums(one_ref) + get_sums(two_ref)
    for k in range(tiles):
        lanes = slice(k * LANES, (k + 1) * LANES)
        mean = total[k : k + 1, :] / bin_count
        square = total[tiles + k : tiles + k + 1, :] / bin_count
        root = lax.rsqrt(square - mean * mean + NORM_EPS)
        gain = root * norm_ref[0:1, lanes]
        vec_ref[0:1, lanes] = root
        vec_ref[1:2, lanes] = -mean * root
        vec_ref[2:3, lanes] = gain
        vec_ref[3:4, lanes] = norm_ref[1:2, lanes] - mean * gain

    def step(k, carry):
        at = pl.multiple_of(k * 16, 16)
        v = x_ref[pl.ds(at, 16), :].astype(F32) * vec_ref[2:3, :] + vec_ref[3:4, :]
        hid_ref[pl.ds(at, 16), :] = gelu_and_slope(v)[0].astype(BF16)
        return carry

    lax.fori_loop(0, rows // 16, step, 0, unroll=2)
    copy.wait()


def place(pieces, relatives, stack, own, slim):
    depth = stack.shape[1]
    at = 0
    for piece in pieces:
        for k in range(piece.shape[0]):
            block = piece[k].astype(F32)
            for j in range(KERNEL_WIDTH):
                part = block[:, j * LANES : (j + 1) * LANES]
                if folds(depth, slim):
                    part = unfold_rows(part, slim)
                stack[own ^ relatives[at], :, j * LANES : (j + 1) * LANES] = part.astype(stack.dtype)
            at += 1
    return stack[...].reshape(-1, stack.shape[2]).astype(BF16)


def place_kernel(*refs, relatives, slim):
    pieces, (out_ref, stack) = refs[:-2], refs[-2:]
    out_ref[...] = place(pieces, relatives, stack, lax.axis_index("seq"), slim)


def mask_kernel(start_ref, rim_ref, ahead_ref, back_ref, far_ref):
    far_ref[...] = rim_ref[...]
    rows = back_ref.shape[1]
    first = lax.axis_index("seq") * rows
    for j, shift in enumerate(SHIFTS):
        for begin in range(0, rows + RIM, 96):
            count = min(96, rows + RIM - begin)
            mask = reach_of(first + begin - EDGE, count, shift, start_ref[0], rows * lax.axis_size("seq"))
            ahead_ref[j, begin : begin + count, :] = jnp.where(mask, 1.0, 0.0)
        for begin in range(0, rows, 128):
            back_ref[j, begin : begin + 128, :] = ahead_ref[
                j, EDGE + begin - shift : EDGE + begin - shift + 128, :
            ]


def slope_kernel(x_ref, vec_ref, slope_ref, *, first):
    def step(k, carry):
        at = pl.multiple_of(k * 16, 16)
        v = x_ref[pl.ds(first + at, 16), :].astype(F32) * vec_ref[2:3, :] + vec_ref[3:4, :]
        slope_ref[pl.ds(at, 16), :] = gelu_and_slope(v)[1]
        return carry

    lax.fori_loop(0, slope_ref.shape[0] // 16, step, 0, unroll=2)


def conv_kernel(mask_ref, hid_ref, near_ref, far_ref, vec_ref, *refs, relatives, slim):
    pieces, refs = refs[:2], refs[2:]
    weight_ref, out_ref, sum_ref, rim_ref, all_ref, stack, prod, edge = refs
    size = all_ref.shape[0] // 2
    for k, piece in enumerate(pieces):
        all_ref[k * size : (k + 1) * size] = piece[...]
    odd = lax.axis_index("seq") % 2
    height, width = far_ref.shape
    rim_ref[odd] = far_ref[...]
    base = near_ref.shape[0] - width // LANES * height
    for k in range(width // LANES):
        at = base + k * height
        rim_ref[1 - odd, :, k * LANES : (k + 1) * LANES] = near_ref[at : at + height, :]
    for side in range(2):
        for k in range(0, RIM, 16):
            v = rim_ref[side, k : k + 16, :].astype(F32) * vec_ref[2:3, :] + vec_ref[3:4, :]
            edge[side * RIM + k : side * RIM + k + 16, :] = gelu_and_slope(v)[0].astype(BF16)
    rows = hid_ref.shape[0]
    weight_ref[...] = place(pieces, relatives, stack, lax.axis_index("seq"), slim)
    for at in range(0, weight_ref.shape[1], 256):
        part = slice(at, min(at + 256, weight_ref.shape[1]))
        prod[RIM : RIM + rows, part] = jnp.dot(
            hid_ref[...], weight_ref[:, part], preferred_element_type=F32
        )
        sides = jnp.dot(edge[...], weight_ref[:, part], preferred_element_type=F32)
        prod[:RIM, part] = sides[:RIM]
        prod[RIM + rows :, part] = sides[RIM:]

    def rows_of(begin, count):
        value = 0.0
        for j, shift in enumerate(SHIFTS):
            part = prod[begin + EDGE + shift : begin + EDGE + shift + count, j * LANES : (j + 1) * LANES]
            value = value + mask_ref[j, begin : begin + count, :] * part
        out_ref[begin : begin + count, :] = value
        return value

    rows_of(0, EDGE)
    rows_of(EDGE + rows, EDGE)
    one = two = jnp.zeros((8, LANES), F32)
    step = 128
    for k in range(rows // step):
        value = rows_of(EDGE + k * step, step).reshape(step // 8, 8, LANES)
        one = one + value.sum(0)
        two = two + (value * value).sum(0)
    one, two = jnp.sum(one, 0, keepdims=True), jnp.sum(two, 0, keepdims=True)
    for d in range(sum_ref.shape[0]):
        sum_ref[d, 0:1, :] = one
        sum_ref[d, 1:2, :] = two


def upstream_kernel(cot_ref, rim_ref, one_ref, two_ref, up_ref, point_ref, stack, *, relatives):
    rows = cot_ref.shape[0]
    depth = stack.shape[1]
    own = lax.axis_index("seq")
    count = len(relatives) // 2
    for k, relative in enumerate(relatives):
        piece = (one_ref, two_ref)[k // count]
        at = SUMS + (k % count) * up_to(depth, 16)
        stack[own ^ relative] = piece[at : at + depth, :].astype(stack.dtype)
    point_ref[...] = stack[...].reshape(point_ref.shape).astype(BF16)
    for side, at in enumerate((0, EDGE + rows)):
        up_ref[at : at + EDGE, :] = jnp.dot(
            rim_ref[side, RIM:, :], point_ref[...], preferred_element_type=F32
        )
    up_ref[EDGE : EDGE + rows, :] = jnp.dot(
        cot_ref[...], point_ref[...], preferred_element_type=F32
    )


def mid_kernel(
    got_ref, conv_ref, up_ref, norm_ref, point_ref, hid_ref, d_ref, cen_ref, sent_ref, vec_ref, both_ref, *, bin_count
):
    rows = hid_ref.shape[0]
    slim = norm_ref.shape[1]
    total = got_ref[0]
    for s in range(1, got_ref.shape[0]):
        total = total + got_ref[s]
    mean = total[0:1] / bin_count
    root = lax.rsqrt(total[1:2] / bin_count - mean * mean + NORM_EPS)
    vec_ref[...] = jnp.zeros_like(vec_ref)
    vec_ref[0:1, :] = root
    vec_ref[1:3, :slim] = norm_ref[...]
    gain, bias = vec_ref[1:2, :], vec_ref[2:3, :]

    def rows_of(begin, count):
        centered = (conv_ref[pl.ds(begin, count), :] - mean) * root
        hidden, slope = gelu_and_slope(centered * gain + bias)
        d = up_ref[pl.ds(begin, count), :] * slope
        cen_ref[pl.ds(begin, count), :] = centered
        d_ref[pl.ds(begin, count), :] = d
        return centered, hidden, d

    rows_of(0, EDGE)
    rows_of(EDGE + rows, EDGE)
    step = 64

    def body(i, carry):
        begin = pl.multiple_of(EDGE + i * step, 16)
        centered, hidden, d = rows_of(begin, step)
        hid_ref[pl.ds(pl.multiple_of(i * step, 16), step), :] = hidden.astype(BF16)
        d = d.reshape(step // 8, 8, LANES)
        return carry[0] + (d * centered.reshape(d.shape)).sum(0), carry[1] + d.sum(0)

    zero = jnp.zeros((8, LANES), F32)
    gain_sum, bias_sum = lax.fori_loop(0, rows // step, body, (zero, zero), unroll=2)
    gain_sum = jnp.sum(gain_sum, 0, keepdims=True)
    bias_sum = jnp.sum(bias_sum, 0, keepdims=True)
    for d in range(sent_ref.shape[0]):
        sent_ref[d, 0:1, :] = gain_sum
        sent_ref[d, 1:2, :] = bias_sum
    if both_ref.shape[0] < rows + point_ref.shape[0]:
        both = jnp.concatenate([hid_ref[...].astype(F32), point_ref[...].astype(F32)], axis=0)
        both_ref[...] = fold_rows(both[:, : 3 * LANES // 4]).astype(BF16)
    else:
        both_ref[:rows, :] = hid_ref[...]
        both_ref[rows:, :] = point_ref[...]


def conv_back_kernel(got_ref, vec_ref, d_ref, cen_ref, grad_ref, total_ref, grad, *, bin_count, slim):
    total = got_ref[0]
    for s in range(1, got_ref.shape[0]):
        total = total + got_ref[s]
    total_ref[...] = total
    scale = vec_ref[0:1, :] * vec_ref[1:2, :]
    pull, level = total[0:1] / bin_count, total[1:2] / bin_count
    count = d_ref.shape[0]
    for begin in range(0, count, 96):
        part = slice(begin, min(begin + 96, count))
        grad[part, :] = scale * (d_ref[part, :] - level - cen_ref[part, :] * pull)
    if folds(count, slim):
        grad_ref[...] = fold_rows(grad[:, :slim]).astype(BF16)
    else:
        grad_ref[...] = grad[...].astype(BF16)


def out_kernel(x_ref, *refs):
    parts, (out_ref, token_ref, hidden, point) = refs[:-4], refs[-4:]
    token_ref[...] = jnp.zeros_like(token_ref)
    rows = x_ref.shape[0]
    side = hidden.shape[1] // LANES // 2
    for r in range(2 * side):
        if r < side:
            part = parts[r][...]
        else:
            at = side + 3 * (r - side)
            part = jnp.concatenate([piece[...] for piece in parts[at : at + 3]], axis=0)
        if part.shape[0] < rows + point.shape[0]:
            part = unfold_rows(part.astype(F32), 3 * LANES // 4).astype(BF16)
        hidden[:, r * LANES : (r + 1) * LANES] = part[:rows, :]
        point[:, r * LANES : (r + 1) * LANES] = part[rows:, :]
    for at in range(0, x_ref.shape[1], 256):
        part = slice(at, at + 256)
        branch = lax.dot_general(
            hidden[...], point[part, :], LANE_DIMS, preferred_element_type=F32
        )
        out_ref[:, part] = (x_ref[:, part].astype(F32) + branch).astype(BF16)


def halve(blocks, kept_ref, sent_ref, high):
    for k in range(kept_ref.shape[0]):
        kept_ref[k] = blocks(2 * k + high)
        sent_ref[k] = blocks(2 * k + 1 - high).astype(BF16)


def bit_of(reach):
    return (lax.axis_index("seq") // reach) % 2


def terms_of(part, grad, term_ref, at, mask_ref):
    rows = term_ref.shape[0]
    step = 64
    count = part.shape[0]
    grad[:count, :] = part[...].astype(F32)
    if count < grad.shape[0]:
        quarter = count // 3
        width = LANES // 4
        side = [grad[p * quarter : (p + 1) * quarter, 3 * width :] for p in range(3)]
        grad[count:, :] = jnp.concatenate(side + [jnp.zeros((quarter, width), F32)], axis=1)
    for j, shift in enumerate(SHIFTS):
        lanes = slice(at + j * LANES, at + (j + 1) * LANES)
        for begin in range(0, rows, step):
            value = grad[EDGE + begin - shift : EDGE + begin - shift + step, :]
            value = value * mask_ref[j, begin : begin + step, :]
            term_ref[begin : begin + step, lanes] = value.astype(BF16)


def weight_grad_kernel(
    mask_ref, part_ref, hid_ref, cot_ref, mid_ref, term_ref, kept_ref, sent_ref, grad, full, *, depth, slim
):
    rows = term_ref.shape[0]
    terms_of(part_ref, grad, term_ref, 0, mask_ref)
    taps = lax.dot_general(
        hid_ref[...], term_ref[...], ROW_DIMS, preferred_element_type=F32
    )
    point = lax.dot_general(cot_ref[...], mid_ref[...], ROW_DIMS, preferred_element_type=F32)
    parts = [taps[:, j * LANES : j * LANES + slim] for j in range(KERNEL_WIDTH)] + [point[:, :slim]]
    full[...] = jnp.concatenate(parts, axis=1)
    halve(
        lambda k: full[pl.ds(pl.multiple_of(k * depth, 8), depth), :], kept_ref, sent_ref, bit_of(1)
    )


def fold_kernel(old_ref, got_ref, kept_ref, sent_ref, *, reach):
    halve(lambda k: old_ref[k] + got_ref[k].astype(F32), kept_ref, sent_ref, bit_of(reach))


def adamw(weights_old, first_moment_state, second_mom, gradient, step_rate, decay_rate):
    first_next = BETA_ONE * first_moment_state + (1.0 - BETA_ONE) * gradient
    second_next = BETA_TWO * second_mom + (1.0 - BETA_TWO) * gradient * gradient
    corrected = (
        first_next
        / (1.0 - BETA_ONE**STEP)
        / (jnp.sqrt(second_next / (1.0 - BETA_TWO**STEP)) + ADAM_EPS)
    )
    weights_new = weights_old - step_rate * (corrected + decay_rate * weights_old)
    return (first_next, second_next, weights_new)


def first_half_kernel(mask_ref, own_ref, *refs):
    up_ref, term, weight, grad = refs[-4:]
    count = (len(refs) - 4 + 1) // 2
    grads, weights = refs[: count - 1], refs[count - 1 : -4]
    wide = KERNEL_WIDTH * LANES
    term[:, :wide] = own_ref[...]
    for r, part in enumerate(grads):
        terms_of(part, grad, term, (r + 1) * wide, mask_ref)
    for r, piece in enumerate(weights):
        weight[:, r * wide : (r + 1) * wide] = piece[...]
    for at in range(0, up_ref.shape[1], 256):
        part = slice(at, at + 256)
        up_ref[:, part] = lax.dot_general(
            term[...], weight[part, :], LANE_DIMS, preferred_element_type=F32
        )


def second_half_kernel(mask_ref, x_ref, slope_one, slope_two, vec_ref, part_ref, *refs):
    d_ref, sum_ref, term, weight, grad = refs[-5:]
    count = (len(refs) - 5) // 2
    grads, weights = refs[:count], refs[count:-5]
    rows, width = x_ref.shape
    wide = KERNEL_WIDTH * LANES
    for r in range(count):
        terms_of(grads[r], grad, term, r * wide, mask_ref)
    for r, piece in enumerate(weights):
        weight[:, r * wide : (r + 1) * wide] = piece[...]
    for at in range(0, width, 256):
        part = slice(at, at + 256)
        up = lax.dot_general(term[...], weight[part, :], LANE_DIMS, preferred_element_type=F32)
        slope = jnp.concatenate([slope_one[:, part], slope_two[:, part]], axis=0)
        d = (up + part_ref[:, part]) * slope
        d_ref[:, part] = d
        centered = x_ref[:, part].astype(F32) * vec_ref[0:1, part] + vec_ref[1:2, part]
        sum_ref[0:1, part] = jnp.sum(d * centered, 0, keepdims=True)
        sum_ref[1:2, part] = jnp.sum(d, 0, keepdims=True)


def final_kernel(
    x_ref, cot_ref, d_ref, vec_ref, one_ref, two_ref, old_ref, got_ref, mid_ref, *refs, bin_count, chunks
):
    states, outs, refs = refs[:12], refs[12:25], refs[25:]
    held, news, out_ref, sems = refs[:12], refs[12:24], refs[24], refs[25]
    fetches = [
        pltpu.make_async_copy(src, dst, sems.at[k]) for k, (src, dst) in enumerate(zip(states, held))
    ]
    for fetch in fetches:
        fetch.start()
    rows, width = x_ref.shape
    total = one_ref[...] + two_ref[...]
    root, offset, scale = vec_ref[0:1, :], vec_ref[1:2, :], vec_ref[2:3, :]
    pull = scale * total[0:1] / bin_count
    slant = pull * root
    level = scale * total[1:2] / bin_count + pull * offset
    step = 16
    chunk = rows // chunks

    def body(i, carry):
        at = pl.ds(pl.multiple_of(i * step, 16), step)
        value = x_ref[at, :].astype(F32) * slant + level
        out_ref[at, :] = cot_ref[at, :].astype(F32) + (d_ref[at, :] * scale - value)
        return carry

    sends = []
    for k in range(chunks):
        lax.fori_loop(k * chunk // step, (k + 1) * chunk // step, body, 0, unroll=4)
        part = pl.ds(k * chunk, chunk)
        sends.append(pltpu.make_async_copy(out_ref.at[part], outs[0].at[part], sems.at[24 + k]))
        sends[-1].start()
    for fetch in fetches:
        fetch.wait()

    def step_of(first, at, grad, rate, decay):
        new = adamw(*(ref[at] for ref in held[first : first + 3]), grad, rate, decay)
        for ref, value in zip(news[first : first + 3], new):
            ref[at] = value

    slim = held[3].shape[2]
    both = old_ref[0] + got_ref[0].astype(F32)
    step_of(0, ..., total, RATE_NORM, 0.0)
    for j in range(KERNEL_WIDTH):
        step_of(3, j, both[:, j * slim : (j + 1) * slim], RATE_WEIGHT, DECAY_WEIGHT)
    step_of(6, ..., both[:, KERNEL_WIDTH * slim :].T, RATE_WEIGHT, DECAY_WEIGHT)
    step_of(9, ..., mid_ref[:, :slim], RATE_NORM, 0.0)
    for k in range(12):
        sends.append(pltpu.make_async_copy(news[k], outs[1 + k], sems.at[12 + k]))
        sends[-1].start()
    for send in sends:
        send.wait()


def flip(axis, reach):
    return [(i, i ^ reach) for i in range(lax.axis_size(axis))]


def relatives_of(order):
    found = [0]
    for reach in order:
        found = found + [r ^ reach for r in found]
    return found


def descending(size):
    return [size >> k for k in range(1, size.bit_length())]


def round_kernel(weight_one, weight_two, one_ref, two_ref, *refs):
    weight_ref, out_ref = refs[-2:]
    size = weight_one.shape[0]
    weight_ref[:size] = weight_one[...]
    weight_ref[size:] = weight_two[...]
    put_sums(out_ref, get_sums(one_ref) + get_sums(two_ref))
    rim = out_ref.shape[0] - one_ref.shape[0] * 2 + SUMS if len(refs) > 2 else 0
    size = (out_ref.shape[0] - SUMS - rim) // 2
    out_ref[SUMS : SUMS + size, :] = one_ref[SUMS : SUMS + size, :]
    out_ref[SUMS + size : SUMS + 2 * size, :] = two_ref[SUMS : SUMS + size, :]
    if rim:
        height, width = refs[0].shape
        for k in range(width // LANES):
            at = SUMS + 2 * size + k * height
            out_ref[at : at + height, :] = refs[0][:, k * LANES : (k + 1) * LANES]


def copy_kernel(*refs):
    count = len(refs) // 2
    for src, out in zip(refs[:count], refs[count:]):
        out[...] = src[...]


def slice_kernel(src_ref, out_ref, *, first):
    out_ref[...] = src_ref[first : first + out_ref.shape[0], :]


def copies(arrays, after):
    return call(copy_kernel, [(x.shape, x.dtype) for x in arrays], arrays, after=after)


def add_kernel(one_ref, two_ref, out_ref):
    out_ref[...] = one_ref[...] + two_ref[...]


def add(one, two, after=()):
    return call(add_kernel, [(one.shape, one.dtype)], [one, two], after=after)[0]


def swap(x, axis, reach):
    return lax.ppermute(x, axis, flip(axis, reach))


def gather_parts(x, reaches):
    parts = [x]
    for reach in reaches:
        parts += [swap(part, "ch", reach) for part in parts]
    return parts


def spread(copies, axes):
    return lax.all_to_all(copies, axes, 0, 0, tiled=True)


def shards(
    inputs,
    cotangent,
    starts,
    master_conv,
    first_conv,
    second_conv,
    master_point,
    first_point,
    second_point,
    norm_in,
    first_in,
    second_in,
    norm_mid,
    first_mid,
    second_mid,
):
    rows, width = inputs.shape
    seq_size, ch_size = lax.axis_size("seq"), lax.axis_size("ch")
    bin_count = rows * seq_size
    depth, slim = master_conv.shape[1:]
    tiles = width // LANES
    wide = KERNEL_WIDTH * LANES
    weight_order = descending(seq_size)
    sum_order = weight_order[::-1]
    last_order = weight_order[:1] + sum_order[:-1]
    point_order = weight_order[:1] + [1] + weight_order[1:-1]
    ch_order = descending(ch_size)
    ext = rows + 2 * EDGE

    rounds = len(weight_order)
    top, lower = ch_order[0], ch_order[1:]
    chunks = 4
    rim = (RIM + EDGE, width)
    packed = 3 * depth // 4 if folds(depth, slim) else depth
    inputs, weight, near, *rims = call(
        first_kernel,
        [
            (inputs.shape, BF16),
            ((1, packed, wide), BF16),
            ((SUMS + up_to(depth, 16), LANES), BF16),
            (rim, BF16),
            (rim, BF16),
        ],
        [inputs, cotangent, master_conv, master_point],
        scratch=[
            ((2, EDGE, width), BF16),
            (master_conv.shape, F32),
            (master_point.shape, F32),
            ((16, LANES), F32),
        ],
        away=(0, 1, 2, 3),
        sems=4 + chunks,
    )
    pairs = [(i, i + 1) for i in range(1, seq_size - 1, 2)]
    for k in range(rounds):
        weight_got = swap(weight, "seq", weight_order[k])
        near_got = swap(near, "seq", point_order[k])
        if k < rounds - 1:
            outs = [
                ((2 * weight.shape[0], packed, wide), BF16),
                ((SUMS + (2 << k) * up_to(depth, 16) + (tiles * rim[0] if k == 0 else 0), LANES), BF16),
            ]
            args = [weight, weight_got, near, near_got]
            if k == 0:
                weight, near = call(round_kernel, outs, args + [rims[0]])
                ahead, back, far = call(
                    mask_kernel,
                    [((KERNEL_WIDTH, ext, LANES), F32), ((KERNEL_WIDTH, rows, LANES), F32), (rim, BF16)],
                    [starts, rims[1]],
                    smem=(0,),
                    after=[near],
                )
                far = lax.ppermute(far, "seq", pairs + [(j, i) for i, j in pairs])
            else:
                if k == 1:
                    near_rim = near_got
                weight, near = call(round_kernel, outs, args, after=[back] if k == 1 else [])
    hidden_in, vec_in, cotangent = call(
        functools.partial(act_kernel, bin_count=bin_count),
        [((rows, width), BF16), ((8, width), F32), (cotangent.shape, BF16)],
        [inputs, cotangent, near, near_got, norm_in],
        away=(1,),
        sems=1,
    )
    slopes = call(
        functools.partial(slope_kernel, first=0),
        [((rows // 2, width), F32)],
        [inputs, vec_in],
        after=[hidden_in],
    )

    stack_type = BF16 if depth % 16 == 0 else F32
    conv_own, conv_out, sums_mid, rims, weight = call(
        functools.partial(
            conv_kernel, relatives=relatives_of(weight_order), slim=slim
        ),
        [
            ((width, wide), BF16),
            ((ext, LANES), F32),
            ((seq_size, 2, LANES), F32),
            ((2, *rim), BF16),
            ((seq_size, packed, wide), BF16),
        ],
        [ahead, hidden_in, near_rim, far, vec_in, weight, weight_got],
        scratch=[
            ((seq_size, depth, wide), stack_type),
            ((rows + 2 * RIM, wide), F32),
            ((2 * RIM, width), BF16),
        ],
        after=slopes,
    )
    weight = swap(weight, "ch", top)
    got_mid = spread(sums_mid, "seq")
    upstream, point_own = call(
        functools.partial(upstream_kernel, relatives=relatives_of(point_order)),
        [((ext, LANES), F32), ((width, LANES), BF16)],
        [cotangent, rims, near, near_got],
        scratch=[((seq_size, depth, LANES), stack_type)],
        after=[got_mid],
    )
    conv_near = gather_parts(conv_own, lower)
    hidden_mid, d_mid, centered, sent_back, vec_mid, both = call(
        functools.partial(mid_kernel, bin_count=bin_count),
        [
            ((rows, LANES), BF16),
            ((ext, LANES), F32),
            ((ext, LANES), F32),
            ((seq_size, 2, LANES), F32),
            ((8, LANES), F32),
            ((3 * (rows + width) // 4 if folds(rows + width, slim) else rows + width, LANES), BF16),
        ],
        [got_mid, conv_out, upstream, norm_mid, point_own],
        after=conv_near[1:],
    )
    got_back = spread(sent_back, "seq")
    grad_own, total_mid = call(
        functools.partial(conv_back_kernel, bin_count=bin_count, slim=slim),
        [((3 * ext // 4 if folds(ext, slim) else ext, LANES), BF16), ((2, LANES), F32)],
        [got_back, vec_mid, d_mid, centered],
        scratch=[((ext, LANES), F32)],
    )
    grad_near = gather_parts(grad_own, lower)
    grad_far = swap(grad_own, "ch", top)
    both_parts = gather_parts(both, lower)
    weight, both_far = copies([weight, swap(both, "ch", top)], [grad_own])
    conv_far = [
        call(
            functools.partial(place_kernel, relatives=relatives_of(weight_order), slim=slim),
            [((width, wide), BF16)],
            [part],
            scratch=[((seq_size, depth, wide), stack_type)],
        )[0]
        for part in gather_parts(weight, lower)
    ]
    half = seq_size // 2
    terms, kept, sent = call(
        functools.partial(weight_grad_kernel, depth=depth, slim=slim),
        [
            ((rows, wide), BF16),
            ((half, depth, 4 * slim), F32),
            ((half, depth, 4 * slim), BF16),
        ],
        [back, grad_own, hidden_in, cotangent, hidden_mid],
        scratch=[((ext, LANES), F32), ((width, 4 * slim), F32)],
    )
    side = ch_size // 2 * wide
    (up_part,) = call(
        first_half_kernel,
        [((rows, width), F32)],
        [back, terms, *grad_near[1:], *conv_near],
        scratch=[((rows, side), BF16), ((width, side), BF16), ((ext, LANES), F32)],
    )
    slopes += call(
        functools.partial(slope_kernel, first=rows // 2),
        [((rows // 2, width), F32)],
        [inputs, vec_in],
        after=[up_part],
    )
    grad_far = gather_parts(copies([grad_far], slopes[1:])[0], lower)
    d_in, sums_back = call(
        second_half_kernel,
        [((rows, width), F32), ((2, width), F32)],
        [back, inputs, *slopes, vec_in, up_part, *grad_far, *conv_far],
        scratch=[((rows, side), BF16), ((width, side), BF16), ((ext, LANES), F32)],
    )
    total_back = sums_back
    size = both_far.shape[0]
    cuts = [0, up_to(63 * size // 100, 16), up_to(79 * size // 100, 16), size]
    for k, reach in enumerate(sum_order):
        total_got = swap(total_back, "seq", last_order[k])
        got = swap(sent, "seq", reach)
        if k < rounds - 1:
            half //= 2
            kept, sent = call(
                functools.partial(fold_kernel, reach=2 * reach),
                [((half, depth, 4 * slim), F32), ((half, depth, 4 * slim), BF16)],
                [kept, got],
                after=[total_back] if k else [],
            )
            total_back = add(total_back, total_got)
        for part in {rounds - 3: [0, 1], rounds - 2: [2]}.get(k, []):
            begin, end = cuts[part : part + 2]
            (far_part,) = call(
                functools.partial(slice_kernel, first=begin),
                [((end - begin, LANES), BF16)],
                [both_far],
                after=[total_back],
            )
            both_parts.append(gather_parts(far_part, lower))
    both_parts = both_parts[:-3] + [part for group in zip(*both_parts[-3:]) for part in group]
    block_out, token = call(
        out_kernel,
        [((rows, width), BF16), ((8, LANES), F32)],
        [inputs, *both_parts],
        scratch=[((rows, ch_size * LANES), BF16), ((width, ch_size * LANES), BF16)],
        after=[total_back],
    )
    states = [norm_in, first_in, second_in, master_conv, first_conv, second_conv]
    states += [master_point, first_point, second_point, norm_mid, first_mid, second_mid]
    arrays = [inputs, cotangent, d_in, vec_in, total_back, total_got, kept, got, total_mid]
    small = [(x.shape, F32) for x in states]
    input_grad, *news = call(
        functools.partial(final_kernel, bin_count=bin_count, chunks=8),
        [((rows, width), F32)] + small,
        arrays + states,
        scratch=small + small + [((rows, width), F32)],
        away=range(len(arrays), len(arrays) + 12),
        away_outs=range(13),
        sems=24 + 8,
        after=[token],
    )
    return (block_out, input_grad, *news[3:9], *news[:3], *news[9:])


def solution(mesh):
    in_specs = (
        P("seq", None),
        P("seq", None),
        P(),
        P(None, "seq", "ch"),
        P(None, "seq", "ch"),
        P(None, "seq", "ch"),
        P("ch", "seq"),
        P("ch", "seq"),
        P("ch", "seq"),
        P(),
        P(),
        P(),
        P(None, "ch"),
        P(None, "ch"),
        P(None, "ch"),
    )
    out_specs = (
        P("seq", None),
        P("seq", None),
        P(None, "seq", "ch"),
        P(None, "seq", "ch"),
        P(None, "seq", "ch"),
        P("ch", "seq"),
        P("ch", "seq"),
        P("ch", "seq"),
        P(),
        P(),
        P(),
        P(None, "ch"),
        P(None, "ch"),
        P(None, "ch"),
    )
    return jax.shard_map(shards, mesh=mesh, in_specs=in_specs, out_specs=out_specs, check_vma=False)
```

```python
import functools

import jax
import jax.numpy as jnp
from jax import lax
from jax.experimental import pallas as pl
from jax.experimental.pallas import tpu as pltpu
from jax.sharding import PartitionSpec as P

KERNEL_WIDTH = 3
DILATION_BINS = 9
WIN = 1024
STEP = 10

NORM_EPS = 1e-05
ADAM_EPS = 1e-08
BETA_ONE = 0.9
BETA_TWO = 0.999
RATE_WEIGHT = 0.05
RATE_NORM = 0.5
DECAY_WEIGHT = 0.01

LANES = 128
EDGE = 16
RIM = 2 * EDGE
SUMS = 48
GELU_A = 0.7978845608028654
GELU_B = 0.044715
SHIFTS = [(j - KERNEL_WIDTH // 2) * DILATION_BINS for j in range(KERNEL_WIDTH)]
ROW_DIMS = (((0,), (0,)), ((), ()))
LANE_DIMS = (((1,), (1,)), ((), ()))
F32, BF16 = jnp.float32, jnp.bfloat16


def call(body, outs, args, scratch=(), smem=(), away=(), after=(), sems=0, away_outs=(), limit=16):
    spaces = [pltpu.SMEM if k in smem else pltpu.VMEM for k in range(len(args))]
    spaces = [pltpu.HBM if k in away else space for k, space in enumerate(spaces)]
    spaces += [pl.ANY] * len(after)

    args = [
        pltpu.with_memory_space_constraint(x, pltpu.HBM) if k in away else x
        for k, x in enumerate(args)
    ]

    def kernel(*refs):
        body(*refs[: len(args)], *refs[len(spaces) :])

    return pl.pallas_call(
        kernel,
        out_shape=[jax.ShapeDtypeStruct(s, t) for s, t in outs],
        in_specs=[pl.BlockSpec(memory_space=s) for s in spaces],
        out_specs=[
            pl.BlockSpec(memory_space=pltpu.HBM if k in away_outs else pltpu.VMEM)
            for k in range(len(outs))
        ],
        scratch_shapes=[pltpu.VMEM(s, t) for s, t in scratch]
        + [pltpu.SemaphoreType.DMA((sems,))] * (sems > 0),
        compiler_params=pltpu.CompilerParams(vmem_limit_bytes=limit * 2**20),
        cost_estimate=pl.CostEstimate(flops=1, bytes_accessed=1, transcendentals=0),
        name=getattr(body, "func", body).__name__,
    )(*args, *after)


def up_to(size, step):
    return -(-size // step) * step


def split_three(v):
    high = v.astype(BF16).astype(F32)
    rest = v - high
    middle = rest.astype(BF16).astype(F32)
    return high, middle, rest - middle


def gelu_and_slope(v):
    square = v * v
    t = jnp.tanh(v * (GELU_A + (GELU_A * GELU_B) * square))
    half = 0.5 * (1.0 + t)
    slope = half + (0.5 * v) * (1.0 - t * t) * (GELU_A + (3.0 * GELU_A * GELU_B) * square)
    return v * half, slope


def reach_of(first, count, shift, start, bin_count):
    here = first + lax.broadcasted_iota(jnp.int32, (count, LANES), 0)
    there = here + shift
    inside = (here >= 0) & (here < bin_count) & (there >= 0) & (there < bin_count)
    return inside & (((here - start) >> 10) == ((there - start) >> 10))


def folds(depth, slim):
    return 3 * (LANES - slim) == slim and depth % 32 == 0


def fold_rows(block):
    rows, slim = block.shape
    quarter, width = rows // 4, LANES - slim
    side = [block[3 * quarter :, p * width : (p + 1) * width] for p in range(3)]
    return jnp.concatenate([block[: 3 * quarter], jnp.concatenate(side, axis=0)], axis=1)


def unfold_rows(block, slim):
    quarter, width = block.shape[0] // 3, LANES - slim
    side = [block[p * quarter : (p + 1) * quarter, slim:] for p in range(3)]
    side.append(jnp.zeros((quarter, width), block.dtype))
    lane = lax.broadcasted_iota(jnp.int32, block.shape, 1)
    return jnp.concatenate([jnp.where(lane < slim, block, 0.0), jnp.concatenate(side, axis=1)], axis=0)


def folded_rows(rows, slim):
    return 3 * rows // 4 if folds(rows, slim) else rows


def put_folded(block, out_ref):
    if out_ref.shape[0] < block.shape[0]:
        block = fold_rows(block[:, : 3 * LANES // 4].astype(F32)).astype(BF16)
    out_ref[...] = block


def get_folded(block, rows):
    if block.shape[0] < rows:
        block = unfold_rows(block.astype(F32), 3 * LANES // 4).astype(BF16)
    return block


def first_kernel(
    x_hbm, cot_hbm, conv_hbm, point_hbm, x_ref, weight_ref, near_ref, near_rim, far_rim, edge_ref, conv_ref, point_ref, sum_ref, sems
):
    rows, width = x_ref.shape
    tiles = width // LANES
    depth, slim = conv_ref.shape[1:]
    chunks = sems.shape[0] - 4
    chunk = rows // chunks
    copies = [
        pltpu.make_async_copy(conv_hbm, conv_ref, sems.at[0]),
        pltpu.make_async_copy(point_hbm, point_ref, sems.at[1]),
        pltpu.make_async_copy(cot_hbm.at[pl.ds(0, EDGE)], edge_ref.at[0], sems.at[2]),
        pltpu.make_async_copy(cot_hbm.at[pl.ds(rows - EDGE, EDGE)], edge_ref.at[1], sems.at[3]),
    ]
    for k in range(chunks):
        part = pl.ds(k * chunk, chunk)
        copies.append(pltpu.make_async_copy(x_hbm.at[part], x_ref.at[part], sems.at[4 + k]))
    for copy in copies:
        copy.start()
    weight_ref[...] = jnp.zeros_like(weight_ref)
    near_ref[...] = jnp.zeros_like(near_ref)
    sum_ref[...] = jnp.zeros_like(sum_ref)
    copies[0].wait()
    for j in range(KERNEL_WIDTH):
        if folds(depth, slim):
            weight_ref[0, :, j * LANES : (j + 1) * LANES] = fold_rows(conv_ref[j]).astype(BF16)
        else:
            weight_ref[0, :, j * LANES : j * LANES + slim] = conv_ref[j].astype(BF16)
    copies[1].wait()
    near_ref[SUMS : SUMS + depth, :slim] = point_ref[...].T.astype(BF16)

    def step(k, carry):
        v = x_ref[pl.ds(pl.multiple_of(k * 32, 32), 32), :].astype(F32)
        v = v.reshape(4, 8, width)
        return carry[0] + v.sum(0), carry[1] + (v * v).sum(0)

    totals = (jnp.zeros((8, width), F32),) * 2
    for k in range(chunks):
        copies[4 + k].wait()
        totals = lax.fori_loop(
            k * chunk // 32, (k + 1) * chunk // 32, step, totals, unroll=chunk // 32
        )
    for stat, total in enumerate(totals):
        total = jnp.sum(total, 0, keepdims=True)
        for k in range(tiles):
            row = stat * tiles + k
            sum_ref[row : row + 1, :] = total[:, k * LANES : (k + 1) * LANES]
    put_sums(near_ref, sum_ref[...])
    copies[2].wait()
    copies[3].wait()
    odd = lax.axis_index("seq") % 2
    for ref, side in ((near_rim, 1 - odd), (far_rim, odd)):
        ref[:RIM, :] = x_ref[pl.ds(pl.multiple_of(side * (rows - RIM), RIM), RIM), :]
        ref[RIM:, :] = edge_ref[side]


def put_sums(ref, value):
    for p, part in enumerate(split_three(value)):
        ref[p * 16 : (p + 1) * 16, :] = part.astype(BF16)


def get_sums(ref):
    return sum(ref[p * 16 : (p + 1) * 16, :].astype(F32) for p in range(3))


def act_kernel(
    x_ref, cot_hbm, one_ref, two_ref, norm_ref, hid_ref, vec_ref, cot_ref, sems, *, bin_count
):
    copy = pltpu.make_async_copy(cot_hbm, cot_ref, sems.at[0])
    copy.start()
    rows, width = x_ref.shape
    tiles = width // LANES
    total = get_sums(one_ref) + get_sums(two_ref)
    for k in range(tiles):
        lanes = slice(k * LANES, (k + 1) * LANES)
        mean = total[k : k + 1, :] / bin_count
        square = total[tiles + k : tiles + k + 1, :] / bin_count
        root = lax.rsqrt(square - mean * mean + NORM_EPS)
        gain = root * norm_ref[0:1, lanes]
        vec_ref[0:1, lanes] = root
        vec_ref[1:2, lanes] = -mean * root
        vec_ref[2:3, lanes] = gain
        vec_ref[3:4, lanes] = norm_ref[1:2, lanes] - mean * gain

    def step(k, carry):
        at = pl.multiple_of(k * 16, 16)
        v = x_ref[pl.ds(at, 16), :].astype(F32) * vec_ref[2:3, :] + vec_ref[3:4, :]
        hid_ref[pl.ds(at, 16), :] = gelu_and_slope(v)[0].astype(BF16)
        return carry

    lax.fori_loop(0, rows // 16, step, 0, unroll=2)
    copy.wait()


def place(pieces, relatives, stack, own, slim):
    depth = stack.shape[1]
    at = 0
    for piece in pieces:
        for k in range(piece.shape[0]):
            block = piece[k].astype(F32)
            for j in range(KERNEL_WIDTH):
                part = block[:, j * LANES : (j + 1) * LANES]
                if folds(depth, slim):
                    part = unfold_rows(part, slim)
                stack[own ^ relatives[at], :, j * LANES : (j + 1) * LANES] = part.astype(stack.dtype)
            at += 1
    return stack[...].reshape(-1, stack.shape[2]).astype(BF16)


def place_kernel(*refs, relatives, slim):
    pieces, (out_ref, stack) = refs[:-2], refs[-2:]
    out_ref[...] = place(pieces, relatives, stack, lax.axis_index("seq"), slim)


def mask_kernel(start_ref, rim_ref, ahead_ref, back_ref, far_ref):
    far_ref[...] = rim_ref[...]
    rows = back_ref.shape[1]
    first = lax.axis_index("seq") * rows
    for j, shift in enumerate(SHIFTS):
        for begin in range(0, rows + RIM, 96):
            count = min(96, rows + RIM - begin)
            mask = reach_of(first + begin - EDGE, count, shift, start_ref[0], rows * lax.axis_size("seq"))
            ahead_ref[j, begin : begin + count, :] = jnp.where(mask, 1.0, 0.0)
        for begin in range(0, rows, 128):
            back_ref[j, begin : begin + 128, :] = ahead_ref[
                j, EDGE + begin - shift : EDGE + begin - shift + 128, :
            ]


def slope_kernel(x_ref, vec_ref, slope_ref, *, first):
    def step(k, carry):
        at = pl.multiple_of(k * 16, 16)
        v = x_ref[pl.ds(first + at, 16), :].astype(F32) * vec_ref[2:3, :] + vec_ref[3:4, :]
        slope_ref[pl.ds(at, 16), :] = gelu_and_slope(v)[1]
        return carry

    lax.fori_loop(0, slope_ref.shape[0] // 16, step, 0, unroll=2)


def conv_kernel(mask_ref, hid_ref, near_ref, far_ref, vec_ref, pack_ref, *refs, relatives, slim):
    pieces, refs = refs[:2], refs[2:]
    weight_ref, out_ref, sum_ref, rim_ref, all_ref, stack, prod, edge = refs
    at, packed = 0, pieces[0].shape[1]
    for piece in pieces:
        all_ref[at : at + piece.shape[0]] = piece[...]
        at += piece.shape[0]
    for k in range(pack_ref.shape[0] // packed):
        lanes = slice(k % KERNEL_WIDTH * LANES, (k % KERNEL_WIDTH + 1) * LANES)
        all_ref[at + k // KERNEL_WIDTH, :, lanes] = pack_ref[k * packed : (k + 1) * packed, :]
    odd = lax.axis_index("seq") % 2
    height, width = far_ref.shape
    rim_ref[odd] = far_ref[...]
    base = near_ref.shape[0] - width // LANES * height
    for k in range(width // LANES):
        at = base + k * height
        rim_ref[1 - odd, :, k * LANES : (k + 1) * LANES] = near_ref[at : at + height, :]
    for side in range(2):
        for k in range(0, RIM, 16):
            v = rim_ref[side, k : k + 16, :].astype(F32) * vec_ref[2:3, :] + vec_ref[3:4, :]
            edge[side * RIM + k : side * RIM + k + 16, :] = gelu_and_slope(v)[0].astype(BF16)
    rows = hid_ref.shape[0]
    weight_ref[...] = place(pieces, relatives, stack, lax.axis_index("seq"), slim)
    for at in range(0, weight_ref.shape[1], 256):
        part = slice(at, min(at + 256, weight_ref.shape[1]))
        prod[RIM : RIM + rows, part] = jnp.dot(
            hid_ref[...], weight_ref[:, part], preferred_element_type=F32
        )
        sides = jnp.dot(edge[...], weight_ref[:, part], preferred_element_type=F32)
        prod[:RIM, part] = sides[:RIM]
        prod[RIM + rows :, part] = sides[RIM:]

    def rows_of(begin, count):
        value = 0.0
        for j, shift in enumerate(SHIFTS):
            part = prod[begin + EDGE + shift : begin + EDGE + shift + count, j * LANES : (j + 1) * LANES]
            value = value + mask_ref[j, begin : begin + count, :] * part
        out_ref[begin : begin + count, :] = value
        return value

    rows_of(0, EDGE)
    rows_of(EDGE + rows, EDGE)
    one = two = jnp.zeros((8, LANES), F32)
    step = 128
    for k in range(rows // step):
        value = rows_of(EDGE + k * step, step).reshape(step // 8, 8, LANES)
        one = one + value.sum(0)
        two = two + (value * value).sum(0)
    one, two = jnp.sum(one, 0, keepdims=True), jnp.sum(two, 0, keepdims=True)
    for d in range(sum_ref.shape[0]):
        sum_ref[d, 0:1, :] = one
        sum_ref[d, 1:2, :] = two


def upstream_kernel(cot_ref, one_ref, two_ref, up_ref, point_ref, pack_ref, stack, *, relatives):
    rows = cot_ref.shape[0]
    depth = stack.shape[1]
    own = lax.axis_index("seq")
    count = len(relatives) // 2
    for k, relative in enumerate(relatives):
        piece = (one_ref, two_ref)[k // count]
        at = SUMS + (k % count) * up_to(depth, 16)
        stack[own ^ relative] = piece[at : at + depth, :].astype(stack.dtype)
    point_ref[...] = stack[...].reshape(point_ref.shape).astype(BF16)
    put_folded(point_ref[...], pack_ref)
    up_ref[...] = jnp.dot(cot_ref[...], point_ref[...], preferred_element_type=F32)


def mid_kernel(
    got_ref, conv_ref, up_ref, rim_ref, norm_ref, point_ref, hid_ref, d_ref, cen_ref, sent_ref, vec_ref, *, bin_count
):
    rows = hid_ref.shape[0]
    slim = norm_ref.shape[1]
    total = got_ref[0]
    for s in range(1, got_ref.shape[0]):
        total = total + got_ref[s]
    mean = total[0:1] / bin_count
    root = lax.rsqrt(total[1:2] / bin_count - mean * mean + NORM_EPS)
    vec_ref[...] = jnp.zeros_like(vec_ref)
    vec_ref[0:1, :] = root
    vec_ref[1:3, :slim] = norm_ref[...]
    gain, bias = vec_ref[1:2, :], vec_ref[2:3, :]

    def rows_of(begin, count, up):
        centered = (conv_ref[pl.ds(begin, count), :] - mean) * root
        hidden, slope = gelu_and_slope(centered * gain + bias)
        d = up * slope
        cen_ref[pl.ds(begin, count), :] = centered
        d_ref[pl.ds(begin, count), :] = d
        return centered, hidden, d

    for side, begin in enumerate((0, EDGE + rows)):
        up = jnp.dot(rim_ref[side, RIM:, :], point_ref[...], preferred_element_type=F32)
        rows_of(begin, EDGE, up)
    step = 64

    def body(i, carry):
        begin = pl.multiple_of(EDGE + i * step, 16)
        up = up_ref[pl.ds(pl.multiple_of(i * step, 16), step), :]
        centered, hidden, d = rows_of(begin, step, up)
        hid_ref[pl.ds(pl.multiple_of(i * step, 16), step), :] = hidden.astype(BF16)
        d = d.reshape(step // 8, 8, LANES)
        return carry[0] + (d * centered.reshape(d.shape)).sum(0), carry[1] + d.sum(0)

    zero = jnp.zeros((8, LANES), F32)
    gain_sum, bias_sum = lax.fori_loop(0, rows // step, body, (zero, zero), unroll=2)
    gain_sum = jnp.sum(gain_sum, 0, keepdims=True)
    bias_sum = jnp.sum(bias_sum, 0, keepdims=True)
    for d in range(sent_ref.shape[0]):
        sent_ref[d, 0:1, :] = gain_sum
        sent_ref[d, 1:2, :] = bias_sum


def conv_back_kernel(got_ref, vec_ref, d_ref, cen_ref, grad_ref, total_ref, grad, *, bin_count, slim):
    total = got_ref[0]
    for s in range(1, got_ref.shape[0]):
        total = total + got_ref[s]
    total_ref[...] = total
    scale = vec_ref[0:1, :] * vec_ref[1:2, :]
    pull, level = total[0:1] / bin_count, total[1:2] / bin_count
    count = d_ref.shape[0]
    for begin in range(0, count, 96):
        part = slice(begin, min(begin + 96, count))
        grad[part, :] = scale * (d_ref[part, :] - level - cen_ref[part, :] * pull)
    if folds(count, slim):
        grad_ref[...] = fold_rows(grad[:, :slim]).astype(BF16)
    else:
        grad_ref[...] = grad[...].astype(BF16)


def out_kernel(x_ref, *refs):
    parts, (out_ref, token_ref, hidden, point) = refs[:-4], refs[-4:]
    token_ref[...] = jnp.zeros_like(token_ref)
    rows = x_ref.shape[0]
    side = hidden.shape[1] // LANES // 2
    for r in range(2 * side):
        if r < side:
            part = parts[r][...]
        else:
            at = side + 3 * (r - side)
            part = jnp.concatenate([piece[...] for piece in parts[at : at + 3]], axis=0)
        width = point.shape[0]
        count = part.shape[0] * rows // (rows + width)
        hidden[:, r * LANES : (r + 1) * LANES] = get_folded(part[:count, :], rows)
        point[:, r * LANES : (r + 1) * LANES] = get_folded(part[count:, :], width)
    for at in range(0, x_ref.shape[1], 256):
        part = slice(at, at + 256)
        branch = lax.dot_general(
            hidden[...], point[part, :], LANE_DIMS, preferred_element_type=F32
        )
        out_ref[:, part] = (x_ref[:, part].astype(F32) + branch).astype(BF16)


def halve(blocks, kept_ref, sent_ref, high):
    for k in range(kept_ref.shape[0]):
        kept_ref[k] = blocks(2 * k + high)
        sent_ref[k] = blocks(2 * k + 1 - high).astype(BF16)


def bit_of(reach):
    return (lax.axis_index("seq") // reach) % 2


def terms_of(part, grad, term_ref, at, mask_ref):
    rows = term_ref.shape[0]
    step = 64
    count = part.shape[0]
    grad[:count, :] = part[...].astype(F32)
    if count < grad.shape[0]:
        quarter = count // 3
        width = LANES // 4
        side = [grad[p * quarter : (p + 1) * quarter, 3 * width :] for p in range(3)]
        grad[count:, :] = jnp.concatenate(side + [jnp.zeros((quarter, width), F32)], axis=1)
    for j, shift in enumerate(SHIFTS):
        lanes = slice(at + j * LANES, at + (j + 1) * LANES)
        for begin in range(0, rows, step):
            value = grad[EDGE + begin - shift : EDGE + begin - shift + step, :]
            value = value * mask_ref[j, begin : begin + step, :]
            term_ref[begin : begin + step, lanes] = value.astype(BF16)


def weight_grad_kernel(
    mask_ref, part_ref, hid_ref, cot_ref, mid_ref, point_ref, term_ref, kept_ref, sent_ref, pack_ref, both_ref, grad, full, *, depth, slim
):
    put_folded(mid_ref[...], pack_ref)
    both_ref[: pack_ref.shape[0], :] = pack_ref[...]
    both_ref[pack_ref.shape[0] :, :] = point_ref[...]

    rows = term_ref.shape[0]
    terms_of(part_ref, grad, term_ref, 0, mask_ref)
    taps = lax.dot_general(
        hid_ref[...], term_ref[...], ROW_DIMS, preferred_element_type=F32
    )
    point = lax.dot_general(cot_ref[...], mid_ref[...], ROW_DIMS, preferred_element_type=F32)
    parts = [taps[:, j * LANES : j * LANES + slim] for j in range(KERNEL_WIDTH)] + [point[:, :slim]]
    full[...] = jnp.concatenate(parts, axis=1)
    halve(
        lambda k: full[pl.ds(pl.multiple_of(k * depth, 8), depth), :], kept_ref, sent_ref, bit_of(1)
    )


def fold_kernel(old_ref, got_ref, kept_ref, sent_ref, *, reach):
    halve(lambda k: old_ref[k] + got_ref[k].astype(F32), kept_ref, sent_ref, bit_of(reach))


def adamw(weights_old, first_moment_state, second_mom, gradient, step_rate, decay_rate):
    first_next = BETA_ONE * first_moment_state + (1.0 - BETA_ONE) * gradient
    second_next = BETA_TWO * second_mom + (1.0 - BETA_TWO) * gradient * gradient
    corrected = (
        first_next
        / (1.0 - BETA_ONE**STEP)
        / (jnp.sqrt(second_next / (1.0 - BETA_TWO**STEP)) + ADAM_EPS)
    )
    weights_new = weights_old - step_rate * (corrected + decay_rate * weights_old)
    return (first_next, second_next, weights_new)


def first_half_kernel(mask_ref, own_ref, *refs):
    up_ref, term, weight, grad = refs[-4:]
    count = (len(refs) - 4 + 1) // 2
    grads, weights = refs[: count - 1], refs[count - 1 : -4]
    wide = KERNEL_WIDTH * LANES
    term[:, :wide] = own_ref[...]
    for r, part in enumerate(grads):
        terms_of(part, grad, term, (r + 1) * wide, mask_ref)
    for r, piece in enumerate(weights):
        weight[:, r * wide : (r + 1) * wide] = piece[...]
    for at in range(0, up_ref.shape[1], 256):
        part = slice(at, at + 256)
        up_ref[:, part] = lax.dot_general(
            term[...], weight[part, :], LANE_DIMS, preferred_element_type=F32
        )


def second_half_kernel(mask_ref, x_ref, slope_one, slope_two, vec_ref, part_ref, *refs):
    d_ref, sum_ref, term, weight, grad = refs[-5:]
    count = (len(refs) - 5) // 2
    grads, weights = refs[:count], refs[count:-5]
    rows, width = x_ref.shape
    wide = KERNEL_WIDTH * LANES
    for r in range(count):
        terms_of(grads[r], grad, term, r * wide, mask_ref)
    for r, piece in enumerate(weights):
        weight[:, r * wide : (r + 1) * wide] = piece[...]
    for at in range(0, width, 256):
        part = slice(at, at + 256)
        up = lax.dot_general(term[...], weight[part, :], LANE_DIMS, preferred_element_type=F32)
        slope = jnp.concatenate([slope_one[:, part], slope_two[:, part]], axis=0)
        d = (up + part_ref[:, part]) * slope
        d_ref[:, part] = d
        centered = x_ref[:, part].astype(F32) * vec_ref[0:1, part] + vec_ref[1:2, part]
        sum_ref[0:1, part] = jnp.sum(d * centered, 0, keepdims=True)
        sum_ref[1:2, part] = jnp.sum(d, 0, keepdims=True)


def final_kernel(
    x_ref, cot_ref, d_ref, vec_ref, one_ref, two_ref, old_ref, got_ref, mid_ref, *refs, bin_count, chunks
):
    states, outs, refs = refs[:12], refs[12:25], refs[25:]
    held, news, out_ref, sems = refs[:12], refs[12:24], refs[24], refs[25]
    fetches = [
        pltpu.make_async_copy(src, dst, sems.at[k]) for k, (src, dst) in enumerate(zip(states, held))
    ]
    for fetch in fetches:
        fetch.start()
    rows, width = x_ref.shape
    total = one_ref[...] + two_ref[...]
    root, offset, scale = vec_ref[0:1, :], vec_ref[1:2, :], vec_ref[2:3, :]
    pull = scale * total[0:1] / bin_count
    slant = pull * root
    level = scale * total[1:2] / bin_count + pull * offset
    step = 16
    chunk = rows // chunks

    def body(i, carry):
        at = pl.ds(pl.multiple_of(i * step, 16), step)
        value = x_ref[at, :].astype(F32) * slant + level
        out_ref[at, :] = cot_ref[at, :].astype(F32) + (d_ref[at, :] * scale - value)
        return carry

    sends = []
    for k in range(chunks):
        lax.fori_loop(k * chunk // step, (k + 1) * chunk // step, body, 0, unroll=4)
        part = pl.ds(k * chunk, chunk)
        sends.append(pltpu.make_async_copy(out_ref.at[part], outs[0].at[part], sems.at[24 + k]))
        sends[-1].start()
    for fetch in fetches:
        fetch.wait()

    def step_of(first, at, grad, rate, decay):
        new = adamw(*(ref[at] for ref in held[first : first + 3]), grad, rate, decay)
        for ref, value in zip(news[first : first + 3], new):
            ref[at] = value

    slim = held[3].shape[2]
    both = old_ref[0] + got_ref[0].astype(F32)
    step_of(0, ..., total, RATE_NORM, 0.0)
    for j in range(KERNEL_WIDTH):
        step_of(3, j, both[:, j * slim : (j + 1) * slim], RATE_WEIGHT, DECAY_WEIGHT)
    step_of(6, ..., both[:, KERNEL_WIDTH * slim :].T, RATE_WEIGHT, DECAY_WEIGHT)
    step_of(9, ..., mid_ref[:, :slim], RATE_NORM, 0.0)
    for k in range(12):
        sends.append(pltpu.make_async_copy(news[k], outs[1 + k], sems.at[12 + k]))
        sends[-1].start()
    for send in sends:
        send.wait()


def flip(axis, reach):
    return [(i, i ^ reach) for i in range(lax.axis_size(axis))]


def relatives_of(order):
    found = [0]
    for reach in order:
        found = found + [r ^ reach for r in found]
    return found


def descending(size):
    return [size >> k for k in range(1, size.bit_length())]


def round_kernel(weight_one, weight_two, one_ref, two_ref, *refs):
    weight_ref, out_ref = refs[-2:]
    size = weight_one.shape[0]
    weight_ref[:size] = weight_one[...]
    weight_ref[size:] = weight_two[...]
    put_sums(out_ref, get_sums(one_ref) + get_sums(two_ref))
    rim = out_ref.shape[0] - one_ref.shape[0] * 2 + SUMS if len(refs) > 2 else 0
    size = (out_ref.shape[0] - SUMS - rim) // 2
    out_ref[SUMS : SUMS + size, :] = one_ref[SUMS : SUMS + size, :]
    out_ref[SUMS + size : SUMS + 2 * size, :] = two_ref[SUMS : SUMS + size, :]
    if rim:
        height, width = refs[0].shape
        for k in range(width // LANES):
            at = SUMS + 2 * size + k * height
            out_ref[at : at + height, :] = refs[0][:, k * LANES : (k + 1) * LANES]


def copy_kernel(*refs):
    count = len(refs) // 2
    for src, out in zip(refs[:count], refs[count:]):
        out[...] = src[...]


def packs(wanted, after):
    arrays, places = [], []
    for pieces in wanted:
        places.append([])
        for piece in pieces:
            array, begin, end = piece if isinstance(piece, tuple) else (piece, 0, piece.shape[0])
            places[-1].append((len(arrays), begin, end))
            arrays.append(array)

    def pack_kernel(*refs):
        for out, group in zip(refs[len(arrays) :], places):
            at = 0
            for index, begin, end in group:
                out[at : at + end - begin, :] = refs[index][begin:end, :]
                at += end - begin

    sizes = [sum(end - begin for _, begin, end in group) for group in places]
    return call(pack_kernel, [((size, LANES), BF16) for size in sizes], arrays, after=after)


def take_kernel(src_ref, weight_ref, pack_ref):
    count, packed = weight_ref.shape[:2]
    weight_ref[...] = src_ref[:count]
    for k in range(pack_ref.shape[0] // packed):
        lanes = slice(k % KERNEL_WIDTH * LANES, (k % KERNEL_WIDTH + 1) * LANES)
        pack_ref[k * packed : (k + 1) * packed, :] = src_ref[count + k // KERNEL_WIDTH, :, lanes]


def copies(arrays, after):
    return call(copy_kernel, [(x.shape, x.dtype) for x in arrays], arrays, after=after)


def add_kernel(one_ref, two_ref, out_ref):
    out_ref[...] = one_ref[...] + two_ref[...]


def add(one, two, after=()):
    return call(add_kernel, [(one.shape, one.dtype)], [one, two], after=after)[0]


def swap(x, axis, reach):
    return lax.ppermute(x, axis, flip(axis, reach))


def gather_parts(x, reaches):
    parts = [x]
    for reach in reaches:
        parts += [swap(part, "ch", reach) for part in parts]
    return parts


def spread(copies, axes):
    return lax.all_to_all(copies, axes, 0, 0, tiled=True)


def shards(
    inputs,
    cotangent,
    starts,
    master_conv,
    first_conv,
    second_conv,
    master_point,
    first_point,
    second_point,
    norm_in,
    first_in,
    second_in,
    norm_mid,
    first_mid,
    second_mid,
):
    rows, width = inputs.shape
    seq_size, ch_size = lax.axis_size("seq"), lax.axis_size("ch")
    bin_count = rows * seq_size
    depth, slim = master_conv.shape[1:]
    tiles = width // LANES
    wide = KERNEL_WIDTH * LANES
    weight_order = descending(seq_size)
    sum_order = weight_order[::-1]
    last_order = weight_order[:1] + sum_order[:-1]
    point_order = weight_order[:1] + [1] + weight_order[1:-1]
    ch_order = descending(ch_size)
    ext = rows + 2 * EDGE

    rounds = len(weight_order)
    top, lower = ch_order[0], ch_order[1:]
    chunks = 4
    rim = (RIM + EDGE, width)
    packed = 3 * depth // 4 if folds(depth, slim) else depth
    inputs, weight, near, *rims = call(
        first_kernel,
        [
            (inputs.shape, BF16),
            ((1, packed, wide), BF16),
            ((SUMS + up_to(depth, 16), LANES), BF16),
            (rim, BF16),
            (rim, BF16),
        ],
        [inputs, cotangent, master_conv, master_point],
        scratch=[
            ((2, EDGE, width), BF16),
            (master_conv.shape, F32),
            (master_point.shape, F32),
            ((16, LANES), F32),
        ],
        away=(0, 1, 2, 3),
        sems=4 + chunks,
    )
    pairs = [(i, i + 1) for i in range(1, seq_size - 1, 2)]
    for k in range(rounds):
        weight_got = swap(weight, "seq", weight_order[k])
        near_got = swap(near, "seq", point_order[k])
        if k < rounds - 1:
            outs = [
                ((2 * weight.shape[0], packed, wide), BF16),
                ((SUMS + (2 << k) * up_to(depth, 16) + (tiles * rim[0] if k == 0 else 0), LANES), BF16),
            ]
            args = [weight, weight_got, near, near_got]
            if k == 0:
                weight, near = call(round_kernel, outs, args + [rims[0]])
                ahead, back, far = call(
                    mask_kernel,
                    [((KERNEL_WIDTH, ext, LANES), F32), ((KERNEL_WIDTH, rows, LANES), F32), (rim, BF16)],
                    [starts, rims[1]],
                    smem=(0,),
                    after=[near],
                )
                far = lax.ppermute(far, "seq", pairs + [(j, i) for i, j in pairs])
            else:
                if k == 1:
                    near_rim = near_got
                weight, near = call(round_kernel, outs, args, after=[back] if k == 1 else [])
    hidden_in, vec_in, cotangent = call(
        functools.partial(act_kernel, bin_count=bin_count),
        [((rows, width), BF16), ((8, width), F32), (cotangent.shape, BF16)],
        [inputs, cotangent, near, near_got, norm_in],
        away=(1,),
        sems=1,
    )
    slopes = call(
        functools.partial(slope_kernel, first=0),
        [((rows // 2, width), F32)],
        [inputs, vec_in],
        after=[hidden_in],
    )
    stack_type = BF16 if depth % 16 == 0 else F32
    upstream, point_own, point_pack = call(
        functools.partial(upstream_kernel, relatives=relatives_of(point_order)),
        [((rows, LANES), F32), ((width, LANES), BF16), ((folded_rows(width, slim), LANES), BF16)],
        [cotangent, near, near_got],
        scratch=[((seq_size, depth, LANES), stack_type)],
        after=slopes,
    )
    blocks = -(-point_pack.shape[0] // (packed * KERNEL_WIDTH))
    conv_own, conv_out, sums_mid, rims, weight = call(
        functools.partial(
            conv_kernel, relatives=relatives_of(weight_order), slim=slim
        ),
        [
            ((width, wide), BF16),
            ((ext, LANES), F32),
            ((seq_size, 2, LANES), F32),
            ((2, *rim), BF16),
            ((seq_size + blocks, packed, wide), BF16),
        ],
        [ahead, hidden_in, near_rim, far, vec_in, point_pack, weight, weight_got],
        scratch=[
            ((seq_size, depth, wide), stack_type),
            ((rows + 2 * RIM, wide), F32),
            ((2 * RIM, width), BF16),
        ],
        after=[upstream],
    )
    weight = swap(weight, "ch", top)
    got_mid = spread(sums_mid, "seq")
    conv_near = gather_parts(conv_own, lower)
    hidden_mid, d_mid, centered, sent_back, vec_mid = call(
        functools.partial(mid_kernel, bin_count=bin_count),
        [
            ((rows, LANES), BF16),
            ((ext, LANES), F32),
            ((ext, LANES), F32),
            ((seq_size, 2, LANES), F32),
            ((8, LANES), F32),
        ],
        [got_mid, conv_out, upstream, rims, norm_mid, point_own],
        after=conv_near[1:],
    )
    got_back = spread(sent_back, "seq")
    grad_own, total_mid = call(
        functools.partial(conv_back_kernel, bin_count=bin_count, slim=slim),
        [((3 * ext // 4 if folds(ext, slim) else ext, LANES), BF16), ((2, LANES), F32)],
        [got_back, vec_mid, d_mid, centered],
        scratch=[((ext, LANES), F32)],
    )
    grad_near = gather_parts(grad_own, lower)
    grad_far = swap(grad_own, "ch", top)
    weight, point_far = call(
        take_kernel,
        [((seq_size, packed, wide), BF16), (point_pack.shape, BF16)],
        [weight],
        after=[grad_own],
    )
    conv_far = [
        call(
            functools.partial(place_kernel, relatives=relatives_of(weight_order), slim=slim),
            [((width, wide), BF16)],
            [part],
            scratch=[((seq_size, depth, wide), stack_type)],
        )[0]
        for part in gather_parts(weight, lower)
    ]
    half = seq_size // 2
    hidden_rows = folded_rows(rows, slim)
    terms, kept, sent, hidden_pack, both = call(
        functools.partial(weight_grad_kernel, depth=depth, slim=slim),
        [
            ((rows, wide), BF16),
            ((half, depth, 4 * slim), F32),
            ((half, depth, 4 * slim), BF16),
            ((hidden_rows, LANES), BF16),
            ((hidden_rows + point_pack.shape[0], LANES), BF16),
        ],
        [back, grad_own, hidden_in, cotangent, hidden_mid, point_pack],
        scratch=[((ext, LANES), F32), ((width, 4 * slim), F32)],
    )
    side = ch_size // 2 * wide
    (up_part,) = call(
        first_half_kernel,
        [((rows, width), F32)],
        [back, terms, *grad_near[1:], *conv_near],
        scratch=[((rows, side), BF16), ((width, side), BF16), ((ext, LANES), F32)],
    )
    slopes += call(
        functools.partial(slope_kernel, first=rows // 2),
        [((rows // 2, width), F32)],
        [inputs, vec_in],
        after=[up_part],
    )
    grad_far = gather_parts(copies([grad_far], slopes[1:])[0], lower)
    both_parts = gather_parts(both, lower)
    d_in, sums_back = call(
        second_half_kernel,
        [((rows, width), F32), ((2, width), F32)],
        [back, inputs, *slopes, vec_in, up_part, *grad_far, *conv_far],
        scratch=[((rows, side), BF16), ((width, side), BF16), ((ext, LANES), F32)],
        after=both_parts[1:],
    )
    total_back = sums_back
    hidden_far = swap(hidden_pack, "ch", top)
    count = point_far.shape[0]
    cuts = [0, up_to(13 * count // 100, 16), up_to(52 * count // 100, 16), count]
    for k, reach in enumerate(sum_order):
        total_got = swap(total_back, "seq", last_order[k])
        got = swap(sent, "seq", reach)
        if k < rounds - 1:
            half //= 2
            kept, sent = call(
                functools.partial(fold_kernel, reach=2 * reach),
                [((half, depth, 4 * slim), F32), ((half, depth, 4 * slim), BF16)],
                [kept, got],
                after=[total_back] if k else [],
            )
            total_back = add(total_back, total_got)
        if k == rounds - 3:
            wanted = [[hidden_far, (point_far, *cuts[:2])], [(point_far, *cuts[1:3])]]
            far_parts = [gather_parts(x, lower) for x in packs(wanted, [total_back])]
        if k == rounds - 2:
            (last,) = packs([[(point_far, *cuts[2:])]], [total_back])
            far_parts.append(gather_parts(last, lower))
    both_parts += [part for group in zip(*far_parts) for part in group]
    block_out, token = call(
        out_kernel,
        [((rows, width), BF16), ((8, LANES), F32)],
        [inputs, *both_parts],
        scratch=[((rows, ch_size * LANES), BF16), ((width, ch_size * LANES), BF16)],
        after=[total_back],
    )
    states = [norm_in, first_in, second_in, master_conv, first_conv, second_conv]
    states += [master_point, first_point, second_point, norm_mid, first_mid, second_mid]
    arrays = [inputs, cotangent, d_in, vec_in, total_back, total_got, kept, got, total_mid]
    small = [(x.shape, F32) for x in states]
    input_grad, *news = call(
        functools.partial(final_kernel, bin_count=bin_count, chunks=8),
        [((rows, width), F32)] + small,
        arrays + states,
        scratch=small + small + [((rows, width), F32)],
        away=range(len(arrays), len(arrays) + 12),
        away_outs=range(13),
        sems=24 + 8,
        after=[token],
    )
    return (block_out, input_grad, *news[3:9], *news[:3], *news[9:])


def solution(mesh):
    in_specs = (
        P("seq", None),
        P("seq", None),
        P(),
        P(None, "seq", "ch"),
        P(None, "seq", "ch"),
        P(None, "seq", "ch"),
        P("ch", "seq"),
        P("ch", "seq"),
        P("ch", "seq"),
        P(),
        P(),
        P(),
        P(None, "ch"),
        P(None, "ch"),
        P(None, "ch"),
    )
    out_specs = (
        P("seq", None),
        P("seq", None),
        P(None, "seq", "ch"),
        P(None, "seq", "ch"),
        P(None, "seq", "ch"),
        P("ch", "seq"),
        P("ch", "seq"),
        P("ch", "seq"),
        P(),
        P(),
        P(),
        P(None, "ch"),
        P(None, "ch"),
        P(None, "ch"),
    )
    return jax.shard_map(shards, mesh=mesh, in_specs=in_specs, out_specs=out_specs, check_vma=False)
```

```python
import functools

import jax
import jax.numpy as jnp
from jax import lax
from jax.experimental import pallas as pl
from jax.experimental.pallas import tpu as pltpu
from jax.sharding import PartitionSpec as P

KERNEL_WIDTH = 3
DILATION_BINS = 9
WIN = 1024
STEP = 10

NORM_EPS = 1e-05
ADAM_EPS = 1e-08
BETA_ONE = 0.9
BETA_TWO = 0.999
RATE_WEIGHT = 0.05
RATE_NORM = 0.5
DECAY_WEIGHT = 0.01

LANES = 128
EDGE = 16
RIM = 2 * EDGE
SUMS = 48
GELU_A = 0.7978845608028654
GELU_B = 0.044715
SHIFTS = [(j - KERNEL_WIDTH // 2) * DILATION_BINS for j in range(KERNEL_WIDTH)]
ROW_DIMS = (((0,), (0,)), ((), ()))
LANE_DIMS = (((1,), (1,)), ((), ()))
F32, BF16 = jnp.float32, jnp.bfloat16


def call(body, outs, args, scratch=(), smem=(), away=(), after=(), sems=0, away_outs=(), limit=16):
    spaces = [pltpu.SMEM if k in smem else pltpu.VMEM for k in range(len(args))]
    spaces = [pltpu.HBM if k in away else space for k, space in enumerate(spaces)]
    spaces += [pl.ANY] * len(after)

    args = [
        pltpu.with_memory_space_constraint(x, pltpu.HBM) if k in away else x
        for k, x in enumerate(args)
    ]

    def kernel(*refs):
        body(*refs[: len(args)], *refs[len(spaces) :])

    return pl.pallas_call(
        kernel,
        out_shape=[jax.ShapeDtypeStruct(s, t) for s, t in outs],
        in_specs=[pl.BlockSpec(memory_space=s) for s in spaces],
        out_specs=[
            pl.BlockSpec(memory_space=pltpu.HBM if k in away_outs else pltpu.VMEM)
            for k in range(len(outs))
        ],
        scratch_shapes=[pltpu.VMEM(s, t) for s, t in scratch]
        + [pltpu.SemaphoreType.DMA((sems,))] * (sems > 0),
        compiler_params=pltpu.CompilerParams(vmem_limit_bytes=limit * 2**20),
        cost_estimate=pl.CostEstimate(flops=1, bytes_accessed=1, transcendentals=0),
        name=getattr(body, "func", body).__name__,
    )(*args, *after)


def up_to(size, step):
    return -(-size // step) * step


def split_three(v):
    high = v.astype(BF16).astype(F32)
    rest = v - high
    middle = rest.astype(BF16).astype(F32)
    return high, middle, rest - middle


def gelu_and_slope(v):
    square = v * v
    t = jnp.tanh(v * (GELU_A + (GELU_A * GELU_B) * square))
    half = 0.5 * (1.0 + t)
    slope = half + (0.5 * v) * (1.0 - t * t) * (GELU_A + (3.0 * GELU_A * GELU_B) * square)
    return v * half, slope


def reach_of(first, count, shift, start, bin_count):
    here = first + lax.broadcasted_iota(jnp.int32, (count, LANES), 0)
    there = here + shift
    inside = (here >= 0) & (here < bin_count) & (there >= 0) & (there < bin_count)
    return inside & (((here - start) >> 10) == ((there - start) >> 10))


def folds(depth, slim):
    return 3 * (LANES - slim) == slim and depth % 32 == 0


def fold_rows(block):
    rows, slim = block.shape
    quarter, width = rows // 4, LANES - slim
    side = [block[3 * quarter :, p * width : (p + 1) * width] for p in range(3)]
    return jnp.concatenate([block[: 3 * quarter], jnp.concatenate(side, axis=0)], axis=1)


def unfold_rows(block, slim):
    quarter, width = block.shape[0] // 3, LANES - slim
    side = [block[p * quarter : (p + 1) * quarter, slim:] for p in range(3)]
    side.append(jnp.zeros((quarter, width), block.dtype))
    lane = lax.broadcasted_iota(jnp.int32, block.shape, 1)
    return jnp.concatenate([jnp.where(lane < slim, block, 0.0), jnp.concatenate(side, axis=1)], axis=0)


def folded_rows(rows, slim):
    return 3 * rows // 4 if folds(rows, slim) else rows


def put_folded(block, out_ref):
    if out_ref.shape[0] < block.shape[0]:
        block = fold_rows(block[:, : 3 * LANES // 4].astype(F32)).astype(BF16)
    out_ref[...] = block


def get_folded(block, rows):
    if block.shape[0] < rows:
        block = unfold_rows(block.astype(F32), 3 * LANES // 4).astype(BF16)
    return block


def first_kernel(
    x_hbm, cot_hbm, conv_hbm, point_hbm, x_ref, weight_ref, near_ref, near_rim, far_rim, edge_ref, conv_ref, point_ref, sum_ref, sems
):
    rows, width = x_ref.shape
    tiles = width // LANES
    depth, slim = conv_ref.shape[1:]
    chunks = sems.shape[0] - 4
    chunk = rows // chunks
    copies = [
        pltpu.make_async_copy(conv_hbm, conv_ref, sems.at[0]),
        pltpu.make_async_copy(point_hbm, point_ref, sems.at[1]),
        pltpu.make_async_copy(cot_hbm.at[pl.ds(0, EDGE)], edge_ref.at[0], sems.at[2]),
        pltpu.make_async_copy(cot_hbm.at[pl.ds(rows - EDGE, EDGE)], edge_ref.at[1], sems.at[3]),
    ]
    for k in range(chunks):
        part = pl.ds(k * chunk, chunk)
        copies.append(pltpu.make_async_copy(x_hbm.at[part], x_ref.at[part], sems.at[4 + k]))
    for copy in copies:
        copy.start()
    weight_ref[...] = jnp.zeros_like(weight_ref)
    near_ref[...] = jnp.zeros_like(near_ref)
    sum_ref[...] = jnp.zeros_like(sum_ref)
    copies[0].wait()
    for j in range(KERNEL_WIDTH):
        if folds(depth, slim):
            weight_ref[0, :, j * LANES : (j + 1) * LANES] = fold_rows(conv_ref[j]).astype(BF16)
        else:
            weight_ref[0, :, j * LANES : j * LANES + slim] = conv_ref[j].astype(BF16)
    copies[1].wait()
    near_ref[SUMS : SUMS + depth, :slim] = point_ref[...].T.astype(BF16)

    def step(k, carry):
        v = x_ref[pl.ds(pl.multiple_of(k * 32, 32), 32), :].astype(F32)
        v = v.reshape(4, 8, width)
        return carry[0] + v.sum(0), carry[1] + (v * v).sum(0)

    totals = (jnp.zeros((8, width), F32),) * 2
    for k in range(chunks):
        copies[4 + k].wait()
        totals = lax.fori_loop(
            k * chunk // 32, (k + 1) * chunk // 32, step, totals, unroll=chunk // 32
        )
    for stat, total in enumerate(totals):
        total = jnp.sum(total, 0, keepdims=True)
        for k in range(tiles):
            row = stat * tiles + k
            sum_ref[row : row + 1, :] = total[:, k * LANES : (k + 1) * LANES]
    put_sums(near_ref, sum_ref[...])
    copies[2].wait()
    copies[3].wait()
    odd = lax.axis_index("seq") % 2
    lanes = half_of(width, lax.axis_index("ch") % 2)
    for ref, side in ((near_rim, 1 - odd), (far_rim, odd)):
        ref[:RIM, :] = x_ref[pl.ds(pl.multiple_of(side * (rows - RIM), RIM), RIM), lanes]
        ref[RIM:, :] = edge_ref[side, :, lanes]


def half_of(width, core):
    return pl.ds(pl.multiple_of(core * (width // 2), LANES), width // 2)


def put_sums(ref, value):
    for p, part in enumerate(split_three(value)):
        ref[p * 16 : (p + 1) * 16, :] = part.astype(BF16)


def get_sums(ref):
    return sum(ref[p * 16 : (p + 1) * 16, :].astype(F32) for p in range(3))


def act_kernel(
    x_ref, cot_hbm, one_ref, two_ref, norm_ref, hid_ref, slope_ref, vec_ref, cot_ref, sems, *, bin_count
):
    copy = pltpu.make_async_copy(cot_hbm, cot_ref, sems.at[0])
    copy.start()
    rows, width = x_ref.shape
    tiles = width // LANES
    total = get_sums(one_ref) + get_sums(two_ref)
    for k in range(tiles):
        lanes = slice(k * LANES, (k + 1) * LANES)
        mean = total[k : k + 1, :] / bin_count
        square = total[tiles + k : tiles + k + 1, :] / bin_count
        root = lax.rsqrt(square - mean * mean + NORM_EPS)
        gain = root * norm_ref[0:1, lanes]
        vec_ref[0:1, lanes] = root
        vec_ref[1:2, lanes] = -mean * root
        vec_ref[2:3, lanes] = gain
        vec_ref[3:4, lanes] = norm_ref[1:2, lanes] - mean * gain

    def step(k, carry):
        at = pl.multiple_of(k * 16, 16)
        v = x_ref[pl.ds(at, 16), :].astype(F32) * vec_ref[2:3, :] + vec_ref[3:4, :]
        hidden, slope = gelu_and_slope(v)
        hid_ref[pl.ds(at, 16), :] = hidden.astype(BF16)
        slope_ref[pl.ds(at, 16), :] = slope
        return carry

    lax.fori_loop(0, rows // 16, step, 0, unroll=2)
    copy.wait()


def place(pieces, relatives, stack, own, slim):
    depth = stack.shape[1]
    at = 0
    for piece in pieces:
        for k in range(piece.shape[0]):
            block = piece[k].astype(F32)
            for j in range(KERNEL_WIDTH):
                part = block[:, j * LANES : (j + 1) * LANES]
                if folds(depth, slim):
                    part = unfold_rows(part, slim)
                stack[own ^ relatives[at], :, j * LANES : (j + 1) * LANES] = part.astype(stack.dtype)
            at += 1
    return stack[...].reshape(-1, stack.shape[2]).astype(BF16)


def place_kernel(*refs, relatives, slim):
    pieces, (out_ref, stack) = refs[:-2], refs[-2:]
    wide = stack.shape[2]
    for r, piece in enumerate(pieces):
        block = place([piece], relatives, stack, lax.axis_index("seq"), slim)
        out_ref[:, r * wide : (r + 1) * wide] = block


def rim_kernel(near_ref, far_ref, out_ref):
    height, width = far_ref.shape
    base = near_ref.shape[0] - width // LANES * height
    for k in range(width // LANES):
        at = base + k * height
        out_ref[:height, k * LANES : (k + 1) * LANES] = near_ref[at : at + height, :]
    out_ref[height : 2 * height, :] = far_ref[...]
    out_ref[2 * height :, :] = jnp.zeros_like(out_ref[2 * height :, :])


def mask_kernel(start_ref, rim_ref, ahead_ref, back_ref, far_ref):
    far_ref[...] = rim_ref[...]
    rows = back_ref.shape[1]
    first = lax.axis_index("seq") * rows
    for j, shift in enumerate(SHIFTS):
        for begin in range(0, rows + RIM, 96):
            count = min(96, rows + RIM - begin)
            mask = reach_of(first + begin - EDGE, count, shift, start_ref[0], rows * lax.axis_size("seq"))
            ahead_ref[j, begin : begin + count, :] = jnp.where(mask, 1.0, 0.0)
        for begin in range(0, rows, 128):
            back_ref[j, begin : begin + 128, :] = ahead_ref[
                j, EDGE + begin - shift : EDGE + begin - shift + 128, :
            ]


def conv_kernel(mask_ref, hid_ref, own_rims, other_rims, vec_ref, pack_ref, *refs, relatives, slim):
    pieces, refs = refs[:-8], refs[-8:]
    weight_ref, out_ref, sum_ref, rim_ref, all_ref, stack, prod, edge = refs
    at, packed = 0, pieces[0].shape[1]
    for piece in pieces:
        all_ref[at : at + piece.shape[0]] = piece[...]
        at += piece.shape[0]
    for k in range(pack_ref.shape[0] // packed):
        lanes = slice(k % KERNEL_WIDTH * LANES, (k % KERNEL_WIDTH + 1) * LANES)
        all_ref[at + k // KERNEL_WIDTH, :, lanes] = pack_ref[k * packed : (k + 1) * packed, :]
    odd, core = lax.axis_index("seq") % 2, lax.axis_index("ch") % 2
    height, width = rim_ref.shape[1:]
    for half, owner in ((own_rims, core), (other_rims, 1 - core)):
        rim_ref[1 - odd, :, half_of(width, owner)] = half[:height, :]
        rim_ref[odd, :, half_of(width, owner)] = half[height : 2 * height, :]
    for side in range(2):
        for k in range(0, RIM, 16):
            v = rim_ref[side, k : k + 16, :].astype(F32) * vec_ref[2:3, :] + vec_ref[3:4, :]
            edge[side * RIM + k : side * RIM + k + 16, :] = gelu_and_slope(v)[0].astype(BF16)
    rows = hid_ref.shape[0]
    weight_ref[...] = place(pieces, relatives, stack, lax.axis_index("seq"), slim)
    for at in range(0, weight_ref.shape[1], 256):
        part = slice(at, min(at + 256, weight_ref.shape[1]))
        prod[RIM : RIM + rows, part] = jnp.dot(
            hid_ref[...], weight_ref[:, part], preferred_element_type=F32
        )
        sides = jnp.dot(edge[...], weight_ref[:, part], preferred_element_type=F32)
        prod[:RIM, part] = sides[:RIM]
        prod[RIM + rows :, part] = sides[RIM:]

    def rows_of(begin, count):
        value = 0.0
        for j, shift in enumerate(SHIFTS):
            part = prod[begin + EDGE + shift : begin + EDGE + shift + count, j * LANES : (j + 1) * LANES]
            value = value + mask_ref[j, begin : begin + count, :] * part
        out_ref[begin : begin + count, :] = value
        return value

    rows_of(0, EDGE)
    rows_of(EDGE + rows, EDGE)
    one = two = jnp.zeros((8, LANES), F32)
    step = 128
    for k in range(rows // step):
        value = rows_of(EDGE + k * step, step).reshape(step // 8, 8, LANES)
        one = one + value.sum(0)
        two = two + (value * value).sum(0)
    one, two = jnp.sum(one, 0, keepdims=True), jnp.sum(two, 0, keepdims=True)
    for d in range(sum_ref.shape[0]):
        sum_ref[d, 0:1, :] = one
        sum_ref[d, 1:2, :] = two


def upstream_kernel(cot_ref, one_ref, two_ref, up_ref, point_ref, pack_ref, stack, *, relatives):
    rows = cot_ref.shape[0]
    depth = stack.shape[1]
    own = lax.axis_index("seq")
    count = len(relatives) // 2
    for k, relative in enumerate(relatives):
        piece = (one_ref, two_ref)[k // count]
        at = SUMS + (k % count) * up_to(depth, 16)
        stack[own ^ relative] = piece[at : at + depth, :].astype(stack.dtype)
    point_ref[...] = stack[...].reshape(point_ref.shape).astype(BF16)
    put_folded(point_ref[...], pack_ref)
    up_ref[...] = jnp.dot(cot_ref[...], point_ref[...], preferred_element_type=F32)


def mid_kernel(
    got_ref, conv_ref, up_ref, rim_ref, norm_ref, point_ref, hid_ref, d_ref, cen_ref, sent_ref, vec_ref, *, bin_count
):
    rows = hid_ref.shape[0]
    slim = norm_ref.shape[1]
    total = got_ref[0]
    for s in range(1, got_ref.shape[0]):
        total = total + got_ref[s]
    mean = total[0:1] / bin_count
    root = lax.rsqrt(total[1:2] / bin_count - mean * mean + NORM_EPS)
    vec_ref[...] = jnp.zeros_like(vec_ref)
    vec_ref[0:1, :] = root
    vec_ref[1:3, :slim] = norm_ref[...]
    gain, bias = vec_ref[1:2, :], vec_ref[2:3, :]

    def rows_of(begin, count, up):
        centered = (conv_ref[pl.ds(begin, count), :] - mean) * root
        hidden, slope = gelu_and_slope(centered * gain + bias)
        d = up * slope
        cen_ref[pl.ds(begin, count), :] = centered
        d_ref[pl.ds(begin, count), :] = d
        return centered, hidden, d

    for side, begin in enumerate((0, EDGE + rows)):
        up = jnp.dot(rim_ref[side, RIM:, :], point_ref[...], preferred_element_type=F32)
        rows_of(begin, EDGE, up)
    step = 64

    def body(i, carry):
        begin = pl.multiple_of(EDGE + i * step, 16)
        up = up_ref[pl.ds(pl.multiple_of(i * step, 16), step), :]
        centered, hidden, d = rows_of(begin, step, up)
        hid_ref[pl.ds(pl.multiple_of(i * step, 16), step), :] = hidden.astype(BF16)
        d = d.reshape(step // 8, 8, LANES)
        return carry[0] + (d * centered.reshape(d.shape)).sum(0), carry[1] + d.sum(0)

    zero = jnp.zeros((8, LANES), F32)
    gain_sum, bias_sum = lax.fori_loop(0, rows // step, body, (zero, zero), unroll=2)
    gain_sum = jnp.sum(gain_sum, 0, keepdims=True)
    bias_sum = jnp.sum(bias_sum, 0, keepdims=True)
    for d in range(sent_ref.shape[0]):
        sent_ref[d, 0:1, :] = gain_sum
        sent_ref[d, 1:2, :] = bias_sum


def conv_back_kernel(got_ref, vec_ref, d_ref, cen_ref, grad_ref, total_ref, grad, *, bin_count, slim):
    total = got_ref[0]
    for s in range(1, got_ref.shape[0]):
        total = total + got_ref[s]
    total_ref[...] = total
    scale = vec_ref[0:1, :] * vec_ref[1:2, :]
    pull, level = total[0:1] / bin_count, total[1:2] / bin_count
    count = d_ref.shape[0]
    for begin in range(0, count, 96):
        part = slice(begin, min(begin + 96, count))
        grad[part, :] = scale * (d_ref[part, :] - level - cen_ref[part, :] * pull)
    if folds(count, slim):
        grad_ref[...] = fold_rows(grad[:, :slim]).astype(BF16)
    else:
        grad_ref[...] = grad[...].astype(BF16)


def out_kernel(x_ref, *refs):
    parts, (out_ref, token_ref, hidden, point) = refs[:-4], refs[-4:]
    token_ref[...] = jnp.zeros_like(token_ref)
    rows = x_ref.shape[0]
    side = hidden.shape[1] // LANES // 2
    for r in range(2 * side):
        if r < side:
            part = parts[r][...]
        else:
            at = side + 3 * (r - side)
            part = jnp.concatenate([piece[...] for piece in parts[at : at + 3]], axis=0)
        width = point.shape[0]
        count = part.shape[0] * rows // (rows + width)
        hidden[:, r * LANES : (r + 1) * LANES] = get_folded(part[:count, :], rows)
        point[:, r * LANES : (r + 1) * LANES] = get_folded(part[count:, :], width)
    for at in range(0, x_ref.shape[1], 256):
        part = slice(at, at + 256)
        branch = lax.dot_general(
            hidden[...], point[part, :], LANE_DIMS, preferred_element_type=F32
        )
        out_ref[:, part] = (x_ref[:, part].astype(F32) + branch).astype(BF16)


def halve(blocks, kept_ref, sent_ref, high):
    for k in range(kept_ref.shape[0]):
        kept_ref[k] = blocks(2 * k + high)
        sent_ref[k] = blocks(2 * k + 1 - high).astype(BF16)


def bit_of(reach):
    return (lax.axis_index("seq") // reach) % 2


def terms_of(part, grad, term_ref, at, mask_ref):
    rows = term_ref.shape[0]
    step = 64
    count = part.shape[0]
    grad[:count, :] = part[...].astype(F32)
    if count < grad.shape[0]:
        quarter = count // 3
        width = LANES // 4
        side = [grad[p * quarter : (p + 1) * quarter, 3 * width :] for p in range(3)]
        grad[count:, :] = jnp.concatenate(side + [jnp.zeros((quarter, width), F32)], axis=1)
    for j, shift in enumerate(SHIFTS):
        lanes = slice(at + j * LANES, at + (j + 1) * LANES)
        for begin in range(0, rows, step):
            value = grad[EDGE + begin - shift : EDGE + begin - shift + step, :]
            value = value * mask_ref[j, begin : begin + step, :]
            term_ref[begin : begin + step, lanes] = value.astype(BF16)


def weight_grad_kernel(
    mask_ref, part_ref, hid_ref, cot_ref, mid_ref, point_ref, term_ref, kept_ref, sent_ref, pack_ref, both_ref, grad, full, *, depth, slim
):
    put_folded(mid_ref[...], pack_ref)
    both_ref[: pack_ref.shape[0], :] = pack_ref[...]
    both_ref[pack_ref.shape[0] :, :] = point_ref[...]

    rows = term_ref.shape[0]
    terms_of(part_ref, grad, term_ref, 0, mask_ref)
    taps = lax.dot_general(
        hid_ref[...], term_ref[...], ROW_DIMS, preferred_element_type=F32
    )
    point = lax.dot_general(cot_ref[...], mid_ref[...], ROW_DIMS, preferred_element_type=F32)
    parts = [taps[:, j * LANES : j * LANES + slim] for j in range(KERNEL_WIDTH)] + [point[:, :slim]]
    full[...] = jnp.concatenate(parts, axis=1)
    halve(
        lambda k: full[pl.ds(pl.multiple_of(k * depth, 8), depth), :], kept_ref, sent_ref, bit_of(1)
    )


def fold_kernel(old_ref, got_ref, kept_ref, sent_ref, *, reach):
    halve(lambda k: old_ref[k] + got_ref[k].astype(F32), kept_ref, sent_ref, bit_of(reach))


def adamw(weights_old, first_moment_state, second_mom, gradient, step_rate, decay_rate):
    first_next = BETA_ONE * first_moment_state + (1.0 - BETA_ONE) * gradient
    second_next = BETA_TWO * second_mom + (1.0 - BETA_TWO) * gradient * gradient
    corrected = (
        first_next
        / (1.0 - BETA_ONE**STEP)
        / (jnp.sqrt(second_next / (1.0 - BETA_TWO**STEP)) + ADAM_EPS)
    )
    weights_new = weights_old - step_rate * (corrected + decay_rate * weights_old)
    return (first_next, second_next, weights_new)


def first_half_kernel(mask_ref, own_ref, *refs):
    up_ref, term, weight, grad = refs[-4:]
    count = (len(refs) - 4 + 1) // 2
    grads, weights = refs[: count - 1], refs[count - 1 : -4]
    wide = KERNEL_WIDTH * LANES
    term[:, :wide] = own_ref[...]
    for r, part in enumerate(grads):
        terms_of(part, grad, term, (r + 1) * wide, mask_ref)
    for r, piece in enumerate(weights):
        weight[:, r * wide : (r + 1) * wide] = piece[...]
    for at in range(0, up_ref.shape[1], 256):
        part = slice(at, at + 256)
        up_ref[:, part] = lax.dot_general(
            term[...], weight[part, :], LANE_DIMS, preferred_element_type=F32
        )


def second_half_kernel(mask_ref, x_ref, slope_ref, vec_ref, part_ref, weight_ref, *refs):
    grads, (d_ref, sum_ref, term, grad) = refs[:-4], refs[-4:]
    rows, width = x_ref.shape
    wide = KERNEL_WIDTH * LANES
    for r, part in enumerate(grads):
        terms_of(part, grad, term, r * wide, mask_ref)
    for at in range(0, width, 256):
        part = slice(at, at + 256)
        up = lax.dot_general(term[...], weight_ref[part, :], LANE_DIMS, preferred_element_type=F32)
        d = (up + part_ref[:, part]) * slope_ref[:, part]
        d_ref[:, part] = d
        centered = x_ref[:, part].astype(F32) * vec_ref[0:1, part] + vec_ref[1:2, part]
        sum_ref[0:1, part] = jnp.sum(d * centered, 0, keepdims=True)
        sum_ref[1:2, part] = jnp.sum(d, 0, keepdims=True)


def final_kernel(
    x_ref, cot_ref, d_ref, vec_ref, one_ref, two_ref, old_ref, got_ref, mid_ref, *refs, bin_count, chunks
):
    states, outs, refs = refs[:12], refs[12:25], refs[25:]
    held, news, out_ref, sems = refs[:12], refs[12:24], refs[24], refs[25]
    fetches = [
        pltpu.make_async_copy(src, dst, sems.at[k]) for k, (src, dst) in enumerate(zip(states, held))
    ]
    for fetch in fetches:
        fetch.start()
    rows, width = x_ref.shape
    total = one_ref[...] + two_ref[...]
    root, offset, scale = vec_ref[0:1, :], vec_ref[1:2, :], vec_ref[2:3, :]
    pull = scale * total[0:1] / bin_count
    slant = pull * root
    level = scale * total[1:2] / bin_count + pull * offset
    step = 16
    chunk = rows // chunks

    def body(i, carry):
        at = pl.ds(pl.multiple_of(i * step, 16), step)
        value = x_ref[at, :].astype(F32) * slant + level
        out_ref[at, :] = cot_ref[at, :].astype(F32) + (d_ref[at, :] * scale - value)
        return carry

    sends = []
    for k in range(chunks):
        lax.fori_loop(k * chunk // step, (k + 1) * chunk // step, body, 0, unroll=4)
        part = pl.ds(k * chunk, chunk)
        sends.append(pltpu.make_async_copy(out_ref.at[part], outs[0].at[part], sems.at[24 + k]))
        sends[-1].start()
    for fetch in fetches:
        fetch.wait()

    def step_of(first, at, grad, rate, decay):
        new = adamw(*(ref[at] for ref in held[first : first + 3]), grad, rate, decay)
        for ref, value in zip(news[first : first + 3], new):
            ref[at] = value

    slim = held[3].shape[2]
    both = old_ref[0] + got_ref[0].astype(F32)
    step_of(0, ..., total, RATE_NORM, 0.0)
    for j in range(KERNEL_WIDTH):
        step_of(3, j, both[:, j * slim : (j + 1) * slim], RATE_WEIGHT, DECAY_WEIGHT)
    step_of(6, ..., both[:, KERNEL_WIDTH * slim :].T, RATE_WEIGHT, DECAY_WEIGHT)
    step_of(9, ..., mid_ref[:, :slim], RATE_NORM, 0.0)
    for k in range(12):
        sends.append(pltpu.make_async_copy(news[k], outs[1 + k], sems.at[12 + k]))
        sends[-1].start()
    for send in sends:
        send.wait()


def flip(axis, reach):
    return [(i, i ^ reach) for i in range(lax.axis_size(axis))]


def relatives_of(order):
    found = [0]
    for reach in order:
        found = found + [r ^ reach for r in found]
    return found


def descending(size):
    return [size >> k for k in range(1, size.bit_length())]


def round_kernel(weight_one, weight_two, one_ref, two_ref, *refs, size, sides):
    rims, (weight_ref, out_ref), halves = refs[: len(refs) - 2 - sides], refs[-2 - sides :][:2], refs[len(refs) - sides :]
    count = weight_one.shape[0]
    weight_ref[:count] = weight_one[...]
    weight_ref[count:] = weight_two[...]
    for half, src in zip(halves, (weight_one, weight_two)):
        half[...] = src[...]
    put_sums(out_ref, get_sums(one_ref) + get_sums(two_ref))
    out_ref[SUMS : SUMS + size, :] = one_ref[SUMS : SUMS + size, :]
    out_ref[SUMS + size : SUMS + 2 * size, :] = two_ref[SUMS : SUMS + size, :]
    for rim in rims:
        height, width = rim.shape
        for k in range(width // LANES):
            at = SUMS + 2 * size + k * height
            out_ref[at : at + height, :] = rim[:, k * LANES : (k + 1) * LANES]


def copy_kernel(*refs):
    count = len(refs) // 2
    for src, out in zip(refs[:count], refs[count:]):
        out[...] = src[...]


def packs(wanted, after):
    arrays, places = [], []
    for pieces in wanted:
        places.append([])
        for piece in pieces:
            array, begin, end = piece if isinstance(piece, tuple) else (piece, 0, piece.shape[0])
            places[-1].append((len(arrays), begin, end))
            arrays.append(array)

    def pack_kernel(*refs):
        for out, group in zip(refs[len(arrays) :], places):
            at = 0
            for index, begin, end in group:
                out[at : at + end - begin, :] = refs[index][begin:end, :]
                at += end - begin

    sizes = [sum(end - begin for _, begin, end in group) for group in places]
    return call(pack_kernel, [((size, LANES), BF16) for size in sizes], arrays, after=after)


def take_kernel(src_ref, weight_ref, pack_ref):
    count, packed = weight_ref.shape[:2]
    weight_ref[...] = src_ref[:count]
    for k in range(pack_ref.shape[0] // packed):
        lanes = slice(k % KERNEL_WIDTH * LANES, (k % KERNEL_WIDTH + 1) * LANES)
        pack_ref[k * packed : (k + 1) * packed, :] = src_ref[count + k // KERNEL_WIDTH, :, lanes]


def copies(arrays, after):
    return call(copy_kernel, [(x.shape, x.dtype) for x in arrays], arrays, after=after)


def add_kernel(one_ref, two_ref, out_ref):
    out_ref[...] = one_ref[...] + two_ref[...]


def add(one, two, after=()):
    return call(add_kernel, [(one.shape, one.dtype)], [one, two], after=after)[0]


def swap(x, axis, reach):
    return lax.ppermute(x, axis, flip(axis, reach))


def gather_parts(x, reaches):
    parts = [x]
    for reach in reaches:
        parts += [swap(part, "ch", reach) for part in parts]
    return parts


def spread(copies, axes):
    return lax.all_to_all(copies, axes, 0, 0, tiled=True)


def shards(
    inputs,
    cotangent,
    starts,
    master_conv,
    first_conv,
    second_conv,
    master_point,
    first_point,
    second_point,
    norm_in,
    first_in,
    second_in,
    norm_mid,
    first_mid,
    second_mid,
):
    rows, width = inputs.shape
    seq_size, ch_size = lax.axis_size("seq"), lax.axis_size("ch")
    bin_count = rows * seq_size
    depth, slim = master_conv.shape[1:]
    tiles = width // LANES
    wide = KERNEL_WIDTH * LANES
    weight_order = descending(seq_size)
    sum_order = weight_order[::-1]
    last_order = weight_order[:1] + sum_order[:-1]
    point_order = weight_order[:1] + [1] + weight_order[1:-1]
    ch_order = descending(ch_size)
    ext = rows + 2 * EDGE

    rounds = len(weight_order)
    top, lower = ch_order[0], ch_order[1:]
    chunks = 4
    rim = (RIM + EDGE, width // 2)
    packed = 3 * depth // 4 if folds(depth, slim) else depth
    inputs, weight, near, *rims = call(
        first_kernel,
        [
            (inputs.shape, BF16),
            ((1, packed, wide), BF16),
            ((SUMS + up_to(depth, 16), LANES), BF16),
            (rim, BF16),
            (rim, BF16),
        ],
        [inputs, cotangent, master_conv, master_point],
        scratch=[
            ((2, EDGE, width), BF16),
            (master_conv.shape, F32),
            (master_point.shape, F32),
            ((16, LANES), F32),
        ],
        away=(0, 1, 2, 3),
        sems=4 + chunks,
    )
    pairs = [(i, i + 1) for i in range(1, seq_size - 1, 2)]
    parts = [weight]
    for k in range(rounds):
        weight_got = [swap(part, "seq", weight_order[k]) for part in parts]
        near_got = swap(near, "seq", point_order[k])
        if k < rounds - 1:
            size = up_to(depth, 16) << k
            spare = {0: tiles // 2 * rim[0], rounds - 2: 16}.get(k, 0)
            outs = [((2 * weight.shape[0], packed, wide), BF16), ((SUMS + 2 * size + spare, LANES), BF16)]
            sides = 2 if k == rounds - 2 else 0
            outs += [(weight.shape, BF16)] * sides
            join = functools.partial(round_kernel, size=size, sides=sides)
            args = [weight, weight_got[0], near, near_got]
            if k == 0:
                weight, near = call(join, outs, args + [rims[0]])
                ahead, back, far = call(
                    mask_kernel,
                    [((KERNEL_WIDTH, ext, LANES), F32), ((KERNEL_WIDTH, rows, LANES), F32), (rim, BF16)],
                    [starts, rims[1]],
                    smem=(0,),
                    after=[near],
                )
                far = lax.ppermute(far, "seq", pairs + [(j, i) for i, j in pairs])
                parts = [weight]
            else:
                if k == 1:
                    (rims,) = call(
                        rim_kernel, [((2 * rim[0] + 16, rim[1]), BF16)], [near_got, far], after=[back]
                    )
                    other_rims = swap(rims, "ch", 1)
                weight, near, *parts = call(join, outs, args, after=[back] if k == 1 else [])
                parts = parts or [weight]
    hidden_in, slope_in, vec_in, cotangent = call(
        functools.partial(act_kernel, bin_count=bin_count),
        [((rows, width), BF16), ((rows, width), F32), ((8, width), F32), (cotangent.shape, BF16)],
        [inputs, cotangent, near, near_got, norm_in],
        away=(1,),
        sems=1,
    )
    stack_type = BF16 if depth % 16 == 0 else F32
    upstream, point_own, point_pack = call(
        functools.partial(upstream_kernel, relatives=relatives_of(point_order)),
        [((rows, LANES), F32), ((width, LANES), BF16), ((folded_rows(width, slim), LANES), BF16)],
        [cotangent, near, near_got],
        scratch=[((seq_size, depth, LANES), stack_type)],
    )
    blocks = -(-point_pack.shape[0] // (packed * KERNEL_WIDTH))
    conv_own, conv_out, sums_mid, rims, weight = call(
        functools.partial(
            conv_kernel, relatives=relatives_of(weight_order), slim=slim
        ),
        [
            ((width, wide), BF16),
            ((ext, LANES), F32),
            ((seq_size, 2, LANES), F32),
            ((2, RIM + EDGE, width), BF16),
            ((seq_size + blocks, packed, wide), BF16),
        ],
        [ahead, hidden_in, rims, other_rims, vec_in, point_pack, weight, *weight_got],
        scratch=[
            ((seq_size, depth, wide), stack_type),
            ((rows + 2 * RIM, wide), F32),
            ((2 * RIM, width), BF16),
        ],
        after=[upstream],
    )
    weight = swap(weight, "ch", top)
    got_mid = spread(sums_mid, "seq")
    conv_near = gather_parts(conv_own, lower)
    hidden_mid, d_mid, centered, sent_back, vec_mid = call(
        functools.partial(mid_kernel, bin_count=bin_count),
        [
            ((rows, LANES), BF16),
            ((ext, LANES), F32),
            ((ext, LANES), F32),
            ((seq_size, 2, LANES), F32),
            ((8, LANES), F32),
        ],
        [got_mid, conv_out, upstream, rims, norm_mid, point_own],
        after=conv_near[1:],
    )
    got_back = spread(sent_back, "seq")
    grad_own, total_mid = call(
        functools.partial(conv_back_kernel, bin_count=bin_count, slim=slim),
        [((3 * ext // 4 if folds(ext, slim) else ext, LANES), BF16), ((2, LANES), F32)],
        [got_back, vec_mid, d_mid, centered],
        scratch=[((ext, LANES), F32)],
    )
    grad_near = gather_parts(grad_own, lower)
    grad_far = swap(grad_own, "ch", top)
    weight, point_far = call(
        take_kernel,
        [((seq_size, packed, wide), BF16), (point_pack.shape, BF16)],
        [weight],
        after=[grad_own],
    )
    side = ch_size // 2 * wide
    (conv_far,) = call(
        functools.partial(place_kernel, relatives=relatives_of(weight_order), slim=slim),
        [((width, side), BF16)],
        gather_parts(weight, lower),
        scratch=[((seq_size, depth, wide), stack_type)],
    )
    half = seq_size // 2
    hidden_rows = folded_rows(rows, slim)
    terms, kept, sent, hidden_pack, both = call(
        functools.partial(weight_grad_kernel, depth=depth, slim=slim),
        [
            ((rows, wide), BF16),
            ((half, depth, 4 * slim), F32),
            ((half, depth, 4 * slim), BF16),
            ((hidden_rows, LANES), BF16),
            ((hidden_rows + point_pack.shape[0], LANES), BF16),
        ],
        [back, grad_own, hidden_in, cotangent, hidden_mid, point_pack],
        scratch=[((ext, LANES), F32), ((width, 4 * slim), F32)],
    )
    (up_part,) = call(
        first_half_kernel,
        [((rows, width), F32)],
        [back, terms, *grad_near[1:], *conv_near],
        scratch=[((rows, side), BF16), ((width, side), BF16), ((ext, LANES), F32)],
    )
    grad_far = gather_parts(copies([grad_far], [up_part, conv_far])[0], lower)
    both_parts = gather_parts(both, lower)
    d_in, sums_back = call(
        second_half_kernel,
        [((rows, width), F32), ((2, width), F32)],
        [back, inputs, slope_in, vec_in, up_part, conv_far, *grad_far],
        scratch=[((rows, side), BF16), ((ext, LANES), F32)],
        after=both_parts[1:],
    )
    total_back = sums_back
    hidden_far = swap(hidden_pack, "ch", top)
    count = point_far.shape[0]
    cuts = [0, up_to(13 * count // 100, 16), up_to(52 * count // 100, 16), count]
    for k, reach in enumerate(sum_order):
        total_got = swap(total_back, "seq", last_order[k])
        got = swap(sent, "seq", reach)
        if k < rounds - 1:
            half //= 2
            kept, sent = call(
                functools.partial(fold_kernel, reach=2 * reach),
                [((half, depth, 4 * slim), F32), ((half, depth, 4 * slim), BF16)],
                [kept, got],
                after=[total_back] if k else [],
            )
            total_back = add(total_back, total_got)
        if k == rounds - 3:
            wanted = [[hidden_far, (point_far, *cuts[:2])], [(point_far, *cuts[1:3])]]
            far_parts = [gather_parts(x, lower) for x in packs(wanted, [total_back])]
        if k == rounds - 2:
            (last,) = packs([[(point_far, *cuts[2:])]], [total_back])
            far_parts.append(gather_parts(last, lower))
    both_parts += [part for group in zip(*far_parts) for part in group]
    block_out, token = call(
        out_kernel,
        [((rows, width), BF16), ((8, LANES), F32)],
        [inputs, *both_parts],
        scratch=[((rows, ch_size * LANES), BF16), ((width, ch_size * LANES), BF16)],
        after=[total_back],
    )
    states = [norm_in, first_in, second_in, master_conv, first_conv, second_conv]
    states += [master_point, first_point, second_point, norm_mid, first_mid, second_mid]
    arrays = [inputs, cotangent, d_in, vec_in, total_back, total_got, kept, got, total_mid]
    small = [(x.shape, F32) for x in states]
    input_grad, *news = call(
        functools.partial(final_kernel, bin_count=bin_count, chunks=8),
        [((rows, width), F32)] + small,
        arrays + states,
        scratch=small + small + [((rows, width), F32)],
        away=range(len(arrays), len(arrays) + 12),
        away_outs=range(13),
        sems=24 + 8,
        after=[token],
    )
    return (block_out, input_grad, *news[3:9], *news[:3], *news[9:])


def solution(mesh):
    in_specs = (
        P("seq", None),
        P("seq", None),
        P(),
        P(None, "seq", "ch"),
        P(None, "seq", "ch"),
        P(None, "seq", "ch"),
        P("ch", "seq"),
        P("ch", "seq"),
        P("ch", "seq"),
        P(),
        P(),
        P(),
        P(None, "ch"),
        P(None, "ch"),
        P(None, "ch"),
    )
    out_specs = (
        P("seq", None),
        P("seq", None),
        P(None, "seq", "ch"),
        P(None, "seq", "ch"),
        P(None, "seq", "ch"),
        P("ch", "seq"),
        P("ch", "seq"),
        P("ch", "seq"),
        P(),
        P(),
        P(),
        P(None, "ch"),
        P(None, "ch"),
        P(None, "ch"),
    )
    return jax.shard_map(shards, mesh=mesh, in_specs=in_specs, out_specs=out_specs, check_vma=False)
```

```python
import functools

import jax
import jax.numpy as jnp
from jax import lax
from jax.experimental import pallas as pl
from jax.experimental.pallas import tpu as pltpu
from jax.sharding import PartitionSpec as P

KERNEL_WIDTH = 3
DILATION_BINS = 9
WIN = 1024
STEP = 10

NORM_EPS = 1e-05
ADAM_EPS = 1e-08
BETA_ONE = 0.9
BETA_TWO = 0.999
RATE_WEIGHT = 0.05
RATE_NORM = 0.5
DECAY_WEIGHT = 0.01

LANES = 128
EDGE = 16
RIM = 2 * EDGE
SUMS = 48
GELU_A = 0.7978845608028654
GELU_B = 0.044715
SHIFTS = [(j - KERNEL_WIDTH // 2) * DILATION_BINS for j in range(KERNEL_WIDTH)]
ROW_DIMS = (((0,), (0,)), ((), ()))
LANE_DIMS = (((1,), (1,)), ((), ()))
F32, BF16 = jnp.float32, jnp.bfloat16


def call(body, outs, args, scratch=(), smem=(), away=(), after=(), sems=0, away_outs=(), limit=16):
    spaces = [pltpu.SMEM if k in smem else pltpu.VMEM for k in range(len(args))]
    spaces = [pltpu.HBM if k in away else space for k, space in enumerate(spaces)]
    spaces += [pl.ANY] * len(after)

    args = [
        pltpu.with_memory_space_constraint(x, pltpu.HBM) if k in away else x
        for k, x in enumerate(args)
    ]

    def kernel(*refs):
        body(*refs[: len(args)], *refs[len(spaces) :])

    return pl.pallas_call(
        kernel,
        out_shape=[jax.ShapeDtypeStruct(s, t) for s, t in outs],
        in_specs=[pl.BlockSpec(memory_space=s) for s in spaces],
        out_specs=[
            pl.BlockSpec(memory_space=pltpu.HBM if k in away_outs else pltpu.VMEM)
            for k in range(len(outs))
        ],
        scratch_shapes=[pltpu.VMEM(s, t) for s, t in scratch]
        + [pltpu.SemaphoreType.DMA((sems,))] * (sems > 0),
        compiler_params=pltpu.CompilerParams(vmem_limit_bytes=limit * 2**20),
        cost_estimate=pl.CostEstimate(flops=1, bytes_accessed=1, transcendentals=0),
        name=getattr(body, "func", body).__name__,
    )(*args, *after)


def up_to(size, step):
    return -(-size // step) * step


def split_three(v):
    high = v.astype(BF16).astype(F32)
    rest = v - high
    middle = rest.astype(BF16).astype(F32)
    return high, middle, rest - middle


def gelu_and_slope(v):
    square = v * v
    t = jnp.tanh(v * (GELU_A + (GELU_A * GELU_B) * square))
    half = 0.5 * (1.0 + t)
    slope = half + (0.5 * v) * (1.0 - t * t) * (GELU_A + (3.0 * GELU_A * GELU_B) * square)
    return v * half, slope


def reach_of(first, count, shift, start, bin_count):
    here = first + lax.broadcasted_iota(jnp.int32, (count, LANES), 0)
    there = here + shift
    inside = (here >= 0) & (here < bin_count) & (there >= 0) & (there < bin_count)
    return inside & (((here - start) >> 10) == ((there - start) >> 10))


def folds(depth, slim):
    return 3 * (LANES - slim) == slim and depth % 32 == 0


def fold_rows(block):
    rows, slim = block.shape
    quarter, width = rows // 4, LANES - slim
    side = [block[3 * quarter :, p * width : (p + 1) * width] for p in range(3)]
    return jnp.concatenate([block[: 3 * quarter], jnp.concatenate(side, axis=0)], axis=1)


def unfold_rows(block, slim):
    quarter, width = block.shape[0] // 3, LANES - slim
    side = [block[p * quarter : (p + 1) * quarter, slim:] for p in range(3)]
    side.append(jnp.zeros((quarter, width), block.dtype))
    lane = lax.broadcasted_iota(jnp.int32, block.shape, 1)
    return jnp.concatenate([jnp.where(lane < slim, block, 0.0), jnp.concatenate(side, axis=1)], axis=0)


def folded_rows(rows, slim):
    return 3 * rows // 4 if folds(rows, slim) else rows


def put_folded(block, out_ref):
    if out_ref.shape[0] < block.shape[0]:
        block = fold_rows(block[:, : 3 * LANES // 4].astype(F32)).astype(BF16)
    out_ref[...] = block


def get_folded(block, rows):
    if block.shape[0] < rows:
        block = unfold_rows(block.astype(F32), 3 * LANES // 4).astype(BF16)
    return block


def first_kernel(
    x_hbm, cot_hbm, conv_hbm, point_hbm, x_ref, weight_ref, near_ref, near_rim, far_rim, edge_ref, conv_ref, point_ref, sum_ref, sems
):
    rows, width = x_ref.shape
    tiles = width // LANES
    depth, slim = conv_ref.shape[1:]
    chunks = sems.shape[0] - 4
    chunk = rows // chunks
    copies = [
        pltpu.make_async_copy(conv_hbm, conv_ref, sems.at[0]),
        pltpu.make_async_copy(point_hbm, point_ref, sems.at[1]),
        pltpu.make_async_copy(cot_hbm.at[pl.ds(0, EDGE)], edge_ref.at[0], sems.at[2]),
        pltpu.make_async_copy(cot_hbm.at[pl.ds(rows - EDGE, EDGE)], edge_ref.at[1], sems.at[3]),
    ]
    for k in range(chunks):
        part = pl.ds(k * chunk, chunk)
        copies.append(pltpu.make_async_copy(x_hbm.at[part], x_ref.at[part], sems.at[4 + k]))
    for copy in copies:
        copy.start()
    weight_ref[...] = jnp.zeros_like(weight_ref)
    near_ref[...] = jnp.zeros_like(near_ref)
    sum_ref[...] = jnp.zeros_like(sum_ref)
    copies[0].wait()
    for j in range(KERNEL_WIDTH):
        if folds(depth, slim):
            weight_ref[0, :, j * LANES : (j + 1) * LANES] = fold_rows(conv_ref[j]).astype(BF16)
        else:
            weight_ref[0, :, j * LANES : j * LANES + slim] = conv_ref[j].astype(BF16)
    copies[1].wait()
    near_ref[SUMS : SUMS + depth, :slim] = point_ref[...].T.astype(BF16)

    def step(k, carry):
        v = x_ref[pl.ds(pl.multiple_of(k * 32, 32), 32), :].astype(F32)
        v = v.reshape(4, 8, width)
        return carry[0] + v.sum(0), carry[1] + (v * v).sum(0)

    totals = (jnp.zeros((8, width), F32),) * 2
    for k in range(chunks):
        copies[4 + k].wait()
        totals = lax.fori_loop(
            k * chunk // 32, (k + 1) * chunk // 32, step, totals, unroll=chunk // 32
        )
    for stat, total in enumerate(totals):
        total = jnp.sum(total, 0, keepdims=True)
        for k in range(tiles):
            row = stat * tiles + k
            sum_ref[row : row + 1, :] = total[:, k * LANES : (k + 1) * LANES]
    put_sums(near_ref, sum_ref[...])
    copies[2].wait()
    copies[3].wait()
    odd = lax.axis_index("seq") % 2
    lanes = half_of(width, lax.axis_index("ch") % 2)
    for ref, side in ((near_rim, 1 - odd), (far_rim, odd)):
        ref[:RIM, :] = x_ref[pl.ds(pl.multiple_of(side * (rows - RIM), RIM), RIM), lanes]
        ref[RIM:, :] = edge_ref[side, :, lanes]


def half_of(width, core):
    return pl.ds(pl.multiple_of(core * (width // 2), LANES), width // 2)


def put_sums(ref, value):
    for p, part in enumerate(split_three(value)):
        ref[p * 16 : (p + 1) * 16, :] = part.astype(BF16)


def get_sums(ref):
    return sum(ref[p * 16 : (p + 1) * 16, :].astype(F32) for p in range(3))


def act_kernel(
    x_ref, cot_hbm, one_ref, two_ref, norm_ref, hid_ref, slope_ref, vec_ref, cot_ref, sems, *, bin_count
):
    copy = pltpu.make_async_copy(cot_hbm, cot_ref, sems.at[0])
    copy.start()
    rows, width = x_ref.shape
    tiles = width // LANES
    total = get_sums(one_ref) + get_sums(two_ref)
    for k in range(tiles):
        lanes = slice(k * LANES, (k + 1) * LANES)
        mean = total[k : k + 1, :] / bin_count
        square = total[tiles + k : tiles + k + 1, :] / bin_count
        root = lax.rsqrt(square - mean * mean + NORM_EPS)
        gain = root * norm_ref[0:1, lanes]
        vec_ref[0:1, lanes] = root
        vec_ref[1:2, lanes] = -mean * root
        vec_ref[2:3, lanes] = gain
        vec_ref[3:4, lanes] = norm_ref[1:2, lanes] - mean * gain

    def step(k, carry):
        at = pl.multiple_of(k * 16, 16)
        v = x_ref[pl.ds(at, 16), :].astype(F32) * vec_ref[2:3, :] + vec_ref[3:4, :]
        hidden, slope = gelu_and_slope(v)
        hid_ref[pl.ds(at, 16), :] = hidden.astype(BF16)
        slope_ref[pl.ds(at, 16), :] = slope
        return carry

    lax.fori_loop(0, rows // 16, step, 0, unroll=2)
    copy.wait()


def place(pieces, relatives, stack, own, slim):
    depth = stack.shape[1]
    at = 0
    for piece in pieces:
        for k in range(piece.shape[0]):
            block = piece[k].astype(F32)
            for j in range(KERNEL_WIDTH):
                part = block[:, j * LANES : (j + 1) * LANES]
                if folds(depth, slim):
                    part = unfold_rows(part, slim)
                stack[own ^ relatives[at], :, j * LANES : (j + 1) * LANES] = part.astype(stack.dtype)
            at += 1
    return stack[...].reshape(-1, stack.shape[2]).astype(BF16)


def place_kernel(*refs, relatives, slim):
    pieces, (out_ref, stack) = refs[:-2], refs[-2:]
    wide = stack.shape[2]
    for r, piece in enumerate(pieces):
        block = place([piece], relatives, stack, lax.axis_index("seq"), slim)
        out_ref[:, r * wide : (r + 1) * wide] = block


def rim_kernel(near_ref, far_ref, out_ref):
    height, width = far_ref.shape
    base = near_ref.shape[0] - width // LANES * height
    for k in range(width // LANES):
        at = base + k * height
        out_ref[:height, k * LANES : (k + 1) * LANES] = near_ref[at : at + height, :]
    out_ref[height : 2 * height, :] = far_ref[...]
    out_ref[2 * height :, :] = jnp.zeros_like(out_ref[2 * height :, :])


def mask_kernel(start_ref, ahead_ref, back_ref):
    rows = back_ref.shape[1]
    first = lax.axis_index("seq") * rows
    for j, shift in enumerate(SHIFTS):
        for begin in range(0, rows + RIM, 96):
            count = min(96, rows + RIM - begin)
            mask = reach_of(first + begin - EDGE, count, shift, start_ref[0], rows * lax.axis_size("seq"))
            ahead_ref[j, begin : begin + count, :] = jnp.where(mask, 1.0, 0.0)
        for begin in range(0, rows, 128):
            back_ref[j, begin : begin + 128, :] = ahead_ref[
                j, EDGE + begin - shift : EDGE + begin - shift + 128, :
            ]


def conv_kernel(mask_ref, hid_ref, own_rims, other_rims, vec_ref, pack_ref, *refs, relatives, slim):
    pieces, refs = refs[:-8], refs[-8:]
    weight_ref, out_ref, sum_ref, rim_ref, all_ref, stack, prod, edge = refs
    at, packed = 0, pieces[0].shape[1]
    for piece in pieces:
        all_ref[at : at + piece.shape[0]] = piece[...]
        at += piece.shape[0]
    for k in range(pack_ref.shape[0] // packed):
        lanes = slice(k % KERNEL_WIDTH * LANES, (k % KERNEL_WIDTH + 1) * LANES)
        all_ref[at + k // KERNEL_WIDTH, :, lanes] = pack_ref[k * packed : (k + 1) * packed, :]
    odd, core = lax.axis_index("seq") % 2, lax.axis_index("ch") % 2
    height, width = rim_ref.shape[1:]
    for half, owner in ((own_rims, core), (other_rims, 1 - core)):
        rim_ref[1 - odd, :, half_of(width, owner)] = half[:height, :]
        rim_ref[odd, :, half_of(width, owner)] = half[height : 2 * height, :]
    for side in range(2):
        for k in range(0, RIM, 16):
            v = rim_ref[side, k : k + 16, :].astype(F32) * vec_ref[2:3, :] + vec_ref[3:4, :]
            edge[side * RIM + k : side * RIM + k + 16, :] = gelu_and_slope(v)[0].astype(BF16)
    rows = hid_ref.shape[0]
    weight_ref[...] = place(pieces, relatives, stack, lax.axis_index("seq"), slim)
    for at in range(0, weight_ref.shape[1], 256):
        part = slice(at, min(at + 256, weight_ref.shape[1]))
        prod[RIM : RIM + rows, part] = jnp.dot(
            hid_ref[...], weight_ref[:, part], preferred_element_type=F32
        )
        sides = jnp.dot(edge[...], weight_ref[:, part], preferred_element_type=F32)
        prod[:RIM, part] = sides[:RIM]
        prod[RIM + rows :, part] = sides[RIM:]

    def rows_of(begin, count):
        value = 0.0
        for j, shift in enumerate(SHIFTS):
            part = prod[begin + EDGE + shift : begin + EDGE + shift + count, j * LANES : (j + 1) * LANES]
            value = value + mask_ref[j, begin : begin + count, :] * part
        out_ref[begin : begin + count, :] = value
        return value

    rows_of(0, EDGE)
    rows_of(EDGE + rows, EDGE)
    one = two = jnp.zeros((8, LANES), F32)
    step = 128
    for k in range(rows // step):
        value = rows_of(EDGE + k * step, step).reshape(step // 8, 8, LANES)
        one = one + value.sum(0)
        two = two + (value * value).sum(0)
    one, two = jnp.sum(one, 0, keepdims=True), jnp.sum(two, 0, keepdims=True)
    for d in range(sum_ref.shape[0]):
        sum_ref[d, 0:1, :] = one
        sum_ref[d, 1:2, :] = two


def upstream_kernel(cot_ref, one_ref, two_ref, up_ref, point_ref, pack_ref, stack, *, relatives):
    rows = cot_ref.shape[0]
    depth = stack.shape[1]
    own = lax.axis_index("seq")
    count = len(relatives) // 2
    for k, relative in enumerate(relatives):
        piece = (one_ref, two_ref)[k // count]
        at = SUMS + (k % count) * up_to(depth, 16)
        stack[own ^ relative] = piece[at : at + depth, :].astype(stack.dtype)
    point_ref[...] = stack[...].reshape(point_ref.shape).astype(BF16)
    put_folded(point_ref[...], pack_ref)
    up_ref[...] = jnp.dot(cot_ref[...], point_ref[...], preferred_element_type=F32)


def mid_kernel(
    got_ref, conv_ref, up_ref, rim_ref, norm_ref, point_ref, hid_ref, d_ref, cen_ref, sent_ref, vec_ref, *, bin_count
):
    rows = hid_ref.shape[0]
    slim = norm_ref.shape[1]
    total = got_ref[0]
    for s in range(1, got_ref.shape[0]):
        total = total + got_ref[s]
    mean = total[0:1] / bin_count
    root = lax.rsqrt(total[1:2] / bin_count - mean * mean + NORM_EPS)
    vec_ref[...] = jnp.zeros_like(vec_ref)
    vec_ref[0:1, :] = root
    vec_ref[1:3, :slim] = norm_ref[...]
    gain, bias = vec_ref[1:2, :], vec_ref[2:3, :]

    def rows_of(begin, count, up):
        centered = (conv_ref[pl.ds(begin, count), :] - mean) * root
        hidden, slope = gelu_and_slope(centered * gain + bias)
        d = up * slope
        cen_ref[pl.ds(begin, count), :] = centered
        d_ref[pl.ds(begin, count), :] = d
        return centered, hidden, d

    for side, begin in enumerate((0, EDGE + rows)):
        up = jnp.dot(rim_ref[side, RIM:, :], point_ref[...], preferred_element_type=F32)
        rows_of(begin, EDGE, up)
    step = 64

    def body(i, carry):
        begin = pl.multiple_of(EDGE + i * step, 16)
        up = up_ref[pl.ds(pl.multiple_of(i * step, 16), step), :]
        centered, hidden, d = rows_of(begin, step, up)
        hid_ref[pl.ds(pl.multiple_of(i * step, 16), step), :] = hidden.astype(BF16)
        d = d.reshape(step // 8, 8, LANES)
        return carry[0] + (d * centered.reshape(d.shape)).sum(0), carry[1] + d.sum(0)

    zero = jnp.zeros((8, LANES), F32)
    gain_sum, bias_sum = lax.fori_loop(0, rows // step, body, (zero, zero), unroll=2)
    gain_sum = jnp.sum(gain_sum, 0, keepdims=True)
    bias_sum = jnp.sum(bias_sum, 0, keepdims=True)
    for d in range(sent_ref.shape[0]):
        sent_ref[d, 0:1, :] = gain_sum
        sent_ref[d, 1:2, :] = bias_sum


def conv_back_kernel(got_ref, vec_ref, d_ref, cen_ref, grad_ref, total_ref, grad, *, bin_count, slim):
    total = got_ref[0]
    for s in range(1, got_ref.shape[0]):
        total = total + got_ref[s]
    total_ref[...] = total
    scale = vec_ref[0:1, :] * vec_ref[1:2, :]
    pull, level = total[0:1] / bin_count, total[1:2] / bin_count
    count = d_ref.shape[0]
    for begin in range(0, count, 96):
        part = slice(begin, min(begin + 96, count))
        grad[part, :] = scale * (d_ref[part, :] - level - cen_ref[part, :] * pull)
    if folds(count, slim):
        grad_ref[...] = fold_rows(grad[:, :slim]).astype(BF16)
    else:
        grad_ref[...] = grad[...].astype(BF16)


def out_kernel(x_ref, *refs):
    parts, (out_ref, token_ref, hidden, point) = refs[:-4], refs[-4:]
    token_ref[...] = jnp.zeros_like(token_ref)
    rows = x_ref.shape[0]
    side = hidden.shape[1] // LANES // 2
    for r in range(2 * side):
        if r < side:
            part = parts[r][...]
        else:
            at = side + 3 * (r - side)
            part = jnp.concatenate([piece[...] for piece in parts[at : at + 3]], axis=0)
        width = point.shape[0]
        count = part.shape[0] * rows // (rows + width)
        hidden[:, r * LANES : (r + 1) * LANES] = get_folded(part[:count, :], rows)
        point[:, r * LANES : (r + 1) * LANES] = get_folded(part[count:, :], width)
    for at in range(0, x_ref.shape[1], 256):
        part = slice(at, at + 256)
        branch = lax.dot_general(
            hidden[...], point[part, :], LANE_DIMS, preferred_element_type=F32
        )
        out_ref[:, part] = (x_ref[:, part].astype(F32) + branch).astype(BF16)


def halve(blocks, kept_ref, sent_ref, high):
    for k in range(kept_ref.shape[0]):
        kept_ref[k] = blocks(2 * k + high)
        sent_ref[k] = blocks(2 * k + 1 - high).astype(BF16)


def bit_of(reach):
    return (lax.axis_index("seq") // reach) % 2


def terms_of(part, grad, term_ref, at, mask_ref):
    rows = term_ref.shape[0]
    step = 64
    count = part.shape[0]
    grad[:count, :] = part[...].astype(F32)
    if count < grad.shape[0]:
        quarter = count // 3
        width = LANES // 4
        side = [grad[p * quarter : (p + 1) * quarter, 3 * width :] for p in range(3)]
        grad[count:, :] = jnp.concatenate(side + [jnp.zeros((quarter, width), F32)], axis=1)
    for j, shift in enumerate(SHIFTS):
        lanes = slice(at + j * LANES, at + (j + 1) * LANES)
        for begin in range(0, rows, step):
            value = grad[EDGE + begin - shift : EDGE + begin - shift + step, :]
            value = value * mask_ref[j, begin : begin + step, :]
            term_ref[begin : begin + step, lanes] = value.astype(BF16)


def weight_grad_kernel(
    mask_ref, part_ref, hid_ref, cot_ref, mid_ref, point_ref, term_ref, kept_ref, sent_ref, pack_ref, both_ref, grad, full, *, depth, slim
):
    put_folded(mid_ref[...], pack_ref)
    both_ref[: pack_ref.shape[0], :] = pack_ref[...]
    both_ref[pack_ref.shape[0] :, :] = point_ref[...]

    rows = term_ref.shape[0]
    terms_of(part_ref, grad, term_ref, 0, mask_ref)
    taps = lax.dot_general(
        hid_ref[...], term_ref[...], ROW_DIMS, preferred_element_type=F32
    )
    point = lax.dot_general(cot_ref[...], mid_ref[...], ROW_DIMS, preferred_element_type=F32)
    parts = [taps[:, j * LANES : j * LANES + slim] for j in range(KERNEL_WIDTH)] + [point[:, :slim]]
    full[...] = jnp.concatenate(parts, axis=1)
    halve(
        lambda k: full[pl.ds(pl.multiple_of(k * depth, 8), depth), :], kept_ref, sent_ref, bit_of(1)
    )


def fold_kernel(old_ref, got_ref, kept_ref, sent_ref, *, reach):
    halve(lambda k: old_ref[k] + got_ref[k].astype(F32), kept_ref, sent_ref, bit_of(reach))


def adamw(weights_old, first_moment_state, second_mom, gradient, step_rate, decay_rate):
    first_next = BETA_ONE * first_moment_state + (1.0 - BETA_ONE) * gradient
    second_next = BETA_TWO * second_mom + (1.0 - BETA_TWO) * gradient * gradient
    corrected = (
        first_next
        / (1.0 - BETA_ONE**STEP)
        / (jnp.sqrt(second_next / (1.0 - BETA_TWO**STEP)) + ADAM_EPS)
    )
    weights_new = weights_old - step_rate * (corrected + decay_rate * weights_old)
    return (first_next, second_next, weights_new)


def first_half_kernel(mask_ref, own_ref, *refs):
    up_ref, term, weight, grad = refs[-4:]
    count = (len(refs) - 4 + 1) // 2
    grads, weights = refs[: count - 1], refs[count - 1 : -4]
    wide = KERNEL_WIDTH * LANES
    term[:, :wide] = own_ref[...]
    for r, part in enumerate(grads):
        terms_of(part, grad, term, (r + 1) * wide, mask_ref)
    for r, piece in enumerate(weights):
        weight[:, r * wide : (r + 1) * wide] = piece[...]
    for at in range(0, up_ref.shape[1], 256):
        part = slice(at, at + 256)
        up_ref[:, part] = lax.dot_general(
            term[...], weight[part, :], LANE_DIMS, preferred_element_type=F32
        )


def second_half_kernel(mask_ref, x_ref, slope_ref, vec_ref, part_ref, weight_ref, *refs):
    grads, (d_ref, sum_ref, term, grad) = refs[:-4], refs[-4:]
    rows, width = x_ref.shape
    wide = KERNEL_WIDTH * LANES
    for r, part in enumerate(grads):
        terms_of(part, grad, term, r * wide, mask_ref)
    for at in range(0, width, 256):
        part = slice(at, at + 256)
        up = lax.dot_general(term[...], weight_ref[part, :], LANE_DIMS, preferred_element_type=F32)
        d = (up + part_ref[:, part]) * slope_ref[:, part]
        d_ref[:, part] = d
        centered = x_ref[:, part].astype(F32) * vec_ref[0:1, part] + vec_ref[1:2, part]
        sum_ref[0:1, part] = jnp.sum(d * centered, 0, keepdims=True)
        sum_ref[1:2, part] = jnp.sum(d, 0, keepdims=True)


def final_kernel(
    x_ref, cot_ref, d_ref, vec_ref, one_ref, two_ref, old_ref, got_ref, mid_ref, *refs, bin_count, chunks
):
    states, outs, refs = refs[:12], refs[12:25], refs[25:]
    held, news, out_ref, sems = refs[:12], refs[12:24], refs[24], refs[25]
    fetches = [
        pltpu.make_async_copy(src, dst, sems.at[k]) for k, (src, dst) in enumerate(zip(states, held))
    ]
    for fetch in fetches:
        fetch.start()
    rows, width = x_ref.shape
    total = one_ref[...] + two_ref[...]
    root, offset, scale = vec_ref[0:1, :], vec_ref[1:2, :], vec_ref[2:3, :]
    pull = scale * total[0:1] / bin_count
    slant = pull * root
    level = scale * total[1:2] / bin_count + pull * offset
    step = 16
    chunk = rows // chunks

    def body(i, carry):
        at = pl.ds(pl.multiple_of(i * step, 16), step)
        value = x_ref[at, :].astype(F32) * slant + level
        out_ref[at, :] = cot_ref[at, :].astype(F32) + (d_ref[at, :] * scale - value)
        return carry

    sends = []
    for k in range(chunks):
        lax.fori_loop(k * chunk // step, (k + 1) * chunk // step, body, 0, unroll=4)
        part = pl.ds(k * chunk, chunk)
        sends.append(pltpu.make_async_copy(out_ref.at[part], outs[0].at[part], sems.at[24 + k]))
        sends[-1].start()
    for fetch in fetches:
        fetch.wait()

    def step_of(first, at, grad, rate, decay):
        new = adamw(*(ref[at] for ref in held[first : first + 3]), grad, rate, decay)
        for ref, value in zip(news[first : first + 3], new):
            ref[at] = value

    slim = held[3].shape[2]
    both = old_ref[0] + got_ref[0].astype(F32)
    step_of(0, ..., total, RATE_NORM, 0.0)
    for j in range(KERNEL_WIDTH):
        step_of(3, j, both[:, j * slim : (j + 1) * slim], RATE_WEIGHT, DECAY_WEIGHT)
    step_of(6, ..., both[:, KERNEL_WIDTH * slim :].T, RATE_WEIGHT, DECAY_WEIGHT)
    step_of(9, ..., mid_ref[:, :slim], RATE_NORM, 0.0)
    for k in range(12):
        sends.append(pltpu.make_async_copy(news[k], outs[1 + k], sems.at[12 + k]))
        sends[-1].start()
    for send in sends:
        send.wait()


def flip(axis, reach):
    return [(i, i ^ reach) for i in range(lax.axis_size(axis))]


def relatives_of(order):
    found = [0]
    for reach in order:
        found = found + [r ^ reach for r in found]
    return found


def descending(size):
    return [size >> k for k in range(1, size.bit_length())]


def round_kernel(weight_one, weight_two, one_ref, two_ref, *refs, size, sides):
    count = (len(refs) - 2 - sides) // 3
    rims, outs = refs[: 2 * count], refs[2 * count :]
    weight_ref, out_ref, halves = outs[0], outs[1], outs[2 : 2 + sides]
    if rims:
        outs[-1][...] = rims[1][...]
    count = weight_one.shape[0]
    weight_ref[:count] = weight_one[...]
    weight_ref[count:] = weight_two[...]
    for half, src in zip(halves, (weight_one, weight_two)):
        half[...] = src[...]
    put_sums(out_ref, get_sums(one_ref) + get_sums(two_ref))
    out_ref[SUMS : SUMS + size, :] = one_ref[SUMS : SUMS + size, :]
    out_ref[SUMS + size : SUMS + 2 * size, :] = two_ref[SUMS : SUMS + size, :]
    for rim in rims[:1]:
        height, width = rim.shape
        for k in range(width // LANES):
            at = SUMS + 2 * size + k * height
            out_ref[at : at + height, :] = rim[:, k * LANES : (k + 1) * LANES]


def copy_kernel(*refs):
    count = len(refs) // 2
    for src, out in zip(refs[:count], refs[count:]):
        out[...] = src[...]


def packs(wanted, after):
    arrays, places = [], []
    for pieces in wanted:
        places.append([])
        for piece in pieces:
            array, begin, end = piece if isinstance(piece, tuple) else (piece, 0, piece.shape[0])
            places[-1].append((len(arrays), begin, end))
            arrays.append(array)

    def pack_kernel(*refs):
        for out, group in zip(refs[len(arrays) :], places):
            at = 0
            for index, begin, end in group:
                out[at : at + end - begin, :] = refs[index][begin:end, :]
                at += end - begin

    sizes = [sum(end - begin for _, begin, end in group) for group in places]
    return call(pack_kernel, [((size, LANES), BF16) for size in sizes], arrays, after=after)


def take_kernel(src_ref, weight_ref, pack_ref):
    count, packed = weight_ref.shape[:2]
    weight_ref[...] = src_ref[:count]
    for k in range(pack_ref.shape[0] // packed):
        lanes = slice(k % KERNEL_WIDTH * LANES, (k % KERNEL_WIDTH + 1) * LANES)
        pack_ref[k * packed : (k + 1) * packed, :] = src_ref[count + k // KERNEL_WIDTH, :, lanes]


def copies(arrays, after):
    return call(copy_kernel, [(x.shape, x.dtype) for x in arrays], arrays, after=after)


def add_kernel(one_ref, two_ref, out_ref):
    out_ref[...] = one_ref[...] + two_ref[...]


def add(one, two, after=()):
    return call(add_kernel, [(one.shape, one.dtype)], [one, two], after=after)[0]


def swap(x, axis, reach):
    return lax.ppermute(x, axis, flip(axis, reach))


def gather_parts(x, reaches):
    parts = [x]
    for reach in reaches:
        parts += [swap(part, "ch", reach) for part in parts]
    return parts


def spread(copies, axes):
    return lax.all_to_all(copies, axes, 0, 0, tiled=True)


def shards(
    inputs,
    cotangent,
    starts,
    master_conv,
    first_conv,
    second_conv,
    master_point,
    first_point,
    second_point,
    norm_in,
    first_in,
    second_in,
    norm_mid,
    first_mid,
    second_mid,
):
    rows, width = inputs.shape
    seq_size, ch_size = lax.axis_size("seq"), lax.axis_size("ch")
    bin_count = rows * seq_size
    depth, slim = master_conv.shape[1:]
    tiles = width // LANES
    wide = KERNEL_WIDTH * LANES
    weight_order = descending(seq_size)
    sum_order = weight_order[::-1]
    last_order = weight_order[:1] + sum_order[:-1]
    point_order = weight_order[:1] + [1] + weight_order[1:-1]
    ch_order = descending(ch_size)
    ext = rows + 2 * EDGE

    rounds = len(weight_order)
    top, lower = ch_order[0], ch_order[1:]
    chunks = 4
    rim = (RIM + EDGE, width // 2)
    packed = 3 * depth // 4 if folds(depth, slim) else depth
    inputs, weight, near, *rims = call(
        first_kernel,
        [
            (inputs.shape, BF16),
            ((1, packed, wide), BF16),
            ((SUMS + up_to(depth, 16), LANES), BF16),
            (rim, BF16),
            (rim, BF16),
        ],
        [inputs, cotangent, master_conv, master_point],
        scratch=[
            ((2, EDGE, width), BF16),
            (master_conv.shape, F32),
            (master_point.shape, F32),
            ((16, LANES), F32),
        ],
        away=(0, 1, 2, 3),
        sems=4 + chunks,
    )
    pairs = [(i, i + 1) for i in range(1, seq_size - 1, 2)]
    ahead, back = call(
        mask_kernel,
        [((KERNEL_WIDTH, ext, LANES), F32), ((KERNEL_WIDTH, rows, LANES), F32)],
        [starts],
        smem=(0,),
        after=[weight],
    )
    parts = [weight]
    for k in range(rounds):
        weight_got = [swap(part, "seq", weight_order[k]) for part in parts]
        near_got = swap(near, "seq", point_order[k])
        if k < rounds - 1:
            size = up_to(depth, 16) << k
            spare = {0: tiles // 2 * rim[0], rounds - 2: 16}.get(k, 0)
            outs = [((2 * weight.shape[0], packed, wide), BF16), ((SUMS + 2 * size + spare, LANES), BF16)]
            sides = 2 if k == rounds - 2 else 0
            outs += [(weight.shape, BF16)] * sides
            join = functools.partial(round_kernel, size=size, sides=sides)
            args = [weight, weight_got[0], near, near_got]
            if k == 0:
                weight, near, far = call(join, outs + [(rim, BF16)], args + rims, after=[back])
                far = lax.ppermute(far, "seq", pairs + [(j, i) for i, j in pairs])
                parts = [weight]
            else:
                if k == 1:
                    (rims,) = call(
                        rim_kernel, [((2 * rim[0] + 16, rim[1]), BF16)], [near_got, far]
                    )
                    other_rims = swap(rims, "ch", 1)
                weight, near, *parts = call(join, outs, args)
                parts = parts or [weight]
    hidden_in, slope_in, vec_in, cotangent = call(
        functools.partial(act_kernel, bin_count=bin_count),
        [((rows, width), BF16), ((rows, width), F32), ((8, width), F32), (cotangent.shape, BF16)],
        [inputs, cotangent, near, near_got, norm_in],
        away=(1,),
        sems=1,
    )
    stack_type = BF16 if depth % 16 == 0 else F32
    upstream, point_own, point_pack = call(
        functools.partial(upstream_kernel, relatives=relatives_of(point_order)),
        [((rows, LANES), F32), ((width, LANES), BF16), ((folded_rows(width, slim), LANES), BF16)],
        [cotangent, near, near_got],
        scratch=[((seq_size, depth, LANES), stack_type)],
    )
    blocks = -(-point_pack.shape[0] // (packed * KERNEL_WIDTH))
    conv_own, conv_out, sums_mid, rims, weight = call(
        functools.partial(
            conv_kernel, relatives=relatives_of(weight_order), slim=slim
        ),
        [
            ((width, wide), BF16),
            ((ext, LANES), F32),
            ((seq_size, 2, LANES), F32),
            ((2, RIM + EDGE, width), BF16),
            ((seq_size + blocks, packed, wide), BF16),
        ],
        [ahead, hidden_in, rims, other_rims, vec_in, point_pack, weight, *weight_got],
        scratch=[
            ((seq_size, depth, wide), stack_type),
            ((rows + 2 * RIM, wide), F32),
            ((2 * RIM, width), BF16),
        ],
        after=[upstream],
    )
    weight = swap(weight, "ch", top)
    got_mid = spread(sums_mid, "seq")
    conv_near = gather_parts(conv_own, lower)
    hidden_mid, d_mid, centered, sent_back, vec_mid = call(
        functools.partial(mid_kernel, bin_count=bin_count),
        [
            ((rows, LANES), BF16),
            ((ext, LANES), F32),
            ((ext, LANES), F32),
            ((seq_size, 2, LANES), F32),
            ((8, LANES), F32),
        ],
        [got_mid, conv_out, upstream, rims, norm_mid, point_own],
        after=conv_near[1:],
    )
    got_back = spread(sent_back, "seq")
    grad_own, total_mid = call(
        functools.partial(conv_back_kernel, bin_count=bin_count, slim=slim),
        [((3 * ext // 4 if folds(ext, slim) else ext, LANES), BF16), ((2, LANES), F32)],
        [got_back, vec_mid, d_mid, centered],
        scratch=[((ext, LANES), F32)],
    )
    grad_near = gather_parts(grad_own, lower)
    grad_far = swap(grad_own, "ch", top)
    weight, point_far = call(
        take_kernel,
        [((seq_size, packed, wide), BF16), (point_pack.shape, BF16)],
        [weight],
        after=[grad_own],
    )
    side = ch_size // 2 * wide
    (conv_far,) = call(
        functools.partial(place_kernel, relatives=relatives_of(weight_order), slim=slim),
        [((width, side), BF16)],
        gather_parts(weight, lower),
        scratch=[((seq_size, depth, wide), stack_type)],
    )
    half = seq_size // 2
    hidden_rows = folded_rows(rows, slim)
    terms, kept, sent, hidden_pack, both = call(
        functools.partial(weight_grad_kernel, depth=depth, slim=slim),
        [
            ((rows, wide), BF16),
            ((half, depth, 4 * slim), F32),
            ((half, depth, 4 * slim), BF16),
            ((hidden_rows, LANES), BF16),
            ((hidden_rows + point_pack.shape[0], LANES), BF16),
        ],
        [back, grad_own, hidden_in, cotangent, hidden_mid, point_pack],
        scratch=[((ext, LANES), F32), ((width, 4 * slim), F32)],
    )
    (up_part,) = call(
        first_half_kernel,
        [((rows, width), F32)],
        [back, terms, *grad_near[1:], *conv_near],
        scratch=[((rows, side), BF16), ((width, side), BF16), ((ext, LANES), F32)],
    )
    grad_far = gather_parts(copies([grad_far], [up_part, conv_far])[0], lower)
    both_parts = gather_parts(both, lower)
    d_in, sums_back = call(
        second_half_kernel,
        [((rows, width), F32), ((2, width), F32)],
        [back, inputs, slope_in, vec_in, up_part, conv_far, *grad_far],
        scratch=[((rows, side), BF16), ((ext, LANES), F32)],
        after=both_parts[1:],
    )
    total_back = sums_back
    hidden_far = swap(hidden_pack, "ch", top)
    count = point_far.shape[0]
    cuts = [0, up_to(13 * count // 100, 16), up_to(52 * count // 100, 16), count]
    for k, reach in enumerate(sum_order):
        total_got = swap(total_back, "seq", last_order[k])
        got = swap(sent, "seq", reach)
        if k < rounds - 1:
            half //= 2
            kept, sent = call(
                functools.partial(fold_kernel, reach=2 * reach),
                [((half, depth, 4 * slim), F32), ((half, depth, 4 * slim), BF16)],
                [kept, got],
                after=[total_back] if k else [],
            )
            total_back = add(total_back, total_got)
        if k == rounds - 3:
            wanted = [[hidden_far, (point_far, *cuts[:2])], [(point_far, *cuts[1:3])]]
            far_parts = [gather_parts(x, lower) for x in packs(wanted, [total_back])]
        if k == rounds - 2:
            (last,) = packs([[(point_far, *cuts[2:])]], [total_back])
            far_parts.append(gather_parts(last, lower))
    both_parts += [part for group in zip(*far_parts) for part in group]
    block_out, token = call(
        out_kernel,
        [((rows, width), BF16), ((8, LANES), F32)],
        [inputs, *both_parts],
        scratch=[((rows, ch_size * LANES), BF16), ((width, ch_size * LANES), BF16)],
        after=[total_back],
    )
    states = [norm_in, first_in, second_in, master_conv, first_conv, second_conv]
    states += [master_point, first_point, second_point, norm_mid, first_mid, second_mid]
    arrays = [inputs, cotangent, d_in, vec_in, total_back, total_got, kept, got, total_mid]
    small = [(x.shape, F32) for x in states]
    input_grad, *news = call(
        functools.partial(final_kernel, bin_count=bin_count, chunks=8),
        [((rows, width), F32)] + small,
        arrays + states,
        scratch=small + small + [((rows, width), F32)],
        away=range(len(arrays), len(arrays) + 12),
        away_outs=range(13),
        sems=24 + 8,
        after=[token],
    )
    return (block_out, input_grad, *news[3:9], *news[:3], *news[9:])


def solution(mesh):
    in_specs = (
        P("seq", None),
        P("seq", None),
        P(),
        P(None, "seq", "ch"),
        P(None, "seq", "ch"),
        P(None, "seq", "ch"),
        P("ch", "seq"),
        P("ch", "seq"),
        P("ch", "seq"),
        P(),
        P(),
        P(),
        P(None, "ch"),
        P(None, "ch"),
        P(None, "ch"),
    )
    out_specs = (
        P("seq", None),
        P("seq", None),
        P(None, "seq", "ch"),
        P(None, "seq", "ch"),
        P(None, "seq", "ch"),
        P("ch", "seq"),
        P("ch", "seq"),
        P("ch", "seq"),
        P(),
        P(),
        P(),
        P(None, "ch"),
        P(None, "ch"),
        P(None, "ch"),
    )
    return jax.shard_map(shards, mesh=mesh, in_specs=in_specs, out_specs=out_specs, check_vma=False)
```

```python
import functools

import jax
import jax.numpy as jnp
from jax import lax
from jax.experimental import pallas as pl
from jax.experimental.pallas import tpu as pltpu
from jax.sharding import PartitionSpec as P

KERNEL_WIDTH = 3
DILATION_BINS = 9
WIN = 1024
STEP = 10

NORM_EPS = 1e-05
ADAM_EPS = 1e-08
BETA_ONE = 0.9
BETA_TWO = 0.999
RATE_WEIGHT = 0.05
RATE_NORM = 0.5
DECAY_WEIGHT = 0.01

LANES = 128
EDGE = 16
RIM = 2 * EDGE
SUMS = 48
GELU_A = 0.7978845608028654
GELU_B = 0.044715
SHIFTS = [(j - KERNEL_WIDTH // 2) * DILATION_BINS for j in range(KERNEL_WIDTH)]
ROW_DIMS = (((0,), (0,)), ((), ()))
LANE_DIMS = (((1,), (1,)), ((), ()))
F32, BF16 = jnp.float32, jnp.bfloat16


def call(body, outs, args, scratch=(), smem=(), away=(), after=(), sems=0, away_outs=(), limit=16):
    spaces = [pltpu.SMEM if k in smem else pltpu.VMEM for k in range(len(args))]
    spaces = [pltpu.HBM if k in away else space for k, space in enumerate(spaces)]
    spaces += [pl.ANY] * len(after)

    args = [
        pltpu.with_memory_space_constraint(x, pltpu.HBM) if k in away else x
        for k, x in enumerate(args)
    ]

    def kernel(*refs):
        body(*refs[: len(args)], *refs[len(spaces) :])

    return pl.pallas_call(
        kernel,
        out_shape=[jax.ShapeDtypeStruct(s, t) for s, t in outs],
        in_specs=[pl.BlockSpec(memory_space=s) for s in spaces],
        out_specs=[
            pl.BlockSpec(memory_space=pltpu.HBM if k in away_outs else pltpu.VMEM)
            for k in range(len(outs))
        ],
        scratch_shapes=[pltpu.VMEM(s, t) for s, t in scratch]
        + [pltpu.SemaphoreType.DMA((sems,))] * (sems > 0),
        compiler_params=pltpu.CompilerParams(vmem_limit_bytes=limit * 2**20),
        cost_estimate=pl.CostEstimate(flops=1, bytes_accessed=1, transcendentals=0),
        name=getattr(body, "func", body).__name__,
    )(*args, *after)


def up_to(size, step):
    return -(-size // step) * step


def split_three(v):
    high = v.astype(BF16).astype(F32)
    rest = v - high
    middle = rest.astype(BF16).astype(F32)
    return high, middle, rest - middle


def gelu_and_slope(v):
    square = v * v
    t = jnp.tanh(v * (GELU_A + (GELU_A * GELU_B) * square))
    half = 0.5 * (1.0 + t)
    slope = half + (0.5 * v) * (1.0 - t * t) * (GELU_A + (3.0 * GELU_A * GELU_B) * square)
    return v * half, slope


def reach_of(first, count, shift, start, bin_count):
    here = first + lax.broadcasted_iota(jnp.int32, (count, LANES), 0)
    there = here + shift
    inside = (here >= 0) & (here < bin_count) & (there >= 0) & (there < bin_count)
    return inside & (((here - start) >> 10) == ((there - start) >> 10))


def folds(depth, slim):
    return 3 * (LANES - slim) == slim and depth % 32 == 0


def fold_rows(block):
    rows, slim = block.shape
    quarter, width = rows // 4, LANES - slim
    side = [block[3 * quarter :, p * width : (p + 1) * width] for p in range(3)]
    return jnp.concatenate([block[: 3 * quarter], jnp.concatenate(side, axis=0)], axis=1)


def unfold_rows(block, slim):
    quarter, width = block.shape[0] // 3, LANES - slim
    side = [block[p * quarter : (p + 1) * quarter, slim:] for p in range(3)]
    side.append(jnp.zeros((quarter, width), block.dtype))
    lane = lax.broadcasted_iota(jnp.int32, block.shape, 1)
    return jnp.concatenate([jnp.where(lane < slim, block, 0.0), jnp.concatenate(side, axis=1)], axis=0)


def folded_rows(rows, slim):
    return 3 * rows // 4 if folds(rows, slim) else rows


def put_folded(block, out_ref):
    if out_ref.shape[0] < block.shape[0]:
        block = fold_rows(block[:, : 3 * LANES // 4].astype(F32)).astype(BF16)
    out_ref[...] = block


def get_folded(block, rows):
    if block.shape[0] < rows:
        block = unfold_rows(block.astype(F32), 3 * LANES // 4).astype(BF16)
    return block


def first_kernel(
    x_hbm, cot_hbm, conv_hbm, point_hbm, x_ref, weight_ref, near_ref, near_rim, far_rim, edge_ref, conv_ref, point_ref, sum_ref, sems
):
    rows, width = x_ref.shape
    tiles = width // LANES
    depth, slim = conv_ref.shape[1:]
    chunks = sems.shape[0] - 4
    chunk = rows // chunks
    copies = [
        pltpu.make_async_copy(conv_hbm, conv_ref, sems.at[0]),
        pltpu.make_async_copy(point_hbm, point_ref, sems.at[1]),
        pltpu.make_async_copy(cot_hbm.at[pl.ds(0, EDGE)], edge_ref.at[0], sems.at[2]),
        pltpu.make_async_copy(cot_hbm.at[pl.ds(rows - EDGE, EDGE)], edge_ref.at[1], sems.at[3]),
    ]
    for k in range(chunks):
        part = pl.ds(k * chunk, chunk)
        copies.append(pltpu.make_async_copy(x_hbm.at[part], x_ref.at[part], sems.at[4 + k]))
    for copy in copies:
        copy.start()
    weight_ref[...] = jnp.zeros_like(weight_ref)
    near_ref[...] = jnp.zeros_like(near_ref)
    sum_ref[...] = jnp.zeros_like(sum_ref)
    copies[0].wait()
    for j in range(KERNEL_WIDTH):
        if folds(depth, slim):
            weight_ref[0, :, j * LANES : (j + 1) * LANES] = fold_rows(conv_ref[j]).astype(BF16)
        else:
            weight_ref[0, :, j * LANES : j * LANES + slim] = conv_ref[j].astype(BF16)
    copies[1].wait()
    near_ref[SUMS : SUMS + depth, :slim] = point_ref[...].T.astype(BF16)

    def step(k, carry):
        v = x_ref[pl.ds(pl.multiple_of(k * 32, 32), 32), :].astype(F32)
        v = v.reshape(4, 8, width)
        return carry[0] + v.sum(0), carry[1] + (v * v).sum(0)

    totals = (jnp.zeros((8, width), F32),) * 2
    for k in range(chunks):
        copies[4 + k].wait()
        totals = lax.fori_loop(
            k * chunk // 32, (k + 1) * chunk // 32, step, totals, unroll=chunk // 32
        )
    for stat, total in enumerate(totals):
        total = jnp.sum(total, 0, keepdims=True)
        for k in range(tiles):
            row = stat * tiles + k
            sum_ref[row : row + 1, :] = total[:, k * LANES : (k + 1) * LANES]
    put_sums(near_ref, sum_ref[...])
    copies[2].wait()
    copies[3].wait()
    odd = lax.axis_index("seq") % 2
    lanes = half_of(width, lax.axis_index("ch") % 2)
    for ref, side in ((near_rim, 1 - odd), (far_rim, odd)):
        ref[:RIM, :] = x_ref[pl.ds(pl.multiple_of(side * (rows - RIM), RIM), RIM), lanes]
        ref[RIM:, :] = edge_ref[side, :, lanes]


def half_of(width, core):
    return pl.ds(pl.multiple_of(core * (width // 2), LANES), width // 2)


def put_sums(ref, value):
    for p, part in enumerate(split_three(value)):
        ref[p * 16 : (p + 1) * 16, :] = part.astype(BF16)


def get_sums(ref):
    return sum(ref[p * 16 : (p + 1) * 16, :].astype(F32) for p in range(3))


def act_kernel(
    x_ref, cot_hbm, one_ref, two_ref, norm_ref, hid_ref, slope_ref, vec_ref, cot_ref, sems, *, bin_count
):
    copy = pltpu.make_async_copy(cot_hbm, cot_ref, sems.at[0])
    copy.start()
    rows, width = x_ref.shape
    tiles = width // LANES
    total = get_sums(one_ref) + get_sums(two_ref)
    for k in range(tiles):
        lanes = slice(k * LANES, (k + 1) * LANES)
        mean = total[k : k + 1, :] / bin_count
        square = total[tiles + k : tiles + k + 1, :] / bin_count
        root = lax.rsqrt(square - mean * mean + NORM_EPS)
        gain = root * norm_ref[0:1, lanes]
        vec_ref[0:1, lanes] = root
        vec_ref[1:2, lanes] = -mean * root
        vec_ref[2:3, lanes] = gain
        vec_ref[3:4, lanes] = norm_ref[1:2, lanes] - mean * gain

    def step(k, carry):
        at = pl.multiple_of(k * 16, 16)
        v = x_ref[pl.ds(at, 16), :].astype(F32) * vec_ref[2:3, :] + vec_ref[3:4, :]
        hidden, slope = gelu_and_slope(v)
        hid_ref[pl.ds(at, 16), :] = hidden.astype(BF16)
        slope_ref[pl.ds(at, 16), :] = slope
        return carry

    lax.fori_loop(0, rows // 16, step, 0, unroll=2)
    copy.wait()


def place(pieces, relatives, stack, own, slim):
    depth = stack.shape[1]
    at = 0
    for piece in pieces:
        for k in range(piece.shape[0]):
            block = piece[k].astype(F32)
            for j in range(KERNEL_WIDTH):
                part = block[:, j * LANES : (j + 1) * LANES]
                if folds(depth, slim):
                    part = unfold_rows(part, slim)
                stack[own ^ relatives[at], :, j * LANES : (j + 1) * LANES] = part.astype(stack.dtype)
            at += 1
    return stack[...].reshape(-1, stack.shape[2]).astype(BF16)


def place_kernel(*refs, relatives, slim):
    pieces, (out_ref, stack) = refs[:-2], refs[-2:]
    wide = stack.shape[2]
    for r, piece in enumerate(pieces):
        block = place([piece], relatives, stack, lax.axis_index("seq"), slim)
        out_ref[:, r * wide : (r + 1) * wide] = block


def rim_kernel(near_ref, far_ref, out_ref):
    height, width = far_ref.shape
    base = near_ref.shape[0] - width // LANES * height
    for k in range(width // LANES):
        at = base + k * height
        out_ref[:height, k * LANES : (k + 1) * LANES] = near_ref[at : at + height, :]
    out_ref[height : 2 * height, :] = far_ref[...]
    out_ref[2 * height :, :] = jnp.zeros_like(out_ref[2 * height :, :])


def mask_kernel(start_ref, ahead_ref, back_ref):
    rows = back_ref.shape[1]
    first = lax.axis_index("seq") * rows
    for j, shift in enumerate(SHIFTS):
        for begin in range(0, rows + RIM, 96):
            count = min(96, rows + RIM - begin)
            mask = reach_of(first + begin - EDGE, count, shift, start_ref[0], rows * lax.axis_size("seq"))
            ahead_ref[j, begin : begin + count, :] = jnp.where(mask, 1.0, 0.0)
        for begin in range(0, rows, 128):
            back_ref[j, begin : begin + 128, :] = ahead_ref[
                j, EDGE + begin - shift : EDGE + begin - shift + 128, :
            ]


def conv_kernel(mask_ref, hid_ref, own_rims, other_rims, vec_ref, pack_ref, *refs, relatives, slim):
    pieces, refs = refs[:-8], refs[-8:]
    weight_ref, out_ref, sum_ref, rim_ref, all_ref, stack, prod, edge = refs
    at, packed = 0, pieces[0].shape[1]
    for piece in pieces:
        all_ref[at : at + piece.shape[0]] = piece[...]
        at += piece.shape[0]
    for k in range(pack_ref.shape[0] // packed):
        lanes = slice(k % KERNEL_WIDTH * LANES, (k % KERNEL_WIDTH + 1) * LANES)
        all_ref[at + k // KERNEL_WIDTH, :, lanes] = pack_ref[k * packed : (k + 1) * packed, :]
    odd, core = lax.axis_index("seq") % 2, lax.axis_index("ch") % 2
    height, width = rim_ref.shape[1:]
    for half, owner in ((own_rims, core), (other_rims, 1 - core)):
        rim_ref[1 - odd, :, half_of(width, owner)] = half[:height, :]
        rim_ref[odd, :, half_of(width, owner)] = half[height : 2 * height, :]
    for side in range(2):
        for k in range(0, RIM, 16):
            v = rim_ref[side, k : k + 16, :].astype(F32) * vec_ref[2:3, :] + vec_ref[3:4, :]
            edge[side * RIM + k : side * RIM + k + 16, :] = gelu_and_slope(v)[0].astype(BF16)
    rows = hid_ref.shape[0]
    weight_ref[...] = place(pieces, relatives, stack, lax.axis_index("seq"), slim)
    for at in range(0, weight_ref.shape[1], 256):
        part = slice(at, min(at + 256, weight_ref.shape[1]))
        prod[RIM : RIM + rows, part] = jnp.dot(
            hid_ref[...], weight_ref[:, part], preferred_element_type=F32
        )
        sides = jnp.dot(edge[...], weight_ref[:, part], preferred_element_type=F32)
        prod[:RIM, part] = sides[:RIM]
        prod[RIM + rows :, part] = sides[RIM:]

    def rows_of(begin, count):
        value = 0.0
        for j, shift in enumerate(SHIFTS):
            part = prod[begin + EDGE + shift : begin + EDGE + shift + count, j * LANES : (j + 1) * LANES]
            value = value + mask_ref[j, begin : begin + count, :] * part
        out_ref[begin : begin + count, :] = value
        return value

    rows_of(0, EDGE)
    rows_of(EDGE + rows, EDGE)
    one = two = jnp.zeros((8, LANES), F32)
    step = 128
    for k in range(rows // step):
        value = rows_of(EDGE + k * step, step).reshape(step // 8, 8, LANES)
        one = one + value.sum(0)
        two = two + (value * value).sum(0)
    one, two = jnp.sum(one, 0, keepdims=True), jnp.sum(two, 0, keepdims=True)
    for d in range(sum_ref.shape[0]):
        sum_ref[d, 0:1, :] = one
        sum_ref[d, 1:2, :] = two


def upstream_kernel(cot_ref, one_ref, two_ref, up_ref, point_ref, pack_ref, stack, *, relatives):
    rows = cot_ref.shape[0]
    depth = stack.shape[1]
    own = lax.axis_index("seq")
    count = len(relatives) // 2
    for k, relative in enumerate(relatives):
        piece = (one_ref, two_ref)[k // count]
        at = SUMS + (k % count) * up_to(depth, 16)
        stack[own ^ relative] = piece[at : at + depth, :].astype(stack.dtype)
    point_ref[...] = stack[...].reshape(point_ref.shape).astype(BF16)
    put_folded(point_ref[...], pack_ref)
    up_ref[...] = jnp.dot(cot_ref[...], point_ref[...], preferred_element_type=F32)


def mid_kernel(
    got_ref, conv_ref, up_ref, rim_ref, norm_ref, point_ref, hid_ref, d_ref, cen_ref, sent_ref, vec_ref, *, bin_count
):
    rows = hid_ref.shape[0]
    slim = norm_ref.shape[1]
    total = got_ref[0]
    for s in range(1, got_ref.shape[0]):
        total = total + got_ref[s]
    mean = total[0:1] / bin_count
    root = lax.rsqrt(total[1:2] / bin_count - mean * mean + NORM_EPS)
    vec_ref[...] = jnp.zeros_like(vec_ref)
    vec_ref[0:1, :] = root
    vec_ref[1:3, :slim] = norm_ref[...]
    gain, bias = vec_ref[1:2, :], vec_ref[2:3, :]

    def rows_of(begin, count, up):
        centered = (conv_ref[pl.ds(begin, count), :] - mean) * root
        hidden, slope = gelu_and_slope(centered * gain + bias)
        d = up * slope
        cen_ref[pl.ds(begin, count), :] = centered
        d_ref[pl.ds(begin, count), :] = d
        return centered, hidden, d

    for side, begin in enumerate((0, EDGE + rows)):
        up = jnp.dot(rim_ref[side, RIM:, :], point_ref[...], preferred_element_type=F32)
        rows_of(begin, EDGE, up)
    step = 64

    def body(i, carry):
        begin = pl.multiple_of(EDGE + i * step, 16)
        up = up_ref[pl.ds(pl.multiple_of(i * step, 16), step), :]
        centered, hidden, d = rows_of(begin, step, up)
        hid_ref[pl.ds(pl.multiple_of(i * step, 16), step), :] = hidden.astype(BF16)
        d = d.reshape(step // 8, 8, LANES)
        return carry[0] + (d * centered.reshape(d.shape)).sum(0), carry[1] + d.sum(0)

    zero = jnp.zeros((8, LANES), F32)
    gain_sum, bias_sum = lax.fori_loop(0, rows // step, body, (zero, zero), unroll=2)
    gain_sum = jnp.sum(gain_sum, 0, keepdims=True)
    bias_sum = jnp.sum(bias_sum, 0, keepdims=True)
    for d in range(sent_ref.shape[0]):
        sent_ref[d, 0:1, :] = gain_sum
        sent_ref[d, 1:2, :] = bias_sum


def conv_back_kernel(got_ref, vec_ref, d_ref, cen_ref, grad_ref, total_ref, grad, *, bin_count, slim):
    total = got_ref[0]
    for s in range(1, got_ref.shape[0]):
        total = total + got_ref[s]
    total_ref[...] = total
    scale = vec_ref[0:1, :] * vec_ref[1:2, :]
    pull, level = total[0:1] / bin_count, total[1:2] / bin_count
    count = d_ref.shape[0]
    for begin in range(0, count, 96):
        part = slice(begin, min(begin + 96, count))
        grad[part, :] = scale * (d_ref[part, :] - level - cen_ref[part, :] * pull)
    if folds(count, slim):
        grad_ref[...] = fold_rows(grad[:, :slim]).astype(BF16)
    else:
        grad_ref[...] = grad[...].astype(BF16)


def near_kernel(*refs, slim):
    parts, (sum_ref, token_ref, hidden, point) = refs[:-4], refs[-4:]
    token_ref[...] = jnp.zeros_like(token_ref)
    rows, width = hidden.shape[0], point.shape[0]
    count, end = folded_rows(rows, slim), folded_rows(rows, slim) + folded_rows(width, slim)
    for r, part in enumerate(parts):
        lanes = slice(r * LANES, (r + 1) * LANES)
        hidden[:, lanes] = get_folded(part[:count, :], rows)
        point[:, lanes] = get_folded(part[count:end, :], width)
    for at in range(0, width, 256):
        part = slice(at, at + 256)
        sum_ref[:, part] = lax.dot_general(
            hidden[...], point[part, :], LANE_DIMS, preferred_element_type=F32
        )


def out_kernel(x_ref, near_ref, *refs, slim):
    parts, (out_ref, token_ref, hidden, point) = refs[:-4], refs[-4:]
    token_ref[...] = jnp.zeros_like(token_ref)
    rows, width = x_ref.shape
    count, end = folded_rows(rows, slim), folded_rows(rows, slim) + folded_rows(width, slim)
    for r in range(len(parts) // 3):
        lanes = slice(r * LANES, (r + 1) * LANES)
        first, middle, last = parts[3 * r : 3 * r + 3]
        hidden[:, lanes] = get_folded(middle[:count, :], rows)
        pieces = [first[end:, :], middle[count:, :], last[...]]
        point[:, lanes] = get_folded(jnp.concatenate(pieces, axis=0), width)
    for at in range(0, width, 256):
        part = slice(at, at + 256)
        branch = near_ref[:, part] + lax.dot_general(
            hidden[...], point[part, :], LANE_DIMS, preferred_element_type=F32
        )
        out_ref[:, part] = (x_ref[:, part].astype(F32) + branch).astype(BF16)


def operands_kernel(mid_ref, point_ref, far_ref, pack_ref, both_ref):
    put_folded(mid_ref[...], pack_ref)
    at = 0
    for src in (pack_ref, point_ref):
        both_ref[at : at + src.shape[0], :] = src[...]
        at += src.shape[0]
    both_ref[at:, :] = far_ref[: both_ref.shape[0] - at, :]


def halve(blocks, kept_ref, sent_ref, high):
    for k in range(kept_ref.shape[0]):
        kept_ref[k] = blocks(2 * k + high)
        sent_ref[k] = blocks(2 * k + 1 - high).astype(BF16)


def bit_of(reach):
    return (lax.axis_index("seq") // reach) % 2


def terms_of(part, grad, term_ref, at, mask_ref):
    rows = term_ref.shape[0]
    step = 64
    count = part.shape[0]
    grad[:count, :] = part[...].astype(F32)
    if count < grad.shape[0]:
        quarter = count // 3
        width = LANES // 4
        side = [grad[p * quarter : (p + 1) * quarter, 3 * width :] for p in range(3)]
        grad[count:, :] = jnp.concatenate(side + [jnp.zeros((quarter, width), F32)], axis=1)
    for j, shift in enumerate(SHIFTS):
        lanes = slice(at + j * LANES, at + (j + 1) * LANES)
        for begin in range(0, rows, step):
            value = grad[EDGE + begin - shift : EDGE + begin - shift + step, :]
            value = value * mask_ref[j, begin : begin + step, :]
            term_ref[begin : begin + step, lanes] = value.astype(BF16)


def weight_grad_kernel(
    mask_ref, part_ref, hid_ref, cot_ref, mid_ref, term_ref, kept_ref, sent_ref, grad, full, *, depth, slim
):
    rows = term_ref.shape[0]
    terms_of(part_ref, grad, term_ref, 0, mask_ref)
    taps = lax.dot_general(
        hid_ref[...], term_ref[...], ROW_DIMS, preferred_element_type=F32
    )
    point = lax.dot_general(cot_ref[...], mid_ref[...], ROW_DIMS, preferred_element_type=F32)
    parts = [taps[:, j * LANES : j * LANES + slim] for j in range(KERNEL_WIDTH)] + [point[:, :slim]]
    full[...] = jnp.concatenate(parts, axis=1)
    halve(
        lambda k: full[pl.ds(pl.multiple_of(k * depth, 8), depth), :], kept_ref, sent_ref, bit_of(1)
    )


def fold_kernel(old_ref, got_ref, kept_ref, sent_ref, *, reach):
    halve(lambda k: old_ref[k] + got_ref[k].astype(F32), kept_ref, sent_ref, bit_of(reach))


def adamw(weights_old, first_moment_state, second_mom, gradient, step_rate, decay_rate):
    first_next = BETA_ONE * first_moment_state + (1.0 - BETA_ONE) * gradient
    second_next = BETA_TWO * second_mom + (1.0 - BETA_TWO) * gradient * gradient
    corrected = (
        first_next
        / (1.0 - BETA_ONE**STEP)
        / (jnp.sqrt(second_next / (1.0 - BETA_TWO**STEP)) + ADAM_EPS)
    )
    weights_new = weights_old - step_rate * (corrected + decay_rate * weights_old)
    return (first_next, second_next, weights_new)


def first_half_kernel(mask_ref, own_ref, *refs):
    up_ref, term, weight, grad = refs[-4:]
    count = (len(refs) - 4 + 1) // 2
    grads, weights = refs[: count - 1], refs[count - 1 : -4]
    wide = KERNEL_WIDTH * LANES
    term[:, :wide] = own_ref[...]
    for r, part in enumerate(grads):
        terms_of(part, grad, term, (r + 1) * wide, mask_ref)
    for r, piece in enumerate(weights):
        weight[:, r * wide : (r + 1) * wide] = piece[...]
    for at in range(0, up_ref.shape[1], 256):
        part = slice(at, at + 256)
        up_ref[:, part] = lax.dot_general(
            term[...], weight[part, :], LANE_DIMS, preferred_element_type=F32
        )


def second_half_kernel(mask_ref, x_ref, slope_ref, vec_ref, part_ref, weight_ref, *refs):
    grads, (d_ref, sum_ref, term, grad) = refs[:-4], refs[-4:]
    rows, width = x_ref.shape
    wide = KERNEL_WIDTH * LANES
    for r, part in enumerate(grads):
        terms_of(part, grad, term, r * wide, mask_ref)
    for at in range(0, width, 256):
        part = slice(at, at + 256)
        up = lax.dot_general(term[...], weight_ref[part, :], LANE_DIMS, preferred_element_type=F32)
        d = (up + part_ref[:, part]) * slope_ref[:, part]
        d_ref[:, part] = d
        centered = x_ref[:, part].astype(F32) * vec_ref[0:1, part] + vec_ref[1:2, part]
        sum_ref[0:1, part] = jnp.sum(d * centered, 0, keepdims=True)
        sum_ref[1:2, part] = jnp.sum(d, 0, keepdims=True)


def final_kernel(
    x_ref, cot_ref, d_ref, vec_ref, one_ref, two_ref, old_ref, got_ref, mid_ref, *refs, bin_count, chunks
):
    states, outs, refs = refs[:12], refs[12:25], refs[25:]
    held, news, out_ref, sems = refs[:12], refs[12:24], refs[24], refs[25]
    fetches = [
        pltpu.make_async_copy(src, dst, sems.at[k]) for k, (src, dst) in enumerate(zip(states, held))
    ]
    for fetch in fetches:
        fetch.start()
    rows, width = x_ref.shape
    total = one_ref[...] + two_ref[...]
    root, offset, scale = vec_ref[0:1, :], vec_ref[1:2, :], vec_ref[2:3, :]
    pull = scale * total[0:1] / bin_count
    slant = pull * root
    level = scale * total[1:2] / bin_count + pull * offset
    step = 16
    chunk = rows // chunks

    def body(i, carry):
        at = pl.ds(pl.multiple_of(i * step, 16), step)
        value = x_ref[at, :].astype(F32) * slant + level
        out_ref[at, :] = cot_ref[at, :].astype(F32) + (d_ref[at, :] * scale - value)
        return carry

    sends = []
    for k in range(chunks):
        lax.fori_loop(k * chunk // step, (k + 1) * chunk // step, body, 0, unroll=4)
        part = pl.ds(k * chunk, chunk)
        sends.append(pltpu.make_async_copy(out_ref.at[part], outs[0].at[part], sems.at[24 + k]))
        sends[-1].start()
    for fetch in fetches:
        fetch.wait()

    def step_of(first, at, grad, rate, decay):
        new = adamw(*(ref[at] for ref in held[first : first + 3]), grad, rate, decay)
        for ref, value in zip(news[first : first + 3], new):
            ref[at] = value

    slim = held[3].shape[2]
    both = old_ref[0] + got_ref[0].astype(F32)
    step_of(0, ..., total, RATE_NORM, 0.0)
    for j in range(KERNEL_WIDTH):
        step_of(3, j, both[:, j * slim : (j + 1) * slim], RATE_WEIGHT, DECAY_WEIGHT)
    step_of(6, ..., both[:, KERNEL_WIDTH * slim :].T, RATE_WEIGHT, DECAY_WEIGHT)
    step_of(9, ..., mid_ref[:, :slim], RATE_NORM, 0.0)
    for k in range(12):
        sends.append(pltpu.make_async_copy(news[k], outs[1 + k], sems.at[12 + k]))
        sends[-1].start()
    for send in sends:
        send.wait()


def flip(axis, reach):
    return [(i, i ^ reach) for i in range(lax.axis_size(axis))]


def relatives_of(order):
    found = [0]
    for reach in order:
        found = found + [r ^ reach for r in found]
    return found


def descending(size):
    return [size >> k for k in range(1, size.bit_length())]


def round_kernel(weight_one, weight_two, one_ref, two_ref, *refs, size, sides):
    count = (len(refs) - 2 - sides) // 3
    rims, outs = refs[: 2 * count], refs[2 * count :]
    weight_ref, out_ref, halves = outs[0], outs[1], outs[2 : 2 + sides]
    if rims:
        outs[-1][...] = rims[1][...]
    count = weight_one.shape[0]
    weight_ref[:count] = weight_one[...]
    weight_ref[count:] = weight_two[...]
    for half, src in zip(halves, (weight_one, weight_two)):
        half[...] = src[...]
    put_sums(out_ref, get_sums(one_ref) + get_sums(two_ref))
    out_ref[SUMS : SUMS + size, :] = one_ref[SUMS : SUMS + size, :]
    out_ref[SUMS + size : SUMS + 2 * size, :] = two_ref[SUMS : SUMS + size, :]
    for rim in rims[:1]:
        height, width = rim.shape
        for k in range(width // LANES):
            at = SUMS + 2 * size + k * height
            out_ref[at : at + height, :] = rim[:, k * LANES : (k + 1) * LANES]


def copy_kernel(*refs):
    count = len(refs) // 2
    for src, out in zip(refs[:count], refs[count:]):
        out[...] = src[...]


def packs(wanted, after):
    arrays, places = [], []
    for pieces in wanted:
        places.append([])
        for piece in pieces:
            array, begin, end = piece if isinstance(piece, tuple) else (piece, 0, piece.shape[0])
            places[-1].append((len(arrays), begin, end))
            arrays.append(array)

    def pack_kernel(*refs):
        for out, group in zip(refs[len(arrays) :], places):
            at = 0
            for index, begin, end in group:
                out[at : at + end - begin, :] = refs[index][begin:end, :]
                at += end - begin

    sizes = [sum(end - begin for _, begin, end in group) for group in places]
    return call(pack_kernel, [((size, LANES), BF16) for size in sizes], arrays, after=after)


def take_kernel(src_ref, weight_ref, pack_ref):
    count, packed = weight_ref.shape[:2]
    weight_ref[...] = src_ref[:count]
    for k in range(pack_ref.shape[0] // packed):
        lanes = slice(k % KERNEL_WIDTH * LANES, (k % KERNEL_WIDTH + 1) * LANES)
        pack_ref[k * packed : (k + 1) * packed, :] = src_ref[count + k // KERNEL_WIDTH, :, lanes]


def copies(arrays, after):
    return call(copy_kernel, [(x.shape, x.dtype) for x in arrays], arrays, after=after)


def add_kernel(one_ref, two_ref, out_ref):
    out_ref[...] = one_ref[...] + two_ref[...]


def add(one, two, after=()):
    return call(add_kernel, [(one.shape, one.dtype)], [one, two], after=after)[0]


def swap(x, axis, reach):
    return lax.ppermute(x, axis, flip(axis, reach))


def gather_parts(x, reaches):
    parts = [x]
    for reach in reaches:
        parts += [swap(part, "ch", reach) for part in parts]
    return parts


def spread(copies, axes):
    return lax.all_to_all(copies, axes, 0, 0, tiled=True)


def shards(
    inputs,
    cotangent,
    starts,
    master_conv,
    first_conv,
    second_conv,
    master_point,
    first_point,
    second_point,
    norm_in,
    first_in,
    second_in,
    norm_mid,
    first_mid,
    second_mid,
):
    rows, width = inputs.shape
    seq_size, ch_size = lax.axis_size("seq"), lax.axis_size("ch")
    bin_count = rows * seq_size
    depth, slim = master_conv.shape[1:]
    tiles = width // LANES
    wide = KERNEL_WIDTH * LANES
    weight_order = descending(seq_size)
    sum_order = weight_order[::-1]
    last_order = weight_order[1::-1] + weight_order[2:]
    point_order = weight_order[:1] + [1] + weight_order[1:-1]
    ch_order = descending(ch_size)
    ext = rows + 2 * EDGE

    rounds = len(weight_order)
    top, lower = ch_order[0], ch_order[1:]
    chunks = 4
    rim = (RIM + EDGE, width // 2)
    packed = 3 * depth // 4 if folds(depth, slim) else depth
    inputs, weight, near, *rims = call(
        first_kernel,
        [
            (inputs.shape, BF16),
            ((1, packed, wide), BF16),
            ((SUMS + up_to(depth, 16), LANES), BF16),
            (rim, BF16),
            (rim, BF16),
        ],
        [inputs, cotangent, master_conv, master_point],
        scratch=[
            ((2, EDGE, width), BF16),
            (master_conv.shape, F32),
            (master_point.shape, F32),
            ((16, LANES), F32),
        ],
        away=(0, 1, 2, 3),
        sems=4 + chunks,
    )
    pairs = [(i, i + 1) for i in range(1, seq_size - 1, 2)]
    ahead, back = call(
        mask_kernel,
        [((KERNEL_WIDTH, ext, LANES), F32), ((KERNEL_WIDTH, rows, LANES), F32)],
        [starts],
        smem=(0,),
        after=[weight],
    )
    parts = [weight]
    for k in range(rounds):
        weight_got = [swap(part, "seq", weight_order[k]) for part in parts]
        near_got = swap(near, "seq", point_order[k])
        if k < rounds - 1:
            size = up_to(depth, 16) << k
            spare = {0: tiles // 2 * rim[0], rounds - 2: 16}.get(k, 0)
            outs = [((2 * weight.shape[0], packed, wide), BF16), ((SUMS + 2 * size + spare, LANES), BF16)]
            sides = 2 if k == rounds - 2 else 0
            outs += [(weight.shape, BF16)] * sides
            join = functools.partial(round_kernel, size=size, sides=sides)
            args = [weight, weight_got[0], near, near_got]
            if k == 0:
                weight, near, far = call(join, outs + [(rim, BF16)], args + rims, after=[back])
                far = lax.ppermute(far, "seq", pairs + [(j, i) for i, j in pairs])
                parts = [weight]
            else:
                if k == 1:
                    (rims,) = call(
                        rim_kernel, [((2 * rim[0] + 16, rim[1]), BF16)], [near_got, far]
                    )
                    other_rims = swap(rims, "ch", 1)
                weight, near, *parts = call(join, outs, args)
                parts = parts or [weight]
    hidden_in, slope_in, vec_in, cotangent = call(
        functools.partial(act_kernel, bin_count=bin_count),
        [((rows, width), BF16), ((rows, width), F32), ((8, width), F32), (cotangent.shape, BF16)],
        [inputs, cotangent, near, near_got, norm_in],
        away=(1,),
        sems=1,
    )
    stack_type = BF16 if depth % 16 == 0 else F32
    upstream, point_own, point_pack = call(
        functools.partial(upstream_kernel, relatives=relatives_of(point_order)),
        [((rows, LANES), F32), ((width, LANES), BF16), ((folded_rows(width, slim), LANES), BF16)],
        [cotangent, near, near_got],
        scratch=[((seq_size, depth, LANES), stack_type)],
    )
    blocks = -(-point_pack.shape[0] // (packed * KERNEL_WIDTH))
    conv_own, conv_out, sums_mid, rims, weight = call(
        functools.partial(
            conv_kernel, relatives=relatives_of(weight_order), slim=slim
        ),
        [
            ((width, wide), BF16),
            ((ext, LANES), F32),
            ((seq_size, 2, LANES), F32),
            ((2, RIM + EDGE, width), BF16),
            ((seq_size + blocks, packed, wide), BF16),
        ],
        [ahead, hidden_in, rims, other_rims, vec_in, point_pack, weight, *weight_got],
        scratch=[
            ((seq_size, depth, wide), stack_type),
            ((rows + 2 * RIM, wide), F32),
            ((2 * RIM, width), BF16),
        ],
        after=[upstream],
    )
    weight = swap(weight, "ch", top)
    got_mid = spread(sums_mid, "seq")
    conv_near = gather_parts(conv_own, lower)
    hidden_mid, d_mid, centered, sent_back, vec_mid = call(
        functools.partial(mid_kernel, bin_count=bin_count),
        [
            ((rows, LANES), BF16),
            ((ext, LANES), F32),
            ((ext, LANES), F32),
            ((seq_size, 2, LANES), F32),
            ((8, LANES), F32),
        ],
        [got_mid, conv_out, upstream, rims, norm_mid, point_own],
        after=conv_near[1:],
    )
    got_back = spread(sent_back, "seq")
    grad_own, total_mid = call(
        functools.partial(conv_back_kernel, bin_count=bin_count, slim=slim),
        [((3 * ext // 4 if folds(ext, slim) else ext, LANES), BF16), ((2, LANES), F32)],
        [got_back, vec_mid, d_mid, centered],
        scratch=[((ext, LANES), F32)],
    )
    grad_near = gather_parts(grad_own, lower)
    grad_far = swap(grad_own, "ch", top)
    weight, point_far = call(
        take_kernel,
        [((seq_size, packed, wide), BF16), (point_pack.shape, BF16)],
        [weight],
        after=[grad_own],
    )
    side = ch_size // 2 * wide
    (conv_far,) = call(
        functools.partial(place_kernel, relatives=relatives_of(weight_order), slim=slim),
        [((width, side), BF16)],
        gather_parts(weight, lower),
        scratch=[((seq_size, depth, wide), stack_type)],
    )
    half = seq_size // 2
    hidden_rows = folded_rows(rows, slim)
    terms, kept, sent = call(
        functools.partial(weight_grad_kernel, depth=depth, slim=slim),
        [
            ((rows, wide), BF16),
            ((half, depth, 4 * slim), F32),
            ((half, depth, 4 * slim), BF16),
        ],
        [back, grad_own, hidden_in, cotangent, hidden_mid],
        scratch=[((ext, LANES), F32), ((width, 4 * slim), F32)],
    )
    (up_part,) = call(
        first_half_kernel,
        [((rows, width), F32)],
        [back, terms, *grad_near[1:], *conv_near],
        scratch=[((rows, side), BF16), ((width, side), BF16), ((ext, LANES), F32)],
    )
    grad_far = gather_parts(copies([grad_far], [up_part, conv_far])[0], lower)
    count = point_far.shape[0]
    cuts = [up_to(k * count // 100, 16) for k in (39, 52)]
    hidden_pack, both = call(
        operands_kernel,
        [((hidden_rows, LANES), BF16), ((hidden_rows + count + cuts[0], LANES), BF16)],
        [hidden_mid, point_pack, point_far],
        after=[sent],
    )
    both_parts = gather_parts(both, lower)
    d_in, sums_back = call(
        second_half_kernel,
        [((rows, width), F32), ((2, width), F32)],
        [back, inputs, slope_in, vec_in, up_part, conv_far, *grad_far],
        scratch=[((rows, side), BF16), ((ext, LANES), F32)],
    )
    total_back = sums_back
    hidden_far = swap(hidden_pack, "ch", top)
    placed = []
    scratch = [((size, ch_size // 2 * LANES), BF16) for size in (rows, width)]
    for k, reach in enumerate(sum_order):
        total_got = swap(total_back, "seq", last_order[k])
        got = swap(sent, "seq", reach)
        if k < rounds - 1:
            half //= 2
            kept, sent = call(
                functools.partial(fold_kernel, reach=2 * reach),
                [((half, depth, 4 * slim), F32), ((half, depth, 4 * slim), BF16)],
                [kept, got],
                after=[total_back, *placed] if k else [],
            )
            total_back = add(total_back, total_got)
        if k == rounds - 3:
            (first,) = packs([[hidden_far, (point_far, *cuts)]], [total_back])
            first_parts = gather_parts(first, lower)
            near_sum, *placed = call(
                functools.partial(near_kernel, slim=slim),
                [((rows, width), F32), ((8, LANES), F32)],
                both_parts,
                scratch=scratch,
                after=[total_back],
            )
        if k == rounds - 2:
            (last,) = packs([[(point_far, cuts[1], count)]], [total_back])
            last_parts = gather_parts(last, lower)
    far_parts = [x for group in zip(both_parts, first_parts, last_parts) for x in group]
    block_out, token = call(
        functools.partial(out_kernel, slim=slim),
        [((rows, width), BF16), ((8, LANES), F32)],
        [inputs, near_sum, *far_parts],
        scratch=scratch,
        after=[total_back],
    )
    states = [norm_in, first_in, second_in, master_conv, first_conv, second_conv]
    states += [master_point, first_point, second_point, norm_mid, first_mid, second_mid]
    arrays = [inputs, cotangent, d_in, vec_in, total_back, total_got, kept, got, total_mid]
    small = [(x.shape, F32) for x in states]
    input_grad, *news = call(
        functools.partial(final_kernel, bin_count=bin_count, chunks=8),
        [((rows, width), F32)] + small,
        arrays + states,
        scratch=small + small + [((rows, width), F32)],
        away=range(len(arrays), len(arrays) + 12),
        away_outs=range(13),
        sems=24 + 8,
        after=[token],
    )
    return (block_out, input_grad, *news[3:9], *news[:3], *news[9:])


def solution(mesh):
    in_specs = (
        P("seq", None),
        P("seq", None),
        P(),
        P(None, "seq", "ch"),
        P(None, "seq", "ch"),
        P(None, "seq", "ch"),
        P("ch", "seq"),
        P("ch", "seq"),
        P("ch", "seq"),
        P(),
        P(),
        P(),
        P(None, "ch"),
        P(None, "ch"),
        P(None, "ch"),
    )
    out_specs = (
        P("seq", None),
        P("seq", None),
        P(None, "seq", "ch"),
        P(None, "seq", "ch"),
        P(None, "seq", "ch"),
        P("ch", "seq"),
        P("ch", "seq"),
        P("ch", "seq"),
        P(),
        P(),
        P(),
        P(None, "ch"),
        P(None, "ch"),
        P(None, "ch"),
    )
    return jax.shard_map(shards, mesh=mesh, in_specs=in_specs, out_specs=out_specs, check_vma=False)
```

```python
import functools

import jax
import jax.numpy as jnp
from jax import lax
from jax.experimental import pallas as pl
from jax.experimental.pallas import tpu as pltpu
from jax.sharding import PartitionSpec as P

KERNEL_WIDTH = 3
DILATION_BINS = 9
WIN = 1024
STEP = 10

NORM_EPS = 1e-05
ADAM_EPS = 1e-08
BETA_ONE = 0.9
BETA_TWO = 0.999
RATE_WEIGHT = 0.05
RATE_NORM = 0.5
DECAY_WEIGHT = 0.01

LANES = 128
EDGE = 16
RIM = 2 * EDGE
SUMS = 48
GELU_A = 0.7978845608028654
GELU_B = 0.044715
SHIFTS = [(j - KERNEL_WIDTH // 2) * DILATION_BINS for j in range(KERNEL_WIDTH)]
ROW_DIMS = (((0,), (0,)), ((), ()))
LANE_DIMS = (((1,), (1,)), ((), ()))
F32, BF16 = jnp.float32, jnp.bfloat16


def call(body, outs, args, scratch=(), smem=(), away=(), after=(), sems=0, away_outs=(), limit=16):
    spaces = [pltpu.SMEM if k in smem else pltpu.VMEM for k in range(len(args))]
    spaces = [pltpu.HBM if k in away else space for k, space in enumerate(spaces)]
    spaces += [pl.ANY] * len(after)

    args = [
        pltpu.with_memory_space_constraint(x, pltpu.HBM) if k in away else x
        for k, x in enumerate(args)
    ]

    def kernel(*refs):
        body(*refs[: len(args)], *refs[len(spaces) :])

    return pl.pallas_call(
        kernel,
        out_shape=[jax.ShapeDtypeStruct(s, t) for s, t in outs],
        in_specs=[pl.BlockSpec(memory_space=s) for s in spaces],
        out_specs=[
            pl.BlockSpec(memory_space=pltpu.HBM if k in away_outs else pltpu.VMEM)
            for k in range(len(outs))
        ],
        scratch_shapes=[pltpu.VMEM(s, t) for s, t in scratch]
        + [pltpu.SemaphoreType.DMA((sems,))] * (sems > 0),
        compiler_params=pltpu.CompilerParams(vmem_limit_bytes=limit * 2**20),
        cost_estimate=pl.CostEstimate(flops=1, bytes_accessed=1, transcendentals=0),
        name=getattr(body, "func", body).__name__,
    )(*args, *after)


def up_to(size, step):
    return -(-size // step) * step


def split_three(v):
    high = v.astype(BF16).astype(F32)
    rest = v - high
    middle = rest.astype(BF16).astype(F32)
    return high, middle, rest - middle


def gelu_and_slope(v):
    square = v * v
    t = jnp.tanh(v * (GELU_A + (GELU_A * GELU_B) * square))
    half = 0.5 * (1.0 + t)
    slope = half + (0.5 * v) * (1.0 - t * t) * (GELU_A + (3.0 * GELU_A * GELU_B) * square)
    return v * half, slope


def reach_of(first, count, shift, start, bin_count):
    here = first + lax.broadcasted_iota(jnp.int32, (count, LANES), 0)
    there = here + shift
    inside = (here >= 0) & (here < bin_count) & (there >= 0) & (there < bin_count)
    return inside & (((here - start) >> 10) == ((there - start) >> 10))


def folds(depth, slim):
    return 3 * (LANES - slim) == slim and depth % 32 == 0


def fold_rows(block):
    rows, slim = block.shape
    quarter, width = rows // 4, LANES - slim
    side = [block[3 * quarter :, p * width : (p + 1) * width] for p in range(3)]
    return jnp.concatenate([block[: 3 * quarter], jnp.concatenate(side, axis=0)], axis=1)


def unfold_rows(block, slim):
    quarter, width = block.shape[0] // 3, LANES - slim
    side = [block[p * quarter : (p + 1) * quarter, slim:] for p in range(3)]
    side.append(jnp.zeros((quarter, width), block.dtype))
    lane = lax.broadcasted_iota(jnp.int32, block.shape, 1)
    return jnp.concatenate([jnp.where(lane < slim, block, 0.0), jnp.concatenate(side, axis=1)], axis=0)


def folded_rows(rows, slim):
    return 3 * rows // 4 if folds(rows, slim) else rows


def put_folded(block, out_ref):
    if out_ref.shape[0] < block.shape[0]:
        block = fold_rows(block[:, : 3 * LANES // 4].astype(F32)).astype(BF16)
    out_ref[...] = block


def get_folded(block, rows):
    if block.shape[0] < rows:
        block = unfold_rows(block.astype(F32), 3 * LANES // 4).astype(BF16)
    return block


def first_kernel(
    x_hbm, cot_hbm, conv_hbm, point_hbm, x_ref, weight_ref, near_ref, near_rim, far_rim, edge_ref, conv_ref, point_ref, sum_ref, sems
):
    rows, width = x_ref.shape
    tiles = width // LANES
    depth, slim = conv_ref.shape[1:]
    chunks = sems.shape[0] - 4
    chunk = rows // chunks
    copies = [
        pltpu.make_async_copy(conv_hbm, conv_ref, sems.at[0]),
        pltpu.make_async_copy(point_hbm, point_ref, sems.at[1]),
        pltpu.make_async_copy(cot_hbm.at[pl.ds(0, EDGE)], edge_ref.at[0], sems.at[2]),
        pltpu.make_async_copy(cot_hbm.at[pl.ds(rows - EDGE, EDGE)], edge_ref.at[1], sems.at[3]),
    ]
    for k in range(chunks):
        part = pl.ds(k * chunk, chunk)
        copies.append(pltpu.make_async_copy(x_hbm.at[part], x_ref.at[part], sems.at[4 + k]))
    for copy in copies:
        copy.start()
    weight_ref[...] = jnp.zeros_like(weight_ref)
    near_ref[...] = jnp.zeros_like(near_ref)
    sum_ref[...] = jnp.zeros_like(sum_ref)
    copies[0].wait()
    for j in range(KERNEL_WIDTH):
        if folds(depth, slim):
            weight_ref[0, :, j * LANES : (j + 1) * LANES] = fold_rows(conv_ref[j]).astype(BF16)
        else:
            weight_ref[0, :, j * LANES : j * LANES + slim] = conv_ref[j].astype(BF16)
    copies[1].wait()
    near_ref[SUMS : SUMS + depth, :slim] = point_ref[...].T.astype(BF16)

    def step(k, carry):
        v = x_ref[pl.ds(pl.multiple_of(k * 32, 32), 32), :].astype(F32)
        v = v.reshape(4, 8, width)
        return carry[0] + v.sum(0), carry[1] + (v * v).sum(0)

    totals = (jnp.zeros((8, width), F32),) * 2
    for k in range(chunks):
        copies[4 + k].wait()
        totals = lax.fori_loop(
            k * chunk // 32, (k + 1) * chunk // 32, step, totals, unroll=chunk // 32
        )
    for stat, total in enumerate(totals):
        total = jnp.sum(total, 0, keepdims=True)
        for k in range(tiles):
            row = stat * tiles + k
            sum_ref[row : row + 1, :] = total[:, k * LANES : (k + 1) * LANES]
    put_sums(near_ref, sum_ref[...])
    copies[2].wait()
    copies[3].wait()
    odd = lax.axis_index("seq") % 2
    lanes = half_of(width, lax.axis_index("ch") % 2)
    for ref, side in ((near_rim, 1 - odd), (far_rim, odd)):
        ref[:RIM, :] = x_ref[pl.ds(pl.multiple_of(side * (rows - RIM), RIM), RIM), lanes]
        ref[RIM:, :] = edge_ref[side, :, lanes]


def half_of(width, core):
    return pl.ds(pl.multiple_of(core * (width // 2), LANES), width // 2)


def put_sums(ref, value):
    for p, part in enumerate(split_three(value)):
        ref[p * 16 : (p + 1) * 16, :] = part.astype(BF16)


def get_sums(ref):
    return sum(ref[p * 16 : (p + 1) * 16, :].astype(F32) for p in range(3))


def act_kernel(
    x_ref, cot_hbm, one_ref, two_ref, norm_ref, hid_ref, slope_ref, vec_ref, cot_ref, sems, *, bin_count
):
    copy = pltpu.make_async_copy(cot_hbm, cot_ref, sems.at[0])
    copy.start()
    rows, width = x_ref.shape
    tiles = width // LANES
    total = get_sums(one_ref) + get_sums(two_ref)
    for k in range(tiles):
        lanes = slice(k * LANES, (k + 1) * LANES)
        mean = total[k : k + 1, :] / bin_count
        square = total[tiles + k : tiles + k + 1, :] / bin_count
        root = lax.rsqrt(square - mean * mean + NORM_EPS)
        gain = root * norm_ref[0:1, lanes]
        vec_ref[0:1, lanes] = root
        vec_ref[1:2, lanes] = -mean * root
        vec_ref[2:3, lanes] = gain
        vec_ref[3:4, lanes] = norm_ref[1:2, lanes] - mean * gain

    gain, offset = vec_ref[2:3, :], vec_ref[3:4, :]

    def step(k, carry):
        at = pl.multiple_of(k * 16, 16)
        v = x_ref[pl.ds(at, 16), :].astype(F32) * gain + offset
        hidden, slope = gelu_and_slope(v)
        hid_ref[pl.ds(at, 16), :] = hidden.astype(BF16)
        slope_ref[pl.ds(at, 16), :] = slope
        return carry

    lax.fori_loop(0, rows // 16, step, 0, unroll=2)
    copy.wait()


def place(pieces, relatives, stack, own, slim):
    depth = stack.shape[1]
    at = 0
    for piece in pieces:
        for k in range(piece.shape[0]):
            block = piece[k].astype(F32)
            for j in range(KERNEL_WIDTH):
                part = block[:, j * LANES : (j + 1) * LANES]
                if folds(depth, slim):
                    part = unfold_rows(part, slim)
                stack[own ^ relatives[at], :, j * LANES : (j + 1) * LANES] = part.astype(stack.dtype)
            at += 1
    return stack[...].reshape(-1, stack.shape[2]).astype(BF16)


def place_kernel(*refs, relatives, slim):
    pieces, (out_ref, stack) = refs[:-2], refs[-2:]
    wide = stack.shape[2]
    for r, piece in enumerate(pieces):
        block = place([piece], relatives, stack, lax.axis_index("seq"), slim)
        out_ref[:, r * wide : (r + 1) * wide] = block


def rim_kernel(near_ref, far_ref, out_ref):
    height, width = far_ref.shape
    base = near_ref.shape[0] - width // LANES * height
    for k in range(width // LANES):
        at = base + k * height
        out_ref[:height, k * LANES : (k + 1) * LANES] = near_ref[at : at + height, :]
    out_ref[height : 2 * height, :] = far_ref[...]
    out_ref[2 * height :, :] = jnp.zeros_like(out_ref[2 * height :, :])


def mask_kernel(start_ref, ahead_ref, back_ref):
    rows = back_ref.shape[1]
    first = lax.axis_index("seq") * rows
    for j, shift in enumerate(SHIFTS):
        for begin in range(0, rows + RIM, 96):
            count = min(96, rows + RIM - begin)
            mask = reach_of(first + begin - EDGE, count, shift, start_ref[0], rows * lax.axis_size("seq"))
            ahead_ref[j, begin : begin + count, :] = jnp.where(mask, 1.0, 0.0)
        for begin in range(0, rows, 128):
            back_ref[j, begin : begin + 128, :] = ahead_ref[
                j, EDGE + begin - shift : EDGE + begin - shift + 128, :
            ]


def conv_kernel(mask_ref, hid_ref, own_rims, other_rims, vec_ref, pack_ref, *refs, relatives, slim):
    pieces, refs = refs[:-8], refs[-8:]
    weight_ref, out_ref, sum_ref, rim_ref, all_ref, stack, prod, edge = refs
    at, packed = 0, pieces[0].shape[1]
    for piece in pieces:
        all_ref[at : at + piece.shape[0]] = piece[...]
        at += piece.shape[0]
    for k in range(pack_ref.shape[0] // packed):
        lanes = slice(k % KERNEL_WIDTH * LANES, (k % KERNEL_WIDTH + 1) * LANES)
        all_ref[at + k // KERNEL_WIDTH, :, lanes] = pack_ref[k * packed : (k + 1) * packed, :]
    odd, core = lax.axis_index("seq") % 2, lax.axis_index("ch") % 2
    height, width = rim_ref.shape[1:]
    for half, owner in ((own_rims, core), (other_rims, 1 - core)):
        rim_ref[1 - odd, :, half_of(width, owner)] = half[:height, :]
        rim_ref[odd, :, half_of(width, owner)] = half[height : 2 * height, :]
    for side in range(2):
        for k in range(0, RIM, 16):
            v = rim_ref[side, k : k + 16, :].astype(F32) * vec_ref[2:3, :] + vec_ref[3:4, :]
            edge[side * RIM + k : side * RIM + k + 16, :] = gelu_and_slope(v)[0].astype(BF16)
    rows = hid_ref.shape[0]
    weight_ref[...] = place(pieces, relatives, stack, lax.axis_index("seq"), slim)
    for at in range(0, weight_ref.shape[1], 256):
        part = slice(at, min(at + 256, weight_ref.shape[1]))
        prod[RIM : RIM + rows, part] = jnp.dot(
            hid_ref[...], weight_ref[:, part], preferred_element_type=F32
        )
        sides = jnp.dot(edge[...], weight_ref[:, part], preferred_element_type=F32)
        prod[:RIM, part] = sides[:RIM]
        prod[RIM + rows :, part] = sides[RIM:]

    def rows_of(begin, count):
        value = 0.0
        for j, shift in enumerate(SHIFTS):
            part = prod[begin + EDGE + shift : begin + EDGE + shift + count, j * LANES : (j + 1) * LANES]
            value = value + mask_ref[j, begin : begin + count, :] * part
        out_ref[begin : begin + count, :] = value
        return value

    rows_of(0, EDGE)
    rows_of(EDGE + rows, EDGE)
    one = two = jnp.zeros((8, LANES), F32)
    step = 128
    for k in range(rows // step):
        value = rows_of(EDGE + k * step, step).reshape(step // 8, 8, LANES)
        one = one + value.sum(0)
        two = two + (value * value).sum(0)
    one, two = jnp.sum(one, 0, keepdims=True), jnp.sum(two, 0, keepdims=True)
    for d in range(sum_ref.shape[0]):
        sum_ref[d, 0:1, :] = one
        sum_ref[d, 1:2, :] = two


def upstream_kernel(cot_ref, one_ref, two_ref, up_ref, point_ref, pack_ref, stack, *, relatives):
    rows = cot_ref.shape[0]
    depth = stack.shape[1]
    own = lax.axis_index("seq")
    count = len(relatives) // 2
    for k, relative in enumerate(relatives):
        piece = (one_ref, two_ref)[k // count]
        at = SUMS + (k % count) * up_to(depth, 16)
        stack[own ^ relative] = piece[at : at + depth, :].astype(stack.dtype)
    point_ref[...] = stack[...].reshape(point_ref.shape).astype(BF16)
    put_folded(point_ref[...], pack_ref)
    up_ref[...] = jnp.dot(cot_ref[...], point_ref[...], preferred_element_type=F32)


def mid_kernel(
    got_ref, conv_ref, up_ref, rim_ref, norm_ref, point_ref, hid_ref, d_ref, cen_ref, sent_ref, vec_ref, *, bin_count
):
    rows = hid_ref.shape[0]
    slim = norm_ref.shape[1]
    total = got_ref[0]
    for s in range(1, got_ref.shape[0]):
        total = total + got_ref[s]
    mean = total[0:1] / bin_count
    root = lax.rsqrt(total[1:2] / bin_count - mean * mean + NORM_EPS)
    vec_ref[...] = jnp.zeros_like(vec_ref)
    vec_ref[0:1, :] = root
    vec_ref[1:3, :slim] = norm_ref[...]
    gain, bias = vec_ref[1:2, :], vec_ref[2:3, :]

    def rows_of(begin, count, up):
        centered = (conv_ref[pl.ds(begin, count), :] - mean) * root
        hidden, slope = gelu_and_slope(centered * gain + bias)
        d = up * slope
        cen_ref[pl.ds(begin, count), :] = centered
        d_ref[pl.ds(begin, count), :] = d
        return centered, hidden, d

    for side, begin in enumerate((0, EDGE + rows)):
        up = jnp.dot(rim_ref[side, RIM:, :], point_ref[...], preferred_element_type=F32)
        rows_of(begin, EDGE, up)
    step = 64

    def body(i, carry):
        begin = pl.multiple_of(EDGE + i * step, 16)
        up = up_ref[pl.ds(pl.multiple_of(i * step, 16), step), :]
        centered, hidden, d = rows_of(begin, step, up)
        hid_ref[pl.ds(pl.multiple_of(i * step, 16), step), :] = hidden.astype(BF16)
        d = d.reshape(step // 8, 8, LANES)
        return carry[0] + (d * centered.reshape(d.shape)).sum(0), carry[1] + d.sum(0)

    zero = jnp.zeros((8, LANES), F32)
    gain_sum, bias_sum = lax.fori_loop(0, rows // step, body, (zero, zero), unroll=2)
    gain_sum = jnp.sum(gain_sum, 0, keepdims=True)
    bias_sum = jnp.sum(bias_sum, 0, keepdims=True)
    for d in range(sent_ref.shape[0]):
        sent_ref[d, 0:1, :] = gain_sum
        sent_ref[d, 1:2, :] = bias_sum


def conv_back_kernel(got_ref, vec_ref, d_ref, cen_ref, grad_ref, total_ref, grad, *, bin_count, slim):
    total = got_ref[0]
    for s in range(1, got_ref.shape[0]):
        total = total + got_ref[s]
    total_ref[...] = total
    scale = vec_ref[0:1, :] * vec_ref[1:2, :]
    pull, level = total[0:1] / bin_count, total[1:2] / bin_count
    count = d_ref.shape[0]
    for begin in range(0, count, 96):
        part = slice(begin, min(begin + 96, count))
        grad[part, :] = scale * (d_ref[part, :] - level - cen_ref[part, :] * pull)
    if folds(count, slim):
        grad_ref[...] = fold_rows(grad[:, :slim]).astype(BF16)
    else:
        grad_ref[...] = grad[...].astype(BF16)


def near_kernel(*refs, slim):
    parts, (sum_ref, token_ref, hidden, point) = refs[:-4], refs[-4:]
    token_ref[...] = jnp.zeros_like(token_ref)
    rows, width = hidden.shape[0], point.shape[0]
    count, end = folded_rows(rows, slim), folded_rows(rows, slim) + folded_rows(width, slim)
    for r, part in enumerate(parts):
        lanes = slice(r * LANES, (r + 1) * LANES)
        hidden[:, lanes] = get_folded(part[:count, :], rows)
        point[:, lanes] = get_folded(part[count:end, :], width)
    for at in range(0, width, 256):
        part = slice(at, at + 256)
        sum_ref[:, part] = lax.dot_general(
            hidden[...], point[part, :], LANE_DIMS, preferred_element_type=F32
        )


def out_kernel(x_ref, near_ref, *refs, slim):
    parts, (out_ref, token_ref, hidden, point) = refs[:-4], refs[-4:]
    token_ref[...] = jnp.zeros_like(token_ref)
    rows, width = x_ref.shape
    count, end = folded_rows(rows, slim), folded_rows(rows, slim) + folded_rows(width, slim)
    for r in range(len(parts) // 3):
        lanes = slice(r * LANES, (r + 1) * LANES)
        first, middle, last = parts[3 * r : 3 * r + 3]
        hidden[:, lanes] = get_folded(middle[:count, :], rows)
        pieces = [first[end:, :], middle[count:, :], last[...]]
        point[:, lanes] = get_folded(jnp.concatenate(pieces, axis=0), width)
    for at in range(0, width, 256):
        part = slice(at, at + 256)
        branch = near_ref[:, part] + lax.dot_general(
            hidden[...], point[part, :], LANE_DIMS, preferred_element_type=F32
        )
        out_ref[:, part] = (x_ref[:, part].astype(F32) + branch).astype(BF16)


def operands_kernel(mid_ref, point_ref, far_ref, pack_ref, both_ref):
    put_folded(mid_ref[...], pack_ref)
    at = 0
    for src in (pack_ref, point_ref):
        both_ref[at : at + src.shape[0], :] = src[...]
        at += src.shape[0]
    both_ref[at:, :] = far_ref[: both_ref.shape[0] - at, :]


def halve(blocks, kept_ref, sent_ref, high):
    for k in range(kept_ref.shape[0]):
        kept_ref[k] = blocks(2 * k + high)
        sent_ref[k] = blocks(2 * k + 1 - high).astype(BF16)


def bit_of(reach):
    return (lax.axis_index("seq") // reach) % 2


def terms_of(part, grad, term_ref, at, mask_ref):
    rows = term_ref.shape[0]
    step = 64
    count = part.shape[0]
    grad[:count, :] = part[...].astype(F32)
    if count < grad.shape[0]:
        quarter = count // 3
        width = LANES // 4
        side = [grad[p * quarter : (p + 1) * quarter, 3 * width :] for p in range(3)]
        grad[count:, :] = jnp.concatenate(side + [jnp.zeros((quarter, width), F32)], axis=1)
    for j, shift in enumerate(SHIFTS):
        lanes = slice(at + j * LANES, at + (j + 1) * LANES)
        for begin in range(0, rows, step):
            value = grad[EDGE + begin - shift : EDGE + begin - shift + step, :]
            value = value * mask_ref[j, begin : begin + step, :]
            term_ref[begin : begin + step, lanes] = value.astype(BF16)


def weight_grad_kernel(
    mask_ref, part_ref, hid_ref, cot_ref, mid_ref, term_ref, kept_ref, sent_ref, grad, full, *, depth, slim
):
    rows = term_ref.shape[0]
    terms_of(part_ref, grad, term_ref, 0, mask_ref)
    taps = lax.dot_general(
        hid_ref[...], term_ref[...], ROW_DIMS, preferred_element_type=F32
    )
    point = lax.dot_general(mid_ref[...], cot_ref[...], ROW_DIMS, preferred_element_type=F32).T
    parts = [taps[:, j * LANES : j * LANES + slim] for j in range(KERNEL_WIDTH)] + [point[:, :slim]]
    full[...] = jnp.concatenate(parts, axis=1)
    halve(
        lambda k: full[pl.ds(pl.multiple_of(k * depth, 8), depth), :], kept_ref, sent_ref, bit_of(1)
    )


def fold_kernel(old_ref, got_ref, kept_ref, sent_ref, *, reach):
    halve(lambda k: old_ref[k] + got_ref[k].astype(F32), kept_ref, sent_ref, bit_of(reach))


def adamw(weights_old, first_moment_state, second_mom, gradient, step_rate, decay_rate):
    first_next = BETA_ONE * first_moment_state + (1.0 - BETA_ONE) * gradient
    second_next = BETA_TWO * second_mom + (1.0 - BETA_TWO) * gradient * gradient
    corrected = (
        first_next
        / (1.0 - BETA_ONE**STEP)
        / (jnp.sqrt(second_next / (1.0 - BETA_TWO**STEP)) + ADAM_EPS)
    )
    weights_new = weights_old - step_rate * (corrected + decay_rate * weights_old)
    return (first_next, second_next, weights_new)


def first_half_kernel(mask_ref, own_ref, *refs):
    up_ref, term, weight, grad = refs[-4:]
    count = (len(refs) - 4 + 1) // 2
    grads, weights = refs[: count - 1], refs[count - 1 : -4]
    wide = KERNEL_WIDTH * LANES
    term[:, :wide] = own_ref[...]
    for r, part in enumerate(grads):
        terms_of(part, grad, term, (r + 1) * wide, mask_ref)
    for r, piece in enumerate(weights):
        weight[:, r * wide : (r + 1) * wide] = piece[...]
    for at in range(0, up_ref.shape[1], 256):
        part = slice(at, at + 256)
        up_ref[:, part] = lax.dot_general(
            term[...], weight[part, :], LANE_DIMS, preferred_element_type=F32
        )


def second_half_kernel(mask_ref, x_ref, slope_ref, vec_ref, part_ref, weight_ref, *refs):
    grads, (d_ref, sum_ref, term, grad) = refs[:-4], refs[-4:]
    rows, width = x_ref.shape
    wide = KERNEL_WIDTH * LANES
    for r, part in enumerate(grads):
        terms_of(part, grad, term, r * wide, mask_ref)
    for at in range(0, width, 256):
        part = slice(at, at + 256)
        up = lax.dot_general(term[...], weight_ref[part, :], LANE_DIMS, preferred_element_type=F32)
        d = (up + part_ref[:, part]) * slope_ref[:, part]
        d_ref[:, part] = d
        centered = x_ref[:, part].astype(F32) * vec_ref[0:1, part] + vec_ref[1:2, part]
        sum_ref[0:1, part] = jnp.sum(d * centered, 0, keepdims=True)
        sum_ref[1:2, part] = jnp.sum(d, 0, keepdims=True)


def final_kernel(
    x_ref, cot_ref, d_ref, vec_ref, one_ref, two_ref, old_ref, got_ref, mid_ref, *refs, bin_count, chunks
):
    states, outs, refs = refs[:12], refs[12:25], refs[25:]
    held, news, out_ref, sems = refs[:12], refs[12:24], refs[24], refs[25]
    fetches = [
        pltpu.make_async_copy(src, dst, sems.at[k]) for k, (src, dst) in enumerate(zip(states, held))
    ]
    for fetch in fetches:
        fetch.start()
    rows, width = x_ref.shape
    total = one_ref[...] + two_ref[...]
    root, offset, scale = vec_ref[0:1, :], vec_ref[1:2, :], vec_ref[2:3, :]
    pull = scale * total[0:1] / bin_count
    slant = pull * root
    level = scale * total[1:2] / bin_count + pull * offset
    step = 16
    chunk = rows // chunks

    def body(i, carry):
        at = pl.ds(pl.multiple_of(i * step, 16), step)
        value = x_ref[at, :].astype(F32) * slant + level
        out_ref[at, :] = cot_ref[at, :].astype(F32) + (d_ref[at, :] * scale - value)
        return carry

    sends = []
    for k in range(chunks):
        lax.fori_loop(k * chunk // step, (k + 1) * chunk // step, body, 0, unroll=4)
        part = pl.ds(k * chunk, chunk)
        sends.append(pltpu.make_async_copy(out_ref.at[part], outs[0].at[part], sems.at[24 + k]))
        sends[-1].start()
    for fetch in fetches:
        fetch.wait()

    def step_of(first, at, grad, rate, decay):
        new = adamw(*(ref[at] for ref in held[first : first + 3]), grad, rate, decay)
        for ref, value in zip(news[first : first + 3], new):
            ref[at] = value

    slim = held[3].shape[2]
    both = old_ref[0] + got_ref[0].astype(F32)
    step_of(0, ..., total, RATE_NORM, 0.0)
    for j in range(KERNEL_WIDTH):
        step_of(3, j, both[:, j * slim : (j + 1) * slim], RATE_WEIGHT, DECAY_WEIGHT)
    step_of(6, ..., both[:, KERNEL_WIDTH * slim :].T, RATE_WEIGHT, DECAY_WEIGHT)
    step_of(9, ..., mid_ref[:, :slim], RATE_NORM, 0.0)
    for k in range(12):
        sends.append(pltpu.make_async_copy(news[k], outs[1 + k], sems.at[12 + k]))
        sends[-1].start()
    for send in sends:
        send.wait()


def flip(axis, reach):
    return [(i, i ^ reach) for i in range(lax.axis_size(axis))]


def relatives_of(order):
    found = [0]
    for reach in order:
        found = found + [r ^ reach for r in found]
    return found


def descending(size):
    return [size >> k for k in range(1, size.bit_length())]


def round_kernel(weight_one, weight_two, one_ref, two_ref, *refs, size, sides):
    count = (len(refs) - 2 - sides) // 3
    rims, outs = refs[: 2 * count], refs[2 * count :]
    weight_ref, out_ref, halves = outs[0], outs[1], outs[2 : 2 + sides]
    if rims:
        outs[-1][...] = rims[1][...]
    count = weight_one.shape[0]
    weight_ref[:count] = weight_one[...]
    weight_ref[count:] = weight_two[...]
    for half, src in zip(halves, (weight_one, weight_two)):
        half[...] = src[...]
    put_sums(out_ref, get_sums(one_ref) + get_sums(two_ref))
    out_ref[SUMS : SUMS + size, :] = one_ref[SUMS : SUMS + size, :]
    out_ref[SUMS + size : SUMS + 2 * size, :] = two_ref[SUMS : SUMS + size, :]
    for rim in rims[:1]:
        height, width = rim.shape
        for k in range(width // LANES):
            at = SUMS + 2 * size + k * height
            out_ref[at : at + height, :] = rim[:, k * LANES : (k + 1) * LANES]


def copy_kernel(*refs):
    count = len(refs) // 2
    for src, out in zip(refs[:count], refs[count:]):
        out[...] = src[...]


def packs(wanted, after):
    arrays, places = [], []
    for pieces in wanted:
        places.append([])
        for piece in pieces:
            array, begin, end = piece if isinstance(piece, tuple) else (piece, 0, piece.shape[0])
            places[-1].append((len(arrays), begin, end))
            arrays.append(array)

    def pack_kernel(*refs):
        for out, group in zip(refs[len(arrays) :], places):
            at = 0
            for index, begin, end in group:
                out[at : at + end - begin, :] = refs[index][begin:end, :]
                at += end - begin

    sizes = [sum(end - begin for _, begin, end in group) for group in places]
    return call(pack_kernel, [((size, LANES), BF16) for size in sizes], arrays, after=after)


def take_kernel(src_ref, weight_ref, pack_ref):
    count, packed = weight_ref.shape[:2]
    weight_ref[...] = src_ref[:count]
    for k in range(pack_ref.shape[0] // packed):
        lanes = slice(k % KERNEL_WIDTH * LANES, (k % KERNEL_WIDTH + 1) * LANES)
        pack_ref[k * packed : (k + 1) * packed, :] = src_ref[count + k // KERNEL_WIDTH, :, lanes]


def copies(arrays, after):
    return call(copy_kernel, [(x.shape, x.dtype) for x in arrays], arrays, after=after)


def add_kernel(one_ref, two_ref, out_ref):
    out_ref[...] = one_ref[...] + two_ref[...]


def add(one, two, after=()):
    return call(add_kernel, [(one.shape, one.dtype)], [one, two], after=after)[0]


def swap(x, axis, reach):
    return lax.ppermute(x, axis, flip(axis, reach))


def gather_parts(x, reaches):
    parts = [x]
    for reach in reaches:
        parts += [swap(part, "ch", reach) for part in parts]
    return parts


def spread(copies, axes):
    return lax.all_to_all(copies, axes, 0, 0, tiled=True)


def shards(
    inputs,
    cotangent,
    starts,
    master_conv,
    first_conv,
    second_conv,
    master_point,
    first_point,
    second_point,
    norm_in,
    first_in,
    second_in,
    norm_mid,
    first_mid,
    second_mid,
):
    rows, width = inputs.shape
    seq_size, ch_size = lax.axis_size("seq"), lax.axis_size("ch")
    bin_count = rows * seq_size
    depth, slim = master_conv.shape[1:]
    tiles = width // LANES
    wide = KERNEL_WIDTH * LANES
    weight_order = descending(seq_size)
    sum_order = weight_order[::-1]
    last_order = weight_order[1::-1] + weight_order[2:]
    point_order = weight_order[:1] + [1] + weight_order[1:-1]
    ch_order = descending(ch_size)
    ext = rows + 2 * EDGE

    rounds = len(weight_order)
    top, lower = ch_order[0], ch_order[1:]
    chunks = 4
    rim = (RIM + EDGE, width // 2)
    packed = 3 * depth // 4 if folds(depth, slim) else depth
    inputs, weight, near, *rims = call(
        first_kernel,
        [
            (inputs.shape, BF16),
            ((1, packed, wide), BF16),
            ((SUMS + up_to(depth, 16), LANES), BF16),
            (rim, BF16),
            (rim, BF16),
        ],
        [inputs, cotangent, master_conv, master_point],
        scratch=[
            ((2, EDGE, width), BF16),
            (master_conv.shape, F32),
            (master_point.shape, F32),
            ((16, LANES), F32),
        ],
        away=(0, 1, 2, 3),
        sems=4 + chunks,
    )
    pairs = [(i, i + 1) for i in range(1, seq_size - 1, 2)]
    ahead, back = call(
        mask_kernel,
        [((KERNEL_WIDTH, ext, LANES), F32), ((KERNEL_WIDTH, rows, LANES), F32)],
        [starts],
        smem=(0,),
        after=[weight],
    )
    parts = [weight]
    for k in range(rounds):
        weight_got = [swap(part, "seq", weight_order[k]) for part in parts]
        near_got = swap(near, "seq", point_order[k])
        if k < rounds - 1:
            size = up_to(depth, 16) << k
            spare = {0: tiles // 2 * rim[0], rounds - 2: 16}.get(k, 0)
            outs = [((2 * weight.shape[0], packed, wide), BF16), ((SUMS + 2 * size + spare, LANES), BF16)]
            sides = 2 if k == rounds - 2 else 0
            outs += [(weight.shape, BF16)] * sides
            join = functools.partial(round_kernel, size=size, sides=sides)
            args = [weight, weight_got[0], near, near_got]
            if k == 0:
                weight, near, far = call(join, outs + [(rim, BF16)], args + rims, after=[back])
                far = lax.ppermute(far, "seq", pairs + [(j, i) for i, j in pairs])
                parts = [weight]
            else:
                if k == 1:
                    (rims,) = call(
                        rim_kernel, [((2 * rim[0] + 16, rim[1]), BF16)], [near_got, far]
                    )
                    other_rims = swap(rims, "ch", 1)
                weight, near, *parts = call(join, outs, args)
                parts = parts or [weight]
    hidden_in, slope_in, vec_in, cotangent = call(
        functools.partial(act_kernel, bin_count=bin_count),
        [((rows, width), BF16), ((rows, width), F32), ((8, width), F32), (cotangent.shape, BF16)],
        [inputs, cotangent, near, near_got, norm_in],
        away=(1,),
        sems=1,
    )
    stack_type = BF16 if depth % 16 == 0 else F32
    upstream, point_own, point_pack = call(
        functools.partial(upstream_kernel, relatives=relatives_of(point_order)),
        [((rows, LANES), F32), ((width, LANES), BF16), ((folded_rows(width, slim), LANES), BF16)],
        [cotangent, near, near_got],
        scratch=[((seq_size, depth, LANES), stack_type)],
    )
    blocks = -(-point_pack.shape[0] // (packed * KERNEL_WIDTH))
    conv_own, conv_out, sums_mid, rims, weight = call(
        functools.partial(
            conv_kernel, relatives=relatives_of(weight_order), slim=slim
        ),
        [
            ((width, wide), BF16),
            ((ext, LANES), F32),
            ((seq_size, 2, LANES), F32),
            ((2, RIM + EDGE, width), BF16),
            ((seq_size + blocks, packed, wide), BF16),
        ],
        [ahead, hidden_in, rims, other_rims, vec_in, point_pack, weight, *weight_got],
        scratch=[
            ((seq_size, depth, wide), stack_type),
            ((rows + 2 * RIM, wide), F32),
            ((2 * RIM, width), BF16),
        ],
        after=[upstream],
    )
    weight = swap(weight, "ch", top)
    got_mid = spread(sums_mid, "seq")
    conv_near = gather_parts(conv_own, lower)
    hidden_mid, d_mid, centered, sent_back, vec_mid = call(
        functools.partial(mid_kernel, bin_count=bin_count),
        [
            ((rows, LANES), BF16),
            ((ext, LANES), F32),
            ((ext, LANES), F32),
            ((seq_size, 2, LANES), F32),
            ((8, LANES), F32),
        ],
        [got_mid, conv_out, upstream, rims, norm_mid, point_own],
        after=conv_near[1:],
    )
    got_back = spread(sent_back, "seq")
    grad_own, total_mid = call(
        functools.partial(conv_back_kernel, bin_count=bin_count, slim=slim),
        [((3 * ext // 4 if folds(ext, slim) else ext, LANES), BF16), ((2, LANES), F32)],
        [got_back, vec_mid, d_mid, centered],
        scratch=[((ext, LANES), F32)],
    )
    grad_near = gather_parts(grad_own, lower)
    grad_far = swap(grad_own, "ch", top)
    weight, point_far = call(
        take_kernel,
        [((seq_size, packed, wide), BF16), (point_pack.shape, BF16)],
        [weight],
        after=[grad_own],
    )
    side = ch_size // 2 * wide
    (conv_far,) = call(
        functools.partial(place_kernel, relatives=relatives_of(weight_order), slim=slim),
        [((width, side), BF16)],
        gather_parts(weight, lower),
        scratch=[((seq_size, depth, wide), stack_type)],
    )
    half = seq_size // 2
    hidden_rows = folded_rows(rows, slim)
    terms, kept, sent = call(
        functools.partial(weight_grad_kernel, depth=depth, slim=slim),
        [
            ((rows, wide), BF16),
            ((half, depth, 4 * slim), F32),
            ((half, depth, 4 * slim), BF16),
        ],
        [back, grad_own, hidden_in, cotangent, hidden_mid],
        scratch=[((ext, LANES), F32), ((width, 4 * slim), F32)],
    )
    (up_part,) = call(
        first_half_kernel,
        [((rows, width), F32)],
        [back, terms, *grad_near[1:], *conv_near],
        scratch=[((rows, side), BF16), ((width, side), BF16), ((ext, LANES), F32)],
    )
    grad_far = gather_parts(copies([grad_far], [up_part, conv_far])[0], lower)
    count = point_far.shape[0]
    cuts = [up_to(k * count // 100, 16) for k in (39, 52)]
    hidden_pack, both = call(
        operands_kernel,
        [((hidden_rows, LANES), BF16), ((hidden_rows + count + cuts[0], LANES), BF16)],
        [hidden_mid, point_pack, point_far],
        after=[sent],
    )
    both_parts = gather_parts(both, lower)
    d_in, sums_back = call(
        second_half_kernel,
        [((rows, width), F32), ((2, width), F32)],
        [back, inputs, slope_in, vec_in, up_part, conv_far, *grad_far],
        scratch=[((rows, side), BF16), ((ext, LANES), F32)],
    )
    total_back = sums_back
    hidden_far = swap(hidden_pack, "ch", top)
    placed = []
    scratch = [((size, ch_size // 2 * LANES), BF16) for size in (rows, width)]
    for k, reach in enumerate(sum_order):
        total_got = swap(total_back, "seq", last_order[k])
        got = swap(sent, "seq", reach)
        if k < rounds - 1:
            half //= 2
            kept, sent = call(
                functools.partial(fold_kernel, reach=2 * reach),
                [((half, depth, 4 * slim), F32), ((half, depth, 4 * slim), BF16)],
                [kept, got],
                after=[total_back, *placed] if k else [],
            )
            total_back = add(total_back, total_got)
        if k == rounds - 3:
            (first,) = packs([[hidden_far, (point_far, *cuts)]], [total_back])
            first_parts = gather_parts(first, lower)
            near_sum, *placed = call(
                functools.partial(near_kernel, slim=slim),
                [((rows, width), F32), ((8, LANES), F32)],
                both_parts,
                scratch=scratch,
                after=[total_back],
            )
        if k == rounds - 2:
            (last,) = packs([[(point_far, cuts[1], count)]], [total_back])
            last_parts = gather_parts(last, lower)
    far_parts = [x for group in zip(both_parts, first_parts, last_parts) for x in group]
    block_out, token = call(
        functools.partial(out_kernel, slim=slim),
        [((rows, width), BF16), ((8, LANES), F32)],
        [inputs, near_sum, *far_parts],
        scratch=scratch,
        after=[total_back],
    )
    states = [norm_in, first_in, second_in, master_conv, first_conv, second_conv]
    states += [master_point, first_point, second_point, norm_mid, first_mid, second_mid]
    arrays = [inputs, cotangent, d_in, vec_in, total_back, total_got, kept, got, total_mid]
    small = [(x.shape, F32) for x in states]
    input_grad, *news = call(
        functools.partial(final_kernel, bin_count=bin_count, chunks=4),
        [((rows, width), F32)] + small,
        arrays + states,
        scratch=small + small + [((rows, width), F32)],
        away=range(len(arrays), len(arrays) + 12),
        away_outs=range(13),
        sems=24 + 4,
        after=[token],
    )
    return (block_out, input_grad, *news[3:9], *news[:3], *news[9:])


def solution(mesh):
    in_specs = (
        P("seq", None),
        P("seq", None),
        P(),
        P(None, "seq", "ch"),
        P(None, "seq", "ch"),
        P(None, "seq", "ch"),
        P("ch", "seq"),
        P("ch", "seq"),
        P("ch", "seq"),
        P(),
        P(),
        P(),
        P(None, "ch"),
        P(None, "ch"),
        P(None, "ch"),
    )
    out_specs = (
        P("seq", None),
        P("seq", None),
        P(None, "seq", "ch"),
        P(None, "seq", "ch"),
        P(None, "seq", "ch"),
        P("ch", "seq"),
        P("ch", "seq"),
        P("ch", "seq"),
        P(),
        P(),
        P(),
        P(None, "ch"),
        P(None, "ch"),
        P(None, "ch"),
    )
    return jax.shard_map(shards, mesh=mesh, in_specs=in_specs, out_specs=out_specs, check_vma=False)
```

```python
import functools

import jax
import jax.numpy as jnp
from jax import lax
from jax.experimental import pallas as pl
from jax.experimental.pallas import tpu as pltpu
from jax.sharding import PartitionSpec as P

KERNEL_WIDTH = 3
DILATION_BINS = 9
WIN = 1024
STEP = 10

NORM_EPS = 1e-05
ADAM_EPS = 1e-08
BETA_ONE = 0.9
BETA_TWO = 0.999
RATE_WEIGHT = 0.05
RATE_NORM = 0.5
DECAY_WEIGHT = 0.01

LANES = 128
EDGE = 16
RIM = 2 * EDGE
SUMS = 48
GELU_A = 0.7978845608028654
GELU_B = 0.044715
SHIFTS = [(j - KERNEL_WIDTH // 2) * DILATION_BINS for j in range(KERNEL_WIDTH)]
ROW_DIMS = (((0,), (0,)), ((), ()))
LANE_DIMS = (((1,), (1,)), ((), ()))
F32, BF16 = jnp.float32, jnp.bfloat16


def call(body, outs, args, scratch=(), smem=(), away=(), after=(), sems=0, away_outs=(), limit=16):
    spaces = [pltpu.SMEM if k in smem else pltpu.VMEM for k in range(len(args))]
    spaces = [pltpu.HBM if k in away else space for k, space in enumerate(spaces)]
    spaces += [pl.ANY] * len(after)

    args = [
        pltpu.with_memory_space_constraint(x, pltpu.HBM) if k in away else x
        for k, x in enumerate(args)
    ]

    def kernel(*refs):
        body(*refs[: len(args)], *refs[len(spaces) :])

    return pl.pallas_call(
        kernel,
        out_shape=[jax.ShapeDtypeStruct(s, t) for s, t in outs],
        in_specs=[pl.BlockSpec(memory_space=s) for s in spaces],
        out_specs=[
            pl.BlockSpec(memory_space=pltpu.HBM if k in away_outs else pltpu.VMEM)
            for k in range(len(outs))
        ],
        scratch_shapes=[pltpu.VMEM(s, t) for s, t in scratch]
        + [pltpu.SemaphoreType.DMA((sems,))] * (sems > 0),
        compiler_params=pltpu.CompilerParams(vmem_limit_bytes=limit * 2**20),
        cost_estimate=pl.CostEstimate(flops=1, bytes_accessed=1, transcendentals=0),
        name=getattr(body, "func", body).__name__,
    )(*args, *after)


def up_to(size, step):
    return -(-size // step) * step


def split_three(v):
    high = v.astype(BF16).astype(F32)
    rest = v - high
    middle = rest.astype(BF16).astype(F32)
    return high, middle, rest - middle


def gelu_and_slope(v):
    square = v * v
    t = jnp.tanh(v * (GELU_A + (GELU_A * GELU_B) * square))
    half = 0.5 * (1.0 + t)
    slope = half + (0.5 * v) * (1.0 - t * t) * (GELU_A + (3.0 * GELU_A * GELU_B) * square)
    return v * half, slope


def reach_of(first, count, shift, start, bin_count):
    here = first + lax.broadcasted_iota(jnp.int32, (count, LANES), 0)
    there = here + shift
    inside = (here >= 0) & (here < bin_count) & (there >= 0) & (there < bin_count)
    return inside & (((here - start) >> 10) == ((there - start) >> 10))


def folds(depth, slim):
    return 3 * (LANES - slim) == slim and depth % 32 == 0


def fold_rows(block):
    rows, slim = block.shape
    quarter, width = rows // 4, LANES - slim
    side = [block[3 * quarter :, p * width : (p + 1) * width] for p in range(3)]
    return jnp.concatenate([block[: 3 * quarter], jnp.concatenate(side, axis=0)], axis=1)


def unfold_rows(block, slim):
    quarter, width = block.shape[0] // 3, LANES - slim
    side = [block[p * quarter : (p + 1) * quarter, slim:] for p in range(3)]
    side.append(jnp.zeros((quarter, width), block.dtype))
    lane = lax.broadcasted_iota(jnp.int32, block.shape, 1)
    return jnp.concatenate([jnp.where(lane < slim, block, 0.0), jnp.concatenate(side, axis=1)], axis=0)


def folded_rows(rows, slim):
    return 3 * rows // 4 if folds(rows, slim) else rows


def put_folded(block, out_ref):
    if out_ref.shape[0] < block.shape[0]:
        block = fold_rows(block[:, : 3 * LANES // 4].astype(F32)).astype(BF16)
    out_ref[...] = block


def get_folded(block, rows):
    if block.shape[0] < rows:
        block = unfold_rows(block.astype(F32), 3 * LANES // 4).astype(BF16)
    return block


def first_kernel(
    x_hbm, cot_hbm, conv_hbm, point_hbm, x_ref, weight_ref, near_ref, near_rim, far_rim, edge_ref, conv_ref, point_ref, sum_ref, sems
):
    rows, width = x_ref.shape
    tiles = width // LANES
    depth, slim = conv_ref.shape[1:]
    chunks = sems.shape[0] - 4
    chunk = rows // chunks
    copies = [
        pltpu.make_async_copy(conv_hbm, conv_ref, sems.at[0]),
        pltpu.make_async_copy(point_hbm, point_ref, sems.at[1]),
        pltpu.make_async_copy(cot_hbm.at[pl.ds(0, EDGE)], edge_ref.at[0], sems.at[2]),
        pltpu.make_async_copy(cot_hbm.at[pl.ds(rows - EDGE, EDGE)], edge_ref.at[1], sems.at[3]),
    ]
    for k in range(chunks):
        part = pl.ds(k * chunk, chunk)
        copies.append(pltpu.make_async_copy(x_hbm.at[part], x_ref.at[part], sems.at[4 + k]))
    for copy in copies:
        copy.start()
    weight_ref[...] = jnp.zeros_like(weight_ref)
    near_ref[...] = jnp.zeros_like(near_ref)
    sum_ref[...] = jnp.zeros_like(sum_ref)
    copies[0].wait()
    for j in range(KERNEL_WIDTH):
        if folds(depth, slim):
            weight_ref[0, :, j * LANES : (j + 1) * LANES] = fold_rows(conv_ref[j]).astype(BF16)
        else:
            weight_ref[0, :, j * LANES : j * LANES + slim] = conv_ref[j].astype(BF16)
    copies[1].wait()
    near_ref[SUMS : SUMS + depth, :slim] = point_ref[...].T.astype(BF16)

    def step(k, carry):
        v = x_ref[pl.ds(pl.multiple_of(k * 32, 32), 32), :].astype(F32)
        v = v.reshape(4, 8, width)
        return carry[0] + v.sum(0), carry[1] + (v * v).sum(0)

    totals = (jnp.zeros((8, width), F32),) * 2
    for k in range(chunks):
        copies[4 + k].wait()
        totals = lax.fori_loop(
            k * chunk // 32, (k + 1) * chunk // 32, step, totals, unroll=chunk // 32
        )
    for stat, total in enumerate(totals):
        total = jnp.sum(total, 0, keepdims=True)
        for k in range(tiles):
            row = stat * tiles + k
            sum_ref[row : row + 1, :] = total[:, k * LANES : (k + 1) * LANES]
    put_sums(near_ref, sum_ref[...])
    copies[2].wait()
    copies[3].wait()
    odd = lax.axis_index("seq") % 2
    lanes = half_of(width, lax.axis_index("ch") % 2)
    for ref, side in ((near_rim, 1 - odd), (far_rim, odd)):
        ref[:RIM, :] = x_ref[pl.ds(pl.multiple_of(side * (rows - RIM), RIM), RIM), lanes]
        ref[RIM:, :] = edge_ref[side, :, lanes]


def half_of(width, core):
    return pl.ds(pl.multiple_of(core * (width // 2), LANES), width // 2)


def put_sums(ref, value):
    for p, part in enumerate(split_three(value)):
        ref[p * 16 : (p + 1) * 16, :] = part.astype(BF16)


def get_sums(ref):
    return sum(ref[p * 16 : (p + 1) * 16, :].astype(F32) for p in range(3))


def act_kernel(
    x_ref, cot_hbm, one_ref, two_ref, norm_ref, hid_ref, slope_ref, vec_ref, cot_ref, sems, *, bin_count
):
    copy = pltpu.make_async_copy(cot_hbm, cot_ref, sems.at[0])
    copy.start()
    rows, width = x_ref.shape
    tiles = width // LANES
    total = get_sums(one_ref) + get_sums(two_ref)
    for k in range(tiles):
        lanes = slice(k * LANES, (k + 1) * LANES)
        mean = total[k : k + 1, :] / bin_count
        square = total[tiles + k : tiles + k + 1, :] / bin_count
        root = lax.rsqrt(square - mean * mean + NORM_EPS)
        gain = root * norm_ref[0:1, lanes]
        vec_ref[0:1, lanes] = root
        vec_ref[1:2, lanes] = -mean * root
        vec_ref[2:3, lanes] = gain
        vec_ref[3:4, lanes] = norm_ref[1:2, lanes] - mean * gain

    gain, offset = vec_ref[2:3, :], vec_ref[3:4, :]

    def step(k, carry):
        at = pl.multiple_of(k * 16, 16)
        v = x_ref[pl.ds(at, 16), :].astype(F32) * gain + offset
        hidden, slope = gelu_and_slope(v)
        hid_ref[pl.ds(at, 16), :] = hidden.astype(BF16)
        slope_ref[pl.ds(at, 16), :] = slope
        return carry

    lax.fori_loop(0, rows // 16, step, 0, unroll=2)
    copy.wait()


def place(pieces, relatives, stack, own, slim):
    depth = stack.shape[1]
    at = 0
    for piece in pieces:
        for k in range(piece.shape[0]):
            block = piece[k].astype(F32)
            for j in range(KERNEL_WIDTH):
                part = block[:, j * LANES : (j + 1) * LANES]
                if folds(depth, slim):
                    part = unfold_rows(part, slim)
                stack[own ^ relatives[at], :, j * LANES : (j + 1) * LANES] = part.astype(stack.dtype)
            at += 1
    return stack[...].reshape(-1, stack.shape[2]).astype(BF16)


def place_kernel(*refs, relatives, slim):
    pieces, (out_ref, stack) = refs[:-2], refs[-2:]
    wide = stack.shape[2]
    for r, piece in enumerate(pieces):
        block = place([piece], relatives, stack, lax.axis_index("seq"), slim)
        out_ref[:, r * wide : (r + 1) * wide] = block


def rim_kernel(near_ref, far_ref, out_ref):
    height, width = far_ref.shape
    base = near_ref.shape[0] - width // LANES * height
    for k in range(width // LANES):
        at = base + k * height
        out_ref[:height, k * LANES : (k + 1) * LANES] = near_ref[at : at + height, :]
    out_ref[height : 2 * height, :] = far_ref[...]
    out_ref[2 * height :, :] = jnp.zeros_like(out_ref[2 * height :, :])


def mask_kernel(start_ref, ahead_ref, back_ref):
    rows = back_ref.shape[1]
    first = lax.axis_index("seq") * rows
    for j, shift in enumerate(SHIFTS):
        for begin in range(0, rows + RIM, 96):
            count = min(96, rows + RIM - begin)
            mask = reach_of(first + begin - EDGE, count, shift, start_ref[0], rows * lax.axis_size("seq"))
            ahead_ref[j, begin : begin + count, :] = jnp.where(mask, 1.0, 0.0)
        for begin in range(0, rows, 128):
            back_ref[j, begin : begin + 128, :] = ahead_ref[
                j, EDGE + begin - shift : EDGE + begin - shift + 128, :
            ]


def conv_kernel(mask_ref, hid_ref, own_rims, other_rims, vec_ref, pack_ref, *refs, relatives, slim):
    pieces, refs = refs[:-8], refs[-8:]
    weight_ref, out_ref, sum_ref, rim_ref, all_ref, stack, prod, edge = refs
    at, packed = 0, pieces[0].shape[1]
    for piece in pieces:
        all_ref[at : at + piece.shape[0]] = piece[...]
        at += piece.shape[0]
    for k in range(pack_ref.shape[0] // packed):
        lanes = slice(k % KERNEL_WIDTH * LANES, (k % KERNEL_WIDTH + 1) * LANES)
        all_ref[at + k // KERNEL_WIDTH, :, lanes] = pack_ref[k * packed : (k + 1) * packed, :]
    odd, core = lax.axis_index("seq") % 2, lax.axis_index("ch") % 2
    height, width = rim_ref.shape[1:]
    for half, owner in ((own_rims, core), (other_rims, 1 - core)):
        rim_ref[1 - odd, :, half_of(width, owner)] = half[:height, :]
        rim_ref[odd, :, half_of(width, owner)] = half[height : 2 * height, :]
    for side in range(2):
        for k in range(0, RIM, 16):
            v = rim_ref[side, k : k + 16, :].astype(F32) * vec_ref[2:3, :] + vec_ref[3:4, :]
            edge[side * RIM + k : side * RIM + k + 16, :] = gelu_and_slope(v)[0].astype(BF16)
    rows = hid_ref.shape[0]
    weight_ref[...] = place(pieces, relatives, stack, lax.axis_index("seq"), slim)
    for at in range(0, weight_ref.shape[1], 256):
        part = slice(at, min(at + 256, weight_ref.shape[1]))
        prod[RIM : RIM + rows, part] = jnp.dot(
            hid_ref[...], weight_ref[:, part], preferred_element_type=F32
        )
        sides = jnp.dot(edge[...], weight_ref[:, part], preferred_element_type=F32)
        prod[:RIM, part] = sides[:RIM]
        prod[RIM + rows :, part] = sides[RIM:]

    def rows_of(begin, count):
        value = 0.0
        for j, shift in enumerate(SHIFTS):
            part = prod[begin + EDGE + shift : begin + EDGE + shift + count, j * LANES : (j + 1) * LANES]
            value = value + mask_ref[j, begin : begin + count, :] * part
        out_ref[begin : begin + count, :] = value
        return value

    rows_of(0, EDGE)
    rows_of(EDGE + rows, EDGE)
    one = two = jnp.zeros((8, LANES), F32)
    step = 128
    for k in range(rows // step):
        value = rows_of(EDGE + k * step, step).reshape(step // 8, 8, LANES)
        one = one + value.sum(0)
        two = two + (value * value).sum(0)
    one, two = jnp.sum(one, 0, keepdims=True), jnp.sum(two, 0, keepdims=True)
    for d in range(sum_ref.shape[0]):
        sum_ref[d, 0:1, :] = one
        sum_ref[d, 1:2, :] = two


def upstream_kernel(cot_ref, one_ref, two_ref, up_ref, point_ref, pack_ref, stack, *, relatives):
    rows = cot_ref.shape[0]
    depth = stack.shape[1]
    own = lax.axis_index("seq")
    count = len(relatives) // 2
    for k, relative in enumerate(relatives):
        piece = (one_ref, two_ref)[k // count]
        at = SUMS + (k % count) * up_to(depth, 16)
        stack[own ^ relative] = piece[at : at + depth, :].astype(stack.dtype)
    point_ref[...] = stack[...].reshape(point_ref.shape).astype(BF16)
    put_folded(point_ref[...], pack_ref)
    up_ref[...] = jnp.dot(cot_ref[...], point_ref[...], preferred_element_type=F32)


def mid_kernel(
    got_ref, conv_ref, up_ref, rim_ref, norm_ref, point_ref, hid_ref, d_ref, cen_ref, sent_ref, vec_ref, *, bin_count
):
    rows = hid_ref.shape[0]
    slim = norm_ref.shape[1]
    total = got_ref[0]
    for s in range(1, got_ref.shape[0]):
        total = total + got_ref[s]
    mean = total[0:1] / bin_count
    root = lax.rsqrt(total[1:2] / bin_count - mean * mean + NORM_EPS)
    vec_ref[...] = jnp.zeros_like(vec_ref)
    vec_ref[0:1, :] = root
    vec_ref[1:3, :slim] = norm_ref[...]
    gain, bias = vec_ref[1:2, :], vec_ref[2:3, :]

    def rows_of(begin, count, up):
        centered = (conv_ref[pl.ds(begin, count), :] - mean) * root
        hidden, slope = gelu_and_slope(centered * gain + bias)
        d = up * slope
        cen_ref[pl.ds(begin, count), :] = centered
        d_ref[pl.ds(begin, count), :] = d
        return centered, hidden, d

    for side, begin in enumerate((0, EDGE + rows)):
        up = jnp.dot(rim_ref[side, RIM:, :], point_ref[...], preferred_element_type=F32)
        rows_of(begin, EDGE, up)
    step = 64

    def body(i, carry):
        begin = pl.multiple_of(EDGE + i * step, 16)
        up = up_ref[pl.ds(pl.multiple_of(i * step, 16), step), :]
        centered, hidden, d = rows_of(begin, step, up)
        hid_ref[pl.ds(pl.multiple_of(i * step, 16), step), :] = hidden.astype(BF16)
        d = d.reshape(step // 8, 8, LANES)
        return carry[0] + (d * centered.reshape(d.shape)).sum(0), carry[1] + d.sum(0)

    zero = jnp.zeros((8, LANES), F32)
    gain_sum, bias_sum = lax.fori_loop(0, rows // step, body, (zero, zero), unroll=2)
    gain_sum = jnp.sum(gain_sum, 0, keepdims=True)
    bias_sum = jnp.sum(bias_sum, 0, keepdims=True)
    for d in range(sent_ref.shape[0]):
        sent_ref[d, 0:1, :] = gain_sum
        sent_ref[d, 1:2, :] = bias_sum


def conv_back_kernel(got_ref, vec_ref, d_ref, cen_ref, grad_ref, total_ref, grad, *, bin_count, slim):
    total = got_ref[0]
    for s in range(1, got_ref.shape[0]):
        total = total + got_ref[s]
    total_ref[...] = total
    scale = vec_ref[0:1, :] * vec_ref[1:2, :]
    pull, level = total[0:1] / bin_count, total[1:2] / bin_count
    count = d_ref.shape[0]
    for begin in range(0, count, 96):
        part = slice(begin, min(begin + 96, count))
        grad[part, :] = scale * (d_ref[part, :] - level - cen_ref[part, :] * pull)
    if folds(count, slim):
        grad_ref[...] = fold_rows(grad[:, :slim]).astype(BF16)
    else:
        grad_ref[...] = grad[...].astype(BF16)


def near_kernel(*refs, slim):
    parts, (sum_ref, token_ref, hidden, point) = refs[:-4], refs[-4:]
    token_ref[...] = jnp.zeros_like(token_ref)
    rows, width = hidden.shape[0], point.shape[0]
    count, end = folded_rows(rows, slim), folded_rows(rows, slim) + folded_rows(width, slim)
    for r, part in enumerate(parts):
        lanes = slice(r * LANES, (r + 1) * LANES)
        hidden[:, lanes] = get_folded(part[:count, :], rows)
        point[:, lanes] = get_folded(part[count:end, :], width)
    for at in range(0, width, 256):
        part = slice(at, at + 256)
        sum_ref[:, part] = lax.dot_general(
            hidden[...], point[part, :], LANE_DIMS, preferred_element_type=F32
        )


def out_kernel(x_ref, near_ref, *refs, slim):
    parts, (out_ref, token_ref, hidden, point) = refs[:-4], refs[-4:]
    token_ref[...] = jnp.zeros_like(token_ref)
    rows, width = x_ref.shape
    count, end = folded_rows(rows, slim), folded_rows(rows, slim) + folded_rows(width, slim)
    for r in range(len(parts) // 3):
        lanes = slice(r * LANES, (r + 1) * LANES)
        first, middle, last = parts[3 * r : 3 * r + 3]
        hidden[:, lanes] = get_folded(middle[:count, :], rows)
        pieces = [first[end:, :], middle[count:, :], last[...]]
        point[:, lanes] = get_folded(jnp.concatenate(pieces, axis=0), width)
    for at in range(0, width, 256):
        part = slice(at, at + 256)
        branch = near_ref[:, part] + lax.dot_general(
            hidden[...], point[part, :], LANE_DIMS, preferred_element_type=F32
        )
        out_ref[:, part] = (x_ref[:, part].astype(F32) + branch).astype(BF16)


def operands_kernel(mid_ref, point_ref, far_ref, pack_ref, both_ref):
    put_folded(mid_ref[...], pack_ref)
    at = 0
    for src in (pack_ref, point_ref):
        both_ref[at : at + src.shape[0], :] = src[...]
        at += src.shape[0]
    both_ref[at:, :] = far_ref[: both_ref.shape[0] - at, :]


def halve(blocks, kept_ref, sent_ref, high):
    for k in range(kept_ref.shape[0]):
        kept_ref[k] = blocks(2 * k + high)
        sent_ref[k] = blocks(2 * k + 1 - high).astype(BF16)


def bit_of(reach):
    return (lax.axis_index("seq") // reach) % 2


def terms_of(part, grad, term_ref, at, mask_ref):
    rows = term_ref.shape[0]
    step = 64
    count = part.shape[0]
    grad[:count, :] = part[...].astype(F32)
    if count < grad.shape[0]:
        quarter = count // 3
        width = LANES // 4
        side = [grad[p * quarter : (p + 1) * quarter, 3 * width :] for p in range(3)]
        grad[count:, :] = jnp.concatenate(side + [jnp.zeros((quarter, width), F32)], axis=1)
    for j, shift in enumerate(SHIFTS):
        lanes = slice(at + j * LANES, at + (j + 1) * LANES)
        for begin in range(0, rows, step):
            value = grad[EDGE + begin - shift : EDGE + begin - shift + step, :]
            value = value * mask_ref[j, begin : begin + step, :]
            term_ref[begin : begin + step, lanes] = value.astype(BF16)


def weight_grad_kernel(
    mask_ref, part_ref, hid_ref, cot_ref, mid_ref, term_ref, kept_ref, sent_ref, grad, full, *, depth, slim
):
    rows = term_ref.shape[0]
    terms_of(part_ref, grad, term_ref, 0, mask_ref)
    taps = lax.dot_general(
        hid_ref[...], term_ref[...], ROW_DIMS, preferred_element_type=F32
    )
    point = lax.dot_general(mid_ref[...], cot_ref[...], ROW_DIMS, preferred_element_type=F32).T
    parts = [taps[:, j * LANES : j * LANES + slim] for j in range(KERNEL_WIDTH)] + [point[:, :slim]]
    full[...] = jnp.concatenate(parts, axis=1)
    halve(
        lambda k: full[pl.ds(pl.multiple_of(k * depth, 8), depth), :], kept_ref, sent_ref, bit_of(1)
    )


def fold_kernel(old_ref, got_ref, kept_ref, sent_ref, *, reach):
    halve(lambda k: old_ref[k] + got_ref[k].astype(F32), kept_ref, sent_ref, bit_of(reach))


def adamw(weights_old, first_moment_state, second_mom, gradient, step_rate, decay_rate):
    first_next = BETA_ONE * first_moment_state + (1.0 - BETA_ONE) * gradient
    second_next = BETA_TWO * second_mom + (1.0 - BETA_TWO) * gradient * gradient
    corrected = (
        first_next
        / (1.0 - BETA_ONE**STEP)
        / (jnp.sqrt(second_next / (1.0 - BETA_TWO**STEP)) + ADAM_EPS)
    )
    weights_new = weights_old - step_rate * (corrected + decay_rate * weights_old)
    return (first_next, second_next, weights_new)


def first_half_kernel(mask_ref, own_ref, *refs):
    up_ref, term, weight, grad = refs[-4:]
    count = (len(refs) - 4 + 1) // 2
    grads, weights = refs[: count - 1], refs[count - 1 : -4]
    wide = KERNEL_WIDTH * LANES
    term[:, :wide] = own_ref[...]
    for r, part in enumerate(grads):
        terms_of(part, grad, term, (r + 1) * wide, mask_ref)
    for r, piece in enumerate(weights):
        weight[:, r * wide : (r + 1) * wide] = piece[...]
    for at in range(0, up_ref.shape[1], 256):
        part = slice(at, at + 256)
        up_ref[:, part] = lax.dot_general(
            term[...], weight[part, :], LANE_DIMS, preferred_element_type=F32
        )


def second_half_kernel(mask_ref, x_ref, slope_ref, vec_ref, part_ref, weight_ref, *refs):
    grads, (d_ref, sum_ref, term, grad) = refs[:-4], refs[-4:]
    rows, width = x_ref.shape
    wide = KERNEL_WIDTH * LANES
    for r, part in enumerate(grads):
        terms_of(part, grad, term, r * wide, mask_ref)
    for at in range(0, width, 256):
        part = slice(at, at + 256)
        up = lax.dot_general(term[...], weight_ref[part, :], LANE_DIMS, preferred_element_type=F32)
        d = (up + part_ref[:, part]) * slope_ref[:, part]
        d_ref[:, part] = d
        centered = x_ref[:, part].astype(F32) * vec_ref[0:1, part] + vec_ref[1:2, part]
        sum_ref[0:1, part] = jnp.sum(d * centered, 0, keepdims=True)
        sum_ref[1:2, part] = jnp.sum(d, 0, keepdims=True)


def final_kernel(
    x_ref, cot_ref, d_ref, vec_ref, one_ref, two_ref, old_ref, got_ref, mid_ref, *refs, bin_count, chunks
):
    states, outs, refs = refs[:12], refs[12:25], refs[25:]
    held, news, out_ref, sems = refs[:12], refs[12:24], refs[24], refs[25]
    fetches = [
        pltpu.make_async_copy(src, dst, sems.at[k]) for k, (src, dst) in enumerate(zip(states, held))
    ]
    for fetch in fetches:
        fetch.start()
    rows, width = x_ref.shape
    total = one_ref[...] + two_ref[...]
    root, offset, scale = vec_ref[0:1, :], vec_ref[1:2, :], vec_ref[2:3, :]
    pull = scale * total[0:1] / bin_count
    slant = pull * root
    level = scale * total[1:2] / bin_count + pull * offset
    step = 16
    chunk = rows // chunks

    def body(i, carry):
        at = pl.ds(pl.multiple_of(i * step, 16), step)
        value = x_ref[at, :].astype(F32) * slant + level
        out_ref[at, :] = cot_ref[at, :].astype(F32) + (d_ref[at, :] * scale - value)
        return carry

    sends = []
    for k in range(chunks):
        lax.fori_loop(k * chunk // step, (k + 1) * chunk // step, body, 0, unroll=4)
        part = pl.ds(k * chunk, chunk)
        sends.append(pltpu.make_async_copy(out_ref.at[part], outs[0].at[part], sems.at[24 + k]))
        sends[-1].start()
    for fetch in fetches:
        fetch.wait()

    def step_of(first, at, grad, rate, decay):
        new = adamw(*(ref[at] for ref in held[first : first + 3]), grad, rate, decay)
        for ref, value in zip(news[first : first + 3], new):
            ref[at] = value

    slim = held[3].shape[2]
    both = old_ref[0] + got_ref[0].astype(F32)
    step_of(0, ..., total, RATE_NORM, 0.0)
    for j in range(KERNEL_WIDTH):
        step_of(3, j, both[:, j * slim : (j + 1) * slim], RATE_WEIGHT, DECAY_WEIGHT)
    step_of(6, ..., both[:, KERNEL_WIDTH * slim :].T, RATE_WEIGHT, DECAY_WEIGHT)
    step_of(9, ..., mid_ref[:, :slim], RATE_NORM, 0.0)
    for k in range(12):
        sends.append(pltpu.make_async_copy(news[k], outs[1 + k], sems.at[12 + k]))
        sends[-1].start()
    for send in sends:
        send.wait()


def flip(axis, reach):
    return [(i, i ^ reach) for i in range(lax.axis_size(axis))]


def relatives_of(order):
    found = [0]
    for reach in order:
        found = found + [r ^ reach for r in found]
    return found


def descending(size):
    return [size >> k for k in range(1, size.bit_length())]


def round_kernel(weight_one, weight_two, one_ref, two_ref, *refs, size, sides):
    count = (len(refs) - 2 - sides) // 3
    rims, outs = refs[: 2 * count], refs[2 * count :]
    weight_ref, out_ref, halves = outs[0], outs[1], outs[2 : 2 + sides]
    if rims:
        outs[-1][...] = rims[1][...]
    count = weight_one.shape[0]
    weight_ref[:count] = weight_one[...]
    weight_ref[count:] = weight_two[...]
    for half, src in zip(halves, (weight_one, weight_two)):
        half[...] = src[...]
    put_sums(out_ref, get_sums(one_ref) + get_sums(two_ref))
    out_ref[SUMS : SUMS + size, :] = one_ref[SUMS : SUMS + size, :]
    out_ref[SUMS + size : SUMS + 2 * size, :] = two_ref[SUMS : SUMS + size, :]
    for rim in rims[:1]:
        height, width = rim.shape
        for k in range(width // LANES):
            at = SUMS + 2 * size + k * height
            out_ref[at : at + height, :] = rim[:, k * LANES : (k + 1) * LANES]


def copy_kernel(*refs):
    count = len(refs) // 2
    for src, out in zip(refs[:count], refs[count:]):
        out[...] = src[...]


def packs(wanted, after):
    arrays, places = [], []
    for pieces in wanted:
        places.append([])
        for piece in pieces:
            array, begin, end = piece if isinstance(piece, tuple) else (piece, 0, piece.shape[0])
            places[-1].append((len(arrays), begin, end))
            arrays.append(array)

    def pack_kernel(*refs):
        for out, group in zip(refs[len(arrays) :], places):
            at = 0
            for index, begin, end in group:
                out[at : at + end - begin, :] = refs[index][begin:end, :]
                at += end - begin

    sizes = [sum(end - begin for _, begin, end in group) for group in places]
    return call(pack_kernel, [((size, LANES), BF16) for size in sizes], arrays, after=after)


def take_kernel(src_ref, weight_ref, pack_ref):
    count, packed = weight_ref.shape[:2]
    weight_ref[...] = src_ref[:count]
    for k in range(pack_ref.shape[0] // packed):
        lanes = slice(k % KERNEL_WIDTH * LANES, (k % KERNEL_WIDTH + 1) * LANES)
        pack_ref[k * packed : (k + 1) * packed, :] = src_ref[count + k // KERNEL_WIDTH, :, lanes]


def copies(arrays, after):
    return call(copy_kernel, [(x.shape, x.dtype) for x in arrays], arrays, after=after)


def add_kernel(one_ref, two_ref, out_ref):
    out_ref[...] = one_ref[...] + two_ref[...]


def add(one, two, after=()):
    return call(add_kernel, [(one.shape, one.dtype)], [one, two], after=after)[0]


def swap(x, axis, reach):
    return lax.ppermute(x, axis, flip(axis, reach))


def gather_parts(x, reaches):
    parts = [x]
    for reach in reaches:
        parts += [swap(part, "ch", reach) for part in parts]
    return parts


def spread(copies, axes):
    return lax.all_to_all(copies, axes, 0, 0, tiled=True)


def shards(
    inputs,
    cotangent,
    starts,
    master_conv,
    first_conv,
    second_conv,
    master_point,
    first_point,
    second_point,
    norm_in,
    first_in,
    second_in,
    norm_mid,
    first_mid,
    second_mid,
):
    rows, width = inputs.shape
    seq_size, ch_size = lax.axis_size("seq"), lax.axis_size("ch")
    bin_count = rows * seq_size
    depth, slim = master_conv.shape[1:]
    tiles = width // LANES
    wide = KERNEL_WIDTH * LANES
    weight_order = descending(seq_size)
    sum_order = weight_order[::-1]
    last_order = weight_order[1::-1] + weight_order[2:]
    point_order = weight_order[:1] + [1] + weight_order[1:-1]
    ch_order = descending(ch_size)
    ext = rows + 2 * EDGE

    rounds = len(weight_order)
    top, lower = ch_order[0], ch_order[1:]
    chunks = 2
    rim = (RIM + EDGE, width // 2)
    packed = 3 * depth // 4 if folds(depth, slim) else depth
    inputs, weight, near, *rims = call(
        first_kernel,
        [
            (inputs.shape, BF16),
            ((1, packed, wide), BF16),
            ((SUMS + up_to(depth, 16), LANES), BF16),
            (rim, BF16),
            (rim, BF16),
        ],
        [inputs, cotangent, master_conv, master_point],
        scratch=[
            ((2, EDGE, width), BF16),
            (master_conv.shape, F32),
            (master_point.shape, F32),
            ((16, LANES), F32),
        ],
        away=(0, 1, 2, 3),
        sems=4 + chunks,
    )
    pairs = [(i, i + 1) for i in range(1, seq_size - 1, 2)]
    ahead, back = call(
        mask_kernel,
        [((KERNEL_WIDTH, ext, LANES), F32), ((KERNEL_WIDTH, rows, LANES), F32)],
        [starts],
        smem=(0,),
        after=[weight],
    )
    parts = [weight]
    for k in range(rounds):
        weight_got = [swap(part, "seq", weight_order[k]) for part in parts]
        near_got = swap(near, "seq", point_order[k])
        if k < rounds - 1:
            size = up_to(depth, 16) << k
            spare = {0: tiles // 2 * rim[0], rounds - 2: 16}.get(k, 0)
            outs = [((2 * weight.shape[0], packed, wide), BF16), ((SUMS + 2 * size + spare, LANES), BF16)]
            sides = 2 if k == rounds - 2 else 0
            outs += [(weight.shape, BF16)] * sides
            join = functools.partial(round_kernel, size=size, sides=sides)
            args = [weight, weight_got[0], near, near_got]
            if k == 0:
                weight, near, far = call(join, outs + [(rim, BF16)], args + rims, after=[back])
                far = lax.ppermute(far, "seq", pairs + [(j, i) for i, j in pairs])
                parts = [weight]
            else:
                if k == 1:
                    (rims,) = call(
                        rim_kernel, [((2 * rim[0] + 16, rim[1]), BF16)], [near_got, far]
                    )
                    other_rims = swap(rims, "ch", 1)
                weight, near, *parts = call(join, outs, args)
                parts = parts or [weight]
    hidden_in, slope_in, vec_in, cotangent = call(
        functools.partial(act_kernel, bin_count=bin_count),
        [((rows, width), BF16), ((rows, width), F32), ((8, width), F32), (cotangent.shape, BF16)],
        [inputs, cotangent, near, near_got, norm_in],
        away=(1,),
        sems=1,
    )
    stack_type = BF16 if depth % 16 == 0 else F32
    upstream, point_own, point_pack = call(
        functools.partial(upstream_kernel, relatives=relatives_of(point_order)),
        [((rows, LANES), F32), ((width, LANES), BF16), ((folded_rows(width, slim), LANES), BF16)],
        [cotangent, near, near_got],
        scratch=[((seq_size, depth, LANES), stack_type)],
    )
    blocks = -(-point_pack.shape[0] // (packed * KERNEL_WIDTH))
    conv_own, conv_out, sums_mid, rims, weight = call(
        functools.partial(
            conv_kernel, relatives=relatives_of(weight_order), slim=slim
        ),
        [
            ((width, wide), BF16),
            ((ext, LANES), F32),
            ((seq_size, 2, LANES), F32),
            ((2, RIM + EDGE, width), BF16),
            ((seq_size + blocks, packed, wide), BF16),
        ],
        [ahead, hidden_in, rims, other_rims, vec_in, point_pack, weight, *weight_got],
        scratch=[
            ((seq_size, depth, wide), stack_type),
            ((rows + 2 * RIM, wide), F32),
            ((2 * RIM, width), BF16),
        ],
        after=[upstream],
    )
    weight = swap(weight, "ch", top)
    got_mid = spread(sums_mid, "seq")
    conv_near = gather_parts(conv_own, lower)
    hidden_mid, d_mid, centered, sent_back, vec_mid = call(
        functools.partial(mid_kernel, bin_count=bin_count),
        [
            ((rows, LANES), BF16),
            ((ext, LANES), F32),
            ((ext, LANES), F32),
            ((seq_size, 2, LANES), F32),
            ((8, LANES), F32),
        ],
        [got_mid, conv_out, upstream, rims, norm_mid, point_own],
        after=conv_near[1:],
    )
    got_back = spread(sent_back, "seq")
    grad_own, total_mid = call(
        functools.partial(conv_back_kernel, bin_count=bin_count, slim=slim),
        [((3 * ext // 4 if folds(ext, slim) else ext, LANES), BF16), ((2, LANES), F32)],
        [got_back, vec_mid, d_mid, centered],
        scratch=[((ext, LANES), F32)],
    )
    grad_near = gather_parts(grad_own, lower)
    grad_far = swap(grad_own, "ch", top)
    weight, point_far = call(
        take_kernel,
        [((seq_size, packed, wide), BF16), (point_pack.shape, BF16)],
        [weight],
        after=[grad_own],
    )
    side = ch_size // 2 * wide
    (conv_far,) = call(
        functools.partial(place_kernel, relatives=relatives_of(weight_order), slim=slim),
        [((width, side), BF16)],
        gather_parts(weight, lower),
        scratch=[((seq_size, depth, wide), stack_type)],
    )
    half = seq_size // 2
    hidden_rows = folded_rows(rows, slim)
    terms, kept, sent = call(
        functools.partial(weight_grad_kernel, depth=depth, slim=slim),
        [
            ((rows, wide), BF16),
            ((half, depth, 4 * slim), F32),
            ((half, depth, 4 * slim), BF16),
        ],
        [back, grad_own, hidden_in, cotangent, hidden_mid],
        scratch=[((ext, LANES), F32), ((width, 4 * slim), F32)],
    )
    (up_part,) = call(
        first_half_kernel,
        [((rows, width), F32)],
        [back, terms, *grad_near[1:], *conv_near],
        scratch=[((rows, side), BF16), ((width, side), BF16), ((ext, LANES), F32)],
    )
    grad_far = gather_parts(copies([grad_far], [up_part, conv_far])[0], lower)
    count = point_far.shape[0]
    cuts = [up_to(k * count // 100, 16) for k in (39, 52)]
    hidden_pack, both = call(
        operands_kernel,
        [((hidden_rows, LANES), BF16), ((hidden_rows + count + cuts[0], LANES), BF16)],
        [hidden_mid, point_pack, point_far],
        after=[sent],
    )
    both_parts = gather_parts(both, lower)
    d_in, sums_back = call(
        second_half_kernel,
        [((rows, width), F32), ((2, width), F32)],
        [back, inputs, slope_in, vec_in, up_part, conv_far, *grad_far],
        scratch=[((rows, side), BF16), ((ext, LANES), F32)],
    )
    total_back = sums_back
    hidden_far = swap(hidden_pack, "ch", top)
    placed = []
    scratch = [((size, ch_size // 2 * LANES), BF16) for size in (rows, width)]
    for k, reach in enumerate(sum_order):
        total_got = swap(total_back, "seq", last_order[k])
        got = swap(sent, "seq", reach)
        if k < rounds - 1:
            half //= 2
            kept, sent = call(
                functools.partial(fold_kernel, reach=2 * reach),
                [((half, depth, 4 * slim), F32), ((half, depth, 4 * slim), BF16)],
                [kept, got],
                after=[total_back, *placed] if k else [],
            )
            total_back = add(total_back, total_got)
        if k == rounds - 3:
            (first,) = packs([[hidden_far, (point_far, *cuts)]], [total_back])
            first_parts = gather_parts(first, lower)
            near_sum, *placed = call(
                functools.partial(near_kernel, slim=slim),
                [((rows, width), F32), ((8, LANES), F32)],
                both_parts,
                scratch=scratch,
                after=[total_back],
            )
        if k == rounds - 2:
            (last,) = packs([[(point_far, cuts[1], count)]], [total_back])
            last_parts = gather_parts(last, lower)
    far_parts = [x for group in zip(both_parts, first_parts, last_parts) for x in group]
    block_out, token = call(
        functools.partial(out_kernel, slim=slim),
        [((rows, width), BF16), ((8, LANES), F32)],
        [inputs, near_sum, *far_parts],
        scratch=scratch,
        after=[total_back],
    )
    states = [norm_in, first_in, second_in, master_conv, first_conv, second_conv]
    states += [master_point, first_point, second_point, norm_mid, first_mid, second_mid]
    arrays = [inputs, cotangent, d_in, vec_in, total_back, total_got, kept, got, total_mid]
    small = [(x.shape, F32) for x in states]
    input_grad, *news = call(
        functools.partial(final_kernel, bin_count=bin_count, chunks=4),
        [((rows, width), F32)] + small,
        arrays + states,
        scratch=small + small + [((rows, width), F32)],
        away=range(len(arrays), len(arrays) + 12),
        away_outs=range(13),
        sems=24 + 4,
        after=[token],
    )
    return (block_out, input_grad, *news[3:9], *news[:3], *news[9:])


def solution(mesh):
    in_specs = (
        P("seq", None),
        P("seq", None),
        P(),
        P(None, "seq", "ch"),
        P(None, "seq", "ch"),
        P(None, "seq", "ch"),
        P("ch", "seq"),
        P("ch", "seq"),
        P("ch", "seq"),
        P(),
        P(),
        P(),
        P(None, "ch"),
        P(None, "ch"),
        P(None, "ch"),
    )
    out_specs = (
        P("seq", None),
        P("seq", None),
        P(None, "seq", "ch"),
        P(None, "seq", "ch"),
        P(None, "seq", "ch"),
        P("ch", "seq"),
        P("ch", "seq"),
        P("ch", "seq"),
        P(),
        P(),
        P(),
        P(None, "ch"),
        P(None, "ch"),
        P(None, "ch"),
    )
    return jax.shard_map(shards, mesh=mesh, in_specs=in_specs, out_specs=out_specs, check_vma=False)
```
